32 devices in a mesh: sec: 2 (over x), band: 4 (over y, core), fld: 4 (over z).
Axes of the slice: x: 2, y: 2, z: 4, core: 2. Of those that a mesh axis runs over, the one named last changes fastest.
Arguments:
- grid: bfloat16 [4, 16, 160, 2688], P('fld', 'sec', 'band'), may hold values from -6 to 6
- legendre: bfloat16 [96, 160, 96], P(('band', 'fld'), None, 'sec'), may hold values from -0.5 to 0.5
- counts: int32 [4], replicated, may hold values from 1 to 1024, 2048 in all
- blocks: int32 [4096], P('band'), may hold values from 0 to 839
- interp: bfloat16 [4096, 128], P('band'), may hold values from -0.5 to 0.5
- source_weights: bfloat16 [64, 2048], replicated, may hold values from -0.75 to 0.75
- inverses: bfloat16 [64, 32, 32], replicated, may hold values from -1 to 1
Outputs:
- spectral: bfloat16 [96, 2, 4, 16, 96], P(('band', 'fld'), None, None, None, 'sec')
- heating: bfloat16 [16, 160, 2688], P(('sec', 'fld'), 'band')
The draws below stay inside these ranges and needn't reach their ends.
Inputs may be any that keep to these rules, and one draw needn't show every extreme that they name: Band b has counts[b] live slots, slots 0 to counts[b] - 1; the counts sum to 2048 and the largest is 1024.
All inputs are finite; a program needn't handle non-finite values.
Results may differ from the reference program's by a relative error of at most 0.0085.
Values may be sent and summed in bfloat16 or wider, within the bound.
No kernel may reach another device: no remote copies, remote signals or barrier semaphores. Data moves between devices by JAX's collectives and lax.ppermute only.
A program may use at most 64 MiB of HBM per device.

```python
import math
import jax
import jax.numpy as jnp
import numpy as np
from jax import lax

FIELDS = 4
LEV = 16
LON = 2688
LAT_DEV = 40
LAT = 160
M = 96
BANDS = 64
FLUX = 32
CAP = 1024
NBLK = 840
COARSE = 2048
N_BAND = 4


def with_ends(entries, rng, low, high):
    dims = entries.shape
    index_at = [jax.random.randint(jax.random.fold_in(rng, axis), (), 0, dims[axis]) for axis in range(len(dims))]
    entries = entries.at[tuple(index_at)].set(low)
    longest = dims.index(max(dims))
    index_at[longest] = (index_at[longest] + 1) % dims[longest]
    return entries.at[tuple(index_at)].set(high)


def steps_of(stream_key, dims, cuts, smallest, top_value):
    factor_of = 1.0
    for dim, shards_of in cuts:
        heights = jax.random.uniform(jax.random.fold_in(jax.random.fold_in(stream_key, 6), dim), (shards_of,), jnp.float32, smallest / len(cuts), top_value / len(cuts))
        factor_of = factor_of * jnp.repeat(jnp.exp(heights), dims[dim] // shards_of).reshape((-1,) + (1,) * (len(dims) - 1 - dim))
    return factor_of


def split_up(number_of, total, most, slope):
    portions = [(1 << 20) // math.isqrt(standing ** slope) + 1 for standing in range(2, number_of + 1)]
    rest, holding = total - most - (number_of - 1), [1] * (number_of - 1)
    while rest > 0:
        candidates = [i for i in range(number_of - 1) if holding[i] < most]
        mass, remaining = sum([portions[i] for i in candidates]), rest
        for i in candidates:
            addition = min(most - holding[i], max(1, remaining * portions[i] // mass), rest)
            holding[i] = holding[i] + addition
            rest = rest - addition
    return np.array([most] + holding)


def uneven_parts(own_key, count, total, limit, lean):
    if count == 2:
        one = jax.random.randint(own_key, (), max(1, total - limit), min(limit, total - 1) + 1)
        return jnp.stack([one, total - one])
    tallies = jnp.asarray(split_up(count, total, limit, lean), jnp.int32)
    pairs = (count - 1) // 2
    donor, receiver = tallies[1:1 + 2 * pairs:2], tallies[2:2 + 2 * pairs:2]
    margin = jnp.minimum(donor - 1, limit - receiver)
    shifted = jax.random.randint(jax.random.fold_in(own_key, 1), (pairs,), 0, 1 << 20) % (margin + 1)
    tallies = tallies.at[1:1 + 2 * pairs:2].set(donor - shifted).at[2:2 + 2 * pairs:2].set(receiver + shifted)
    return tallies[jax.random.permutation(jax.random.fold_in(own_key, 2), count)]


def scatter_about(stream_key, dims, scale, reach, split=(), kind=jnp.bfloat16):
    array = scale * jax.random.normal(stream_key, dims, jnp.float32)
    if split:
        array = array * steps_of(stream_key, dims, split, -0.22, 0.18)
    return jnp.clip(array, -reach, reach).astype(kind)


def setup_inputs(seed: int = 0) -> dict:
    streams_of = jax.random.split(jax.random.key(seed), 8)
    return {
        "grid": scatter_about(streams_of[0], (FIELDS, LEV, LAT, LON), 1.0, 6.0, ((0, 4), (1, 2), (2, 4))),
        "legendre": scatter_about(streams_of[1], (M, LAT, M), LAT ** -0.5, 0.5, ((0, 16), (2, 2))),
        "counts": uneven_parts(streams_of[2], N_BAND, COARSE, CAP, 2).astype(jnp.int32),
        "blocks": with_ends(jax.random.randint(streams_of[3], (N_BAND * CAP,), 0, NBLK), jax.random.fold_in(streams_of[3], 1), 0, NBLK - 1).astype(jnp.int32),
        "interp": scatter_about(streams_of[4], (N_BAND * CAP, 128), 128 ** -0.5, 0.5, ((0, 4),)),
        "source_weights": scatter_about(streams_of[5], (FIELDS * LEV, BANDS * FLUX), (FIELDS * LEV) ** -0.5, 0.75),
        "inverses": scatter_about(streams_of[6], (BANDS, FLUX, FLUX), FLUX ** -0.5, 1.0),
    }


def dft_table(lon, waves):
    column = jnp.arange(2 * waves, dtype=jnp.int32)
    wave = column // 2
    part = column % 2
    place = jnp.arange(lon, dtype=jnp.int32)
    phase = place[:, None] * wave[None, :] % lon
    angle = phase.astype(jnp.float32) * (2.0 * math.pi / lon)
    values = jnp.where(part[None, :] == 0, jnp.cos(angle), -jnp.sin(angle))
    return (values * (1.0 / math.sqrt(lon))).astype(jnp.bfloat16)

def heat_rates(flux, count, start):
    levels = flux.shape[0] // 2
    width = flux.shape[1]
    upward = flux[:levels]
    downward = flux[levels:]
    empty = jnp.zeros((1, width), jnp.float32)
    up_next = jnp.concatenate([upward[1:], empty], axis=0)
    down_next = jnp.concatenate([downward[1:], empty], axis=0)
    heat = upward - up_next - (downward - down_next)
    slots = start + jnp.arange(width, dtype=jnp.int32)
    heat = jnp.where(slots[None, :] < count, heat, jnp.zeros_like(heat))
    return heat.astype(jnp.bfloat16)

def reference(grid, legendre, counts, blocks, interp, source_weights, inverses):
    table = dft_table(LON, M)
    fourier = jnp.dot(grid.reshape(FIELDS * LEV * LAT, LON), table, preferred_element_type=jnp.float32)
    fourier = fourier.astype(jnp.bfloat16).reshape(FIELDS, LEV, LAT, M, 2)
    fourier = jnp.transpose(fourier, (3, 0, 1, 2, 4))

    def legendre_one(pair):
        data, weights = pair
        out = jnp.einsum('flar,an->rfln', data.astype(jnp.float32), weights.astype(jnp.float32))
        return out.astype(jnp.bfloat16)
    spectral = lax.map(legendre_one, (fourier, legendre))
    patches = grid.reshape(FIELDS, LEV, N_BAND, NBLK, 128)
    patches = jnp.transpose(patches, (2, 0, 1, 3, 4))
    band_blocks = blocks.reshape(N_BAND, CAP)
    band_weights = interp.reshape(N_BAND, CAP, 128)

    def band_one(item):
        patch, chosen, weights, count = item
        picked = jnp.take(patch, chosen, axis=2)
        state = jnp.einsum('fljk,jk->flj', picked.astype(jnp.float32), weights.astype(jnp.float32))
        state = state.astype(jnp.bfloat16).reshape(FIELDS * LEV, CAP)
        gates = jnp.dot(source_weights.T, state, preferred_element_type=jnp.float32)
        source = jax.nn.softplus(gates).astype(jnp.bfloat16).reshape(BANDS, FLUX, CAP)
        flux = jnp.einsum('bpq,bqj->pj', inverses.astype(jnp.float32), source.astype(jnp.float32))
        heat = heat_rates(flux, count, jnp.int32(0))
        spread = heat.astype(jnp.float32)[:, :, None] * weights.astype(jnp.float32)[None, :, :]
        summed = jax.ops.segment_sum(jnp.transpose(spread, (1, 0, 2)), chosen, num_segments=NBLK)
        return jnp.transpose(summed, (1, 0, 2)).reshape(LEV, LAT_DEV, LON).astype(jnp.bfloat16)
    heating = lax.map(band_one, (patches, band_blocks, band_weights, counts))
    heating = jnp.transpose(heating, (1, 0, 2, 3)).reshape(LEV, LAT, LON)
    return (spectral, heating)
```

```python
import functools
import math

import jax
import jax.numpy as jnp
import numpy as np
from jax import lax
from jax.experimental import pallas as pl
from jax.experimental.pallas import tpu as pltpu
from jax.sharding import PartitionSpec as P

BF16 = jnp.bfloat16
F32 = jnp.float32
LANES = 128
THIRDS = 3
VMEM = pl.BlockSpec(memory_space=pltpu.VMEM)
SMEM = pl.BlockSpec(memory_space=pltpu.SMEM)
LIMIT = 40 * 1024 * 1024
NT = (((1,), (1,)), ((), ()))


def dft_table(lon, wave_dev, n_band, n_fld):
    values_dev = 2 * wave_dev
    rest = values_dev // THIRDS
    third, fld, band, low = np.meshgrid(
        np.arange(THIRDS), np.arange(n_fld), np.arange(n_band), np.arange(rest), indexing="ij"
    )
    value = third * rest + low
    wave = ((band * n_fld + fld) * wave_dev + value // 2).reshape(-1)
    part = (value % 2).reshape(-1)
    phase = np.arange(lon, dtype=np.int64)[:, None] * wave[None, :] % lon
    angle = phase * (2.0 * math.pi / lon)
    values = np.where(part[None, :] == 0, np.cos(angle), -np.sin(angle)) / math.sqrt(lon)
    return values.astype(np.float32).astype(BF16)


def dft_kernel(lev, lat, n_fld, place, grid, table, *refs):
    outs, (padded, rows) = refs[:n_fld], refs[n_fld:]
    coeffs = jnp.dot(grid[...], table[...], preferred_element_type=F32)
    group = coeffs.shape[1] // THIRDS
    padded[...] = jnp.zeros_like(padded)
    for level in range(lev):
        one = coeffs[level * lat : (level + 1) * lat]
        for third in range(THIRDS):
            padded[third * lat : (third + 1) * lat, :group] = one[
                :, third * group : (third + 1) * group
            ]
        rows[pl.ds(level, group, stride=lev), :] = jnp.transpose(padded[...])[:group]
    size = outs[0].shape[0]
    for shift in range(n_fld):
        start = pl.multiple_of((place[0] ^ shift) * size, size)
        outs[shift][...] = rows[pl.ds(start, size), :].astype(BF16)


def regroup_kernel(n_fld, n_band, place, *refs):
    pieces, outs = refs[:n_fld], refs[n_fld:]
    size = outs[0].shape[0] // n_fld
    for shift in range(n_band):
        start = pl.multiple_of((place[1] ^ shift) * size, size)
        for piece in range(n_fld):
            outs[shift][piece * size : (piece + 1) * size, :] = pieces[piece][pl.ds(start, size), :]


def spread_kernel(lat, n_band, legendre, out, wide):
    waves, degrees, _ = legendre.shape
    wide[...] = jnp.zeros_like(wide)
    lane = lax.broadcasted_iota(jnp.int32, (degrees, LANES), 1)
    for wave in range(waves):
        third, parity = wave // 2, wave % 2
        wide[:, : n_band * lat] = legendre[wave].astype(F32)
        place = third * lat
        live = (lane >= place) & (lane < place + lat)
        for band in range(n_band):
            base = band * lat // LANES * LANES
            moved = pltpu.roll(
                wide[:, base : base + 2 * LANES], (place - (band * lat - base)) % (2 * LANES), 1
            )
            out[band, parity, third * degrees : (third + 1) * degrees, :] = jnp.where(
                live, moved[:, :LANES], 0.0
            ).astype(BF16)


def legendre_kernel(n_sec, n_band, n_fld, lev, place, weights, *refs):
    pieces, out = refs[: n_sec * n_band], refs[n_sec * n_band]
    degrees = out.shape[4]
    size = pieces[0].shape[0] // n_fld
    half = size // 2
    first = place[2] == 0
    for parity in range(2):
        basis = jnp.concatenate(
            [weights[place[1] ^ shift, parity] for shift in range(n_band)], axis=1
        )
        left = jnp.concatenate(
            [
                jnp.concatenate(
                    [
                        pieces[sec * n_band + shift][
                            fld * size + parity * half : fld * size + (parity + 1) * half, :
                        ]
                        for shift in range(n_band)
                    ],
                    axis=1,
                )
                for sec in range(n_sec)
                for fld in range(n_fld)
            ],
            axis=0,
        )
        result = lax.dot_general(left, basis, NT, preferred_element_type=F32)
        for third in range(THIRDS):
            part = result[:, third * degrees : (third + 1) * degrees]
            for fld in range(n_fld):
                for real in range(2):
                    near = part[fld * half + real * lev : fld * half + (real + 1) * lev]
                    base = (n_fld + fld) * half + real * lev
                    far = part[base : base + lev]
                    levels = jnp.concatenate(
                        [jnp.where(first, near, far), jnp.where(first, far, near)], axis=0
                    )
                    out[2 * third + parity, real, place[0] ^ fld] = levels.astype(BF16)


def slot_rows(blocks, across, lat_pad):
    shift = 16
    factor = -(-(1 << shift) // across)
    lat = lax.shift_right_logical(blocks * factor, shift)
    return (blocks - lat * across) * lat_pad + lat


def pick_kernel(lat_pad, grid, blocks, interp, state, patch, column):
    lev, lat, lon = grid.shape
    across = lon // LANES
    slots = interp.shape[0]
    depth = patch.shape[0]
    for tile in range(across):
        patch[tile * lat_pad + lat : (tile + 1) * lat_pad, :] = jnp.zeros(
            (lat_pad - lat, lev * LANES), BF16
        )
        for level in range(lev):
            patch[
                tile * lat_pad : tile * lat_pad + lat, level * LANES : (level + 1) * LANES
            ] = grid[level, :, tile * LANES : (tile + 1) * LANES]
    if depth > across * lat_pad:
        patch[across * lat_pad :, :] = jnp.zeros((depth - across * lat_pad, lev * LANES), BF16)
    row = slot_rows(blocks[...], across, lat_pad)
    column[...] = jnp.transpose(jnp.broadcast_to(row, (LANES, slots)))
    chunk = 256
    lane = lax.broadcasted_iota(jnp.int32, (chunk, LANES), 1)
    for start in range(0, slots, chunk):
        mine = column[start : start + chunk, :]
        selector = jnp.concatenate(
            [
                jnp.where(mine == lane + base, 1.0, 0.0).astype(BF16)
                for base in range(0, depth, LANES)
            ],
            axis=1,
        )
        picked = jnp.dot(selector, patch[...], preferred_element_type=F32)
        weights = interp[start : start + chunk, :].astype(F32)
        total = jnp.zeros((chunk, LANES), F32)
        for level in range(lev):
            product = picked[:, level * LANES : (level + 1) * LANES] * weights
            total = jnp.where(lane == level, jnp.sum(product, axis=1, keepdims=True), total)
        state[:, start : start + chunk] = jnp.transpose(total)[:lev].astype(BF16)


def softplus(x):
    small = jnp.exp(-jnp.abs(x))
    tail = jnp.where(small < 2.0**-11, small, jnp.log(1.0 + small))
    return jnp.maximum(x, 0.0) + tail


def column_kernel(n_sec, n_fld, lat_pad, place, counts, weights, inverses, blocks, interp, *refs):
    pieces = refs[: n_sec * n_fld]
    out, state, flux_up, flux_down = refs[n_sec * n_fld :]
    lev = pieces[0].shape[0]
    slots = pieces[0].shape[1]
    for sec in range(n_sec):
        for fld in range(n_fld):
            row = ((place[0] ^ fld) * n_sec + (place[2] ^ sec)) * lev
            state[pl.ds(pl.multiple_of(row, lev), lev), :] = pieces[sec * n_fld + fld][...].astype(F32)
    column = state[...].astype(BF16)
    flux_rows = inverses.shape[0]
    flux = jnp.zeros((flux_rows, slots), F32)
    chunk = 256
    for start in range(0, weights.shape[0], chunk):
        gates = jnp.dot(weights[start : start + chunk, :], column, preferred_element_type=F32)
        source = softplus(gates).astype(BF16)
        flux = flux + jnp.dot(
            inverses[:, start : start + chunk], source, preferred_element_type=F32
        )
    levels = flux_rows // 2
    flux_up[:levels, :] = flux[:levels]
    flux_down[:levels, :] = flux[levels:]
    flux_up[levels:, :] = jnp.zeros((8, slots), F32)
    flux_down[levels:, :] = jnp.zeros((8, slots), F32)
    mine, lat, lon = out.shape
    across = lon // LANES
    live = lax.broadcasted_iota(jnp.int32, (1, slots), 1) < counts[place[1]]
    base = (place[2] * n_fld + place[0]) * mine
    heats = []
    for level in range(mine):
        at = base + level
        heat = (flux_up[pl.ds(at, 1), :] - flux_up[pl.ds(at + 1, 1), :]) - (
            flux_down[pl.ds(at, 1), :] - flux_down[pl.ds(at + 1, 1), :]
        )
        heats.append(jnp.where(live, heat, 0.0).astype(BF16).astype(F32))
    row = slot_rows(blocks[...], across, lat_pad)
    tiles = max(t for t in range(1, 8) if across % t == 0)
    height = tiles * lat_pad
    for first in range(0, across, tiles):
        match = row == lax.broadcasted_iota(jnp.int32, (height, slots), 0) + first * lat_pad
        for level in range(mine):
            left = jnp.where(match, heats[level], 0.0).astype(BF16)
            summed = jnp.dot(left, interp[...], preferred_element_type=F32).astype(BF16)
            for tile in range(tiles):
                out[level, :, (first + tile) * LANES : (first + tile + 1) * LANES] = summed[
                    tile * lat_pad : tile * lat_pad + lat
                ]


def call(kernel, outs, specs, scratch, args, flops, size, name):
    shapes = [jax.ShapeDtypeStruct(shape, dtype) for shape, dtype in outs]
    single = len(outs) == 1
    return pl.pallas_call(
        kernel,
        out_shape=shapes[0] if single else shapes,
        in_specs=specs,
        out_specs=VMEM if single else [VMEM] * len(outs),
        scratch_shapes=scratch,
        compiler_params=pltpu.CompilerParams(vmem_limit_bytes=LIMIT),
        cost_estimate=pl.CostEstimate(flops=flops, bytes_accessed=size, transcendentals=0),
        name=name,
    )(*args)


def exchange(value, axes, shifts):
    sizes = [lax.axis_size(axis) for axis in axes]
    pairs = []
    for i in range(math.prod(sizes)):
        at = np.unravel_index(i, sizes)
        to = tuple(int(a) ^ s for a, s in zip(at, shifts))
        pairs.append((i, int(np.ravel_multi_index(to, sizes))))
    return lax.ppermute(value, axes, pairs)


def body(grid, legendre, counts, blocks, interp, source_weights, inverses):
    n_sec = lax.axis_size("sec")
    n_band = lax.axis_size("band")
    n_fld = lax.axis_size("fld")
    lev, lat, lon = grid.shape[1:]
    wave_dev, _, degrees = legendre.shape
    slots = blocks.shape[0]
    across = lon // LANES
    lat_pad = -(-lat // 16) * 16
    rest = 2 * wave_dev // THIRDS
    piece = rest * lev
    place = jnp.stack([lax.axis_index("fld"), lax.axis_index("band"), lax.axis_index("sec")]).astype(
        jnp.int32
    )
    block_row = blocks.reshape(1, slots)

    table = jnp.asarray(dft_table(lon, wave_dev, n_band, n_fld))
    group = n_fld * n_band * rest
    padded_group = -(-group // LANES) * LANES
    sent = call(
        functools.partial(dft_kernel, lev, lat, n_fld),
        [((n_band * piece, LANES), BF16)] * n_fld,
        [SMEM, VMEM, VMEM],
        [pltpu.VMEM((LANES, padded_group), F32), pltpu.VMEM((group * lev, LANES), F32)],
        (place, grid.reshape(lev * lat, lon), table),
        2 * lev * lat * lon * THIRDS * group,
        2 * lon * (lev * lat + THIRDS * group),
        "fourier",
    )
    fields = [sent[0]] + [exchange(sent[d], ("fld",), (d,)) for d in range(1, n_fld)]

    depth = -(-across * lat_pad // LANES) * LANES
    state = call(
        functools.partial(pick_kernel, lat_pad),
        [((lev, slots), BF16)],
        [VMEM, VMEM, VMEM],
        [pltpu.VMEM((depth, lev * LANES), BF16), pltpu.VMEM((slots, LANES), jnp.int32)],
        (grid.reshape(lev, lat, lon), block_row, interp),
        2 * slots * depth * lev * LANES,
        2 * lev * lat * lon + 2 * slots * LANES,
        "pick",
    )
    columns = [
        state if sec == 0 and fld == 0 else exchange(state, ("sec", "fld"), (sec, fld))
        for sec in range(n_sec)
        for fld in range(n_fld)
    ]

    basis = call(
        functools.partial(spread_kernel, lat, n_band),
        [((n_band, 2, THIRDS * degrees, LANES), BF16)],
        [VMEM],
        [pltpu.VMEM((degrees, (n_band * lat // LANES + 2) * LANES), F32)],
        (jnp.swapaxes(legendre, 1, 2),),
        0,
        8 * wave_dev * degrees * n_band * LANES,
        "basis",
    )
    grouped = call(
        functools.partial(regroup_kernel, n_fld, n_band),
        [((n_fld * piece, LANES), BF16)] * n_band,
        [SMEM] + [VMEM] * n_fld,
        [],
        (place, *fields),
        0,
        4 * n_fld * n_band * piece * LANES,
        "regroup",
    )
    bands = [
        grouped[0] if sec == 0 and band == 0 else exchange(grouped[band], ("sec", "band"), (sec, band))
        for sec in range(n_sec)
        for band in range(n_band)
    ]

    spec_bands, flux_rows, _ = inverses.shape
    heating = call(
        functools.partial(column_kernel, n_sec, n_fld, lat_pad),
        [((n_sec * lev // (n_sec * n_fld), lat, lon), BF16)],
        [SMEM, SMEM] + [VMEM] * (4 + n_sec * n_fld),
        [
            pltpu.VMEM((n_sec * n_fld * lev, slots), F32),
            pltpu.VMEM((flux_rows // 2 + 8, slots), F32),
            pltpu.VMEM((flux_rows // 2 + 8, slots), F32),
        ],
        (
            place,
            counts,
            jnp.transpose(source_weights),
            jnp.transpose(inverses, (1, 0, 2)).reshape(flux_rows, spec_bands * flux_rows),
            block_row,
            interp,
            *columns,
        ),
        8 * slots * slots * 1024,
        2 * slots * slots,
        "columns",
    )

    spectral = call(
        functools.partial(legendre_kernel, n_sec, n_band, n_fld, lev),
        [((wave_dev, 2, n_fld, n_sec * lev, degrees), BF16)],
        [SMEM] + [VMEM] * (1 + n_sec * n_band),
        [],
        (place, basis, *bands),
        4 * n_sec * n_fld * piece * n_band * LANES * degrees * THIRDS,
        2 * n_sec * n_band * n_fld * piece * LANES,
        "legendre",
    )
    return (spectral, heating)


def solution(mesh):
    return jax.shard_map(
        body,
        mesh=mesh,
        in_specs=(
            P("fld", "sec", "band", None),
            P(("band", "fld"), None, "sec"),
            P(),
            P("band"),
            P("band", None),
            P(),
            P(),
        ),
        out_specs=(P(("band", "fld"), None, None, None, "sec"), P(("sec", "fld"), "band", None)),
        check_vma=False,
    )
```

```python
import functools
import math

import jax
import jax.numpy as jnp
import numpy as np
from jax import lax
from jax.experimental import pallas as pl
from jax.experimental.pallas import tpu as pltpu
from jax.sharding import PartitionSpec as P

BF16 = jnp.bfloat16
F32 = jnp.float32
LANES = 128
THIRDS = 3
VMEM = pl.BlockSpec(memory_space=pltpu.VMEM)
SMEM = pl.BlockSpec(memory_space=pltpu.SMEM)
LIMIT = 40 * 1024 * 1024
NT = (((1,), (1,)), ((), ()))


def dft_table(lon, wave_dev, n_band, n_fld):
    values_dev = 2 * wave_dev
    rest = values_dev // THIRDS
    third, band, fld, low = np.meshgrid(
        np.arange(THIRDS), np.arange(n_band), np.arange(n_fld), np.arange(rest), indexing="ij"
    )
    value = third * rest + low
    wave = ((band * n_fld + fld) * wave_dev + value // 2).reshape(-1)
    part = (value % 2).reshape(-1)
    phase = np.arange(lon, dtype=np.int64)[:, None] * wave[None, :] % lon
    angle = phase * (2.0 * math.pi / lon)
    values = np.where(part[None, :] == 0, np.cos(angle), -np.sin(angle)) / math.sqrt(lon)
    return values.astype(np.float32).astype(BF16)


def dft_kernel(lev, lat, n_sec, n_band, n_fld, grid, table, out, padded, rows):
    coeffs = jnp.dot(grid[...], table[...], preferred_element_type=F32)
    group = coeffs.shape[1] // THIRDS
    padded[...] = jnp.zeros_like(padded)
    for level in range(lev):
        one = coeffs[level * lat : (level + 1) * lat]
        for third in range(THIRDS):
            padded[third * lat : (third + 1) * lat, :group] = one[
                :, third * group : (third + 1) * group
            ]
        rows[pl.ds(level, group, stride=lev), :] = jnp.transpose(padded[...])[:group]
    size = out.shape[1]
    values = rows[...].astype(BF16).reshape(n_band * n_fld, size, LANES)
    for sec in range(n_sec):
        out[sec * n_band * n_fld : (sec + 1) * n_band * n_fld] = values


def spread_kernel(lat, n_band, legendre, out, wide):
    waves, degrees, _ = legendre.shape
    wide[...] = jnp.zeros_like(wide)
    lane = lax.broadcasted_iota(jnp.int32, (degrees, LANES), 1)
    for wave in range(waves):
        third, parity = wave // 2, wave % 2
        wide[:, : n_band * lat] = legendre[wave].astype(F32)
        place = third * lat
        live = (lane >= place) & (lane < place + lat)
        for band in range(n_band):
            base = band * lat // LANES * LANES
            moved = pltpu.roll(
                wide[:, base : base + 2 * LANES], (place - (band * lat - base)) % (2 * LANES), 1
            )
            out[band, parity, third * degrees : (third + 1) * degrees, :] = jnp.where(
                live, moved[:, :LANES], 0.0
            ).astype(BF16)


def legendre_kernel(n_sec, n_band, n_fld, lev, weights, pieces, out):
    degrees = out.shape[4]
    half = pieces.shape[1] // 2
    for parity in range(2):
        rows = slice(parity * half, (parity + 1) * half)
        basis = jnp.concatenate([weights[band, parity] for band in range(n_band)], axis=1)
        left = jnp.concatenate(
            [
                jnp.concatenate(
                    [
                        pieces[(sec * n_band + band) * n_fld + fld, rows, :]
                        for band in range(n_band)
                    ],
                    axis=1,
                )
                for fld in range(n_fld)
                for sec in range(n_sec)
            ],
            axis=0,
        )
        result = lax.dot_general(left, basis, NT, preferred_element_type=F32)
        for third in range(THIRDS):
            part = result[:, third * degrees : (third + 1) * degrees]
            for fld in range(n_fld):
                for real in range(2):
                    levels = [
                        part[(fld * n_sec + sec) * half + real * lev :][:lev]
                        for sec in range(n_sec)
                    ]
                    out[2 * third + parity, real, fld] = jnp.concatenate(levels, axis=0).astype(
                        BF16
                    )


def slot_rows(blocks, across, lat_pad):
    shift = 16
    factor = -(-(1 << shift) // across)
    lat = lax.shift_right_logical(blocks * factor, shift)
    return (blocks - lat * across) * lat_pad + lat


def pick_kernel(lat_pad, grid, blocks, interp, state, patch, column):
    lev, lat, lon = grid.shape
    across = lon // LANES
    slots = interp.shape[0]
    depth = patch.shape[0]
    for tile in range(across):
        patch[tile * lat_pad + lat : (tile + 1) * lat_pad, :] = jnp.zeros(
            (lat_pad - lat, lev * LANES), BF16
        )
        for level in range(lev):
            patch[
                tile * lat_pad : tile * lat_pad + lat, level * LANES : (level + 1) * LANES
            ] = grid[level, :, tile * LANES : (tile + 1) * LANES]
    if depth > across * lat_pad:
        patch[across * lat_pad :, :] = jnp.zeros((depth - across * lat_pad, lev * LANES), BF16)
    row = slot_rows(blocks[...], across, lat_pad)
    column[...] = jnp.transpose(jnp.broadcast_to(row, (LANES, slots)))
    chunk = 256
    lane = lax.broadcasted_iota(jnp.int32, (chunk, LANES), 1)
    for start in range(0, slots, chunk):
        mine = column[start : start + chunk, :]
        selector = jnp.concatenate(
            [
                jnp.where(mine == lane + base, 1.0, 0.0).astype(BF16)
                for base in range(0, depth, LANES)
            ],
            axis=1,
        )
        picked = jnp.dot(selector, patch[...], preferred_element_type=F32)
        weights = interp[start : start + chunk, :].astype(F32)
        total = jnp.zeros((chunk, LANES), F32)
        for level in range(lev):
            product = picked[:, level * LANES : (level + 1) * LANES] * weights
            total = jnp.where(lane == level, jnp.sum(product, axis=1, keepdims=True), total)
        values = jnp.transpose(total)[:lev].astype(BF16)
        for copy in range(state.shape[0]):
            state[copy, :, start : start + chunk] = values


def softplus(x):
    small = jnp.exp(-jnp.abs(x))
    tail = jnp.where(small < 2.0**-11, small, jnp.log(1.0 + small))
    return jnp.maximum(x, 0.0) + tail


def column_kernel(n_sec, n_fld, lat_pad, place, counts, weights, inverses, blocks, interp, pieces,
                  out, state, flux_up, flux_down):
    lev, slots = pieces.shape[1:]
    for fld in range(n_fld):
        for sec in range(n_sec):
            row = (fld * n_sec + sec) * lev
            state[row : row + lev, :] = pieces[sec * n_fld + fld].astype(F32)
    column = state[...].astype(BF16)
    flux_rows = inverses.shape[0]
    flux = jnp.zeros((flux_rows, slots), F32)
    chunk = 256
    for start in range(0, weights.shape[0], chunk):
        gates = jnp.dot(weights[start : start + chunk, :], column, preferred_element_type=F32)
        source = softplus(gates).astype(BF16)
        flux = flux + jnp.dot(
            inverses[:, start : start + chunk], source, preferred_element_type=F32
        )
    levels = flux_rows // 2
    flux_up[:levels, :] = flux[:levels]
    flux_down[:levels, :] = flux[levels:]
    flux_up[levels:, :] = jnp.zeros((8, slots), F32)
    flux_down[levels:, :] = jnp.zeros((8, slots), F32)
    mine, lat, lon = out.shape
    across = lon // LANES
    live = lax.broadcasted_iota(jnp.int32, (1, slots), 1) < counts[place[1]]
    base = (place[2] * n_fld + place[0]) * mine
    heats = []
    for level in range(mine):
        at = base + level
        heat = (flux_up[pl.ds(at, 1), :] - flux_up[pl.ds(at + 1, 1), :]) - (
            flux_down[pl.ds(at, 1), :] - flux_down[pl.ds(at + 1, 1), :]
        )
        heats.append(jnp.where(live, heat, 0.0).astype(BF16).astype(F32))
    row = slot_rows(blocks[...], across, lat_pad)
    tiles = max(t for t in range(1, 8) if across % t == 0)
    height = tiles * lat_pad
    for first in range(0, across, tiles):
        match = row == lax.broadcasted_iota(jnp.int32, (height, slots), 0) + first * lat_pad
        for level in range(mine):
            left = jnp.where(match, heats[level], 0.0).astype(BF16)
            summed = jnp.dot(left, interp[...], preferred_element_type=F32).astype(BF16)
            for tile in range(tiles):
                out[level, :, (first + tile) * LANES : (first + tile + 1) * LANES] = summed[
                    tile * lat_pad : tile * lat_pad + lat
                ]


def call(kernel, outs, specs, scratch, args, flops, size, name):
    shapes = [jax.ShapeDtypeStruct(shape, dtype) for shape, dtype in outs]
    single = len(outs) == 1
    return pl.pallas_call(
        kernel,
        out_shape=shapes[0] if single else shapes,
        in_specs=specs,
        out_specs=VMEM if single else [VMEM] * len(outs),
        scratch_shapes=scratch,
        compiler_params=pltpu.CompilerParams(vmem_limit_bytes=LIMIT),
        cost_estimate=pl.CostEstimate(flops=flops, bytes_accessed=size, transcendentals=0),
        name=name,
    )(*args)


def body(grid, legendre, counts, blocks, interp, source_weights, inverses):
    n_sec = lax.axis_size("sec")
    n_band = lax.axis_size("band")
    n_fld = lax.axis_size("fld")
    lev, lat, lon = grid.shape[1:]
    wave_dev, _, degrees = legendre.shape
    slots = blocks.shape[0]
    across = lon // LANES
    lat_pad = -(-lat // 16) * 16
    rest = 2 * wave_dev // THIRDS
    piece = rest * lev
    place = jnp.stack([lax.axis_index("fld"), lax.axis_index("band"), lax.axis_index("sec")]).astype(
        jnp.int32
    )
    block_row = blocks.reshape(1, slots)

    table = jnp.asarray(dft_table(lon, wave_dev, n_band, n_fld))
    group = n_fld * n_band * rest
    padded_group = -(-group // LANES) * LANES
    devices = n_sec * n_band * n_fld
    sent = call(
        functools.partial(dft_kernel, lev, lat, n_sec, n_band, n_fld),
        [((devices, piece, LANES), BF16)],
        [VMEM, VMEM],
        [pltpu.VMEM((LANES, padded_group), F32), pltpu.VMEM((group * lev, LANES), F32)],
        (grid.reshape(lev * lat, lon), table),
        2 * lev * lat * lon * THIRDS * group,
        2 * lon * (lev * lat + THIRDS * group),
        "fourier",
    )
    depth = -(-across * lat_pad // LANES) * LANES
    state = call(
        functools.partial(pick_kernel, lat_pad),
        [((n_sec * n_fld, lev, slots), BF16)],
        [VMEM, VMEM, VMEM],
        [pltpu.VMEM((depth, lev * LANES), BF16), pltpu.VMEM((slots, LANES), jnp.int32)],
        (grid.reshape(lev, lat, lon), block_row, interp),
        2 * slots * depth * lev * LANES,
        2 * lev * lat * lon + 2 * slots * LANES,
        "pick",
    )
    columns = lax.all_to_all(state, ("sec", "fld"), 0, 0, tiled=True)
    pieces = lax.all_to_all(sent, ("sec", "band", "fld"), 0, 0, tiled=True)
    basis = call(
        functools.partial(spread_kernel, lat, n_band),
        [((n_band, 2, THIRDS * degrees, LANES), BF16)],
        [VMEM],
        [pltpu.VMEM((degrees, (n_band * lat // LANES + 2) * LANES), F32)],
        (jnp.swapaxes(legendre, 1, 2),),
        0,
        8 * wave_dev * degrees * n_band * LANES,
        "basis",
    )

    spec_bands, flux_rows, _ = inverses.shape
    heating = call(
        functools.partial(column_kernel, n_sec, n_fld, lat_pad),
        [((n_sec * lev // (n_sec * n_fld), lat, lon), BF16)],
        [SMEM, SMEM] + [VMEM] * 5,
        [
            pltpu.VMEM((n_sec * n_fld * lev, slots), F32),
            pltpu.VMEM((flux_rows // 2 + 8, slots), F32),
            pltpu.VMEM((flux_rows // 2 + 8, slots), F32),
        ],
        (
            place,
            counts,
            jnp.transpose(source_weights),
            jnp.transpose(inverses, (1, 0, 2)).reshape(flux_rows, spec_bands * flux_rows),
            block_row,
            interp,
            columns,
        ),
        8 * slots * slots * 1024,
        2 * slots * slots,
        "columns",
    )

    spectral = call(
        functools.partial(legendre_kernel, n_sec, n_band, n_fld, lev),
        [((wave_dev, 2, n_fld, n_sec * lev, degrees), BF16)],
        [VMEM, VMEM],
        [],
        (basis, pieces),
        4 * n_sec * n_fld * piece * n_band * LANES * degrees * THIRDS,
        2 * n_sec * n_band * n_fld * piece * LANES,
        "legendre",
    )
    return (spectral, heating)


def solution(mesh):
    return jax.shard_map(
        body,
        mesh=mesh,
        in_specs=(
            P("fld", "sec", "band", None),
            P(("band", "fld"), None, "sec"),
            P(),
            P("band"),
            P("band", None),
            P(),
            P(),
        ),
        out_specs=(P(("band", "fld"), None, None, None, "sec"), P(("sec", "fld"), "band", None)),
        check_vma=False,
    )
```

```python
import functools
import math

import jax
import jax.numpy as jnp
import numpy as np
from jax import lax
from jax.experimental import pallas as pl
from jax.experimental.pallas import tpu as pltpu
from jax.sharding import PartitionSpec as P

BF16 = jnp.bfloat16
F32 = jnp.float32
LANES = 128
THIRDS = 3
VMEM = pl.BlockSpec(memory_space=pltpu.VMEM)
SMEM = pl.BlockSpec(memory_space=pltpu.SMEM)
LIMIT = 40 * 1024 * 1024
NT = (((1,), (1,)), ((), ()))


def dft_table(lon, wave_dev, n_band, n_fld):
    values_dev = 2 * wave_dev
    rest = values_dev // THIRDS
    third, band, fld, low = np.meshgrid(
        np.arange(THIRDS), np.arange(n_band), np.arange(n_fld), np.arange(rest), indexing="ij"
    )
    value = third * rest + low
    wave = ((band * n_fld + fld) * wave_dev + value // 2).reshape(-1)
    part = (value % 2).reshape(-1)
    phase = np.arange(lon, dtype=np.int64)[:, None] * wave[None, :] % lon
    angle = phase * (2.0 * math.pi / lon)
    values = np.where(part[None, :] == 0, np.cos(angle), -np.sin(angle)) / math.sqrt(lon)
    return values.astype(np.float32).astype(BF16)


def dft_kernel(lev, lat, n_sec, n_band, n_fld, grid, table, out, padded, rows):
    coeffs = jnp.dot(grid[...], table[...], preferred_element_type=F32)
    group = coeffs.shape[1] // THIRDS
    padded[...] = jnp.zeros_like(padded)
    for level in range(lev):
        one = coeffs[level * lat : (level + 1) * lat]
        for third in range(THIRDS):
            padded[third * lat : (third + 1) * lat, :group] = one[
                :, third * group : (third + 1) * group
            ]
        rows[pl.ds(level, group, stride=lev), :] = jnp.transpose(padded[...])[:group]
    size = out.shape[1]
    values = rows[...].astype(BF16).reshape(n_band * n_fld, size, LANES)
    for sec in range(n_sec):
        out[sec * n_band * n_fld : (sec + 1) * n_band * n_fld] = values


def spread_kernel(lat, n_band, legendre, out, wide):
    waves, degrees, _ = legendre.shape
    wide[...] = jnp.zeros_like(wide)
    lane = lax.broadcasted_iota(jnp.int32, (degrees, LANES), 1)
    for wave in range(waves):
        third, parity = wave // 2, wave % 2
        wide[:, : n_band * lat] = legendre[wave].astype(F32)
        place = third * lat
        live = (lane >= place) & (lane < place + lat)
        for band in range(n_band):
            base = band * lat // LANES * LANES
            moved = pltpu.roll(
                wide[:, base : base + 2 * LANES], (place - (band * lat - base)) % (2 * LANES), 1
            )
            out[band, parity, third * degrees : (third + 1) * degrees, :] = jnp.where(
                live, moved[:, :LANES], 0.0
            ).astype(BF16)


def legendre_kernel(n_sec, n_band, n_fld, lev, weights, pieces, out):
    degrees = out.shape[4]
    half = pieces.shape[1] // 2
    for parity in range(2):
        rows = slice(parity * half, (parity + 1) * half)
        basis = jnp.concatenate([weights[band, parity] for band in range(n_band)], axis=1)
        left = jnp.concatenate(
            [
                jnp.concatenate(
                    [
                        pieces[(sec * n_band + band) * n_fld + fld, rows, :]
                        for band in range(n_band)
                    ],
                    axis=1,
                )
                for fld in range(n_fld)
                for sec in range(n_sec)
            ],
            axis=0,
        )
        result = lax.dot_general(left, basis, NT, preferred_element_type=F32)
        for third in range(THIRDS):
            part = result[:, third * degrees : (third + 1) * degrees]
            for fld in range(n_fld):
                for real in range(2):
                    levels = [
                        part[(fld * n_sec + sec) * half + real * lev :][:lev]
                        for sec in range(n_sec)
                    ]
                    out[2 * third + parity, real, fld] = jnp.concatenate(levels, axis=0).astype(
                        BF16
                    )


def slot_rows(blocks, across, lat_pad):
    shift = 16
    factor = -(-(1 << shift) // across)
    lat = lax.shift_right_logical(blocks * factor, shift)
    return (blocks - lat * across) * lat_pad + lat


def pick_kernel(lat_pad, grid, blocks, interp, state, patch, column):
    lev, lat, lon = grid.shape
    across = lon // LANES
    slots = interp.shape[0]
    depth = patch.shape[0]
    for tile in range(across):
        patch[tile * lat_pad + lat : (tile + 1) * lat_pad, :] = jnp.zeros(
            (lat_pad - lat, lev * LANES), BF16
        )
        for level in range(lev):
            patch[
                tile * lat_pad : tile * lat_pad + lat, level * LANES : (level + 1) * LANES
            ] = grid[level, :, tile * LANES : (tile + 1) * LANES]
    if depth > across * lat_pad:
        patch[across * lat_pad :, :] = jnp.zeros((depth - across * lat_pad, lev * LANES), BF16)
    row = slot_rows(blocks[...], across, lat_pad)
    column[...] = jnp.transpose(jnp.broadcast_to(row, (LANES, slots)))
    chunk = 256
    lane = lax.broadcasted_iota(jnp.int32, (chunk, LANES), 1)
    for start in range(0, slots, chunk):
        mine = column[start : start + chunk, :]
        selector = jnp.concatenate(
            [
                jnp.where(mine == lane + base, 1.0, 0.0).astype(BF16)
                for base in range(0, depth, LANES)
            ],
            axis=1,
        )
        picked = jnp.dot(selector, patch[...], preferred_element_type=F32)
        weights = interp[start : start + chunk, :].astype(F32)
        total = jnp.zeros((chunk, LANES), F32)
        for level in range(lev):
            product = picked[:, level * LANES : (level + 1) * LANES] * weights
            total = jnp.where(lane == level, jnp.sum(product, axis=1, keepdims=True), total)
        state[0, :, start : start + chunk] = jnp.transpose(total)[:lev].astype(BF16)


def softplus(x):
    small = jnp.exp(-jnp.abs(x))
    tail = jnp.where(small < 2.0**-11, small, jnp.log(1.0 + small))
    return jnp.maximum(x, 0.0) + tail


def column_kernel(n_sec, n_fld, lat_pad, place, counts, weights, inverses, blocks, interp, pieces,
                  out, state, flux_up, flux_down):
    lev, slots = pieces.shape[1:]
    for fld in range(n_fld):
        for sec in range(n_sec):
            row = (fld * n_sec + sec) * lev
            state[row : row + lev, :] = pieces[sec * n_fld + fld].astype(F32)
    column = state[...].astype(BF16)
    flux_rows = inverses.shape[0]
    flux = jnp.zeros((flux_rows, slots), F32)
    chunk = 256
    for start in range(0, weights.shape[0], chunk):
        gates = jnp.dot(weights[start : start + chunk, :], column, preferred_element_type=F32)
        source = softplus(gates).astype(BF16)
        flux = flux + jnp.dot(
            inverses[:, start : start + chunk], source, preferred_element_type=F32
        )
    levels = flux_rows // 2
    flux_up[:levels, :] = flux[:levels]
    flux_down[:levels, :] = flux[levels:]
    flux_up[levels:, :] = jnp.zeros((8, slots), F32)
    flux_down[levels:, :] = jnp.zeros((8, slots), F32)
    mine, lat, lon = out.shape
    across = lon // LANES
    live = lax.broadcasted_iota(jnp.int32, (1, slots), 1) < counts[place[1]]
    base = (place[2] * n_fld + place[0]) * mine
    heats = []
    for level in range(mine):
        at = base + level
        heat = (flux_up[pl.ds(at, 1), :] - flux_up[pl.ds(at + 1, 1), :]) - (
            flux_down[pl.ds(at, 1), :] - flux_down[pl.ds(at + 1, 1), :]
        )
        heats.append(jnp.where(live, heat, 0.0).astype(BF16).astype(F32))
    row = slot_rows(blocks[...], across, lat_pad)
    tiles = max(t for t in range(1, 8) if across % t == 0)
    height = tiles * lat_pad
    for first in range(0, across, tiles):
        match = row == lax.broadcasted_iota(jnp.int32, (height, slots), 0) + first * lat_pad
        for level in range(mine):
            left = jnp.where(match, heats[level], 0.0).astype(BF16)
            summed = jnp.dot(left, interp[...], preferred_element_type=F32).astype(BF16)
            for tile in range(tiles):
                out[level, :, (first + tile) * LANES : (first + tile + 1) * LANES] = summed[
                    tile * lat_pad : tile * lat_pad + lat
                ]


def call(kernel, outs, specs, scratch, args, flops, size, name):
    shapes = [jax.ShapeDtypeStruct(shape, dtype) for shape, dtype in outs]
    single = len(outs) == 1
    return pl.pallas_call(
        kernel,
        out_shape=shapes[0] if single else shapes,
        in_specs=specs,
        out_specs=VMEM if single else [VMEM] * len(outs),
        scratch_shapes=scratch,
        compiler_params=pltpu.CompilerParams(vmem_limit_bytes=LIMIT),
        cost_estimate=pl.CostEstimate(flops=flops, bytes_accessed=size, transcendentals=0),
        name=name,
    )(*args)


def body(grid, legendre, counts, blocks, interp, source_weights, inverses):
    n_sec = lax.axis_size("sec")
    n_band = lax.axis_size("band")
    n_fld = lax.axis_size("fld")
    lev, lat, lon = grid.shape[1:]
    wave_dev, _, degrees = legendre.shape
    slots = blocks.shape[0]
    across = lon // LANES
    lat_pad = -(-lat // 16) * 16
    rest = 2 * wave_dev // THIRDS
    piece = rest * lev
    place = jnp.stack([lax.axis_index("fld"), lax.axis_index("band"), lax.axis_index("sec")]).astype(
        jnp.int32
    )
    block_row = blocks.reshape(1, slots)

    table = jnp.asarray(dft_table(lon, wave_dev, n_band, n_fld))
    group = n_fld * n_band * rest
    padded_group = -(-group // LANES) * LANES
    devices = n_sec * n_band * n_fld
    sent = call(
        functools.partial(dft_kernel, lev, lat, n_sec, n_band, n_fld),
        [((devices, piece, LANES), BF16)],
        [VMEM, VMEM],
        [pltpu.VMEM((LANES, padded_group), F32), pltpu.VMEM((group * lev, LANES), F32)],
        (grid.reshape(lev * lat, lon), table),
        2 * lev * lat * lon * THIRDS * group,
        2 * lon * (lev * lat + THIRDS * group),
        "fourier",
    )
    depth = -(-across * lat_pad // LANES) * LANES
    state = call(
        functools.partial(pick_kernel, lat_pad),
        [((1, lev, slots), BF16)],
        [VMEM, VMEM, VMEM],
        [pltpu.VMEM((depth, lev * LANES), BF16), pltpu.VMEM((slots, LANES), jnp.int32)],
        (grid.reshape(lev, lat, lon), block_row, interp),
        2 * slots * depth * lev * LANES,
        2 * lev * lat * lon + 2 * slots * LANES,
        "pick",
    )
    columns = lax.all_gather(state, ("sec", "fld"), axis=0, tiled=True)
    pieces = lax.all_to_all(sent, ("sec", "band", "fld"), 0, 0, tiled=True)
    basis = call(
        functools.partial(spread_kernel, lat, n_band),
        [((n_band, 2, THIRDS * degrees, LANES), BF16)],
        [VMEM],
        [pltpu.VMEM((degrees, (n_band * lat // LANES + 2) * LANES), F32)],
        (jnp.swapaxes(legendre, 1, 2),),
        0,
        8 * wave_dev * degrees * n_band * LANES,
        "basis",
    )

    spec_bands, flux_rows, _ = inverses.shape
    heating = call(
        functools.partial(column_kernel, n_sec, n_fld, lat_pad),
        [((n_sec * lev // (n_sec * n_fld), lat, lon), BF16)],
        [SMEM, SMEM] + [VMEM] * 5,
        [
            pltpu.VMEM((n_sec * n_fld * lev, slots), F32),
            pltpu.VMEM((flux_rows // 2 + 8, slots), F32),
            pltpu.VMEM((flux_rows // 2 + 8, slots), F32),
        ],
        (
            place,
            counts,
            jnp.transpose(source_weights),
            jnp.transpose(inverses, (1, 0, 2)).reshape(flux_rows, spec_bands * flux_rows),
            block_row,
            interp,
            columns,
        ),
        8 * slots * slots * 1024,
        2 * slots * slots,
        "columns",
    )

    spectral = call(
        functools.partial(legendre_kernel, n_sec, n_band, n_fld, lev),
        [((wave_dev, 2, n_fld, n_sec * lev, degrees), BF16)],
        [VMEM, VMEM],
        [],
        (basis, pieces),
        4 * n_sec * n_fld * piece * n_band * LANES * degrees * THIRDS,
        2 * n_sec * n_band * n_fld * piece * LANES,
        "legendre",
    )
    return (spectral, heating)


def solution(mesh):
    return jax.shard_map(
        body,
        mesh=mesh,
        in_specs=(
            P("fld", "sec", "band", None),
            P(("band", "fld"), None, "sec"),
            P(),
            P("band"),
            P("band", None),
            P(),
            P(),
        ),
        out_specs=(P(("band", "fld"), None, None, None, "sec"), P(("sec", "fld"), "band", None)),
        check_vma=False,
    )
```

```python
import functools
import math

import jax
import jax.numpy as jnp
import numpy as np
from jax import lax
from jax.experimental import pallas as pl
from jax.experimental.pallas import tpu as pltpu
from jax.sharding import PartitionSpec as P

BF16 = jnp.bfloat16
F32 = jnp.float32
LANES = 128
THIRDS = 3
VMEM = pl.BlockSpec(memory_space=pltpu.VMEM)
HBM = pl.BlockSpec(memory_space=pltpu.HBM)
SMEM = pl.BlockSpec(memory_space=pltpu.SMEM)
LIMIT = 40 * 1024 * 1024
WHOLE = 64 * 1024 * 1024
NT = (((1,), (1,)), ((), ()))


def dft_table(lon, wave_dev, n_band, n_fld):
    values_dev = 2 * wave_dev
    rest = values_dev // THIRDS
    third, band, fld, low = np.meshgrid(
        np.arange(THIRDS), np.arange(n_band), np.arange(n_fld), np.arange(rest), indexing="ij"
    )
    value = third * rest + low
    wave = ((band * n_fld + fld) * wave_dev + value // 2).reshape(-1)
    part = (value % 2).reshape(-1)
    phase = np.arange(lon, dtype=np.int64)[:, None] * wave[None, :] % lon
    angle = phase * (2.0 * math.pi / lon)
    values = np.where(part[None, :] == 0, np.cos(angle), -np.sin(angle)) / math.sqrt(lon)
    return values.astype(np.float32).astype(BF16)


def fourier(lev, lat, grid, table, packed, padded, rows):
    flat = jnp.concatenate([grid[level] for level in range(lev)], axis=0)
    coeffs = jnp.dot(flat, table[...], preferred_element_type=F32)
    group = coeffs.shape[1] // THIRDS
    padded[...] = jnp.zeros_like(padded)
    for level in range(lev):
        one = coeffs[level * lat : (level + 1) * lat]
        for third in range(THIRDS):
            padded[third * lat : (third + 1) * lat, :group] = one[
                :, third * group : (third + 1) * group
            ]
        rows[pl.ds(level, group, stride=lev), :] = jnp.transpose(padded[...])[:group]
    packed[...] = rows[...].astype(BF16).reshape(packed.shape)


def prepare_kernel(lat, n_band, legendre, weights, inverses, out, out_weights, out_inverses,
                   wide, flipped, rows):
    states, sources = weights.shape
    flux_rows, _, spec_bands = inverses.shape
    for start in range(0, sources, LANES):
        flipped[start : start + LANES, :] = jnp.transpose(
            weights[:, start : start + LANES].astype(F32)
        )
    for row in range(flux_rows):
        rows[row * flux_rows : (row + 1) * flux_rows, :] = inverses[row].astype(F32)
    for row in range(flux_rows):
        out_weights[row * spec_bands : (row + 1) * spec_bands, :] = flipped[
            pl.ds(row, spec_bands, stride=flux_rows), :
        ].astype(BF16)
    for row in range(0, flux_rows, 2):
        pair = [rows[pl.ds(row + i, flux_rows, stride=flux_rows), :] for i in range(2)]
        out_inverses[:, row * spec_bands : (row + 2) * spec_bands] = jnp.concatenate(
            pair, axis=1
        ).astype(BF16)
    waves, degrees, _ = legendre.shape
    wide[...] = jnp.zeros_like(wide)
    lane = lax.broadcasted_iota(jnp.int32, (degrees, LANES), 1)
    for wave in range(waves):
        third, parity = wave // 2, wave % 2
        wide[:, : n_band * lat] = legendre[wave].astype(F32)
        place = third * lat
        live = (lane >= place) & (lane < place + lat)
        for band in range(n_band):
            base = band * lat // LANES * LANES
            moved = pltpu.roll(
                wide[:, base : base + 2 * LANES], (place - (band * lat - base)) % (2 * LANES), 1
            )
            out[band, parity, third * degrees : (third + 1) * degrees, :] = jnp.where(
                live, moved[:, :LANES], 0.0
            ).astype(BF16)


def legendre_kernel(n_sec, n_band, n_fld, lev, weights, pieces, out):
    degrees = out.shape[4]
    half = pieces.shape[1] // 2
    for parity in range(2):
        rows = slice(parity * half, (parity + 1) * half)
        basis = jnp.concatenate([weights[band, parity] for band in range(n_band)], axis=1)
        left = jnp.concatenate(
            [
                jnp.concatenate(
                    [
                        pieces[(sec * n_band + band) * n_fld + fld, rows, :]
                        for band in range(n_band)
                    ],
                    axis=1,
                )
                for fld in range(n_fld)
                for sec in range(n_sec)
            ],
            axis=0,
        )
        result = lax.dot_general(left, basis, NT, preferred_element_type=F32)
        for third in range(THIRDS):
            part = result[:, third * degrees : (third + 1) * degrees]
            for fld in range(n_fld):
                for real in range(2):
                    levels = [
                        part[(fld * n_sec + sec) * half + real * lev :][:lev]
                        for sec in range(n_sec)
                    ]
                    out[2 * third + parity, real, fld] = jnp.concatenate(levels, axis=0).astype(
                        BF16
                    )


def slot_rows(blocks, across, lat_pad):
    shift = 16
    factor = -(-(1 << shift) // across)
    lat = lax.shift_right_logical(blocks * factor, shift)
    return (blocks - lat * across) * lat_pad + lat


def local_kernel(lat_pad, parts, grid_hbm, blocks_hbm, interp_hbm, table_hbm, out, out_fourier,
                 grid, blocks, interp, table, patch, column, selector, state, packed, padded,
                 rows, sems, sends):
    lev, lat, lon = grid.shape
    across = lon // LANES
    slots = interp.shape[0]
    depth = patch.shape[0]
    step = lon // parts
    small = [
        pltpu.make_async_copy(blocks_hbm, blocks, sems.at[parts]),
        pltpu.make_async_copy(interp_hbm, interp, sems.at[parts + 1]),
        pltpu.make_async_copy(table_hbm, table, sems.at[parts + 2]),
    ]
    loads = [
        pltpu.make_async_copy(
            grid_hbm.at[:, :, pl.ds(part * step, step)],
            grid.at[:, :, pl.ds(part * step, step)],
            sems.at[part],
        )
        for part in range(parts)
    ]
    small[0].start()
    for copy in loads:
        copy.start()
    small[1].start()
    small[2].start()
    small[0].wait()
    row = slot_rows(blocks[...], across, lat_pad)
    column[...] = jnp.transpose(jnp.broadcast_to(row, (LANES, slots)))
    chunk = 256
    lane = lax.broadcasted_iota(jnp.int32, (chunk, LANES), 1)
    for start in range(0, slots, chunk):
        mine = column[start : start + chunk, :]
        for base in range(0, depth, LANES):
            selector[start : start + chunk, base : base + LANES] = jnp.where(
                mine == lane + base, 1.0, 0.0
            ).astype(BF16)
    for part in range(parts):
        loads[part].wait()
        for tile in range(part * across // parts, (part + 1) * across // parts):
            patch[tile * lat_pad + lat : (tile + 1) * lat_pad, :] = jnp.zeros(
                (lat_pad - lat, lev * LANES), BF16
            )
            for level in range(lev):
                patch[
                    tile * lat_pad : tile * lat_pad + lat, level * LANES : (level + 1) * LANES
                ] = grid[level, :, tile * LANES : (tile + 1) * LANES]
    if depth > across * lat_pad:
        patch[across * lat_pad :, :] = jnp.zeros((depth - across * lat_pad, lev * LANES), BF16)
    small[1].wait()
    for start in range(0, slots, chunk):
        picked = jnp.dot(
            selector[start : start + chunk, :], patch[...], preferred_element_type=F32
        )
        weights = interp[start : start + chunk, :].astype(F32)
        total = jnp.zeros((chunk, LANES), F32)
        for level in range(lev):
            product = picked[:, level * LANES : (level + 1) * LANES] * weights
            total = jnp.where(lane == level, jnp.sum(product, axis=1, keepdims=True), total)
        state[:, start : start + chunk] = jnp.transpose(total)[:lev].astype(BF16)
    copies = [pltpu.make_async_copy(state, out.at[i], sends.at[i]) for i in range(out.shape[0])]
    for copy in copies:
        copy.start()
    small[2].wait()
    fourier(lev, lat, grid, table, packed, padded, rows)
    targets = packed.shape[0]
    for part in range(out_fourier.shape[0] // targets):
        copies.append(
            pltpu.make_async_copy(
                packed,
                out_fourier.at[pl.ds(part * targets, targets)],
                sends.at[out.shape[0] + part],
            )
        )
        copies[-1].start()
    for copy in copies:
        copy.wait()


def softplus(x):
    power = jnp.exp(jnp.minimum(x, 80.0))
    return jnp.where(x < -8.0, power, jnp.maximum(x, jnp.log(1.0 + power)))


def column_kernel(n_sec, n_fld, lat_pad, counts, weights, inverses, blocks, interp, pieces,
                  out, state, flux_up, flux_down, spread, result, sems):
    lev, slots = pieces.shape[1:]
    for fld in range(n_fld):
        for sec in range(n_sec):
            row = (fld * n_sec + sec) * lev
            state[row : row + lev, :] = pieces[sec * n_fld + fld].astype(F32)
    column = state[...].astype(BF16)
    flux_rows = inverses.shape[0]
    flux = jnp.zeros((flux_rows, slots), F32)
    chunk = 256
    for start in range(0, weights.shape[0], chunk):
        gates = jnp.dot(weights[start : start + chunk, :], column, preferred_element_type=F32)
        source = softplus(gates).astype(BF16)
        flux = flux + jnp.dot(
            inverses[:, start : start + chunk], source, preferred_element_type=F32
        )
    levels = flux_rows // 2
    flux_up[:levels, :] = flux[:levels]
    flux_down[:levels, :] = flux[levels:]
    flux_up[levels:, :] = jnp.zeros((8, slots), F32)
    flux_down[levels:, :] = jnp.zeros((8, slots), F32)
    mine, lat, lon = result.shape
    across = lon // LANES
    live = lax.broadcasted_iota(jnp.int32, (1, slots), 1) < counts[lax.axis_index("band")]
    base = (lax.axis_index("sec") * n_fld + lax.axis_index("fld")) * mine
    for level in range(mine):
        at = base + level
        heat = (flux_up[pl.ds(at, 1), :] - flux_up[pl.ds(at + 1, 1), :]) - (
            flux_down[pl.ds(at, 1), :] - flux_down[pl.ds(at + 1, 1), :]
        )
        heat = jnp.where(live, heat, 0.0).astype(BF16).astype(F32)
        for start in range(0, slots, LANES):
            down = jnp.transpose(
                jnp.broadcast_to(heat[:, start : start + LANES], (LANES, LANES))
            )
            spread[start : start + LANES, level * LANES : (level + 1) * LANES] = (
                down * interp[start : start + LANES, :].astype(F32)
            ).astype(BF16)
    row = slot_rows(blocks[...], across, lat_pad)
    tiles = max(t for t in range(1, 8) if across % t == 0)
    height = tiles * lat_pad
    copies = []
    for first in range(0, across, tiles):
        match = row == lax.broadcasted_iota(jnp.int32, (height, slots), 0) + first * lat_pad
        left = jnp.where(match, 1.0, 0.0).astype(BF16)
        summed = jnp.dot(left, spread[...], preferred_element_type=F32).astype(BF16)
        for level in range(mine):
            for tile in range(tiles):
                result[level, :, (first + tile) * LANES : (first + tile + 1) * LANES] = summed[
                    tile * lat_pad : tile * lat_pad + lat, level * LANES : (level + 1) * LANES
                ]
        columns = pl.ds(first * LANES, tiles * LANES)
        copies.append(
            pltpu.make_async_copy(
                result.at[:, :, columns], out.at[:, :, columns], sems.at[first // tiles]
            )
        )
        copies[-1].start()
    for copy in copies:
        copy.wait()


def call(kernel, outs, specs, scratch, args, flops, size, name, out_spec=VMEM, limit=LIMIT):
    shapes = [jax.ShapeDtypeStruct(shape, dtype) for shape, dtype in outs]
    single = len(outs) == 1
    return pl.pallas_call(
        kernel,
        out_shape=shapes[0] if single else shapes,
        in_specs=specs,
        out_specs=out_spec if single else [out_spec] * len(outs),
        scratch_shapes=scratch,
        compiler_params=pltpu.CompilerParams(vmem_limit_bytes=limit),
        cost_estimate=pl.CostEstimate(flops=flops, bytes_accessed=size, transcendentals=0),
        name=name,
    )(*args)


def body(grid, legendre, counts, blocks, interp, source_weights, inverses):
    n_sec = lax.axis_size("sec")
    n_band = lax.axis_size("band")
    n_fld = lax.axis_size("fld")
    lev, lat, lon = grid.shape[1:]
    wave_dev, _, degrees = legendre.shape
    slots = blocks.shape[0]
    across = lon // LANES
    lat_pad = -(-lat // 16) * 16
    rest = 2 * wave_dev // THIRDS
    piece = rest * lev
    block_row = blocks.reshape(1, slots)

    table = jnp.asarray(dft_table(lon, wave_dev, n_band, n_fld))
    group = n_fld * n_band * rest
    padded_group = -(-group // LANES) * LANES
    devices = n_sec * n_band * n_fld
    devices = n_sec * n_band * n_fld
    depth = -(-across * lat_pad // LANES) * LANES
    parts = max(t for t in range(1, 8) if across % t == 0)
    state, sent = call(
        functools.partial(local_kernel, lat_pad, parts),
        [((n_sec * n_fld, lev, slots), BF16), ((devices, piece, LANES), BF16)],
        [HBM] * 4,
        [
            pltpu.VMEM((lev, lat, lon), BF16),
            pltpu.VMEM((1, slots), jnp.int32),
            pltpu.VMEM((slots, LANES), BF16),
            pltpu.VMEM(table.shape, BF16),
            pltpu.VMEM((depth, lev * LANES), BF16),
            pltpu.VMEM((slots, LANES), jnp.int32),
            pltpu.VMEM((slots, depth), BF16),
            pltpu.VMEM((lev, slots), BF16),
            pltpu.VMEM((n_band * n_fld, piece, LANES), BF16),
            pltpu.VMEM((LANES, padded_group), F32),
            pltpu.VMEM((group * lev, LANES), F32),
            pltpu.SemaphoreType.DMA((parts + 3,)),
            pltpu.SemaphoreType.DMA((n_sec * n_fld + n_sec,)),
        ],
        (grid.reshape(lev, lat, lon), block_row, interp, table),
        2 * slots * depth * lev * LANES + 2 * lev * lat * lon * THIRDS * group,
        2 * lev * lat * lon + 2 * slots * LANES,
        "local",
        HBM,
        WHOLE,
    )
    columns = lax.all_to_all(state, ("sec", "fld"), 0, 0, tiled=True)
    pieces = lax.all_to_all(sent, ("sec", "band", "fld"), 0, 0, tiled=True)
    spec_bands, flux_rows, _ = inverses.shape
    sources = spec_bands * flux_rows
    states = source_weights.shape[0]
    basis, weights, inverse_rows = call(
        functools.partial(prepare_kernel, lat, n_band),
        [
            ((n_band, 2, THIRDS * degrees, LANES), BF16),
            ((sources, states), BF16),
            ((flux_rows, sources), BF16),
        ],
        [VMEM, VMEM, VMEM],
        [
            pltpu.VMEM((degrees, (n_band * lat // LANES + 2) * LANES), F32),
            pltpu.VMEM((sources, states), F32),
            pltpu.VMEM((flux_rows * flux_rows, spec_bands), F32),
        ],
        (
            jnp.swapaxes(legendre, 1, 2),
            source_weights,
            jnp.transpose(inverses, (1, 2, 0)),
        ),
        0,
        8 * wave_dev * degrees * n_band * LANES,
        "prepare",
    )
    mine = n_sec * lev // (n_sec * n_fld)
    heating = call(
        functools.partial(column_kernel, n_sec, n_fld, lat_pad),
        [((mine, lat, lon), BF16)],
        [SMEM] + [VMEM] * 5,
        [
            pltpu.VMEM((states, slots), F32),
            pltpu.VMEM((flux_rows // 2 + 8, slots), F32),
            pltpu.VMEM((flux_rows // 2 + 8, slots), F32),
            pltpu.VMEM((slots, mine * LANES), BF16),
            pltpu.VMEM((mine, lat, lon), BF16),
            pltpu.SemaphoreType.DMA((across,)),
        ],
        (counts, weights, inverse_rows, block_row, interp, columns),
        8 * slots * slots * 1024,
        2 * slots * slots,
        "columns",
        HBM,
    )

    spectral = call(
        functools.partial(legendre_kernel, n_sec, n_band, n_fld, lev),
        [((wave_dev, 2, n_fld, n_sec * lev, degrees), BF16)],
        [VMEM, VMEM],
        [],
        (basis, pieces),
        4 * n_sec * n_fld * piece * n_band * LANES * degrees * THIRDS,
        2 * n_sec * n_band * n_fld * piece * LANES,
        "legendre",
    )
    return (spectral, heating)


def solution(mesh):
    return jax.shard_map(
        body,
        mesh=mesh,
        in_specs=(
            P("fld", "sec", "band", None),
            P(("band", "fld"), None, "sec"),
            P(),
            P("band"),
            P("band", None),
            P(),
            P(),
        ),
        out_specs=(P(("band", "fld"), None, None, None, "sec"), P(("sec", "fld"), "band", None)),
        check_vma=False,
    )
```

```python
import functools
import math

import jax
import jax.numpy as jnp
import numpy as np
from jax import lax
from jax.experimental import pallas as pl
from jax.experimental.pallas import tpu as pltpu
from jax.sharding import PartitionSpec as P

BF16 = jnp.bfloat16
F32 = jnp.float32
LANES = 128
THIRDS = 3
VMEM = pl.BlockSpec(memory_space=pltpu.VMEM)
HBM = pl.BlockSpec(memory_space=pltpu.HBM)
SMEM = pl.BlockSpec(memory_space=pltpu.SMEM)
LIMIT = 40 * 1024 * 1024
ROOM = 1200 * 1024
WHOLE = 64 * 1024 * 1024 - ROOM
NT = (((1,), (1,)), ((), ()))


def dft_table(lon, wave_dev, n_band, n_fld):
    values_dev = 2 * wave_dev
    rest = values_dev // THIRDS
    third, band, fld, low = np.meshgrid(
        np.arange(THIRDS), np.arange(n_band), np.arange(n_fld), np.arange(rest), indexing="ij"
    )
    value = third * rest + low
    wave = ((band * n_fld + fld) * wave_dev + value // 2).reshape(-1)
    part = (value % 2).reshape(-1)
    phase = np.arange(lon, dtype=np.int64)[:, None] * wave[None, :] % lon
    angle = phase * (2.0 * math.pi / lon)
    values = np.where(part[None, :] == 0, np.cos(angle), -np.sin(angle)) / math.sqrt(lon)
    return values.astype(np.float32).astype(BF16)


def fourier(lev, lat, grid, table, packed, padded, rows):
    flat = jnp.concatenate([grid[level] for level in range(lev)], axis=0)
    coeffs = jnp.dot(flat, table[...], preferred_element_type=F32)
    group = coeffs.shape[1] // THIRDS
    padded[...] = jnp.zeros_like(padded)
    for level in range(lev):
        one = coeffs[level * lat : (level + 1) * lat]
        for third in range(THIRDS):
            padded[third * lat : (third + 1) * lat, :group] = one[
                :, third * group : (third + 1) * group
            ]
        rows[pl.ds(level, group, stride=lev), :] = jnp.transpose(padded[...])[:group]
    packed[...] = rows[...].astype(BF16).reshape(packed.shape)


def prepare_kernel(lat, n_band, legendre, weights, inverses, out, out_weights, out_inverses,
                   wide, flipped, rows):
    states, sources = weights.shape
    flux_rows, _, spec_bands = inverses.shape
    for start in range(0, sources, LANES):
        flipped[start : start + LANES, :] = jnp.transpose(
            weights[:, start : start + LANES].astype(F32)
        )
    for row in range(flux_rows):
        rows[row * flux_rows : (row + 1) * flux_rows, :] = inverses[row].astype(F32)
    for row in range(flux_rows):
        out_weights[row * spec_bands : (row + 1) * spec_bands, :] = flipped[
            pl.ds(row, spec_bands, stride=flux_rows), :
        ].astype(BF16)
    for row in range(0, flux_rows, 2):
        pair = [rows[pl.ds(row + i, flux_rows, stride=flux_rows), :] for i in range(2)]
        out_inverses[:, row * spec_bands : (row + 2) * spec_bands] = jnp.concatenate(
            pair, axis=1
        ).astype(BF16)
    waves, degrees, _ = legendre.shape
    wide[...] = jnp.zeros_like(wide)
    lane = lax.broadcasted_iota(jnp.int32, (degrees, LANES), 1)
    for wave in range(waves):
        third, parity = wave // 2, wave % 2
        wide[:, : n_band * lat] = legendre[wave].astype(F32)
        place = third * lat
        live = (lane >= place) & (lane < place + lat)
        for band in range(n_band):
            base = band * lat // LANES * LANES
            moved = pltpu.roll(
                wide[:, base : base + 2 * LANES], (place - (band * lat - base)) % (2 * LANES), 1
            )
            out[band, parity, third * degrees : (third + 1) * degrees, :] = jnp.where(
                live, moved[:, :LANES], 0.0
            ).astype(BF16)


def legendre_kernel(n_sec, n_band, n_fld, lev, weights, pieces, out):
    degrees = out.shape[4]
    half = pieces.shape[1] // 2
    for parity in range(2):
        rows = slice(parity * half, (parity + 1) * half)
        basis = jnp.concatenate([weights[band, parity] for band in range(n_band)], axis=1)
        left = jnp.concatenate(
            [
                jnp.concatenate(
                    [
                        pieces[(sec * n_band + band) * n_fld + fld, rows, :]
                        for band in range(n_band)
                    ],
                    axis=1,
                )
                for fld in range(n_fld)
                for sec in range(n_sec)
            ],
            axis=0,
        )
        result = lax.dot_general(left, basis, NT, preferred_element_type=F32)
        for third in range(THIRDS):
            part = result[:, third * degrees : (third + 1) * degrees]
            for fld in range(n_fld):
                for real in range(2):
                    levels = [
                        part[(fld * n_sec + sec) * half + real * lev :][:lev]
                        for sec in range(n_sec)
                    ]
                    out[2 * third + parity, real, fld] = jnp.concatenate(levels, axis=0).astype(
                        BF16
                    )


def slot_rows(blocks, across, lat_pad):
    shift = 16
    factor = -(-(1 << shift) // across)
    lat = lax.shift_right_logical(blocks * factor, shift)
    return (blocks - lat * across) * lat_pad + lat


def local_kernel(lat_pad, parts, grid_hbm, blocks_hbm, interp_hbm, table_hbm, out, out_fourier,
                 grid, blocks, interp, table, patch, column, selector, state, packed, padded,
                 rows, sems, sends):
    lev, lat, lon = grid.shape
    across = lon // LANES
    slots = interp.shape[0]
    depth = patch.shape[0]
    step = lon // parts
    small = [
        pltpu.make_async_copy(blocks_hbm, blocks, sems.at[parts]),
        pltpu.make_async_copy(interp_hbm, interp, sems.at[parts + 1]),
        pltpu.make_async_copy(table_hbm, table, sems.at[parts + 2]),
    ]
    loads = [
        pltpu.make_async_copy(
            grid_hbm.at[:, :, pl.ds(part * step, step)],
            grid.at[:, :, pl.ds(part * step, step)],
            sems.at[part],
        )
        for part in range(parts)
    ]
    small[0].start()
    for copy in loads:
        copy.start()
    small[1].start()
    small[2].start()
    small[0].wait()
    row = slot_rows(blocks[...], across, lat_pad)
    column[...] = jnp.transpose(jnp.broadcast_to(row, (LANES, slots)))
    chunk = 256
    lane = lax.broadcasted_iota(jnp.int32, (chunk, LANES), 1)
    for start in range(0, slots, chunk):
        mine = column[start : start + chunk, :]
        for base in range(0, depth, LANES):
            selector[start : start + chunk, base : base + LANES] = jnp.where(
                mine == lane + base, 1.0, 0.0
            ).astype(BF16)
    for part in range(parts):
        loads[part].wait()
        for tile in range(part * across // parts, (part + 1) * across // parts):
            patch[tile * lat_pad + lat : (tile + 1) * lat_pad, :] = jnp.zeros(
                (lat_pad - lat, lev * LANES), BF16
            )
            for level in range(lev):
                patch[
                    tile * lat_pad : tile * lat_pad + lat, level * LANES : (level + 1) * LANES
                ] = grid[level, :, tile * LANES : (tile + 1) * LANES]
    if depth > across * lat_pad:
        patch[across * lat_pad :, :] = jnp.zeros((depth - across * lat_pad, lev * LANES), BF16)
    small[1].wait()
    for start in range(0, slots, chunk):
        picked = jnp.dot(
            selector[start : start + chunk, :], patch[...], preferred_element_type=F32
        )
        weights = interp[start : start + chunk, :].astype(F32)
        total = jnp.zeros((chunk, LANES), F32)
        for level in range(lev):
            product = picked[:, level * LANES : (level + 1) * LANES] * weights
            total = jnp.where(lane == level, jnp.sum(product, axis=1, keepdims=True), total)
        state[:, start : start + chunk] = jnp.transpose(total)[:lev].astype(BF16)
    copies = [pltpu.make_async_copy(state, out.at[i], sends.at[i]) for i in range(out.shape[0])]
    for copy in copies:
        copy.start()
    small[2].wait()
    fourier(lev, lat, grid, table, packed, padded, rows)
    targets = packed.shape[0]
    for part in range(out_fourier.shape[0] // targets):
        copies.append(
            pltpu.make_async_copy(
                packed,
                out_fourier.at[pl.ds(part * targets, targets)],
                sends.at[out.shape[0] + part],
            )
        )
        copies[-1].start()
    for copy in copies:
        copy.wait()


def softplus(x):
    power = jnp.exp(jnp.minimum(x, 80.0))
    return jnp.where(x < -8.0, power, jnp.maximum(x, jnp.log(1.0 + power)))


def column_kernel(n_sec, n_fld, lat_pad, counts, weights, inverses, blocks, interp, near, far,
                  out, state, flux_up, flux_down, spread, result, sems):
    lev, slots = near.shape[1:]
    place = lax.axis_index("sec")
    for fld in range(n_fld):
        for shift, pieces in enumerate((near, far)):
            row = (fld * n_sec + (place ^ shift)) * lev
            state[pl.ds(pl.multiple_of(row, lev), lev), :] = pieces[fld].astype(F32)
    column = state[...].astype(BF16)
    flux_rows = inverses.shape[0]
    flux = jnp.zeros((flux_rows, slots), F32)
    chunk = 256
    for start in range(0, weights.shape[0], chunk):
        gates = jnp.dot(weights[start : start + chunk, :], column, preferred_element_type=F32)
        source = softplus(gates).astype(BF16)
        flux = flux + jnp.dot(
            inverses[:, start : start + chunk], source, preferred_element_type=F32
        )
    levels = flux_rows // 2
    flux_up[:levels, :] = flux[:levels]
    flux_down[:levels, :] = flux[levels:]
    flux_up[levels:, :] = jnp.zeros((8, slots), F32)
    flux_down[levels:, :] = jnp.zeros((8, slots), F32)
    mine, lat, lon = result.shape
    across = lon // LANES
    live = lax.broadcasted_iota(jnp.int32, (1, slots), 1) < counts[lax.axis_index("band")]
    base = (lax.axis_index("sec") * n_fld + lax.axis_index("fld")) * mine
    for level in range(mine):
        at = base + level
        heat = (flux_up[pl.ds(at, 1), :] - flux_up[pl.ds(at + 1, 1), :]) - (
            flux_down[pl.ds(at, 1), :] - flux_down[pl.ds(at + 1, 1), :]
        )
        heat = jnp.where(live, heat, 0.0).astype(BF16).astype(F32)
        for start in range(0, slots, LANES):
            down = jnp.transpose(
                jnp.broadcast_to(heat[:, start : start + LANES], (LANES, LANES))
            )
            spread[start : start + LANES, level * LANES : (level + 1) * LANES] = (
                down * interp[start : start + LANES, :].astype(F32)
            ).astype(BF16)
    row = slot_rows(blocks[...], across, lat_pad)
    tiles = max(t for t in range(1, 8) if across % t == 0)
    height = tiles * lat_pad
    copies = []
    for first in range(0, across, tiles):
        match = row == lax.broadcasted_iota(jnp.int32, (height, slots), 0) + first * lat_pad
        left = jnp.where(match, 1.0, 0.0).astype(BF16)
        summed = jnp.dot(left, spread[...], preferred_element_type=F32).astype(BF16)
        for level in range(mine):
            for tile in range(tiles):
                result[level, :, (first + tile) * LANES : (first + tile + 1) * LANES] = summed[
                    tile * lat_pad : tile * lat_pad + lat, level * LANES : (level + 1) * LANES
                ]
        columns = pl.ds(first * LANES, tiles * LANES)
        copies.append(
            pltpu.make_async_copy(
                result.at[:, :, columns], out.at[:, :, columns], sems.at[first // tiles]
            )
        )
        copies[-1].start()
    for copy in copies:
        copy.wait()


def call(kernel, outs, specs, scratch, args, flops, size, name, out_spec=VMEM, limit=LIMIT):
    shapes = [jax.ShapeDtypeStruct(shape, dtype) for shape, dtype in outs]
    single = len(outs) == 1
    return pl.pallas_call(
        kernel,
        out_shape=shapes[0] if single else shapes,
        in_specs=specs,
        out_specs=out_spec if single else [out_spec] * len(outs),
        scratch_shapes=scratch,
        compiler_params=pltpu.CompilerParams(vmem_limit_bytes=limit),
        cost_estimate=pl.CostEstimate(flops=flops, bytes_accessed=size, transcendentals=0),
        name=name,
    )(*args)


def body(grid, legendre, counts, blocks, interp, source_weights, inverses):
    n_sec = lax.axis_size("sec")
    n_band = lax.axis_size("band")
    n_fld = lax.axis_size("fld")
    lev, lat, lon = grid.shape[1:]
    wave_dev, _, degrees = legendre.shape
    slots = blocks.shape[0]
    across = lon // LANES
    lat_pad = -(-lat // 16) * 16
    rest = 2 * wave_dev // THIRDS
    piece = rest * lev
    block_row = blocks.reshape(1, slots)

    table = jnp.asarray(dft_table(lon, wave_dev, n_band, n_fld))
    group = n_fld * n_band * rest
    padded_group = -(-group // LANES) * LANES
    devices = n_sec * n_band * n_fld
    devices = n_sec * n_band * n_fld
    depth = -(-across * lat_pad // LANES) * LANES
    parts = max(t for t in range(1, 8) if across % t == 0)
    state, sent = call(
        functools.partial(local_kernel, lat_pad, parts),
        [((n_fld, lev, slots), BF16), ((devices, piece, LANES), BF16)],
        [HBM] * 4,
        [
            pltpu.VMEM((lev, lat, lon), BF16),
            pltpu.VMEM((1, slots), jnp.int32),
            pltpu.VMEM((slots, LANES), BF16),
            pltpu.VMEM(table.shape, BF16),
            pltpu.VMEM((depth, lev * LANES), BF16),
            pltpu.VMEM((slots, LANES), jnp.int32),
            pltpu.VMEM((slots, depth), BF16),
            pltpu.VMEM((lev, slots), BF16),
            pltpu.VMEM((n_band * n_fld, piece, LANES), BF16),
            pltpu.VMEM((LANES, padded_group), F32),
            pltpu.VMEM((group * lev, LANES), F32),
            pltpu.SemaphoreType.DMA((parts + 3,)),
            pltpu.SemaphoreType.DMA((n_fld + n_sec,)),
        ],
        (grid.reshape(lev, lat, lon), block_row, interp, table),
        2 * slots * depth * lev * LANES + 2 * lev * lat * lon * THIRDS * group,
        2 * lev * lat * lon + 2 * slots * LANES,
        "local",
        HBM,
        WHOLE,
    )
    near = lax.all_to_all(state, "fld", 0, 0, tiled=True)
    pieces = lax.all_to_all(sent, ("sec", "band", "fld"), 0, 0, tiled=True)
    far = lax.ppermute(near, "sec", [(i, 1 - i) for i in range(n_sec)])
    spec_bands, flux_rows, _ = inverses.shape
    sources = spec_bands * flux_rows
    states = source_weights.shape[0]
    basis, weights, inverse_rows = call(
        functools.partial(prepare_kernel, lat, n_band),
        [
            ((n_band, 2, THIRDS * degrees, LANES), BF16),
            ((sources, states), BF16),
            ((flux_rows, sources), BF16),
        ],
        [VMEM, VMEM, VMEM],
        [
            pltpu.VMEM((degrees, (n_band * lat // LANES + 2) * LANES), F32),
            pltpu.VMEM((sources, states), F32),
            pltpu.VMEM((flux_rows * flux_rows, spec_bands), F32),
        ],
        (
            jnp.swapaxes(legendre, 1, 2),
            source_weights,
            jnp.transpose(inverses, (1, 2, 0)),
        ),
        0,
        8 * wave_dev * degrees * n_band * LANES,
        "prepare",
    )
    mine = n_sec * lev // (n_sec * n_fld)
    heating = call(
        functools.partial(column_kernel, n_sec, n_fld, lat_pad),
        [((mine, lat, lon), BF16)],
        [SMEM] + [VMEM] * 6,
        [
            pltpu.VMEM((states, slots), F32),
            pltpu.VMEM((flux_rows // 2 + 8, slots), F32),
            pltpu.VMEM((flux_rows // 2 + 8, slots), F32),
            pltpu.VMEM((slots, mine * LANES), BF16),
            pltpu.VMEM((mine, lat, lon), BF16),
            pltpu.SemaphoreType.DMA((across,)),
        ],
        (counts, weights, inverse_rows, block_row, interp, near, far),
        8 * slots * slots * 1024,
        2 * slots * slots,
        "columns",
        HBM,
    )

    spectral = call(
        functools.partial(legendre_kernel, n_sec, n_band, n_fld, lev),
        [((wave_dev, 2, n_fld, n_sec * lev, degrees), BF16)],
        [VMEM, VMEM],
        [],
        (basis, pieces),
        4 * n_sec * n_fld * piece * n_band * LANES * degrees * THIRDS,
        2 * n_sec * n_band * n_fld * piece * LANES,
        "legendre",
    )
    return (spectral, heating)


def solution(mesh):
    return jax.shard_map(
        body,
        mesh=mesh,
        in_specs=(
            P("fld", "sec", "band", None),
            P(("band", "fld"), None, "sec"),
            P(),
            P("band"),
            P("band", None),
            P(),
            P(),
        ),
        out_specs=(P(("band", "fld"), None, None, None, "sec"), P(("sec", "fld"), "band", None)),
        check_vma=False,
    )
```

```python
import functools
import math

import jax
import jax.numpy as jnp
import numpy as np
from jax import lax
from jax.experimental import pallas as pl
from jax.experimental.pallas import tpu as pltpu
from jax.sharding import PartitionSpec as P

BF16 = jnp.bfloat16
F32 = jnp.float32
LANES = 128
THIRDS = 3
VMEM = pl.BlockSpec(memory_space=pltpu.VMEM)
HBM = pl.BlockSpec(memory_space=pltpu.HBM)
SMEM = pl.BlockSpec(memory_space=pltpu.SMEM)
LIMIT = 40 * 1024 * 1024
ROOM = 1200 * 1024
WHOLE = 64 * 1024 * 1024 - ROOM
NT = (((1,), (1,)), ((), ()))


def dft_table(lon, wave_dev, n_band, n_fld):
    values_dev = 2 * wave_dev
    rest = values_dev // THIRDS
    third, fld, band, low = np.meshgrid(
        np.arange(THIRDS), np.arange(n_fld), np.arange(n_band), np.arange(rest), indexing="ij"
    )
    value = third * rest + low
    wave = ((band * n_fld + fld) * wave_dev + value // 2).reshape(-1)
    part = (value % 2).reshape(-1)
    phase = np.arange(lon, dtype=np.int64)[:, None] * wave[None, :] % lon
    angle = phase * (2.0 * math.pi / lon)
    values = np.where(part[None, :] == 0, np.cos(angle), -np.sin(angle)) / math.sqrt(lon)
    return values.astype(np.float32).astype(BF16)


def fourier(lev, lat, grid, table, message, padded, rows):
    flat = jnp.concatenate([grid[level] for level in range(lev)], axis=0)
    coeffs = jnp.dot(flat, table[...], preferred_element_type=F32)
    group = coeffs.shape[1] // THIRDS
    padded[...] = jnp.zeros_like(padded)
    for level in range(lev):
        one = coeffs[level * lat : (level + 1) * lat]
        for third in range(THIRDS):
            padded[third * lat : (third + 1) * lat, :group] = one[
                :, third * group : (third + 1) * group
            ]
        rows[pl.ds(level, group, stride=lev), :] = jnp.transpose(padded[...])[:group]
    targets = message.shape[0]
    size = rows.shape[0] // targets
    message[:, :size, :] = rows[...].astype(BF16).reshape(targets, size, LANES)


def prepare_kernel(lat, n_band, legendre, weights, inverses, out, out_weights, out_inverses,
                   wide, flipped, rows):
    states, sources = weights.shape
    flux_rows, _, spec_bands = inverses.shape
    for start in range(0, sources, LANES):
        flipped[start : start + LANES, :] = jnp.transpose(
            weights[:, start : start + LANES].astype(F32)
        )
    for row in range(flux_rows):
        rows[row * flux_rows : (row + 1) * flux_rows, :] = inverses[row].astype(F32)
    for row in range(flux_rows):
        out_weights[row * spec_bands : (row + 1) * spec_bands, :] = flipped[
            pl.ds(row, spec_bands, stride=flux_rows), :
        ].astype(BF16)
    for row in range(0, flux_rows, 2):
        pair = [rows[pl.ds(row + i, flux_rows, stride=flux_rows), :] for i in range(2)]
        out_inverses[:, row * spec_bands : (row + 2) * spec_bands] = jnp.concatenate(
            pair, axis=1
        ).astype(BF16)
    waves, degrees, _ = legendre.shape
    wide[...] = jnp.zeros_like(wide)
    lane = lax.broadcasted_iota(jnp.int32, (degrees, LANES), 1)
    for wave in range(waves):
        third, parity = wave // 2, wave % 2
        wide[:, : n_band * lat] = legendre[wave].astype(F32)
        place = third * lat
        live = (lane >= place) & (lane < place + lat)
        for band in range(n_band):
            base = band * lat // LANES * LANES
            moved = pltpu.roll(
                wide[:, base : base + 2 * LANES], (place - (band * lat - base)) % (2 * LANES), 1
            )
            out[band, parity, third * degrees : (third + 1) * degrees, :] = jnp.where(
                live, moved[:, :LANES], 0.0
            ).astype(BF16)


def legendre_kernel(n_sec, n_band, n_fld, lev, weights, pieces, out):
    degrees = out.shape[4]
    half = pieces.shape[2] // 2
    for parity in range(2):
        rows = slice(parity * half, (parity + 1) * half)
        basis = jnp.concatenate([weights[band, parity] for band in range(n_band)], axis=1)
        left = jnp.concatenate(
            [
                jnp.concatenate(
                    [
                        pieces[sec * n_band + band, fld, rows, :]
                        for band in range(n_band)
                    ],
                    axis=1,
                )
                for fld in range(n_fld)
                for sec in range(n_sec)
            ],
            axis=0,
        )
        result = lax.dot_general(left, basis, NT, preferred_element_type=F32)
        for third in range(THIRDS):
            part = result[:, third * degrees : (third + 1) * degrees]
            for fld in range(n_fld):
                for real in range(2):
                    levels = [
                        part[(fld * n_sec + sec) * half + real * lev :][:lev]
                        for sec in range(n_sec)
                    ]
                    out[2 * third + parity, real, fld] = jnp.concatenate(levels, axis=0).astype(
                        BF16
                    )


def slot_rows(blocks, across, lat_pad):
    shift = 16
    factor = -(-(1 << shift) // across)
    lat = lax.shift_right_logical(blocks * factor, shift)
    return (blocks - lat * across) * lat_pad + lat


def local_kernel(lat_pad, parts, grid_hbm, blocks_hbm, interp_hbm, table_hbm, out,
                 grid, blocks, interp, table, patch, column, selector, message, padded, rows,
                 sems, send):
    lev, lat, lon = grid.shape
    across = lon // LANES
    slots = interp.shape[0]
    depth = patch.shape[0]
    step = lon // parts
    small = [
        pltpu.make_async_copy(blocks_hbm, blocks, sems.at[parts]),
        pltpu.make_async_copy(interp_hbm, interp, sems.at[parts + 1]),
        pltpu.make_async_copy(table_hbm, table, sems.at[parts + 2]),
    ]
    loads = [
        pltpu.make_async_copy(
            grid_hbm.at[:, :, pl.ds(part * step, step)],
            grid.at[:, :, pl.ds(part * step, step)],
            sems.at[part],
        )
        for part in range(parts)
    ]
    small[0].start()
    for copy in loads:
        copy.start()
    small[1].start()
    small[2].start()
    small[0].wait()
    row = slot_rows(blocks[...], across, lat_pad)
    column[...] = jnp.transpose(jnp.broadcast_to(row, (LANES, slots)))
    chunk = 256
    lane = lax.broadcasted_iota(jnp.int32, (chunk, LANES), 1)
    for start in range(0, slots, chunk):
        mine = column[start : start + chunk, :]
        for base in range(0, depth, LANES):
            selector[start : start + chunk, base : base + LANES] = jnp.where(
                mine == lane + base, 1.0, 0.0
            ).astype(BF16)
    for part in range(parts):
        loads[part].wait()
        for tile in range(part * across // parts, (part + 1) * across // parts):
            patch[tile * lat_pad + lat : (tile + 1) * lat_pad, :] = jnp.zeros(
                (lat_pad - lat, lev * LANES), BF16
            )
            for level in range(lev):
                patch[
                    tile * lat_pad : tile * lat_pad + lat, level * LANES : (level + 1) * LANES
                ] = grid[level, :, tile * LANES : (tile + 1) * LANES]
    if depth > across * lat_pad:
        patch[across * lat_pad :, :] = jnp.zeros((depth - across * lat_pad, lev * LANES), BF16)
    small[1].wait()
    for start in range(0, slots, chunk):
        picked = jnp.dot(
            selector[start : start + chunk, :], patch[...], preferred_element_type=F32
        )
        weights = interp[start : start + chunk, :].astype(F32)
        total = jnp.zeros((chunk, LANES), F32)
        for level in range(lev):
            product = picked[:, level * LANES : (level + 1) * LANES] * weights
            total = jnp.where(lane == level, jnp.sum(product, axis=1, keepdims=True), total)
        state = jnp.transpose(total)[:lev].astype(BF16)
        for tile in range(chunk // LANES):
            row = message.shape[1] - slots // LANES * lev + (start // LANES + tile) * lev
            for target in range(message.shape[0]):
                message[target, row : row + lev, :] = state[:, tile * LANES : (tile + 1) * LANES]
    small[2].wait()
    fourier(lev, lat, grid, table, message, padded, rows)
    copy = pltpu.make_async_copy(message, out, send.at[0])
    copy.start()
    copy.wait()


def regroup_kernel(n_band, arrived, out, out_state, sems):
    size = out.shape[2]
    copies = []
    for target in range(out.shape[0]):
        rows = pl.ds(target % n_band * size, size)
        copies.append(
            pltpu.make_async_copy(arrived.at[:, rows, :], out.at[target], sems.at[target])
        )
    rows = pl.ds(n_band * size, out_state.shape[1])
    copies.append(
        pltpu.make_async_copy(arrived.at[:, rows, :], out_state, sems.at[out.shape[0]])
    )
    for copy in copies:
        copy.start()
    for copy in copies:
        copy.wait()


def softplus(x):
    power = jnp.exp(jnp.minimum(x, 80.0))
    return jnp.where(x < -8.0, power, jnp.maximum(x, jnp.log(1.0 + power)))


def column_kernel(n_sec, n_fld, lat_pad, slots, counts, weights, inverses, blocks, interp, near, far,
                  out, state, flux_up, flux_down, spread, result, sems):
    lev = near.shape[1] * LANES // slots
    place = lax.axis_index("sec")
    for fld in range(n_fld):
        for shift, pieces in enumerate((near, far)):
            row = (fld * n_sec + (place ^ shift)) * lev
            for tile in range(slots // LANES):
                state[
                    pl.ds(pl.multiple_of(row, lev), lev), tile * LANES : (tile + 1) * LANES
                ] = pieces[fld, tile * lev : (tile + 1) * lev, :].astype(F32)
    column = state[...].astype(BF16)
    flux_rows = inverses.shape[0]
    flux = jnp.zeros((flux_rows, slots), F32)
    chunk = 256
    for start in range(0, weights.shape[0], chunk):
        gates = jnp.dot(weights[start : start + chunk, :], column, preferred_element_type=F32)
        source = softplus(gates).astype(BF16)
        flux = flux + jnp.dot(
            inverses[:, start : start + chunk], source, preferred_element_type=F32
        )
    levels = flux_rows // 2
    flux_up[:levels, :] = flux[:levels]
    flux_down[:levels, :] = flux[levels:]
    flux_up[levels:, :] = jnp.zeros((8, slots), F32)
    flux_down[levels:, :] = jnp.zeros((8, slots), F32)
    mine, lat, lon = result.shape
    across = lon // LANES
    live = lax.broadcasted_iota(jnp.int32, (1, slots), 1) < counts[lax.axis_index("band")]
    base = (lax.axis_index("sec") * n_fld + lax.axis_index("fld")) * mine
    for level in range(mine):
        at = base + level
        heat = (flux_up[pl.ds(at, 1), :] - flux_up[pl.ds(at + 1, 1), :]) - (
            flux_down[pl.ds(at, 1), :] - flux_down[pl.ds(at + 1, 1), :]
        )
        heat = jnp.where(live, heat, 0.0).astype(BF16).astype(F32)
        for start in range(0, slots, LANES):
            down = jnp.transpose(
                jnp.broadcast_to(heat[:, start : start + LANES], (LANES, LANES))
            )
            spread[start : start + LANES, level * LANES : (level + 1) * LANES] = (
                down * interp[start : start + LANES, :].astype(F32)
            ).astype(BF16)
    row = slot_rows(blocks[...], across, lat_pad)
    tiles = max(t for t in range(1, 8) if across % t == 0)
    height = tiles * lat_pad
    copies = []
    for first in range(0, across, tiles):
        match = row == lax.broadcasted_iota(jnp.int32, (height, slots), 0) + first * lat_pad
        left = jnp.where(match, 1.0, 0.0).astype(BF16)
        summed = jnp.dot(left, spread[...], preferred_element_type=F32).astype(BF16)
        for level in range(mine):
            for tile in range(tiles):
                result[level, :, (first + tile) * LANES : (first + tile + 1) * LANES] = summed[
                    tile * lat_pad : tile * lat_pad + lat, level * LANES : (level + 1) * LANES
                ]
        columns = pl.ds(first * LANES, tiles * LANES)
        copies.append(
            pltpu.make_async_copy(
                result.at[:, :, columns], out.at[:, :, columns], sems.at[first // tiles]
            )
        )
        copies[-1].start()
    for copy in copies:
        copy.wait()


def call(kernel, outs, specs, scratch, args, flops, size, name, out_spec=VMEM, limit=LIMIT):
    shapes = [jax.ShapeDtypeStruct(shape, dtype) for shape, dtype in outs]
    single = len(outs) == 1
    return pl.pallas_call(
        kernel,
        out_shape=shapes[0] if single else shapes,
        in_specs=specs,
        out_specs=out_spec if single else [out_spec] * len(outs),
        scratch_shapes=scratch,
        compiler_params=pltpu.CompilerParams(vmem_limit_bytes=limit),
        cost_estimate=pl.CostEstimate(flops=flops, bytes_accessed=size, transcendentals=0),
        name=name,
    )(*args)


def body(grid, legendre, counts, blocks, interp, source_weights, inverses):
    n_sec = lax.axis_size("sec")
    n_band = lax.axis_size("band")
    n_fld = lax.axis_size("fld")
    lev, lat, lon = grid.shape[1:]
    wave_dev, _, degrees = legendre.shape
    slots = blocks.shape[0]
    across = lon // LANES
    lat_pad = -(-lat // 16) * 16
    rest = 2 * wave_dev // THIRDS
    piece = rest * lev
    block_row = blocks.reshape(1, slots)

    table = jnp.asarray(dft_table(lon, wave_dev, n_band, n_fld))
    group = n_fld * n_band * rest
    padded_group = -(-group // LANES) * LANES
    depth = -(-across * lat_pad // LANES) * LANES
    parts = max(t for t in range(1, 8) if across % t == 0)
    state_rows = slots * lev // LANES
    message_rows = n_band * piece + state_rows
    message = call(
        functools.partial(local_kernel, lat_pad, parts),
        [((n_fld, message_rows, LANES), BF16)],
        [HBM] * 4,
        [
            pltpu.VMEM((lev, lat, lon), BF16),
            pltpu.VMEM((1, slots), jnp.int32),
            pltpu.VMEM((slots, LANES), BF16),
            pltpu.VMEM(table.shape, BF16),
            pltpu.VMEM((depth, lev * LANES), BF16),
            pltpu.VMEM((slots, LANES), jnp.int32),
            pltpu.VMEM((slots, depth), BF16),
            pltpu.VMEM((n_fld, message_rows, LANES), BF16),
            pltpu.VMEM((LANES, padded_group), F32),
            pltpu.VMEM((group * lev, LANES), F32),
            pltpu.SemaphoreType.DMA((parts + 3,)),
            pltpu.SemaphoreType.DMA((1,)),
        ],
        (grid.reshape(lev, lat, lon), block_row, interp, table),
        2 * slots * depth * lev * LANES + 2 * lev * lat * lon * THIRDS * group,
        2 * lev * lat * lon + 2 * slots * LANES,
        "local",
        HBM,
        WHOLE,
    )
    arrived = lax.all_to_all(message, "fld", 0, 0, tiled=True)
    sent, near = call(
        functools.partial(regroup_kernel, n_band),
        [((n_sec * n_band, n_fld, piece, LANES), BF16), ((n_fld, state_rows, LANES), BF16)],
        [HBM],
        [pltpu.SemaphoreType.DMA((n_sec * n_band + 1,))],
        (arrived,),
        0,
        4 * n_sec * n_band * n_fld * piece * LANES,
        "regroup",
        HBM,
    )
    far = lax.ppermute(near, "sec", [(i, 1 - i) for i in range(n_sec)])
    pieces = lax.all_to_all(sent, ("sec", "band"), 0, 0, tiled=True)
    spec_bands, flux_rows, _ = inverses.shape
    sources = spec_bands * flux_rows
    states = source_weights.shape[0]
    basis, weights, inverse_rows = call(
        functools.partial(prepare_kernel, lat, n_band),
        [
            ((n_band, 2, THIRDS * degrees, LANES), BF16),
            ((sources, states), BF16),
            ((flux_rows, sources), BF16),
        ],
        [VMEM, VMEM, VMEM],
        [
            pltpu.VMEM((degrees, (n_band * lat // LANES + 2) * LANES), F32),
            pltpu.VMEM((sources, states), F32),
            pltpu.VMEM((flux_rows * flux_rows, spec_bands), F32),
        ],
        (
            jnp.swapaxes(legendre, 1, 2),
            source_weights,
            jnp.transpose(inverses, (1, 2, 0)),
        ),
        0,
        8 * wave_dev * degrees * n_band * LANES,
        "prepare",
    )
    mine = n_sec * lev // (n_sec * n_fld)
    heating = call(
        functools.partial(column_kernel, n_sec, n_fld, lat_pad, slots),
        [((mine, lat, lon), BF16)],
        [SMEM] + [VMEM] * 6,
        [
            pltpu.VMEM((states, slots), F32),
            pltpu.VMEM((flux_rows // 2 + 8, slots), F32),
            pltpu.VMEM((flux_rows // 2 + 8, slots), F32),
            pltpu.VMEM((slots, mine * LANES), BF16),
            pltpu.VMEM((mine, lat, lon), BF16),
            pltpu.SemaphoreType.DMA((across,)),
        ],
        (counts, weights, inverse_rows, block_row, interp, near, far),
        8 * slots * slots * 1024,
        2 * slots * slots,
        "columns",
        HBM,
    )

    spectral = call(
        functools.partial(legendre_kernel, n_sec, n_band, n_fld, lev),
        [((wave_dev, 2, n_fld, n_sec * lev, degrees), BF16)],
        [VMEM, VMEM],
        [],
        (basis, pieces),
        4 * n_sec * n_fld * piece * n_band * LANES * degrees * THIRDS,
        2 * n_sec * n_band * n_fld * piece * LANES,
        "legendre",
    )
    return (spectral, heating)


def solution(mesh):
    return jax.shard_map(
        body,
        mesh=mesh,
        in_specs=(
            P("fld", "sec", "band", None),
            P(("band", "fld"), None, "sec"),
            P(),
            P("band"),
            P("band", None),
            P(),
            P(),
        ),
        out_specs=(P(("band", "fld"), None, None, None, "sec"), P(("sec", "fld"), "band", None)),
        check_vma=False,
    )
```

```python
import functools
import math

import jax
import jax.numpy as jnp
import numpy as np
from jax import lax
from jax.experimental import pallas as pl
from jax.experimental.pallas import tpu as pltpu
from jax.sharding import PartitionSpec as P

BF16 = jnp.bfloat16
F32 = jnp.float32
LANES = 128
THIRDS = 3
VMEM = pl.BlockSpec(memory_space=pltpu.VMEM)
HBM = pl.BlockSpec(memory_space=pltpu.HBM)
SMEM = pl.BlockSpec(memory_space=pltpu.SMEM)
LIMIT = 40 * 1024 * 1024
ROOM = 1200 * 1024
WHOLE = 64 * 1024 * 1024 - ROOM
NT = (((1,), (1,)), ((), ()))


def dft_table(lon, wave_dev, n_band, n_fld):
    values_dev = 2 * wave_dev
    rest = values_dev // THIRDS
    third, fld, band, low = np.meshgrid(
        np.arange(THIRDS), np.arange(n_fld), np.arange(n_band), np.arange(rest), indexing="ij"
    )
    value = third * rest + low
    wave = ((band * n_fld + fld) * wave_dev + value // 2).reshape(-1)
    part = (value % 2).reshape(-1)
    phase = np.arange(lon, dtype=np.int64)[:, None] * wave[None, :] % lon
    angle = phase * (2.0 * math.pi / lon)
    values = np.where(part[None, :] == 0, np.cos(angle), -np.sin(angle)) / math.sqrt(lon)
    return values.astype(np.float32).astype(BF16)


def pack(lev, lat, coeffs, message, padded, rows):
    group = coeffs.shape[1] // THIRDS
    padded[...] = jnp.zeros_like(padded)
    for level in range(lev):
        for third in range(THIRDS):
            padded[third * lat : (third + 1) * lat, :group] = coeffs[
                level * lat : (level + 1) * lat, third * group : (third + 1) * group
            ]
        rows[pl.ds(level, group, stride=lev), :] = jnp.transpose(padded[...])[:group]
    targets = message.shape[0]
    size = rows.shape[0] // targets
    message[:, :size, :] = rows[...].astype(BF16).reshape(targets, size, LANES)


def prepare_kernel(lat, n_band, legendre, inverses, out, out_inverses, wide, rows, turned):
    flux_rows, _, spec_bands = inverses.shape
    for row in range(flux_rows):
        rows[row * flux_rows : (row + 1) * flux_rows, :] = inverses[row].astype(F32)
    for row in range(flux_rows):
        turned[pl.ds(row, spec_bands, stride=flux_rows), :] = jnp.transpose(
            rows[pl.ds(row, flux_rows, stride=flux_rows), :]
        )
    out_inverses[...] = turned[...].astype(BF16)
    waves, degrees, _ = legendre.shape
    wide[...] = jnp.zeros_like(wide)
    lane = lax.broadcasted_iota(jnp.int32, (degrees, LANES), 1)
    for wave in range(waves):
        third, parity = wave // 2, wave % 2
        wide[:, : n_band * lat] = legendre[wave].astype(F32)
        place = third * lat
        live = (lane >= place) & (lane < place + lat)
        for band in range(n_band):
            base = band * lat // LANES * LANES
            moved = pltpu.roll(
                wide[:, base : base + 2 * LANES], (place - (band * lat - base)) % (2 * LANES), 1
            )
            out[band, parity, third * degrees : (third + 1) * degrees, :] = jnp.where(
                live, moved[:, :LANES], 0.0
            ).astype(BF16)


def legendre_kernel(n_sec, n_band, n_fld, lev, weights, pieces, out):
    degrees = out.shape[4]
    half = pieces.shape[2] // 2
    for parity in range(2):
        rows = slice(parity * half, (parity + 1) * half)
        basis = jnp.concatenate([weights[band, parity] for band in range(n_band)], axis=1)
        left = jnp.concatenate(
            [
                jnp.concatenate(
                    [
                        pieces[sec * n_band + band, fld, rows, :]
                        for band in range(n_band)
                    ],
                    axis=1,
                )
                for fld in range(n_fld)
                for sec in range(n_sec)
            ],
            axis=0,
        )
        result = lax.dot_general(left, basis, NT, preferred_element_type=F32)
        for third in range(THIRDS):
            part = result[:, third * degrees : (third + 1) * degrees]
            for fld in range(n_fld):
                for real in range(2):
                    levels = [
                        part[(fld * n_sec + sec) * half + real * lev :][:lev]
                        for sec in range(n_sec)
                    ]
                    out[2 * third + parity, real, fld] = jnp.concatenate(levels, axis=0).astype(
                        BF16
                    )


def slot_rows(blocks, across, lat_pad):
    shift = 16
    factor = -(-(1 << shift) // across)
    lat = lax.shift_right_logical(blocks * factor, shift)
    return (blocks - lat * across) * lat_pad + lat


def local_kernel(lat_pad, parts, grid_hbm, blocks_hbm, interp_hbm, table_hbm, out,
                 grid, blocks, interp, table, patch, column, selector, message, padded, rows,
                 sems, send):
    lev, lat, lon = grid.shape
    across = lon // LANES
    slots = interp.shape[0]
    depth = patch.shape[0]
    step = lon // parts
    small = [
        pltpu.make_async_copy(blocks_hbm, blocks, sems.at[parts]),
        pltpu.make_async_copy(interp_hbm, interp, sems.at[parts + 1]),
    ]
    loads = [
        pltpu.make_async_copy(
            grid_hbm.at[:, :, pl.ds(part * step, step)],
            grid.at[:, :, pl.ds(part * step, step)],
            sems.at[part],
        )
        for part in range(parts)
    ]
    tables = [
        pltpu.make_async_copy(
            table_hbm.at[pl.ds(part * step, step)],
            table.at[pl.ds(part * step, step)],
            sems.at[parts + 2 + part],
        )
        for part in range(parts)
    ]
    small[0].start()
    for part in range(parts):
        loads[part].start()
        tables[part].start()
    small[1].start()
    small[0].wait()
    row = slot_rows(blocks[...], across, lat_pad)
    column[...] = jnp.transpose(jnp.broadcast_to(row, (LANES, slots)))
    chunk = 256
    lane = lax.broadcasted_iota(jnp.int32, (chunk, LANES), 1)
    for start in range(0, slots, chunk):
        mine = column[start : start + chunk, :]
        for base in range(0, depth, LANES):
            selector[start : start + chunk, base : base + LANES] = jnp.where(
                mine == lane + base, 1.0, 0.0
            ).astype(BF16)
    coeffs = jnp.zeros((lev * lat, table.shape[1]), F32)
    for part in range(parts):
        loads[part].wait()
        tables[part].wait()
        flat = jnp.concatenate(
            [grid[level, :, part * step : (part + 1) * step] for level in range(lev)], axis=0
        )
        coeffs = coeffs + jnp.dot(
            flat, table[part * step : (part + 1) * step, :], preferred_element_type=F32
        )
        for tile in range(part * across // parts, (part + 1) * across // parts):
            patch[tile * lat_pad + lat : (tile + 1) * lat_pad, :] = jnp.zeros(
                (lat_pad - lat, lev * LANES), BF16
            )
            for level in range(lev):
                patch[
                    tile * lat_pad : tile * lat_pad + lat, level * LANES : (level + 1) * LANES
                ] = grid[level, :, tile * LANES : (tile + 1) * LANES]
    if depth > across * lat_pad:
        patch[across * lat_pad :, :] = jnp.zeros((depth - across * lat_pad, lev * LANES), BF16)
    small[1].wait()
    for start in range(0, slots, chunk):
        picked = jnp.dot(
            selector[start : start + chunk, :], patch[...], preferred_element_type=F32
        )
        weights = interp[start : start + chunk, :].astype(F32)
        total = jnp.zeros((chunk, LANES), F32)
        for level in range(lev):
            product = picked[:, level * LANES : (level + 1) * LANES] * weights
            total = jnp.where(lane == level, jnp.sum(product, axis=1, keepdims=True), total)
        state = jnp.transpose(total)[:lev].astype(BF16)
        for tile in range(chunk // LANES):
            row = message.shape[1] - slots // LANES * lev + (start // LANES + tile) * lev
            for target in range(message.shape[0]):
                message[target, row : row + lev, :] = state[:, tile * LANES : (tile + 1) * LANES]
    pack(lev, lat, coeffs, message, padded, rows)
    copy = pltpu.make_async_copy(message, out, send.at[0])
    copy.start()
    copy.wait()


def regroup_kernel(n_band, arrived, _, out, out_state, sems):
    size = out.shape[2]
    copies = []
    for target in range(out.shape[0]):
        rows = pl.ds(target % n_band * size, size)
        copies.append(
            pltpu.make_async_copy(arrived.at[:, rows, :], out.at[target], sems.at[target])
        )
    rows = pl.ds(n_band * size, out_state.shape[1])
    copies.append(
        pltpu.make_async_copy(arrived.at[:, rows, :], out_state, sems.at[out.shape[0]])
    )
    for copy in copies:
        copy.start()
    for copy in copies:
        copy.wait()


def softplus(x):
    power = jnp.exp(jnp.minimum(x, 80.0))
    return jnp.where(x < -8.0, power, jnp.maximum(x, jnp.log(1.0 + power)))


def column_kernel(n_sec, n_fld, lat_pad, slots, counts, weights, inverses, blocks, interp,
                  near, far, out, state, spread, result, sems):
    lev = near.shape[1] * LANES // slots
    place = lax.axis_index("sec")
    for fld in range(n_fld):
        for shift, pieces in enumerate((near, far)):
            row = (fld * n_sec + (place ^ shift)) * lev
            for tile in range(slots // LANES):
                state[
                    pl.ds(pl.multiple_of(row, lev), lev), tile * LANES : (tile + 1) * LANES
                ] = pieces[fld, tile * lev : (tile + 1) * lev, :].astype(F32)
    mine, lat, lon = result.shape
    across = lon // LANES
    sources, flux_rows = inverses.shape
    levels = flux_rows // 2
    count = counts[lax.axis_index("band")]
    base = (place * n_fld + lax.axis_index("fld")) * mine
    chunk = 256
    lane = lax.broadcasted_iota(jnp.int32, (1, flux_rows), 1)
    slot = lax.broadcasted_iota(jnp.int32, (chunk, 1), 0)
    for start in range(0, slots, chunk):
        column = jnp.transpose(state[:, start : start + chunk]).astype(BF16)
        flux = jnp.zeros((chunk, flux_rows), F32)
        for source in range(0, sources, chunk):
            gates = jnp.dot(
                column, weights[:, source : source + chunk], preferred_element_type=F32
            )
            flux = flux + jnp.dot(
                softplus(gates).astype(BF16),
                inverses[source : source + chunk, :],
                preferred_element_type=F32,
            )
        for level in range(mine):
            at = base + level
            plus = (lane == at) | ((lane == at + levels + 1) & (at + 1 < levels))
            minus = (lane == at + levels) | ((lane == at + 1) & (at + 1 < levels))
            terms = jnp.where(plus, flux, 0.0) - jnp.where(minus, flux, 0.0)
            heat = jnp.sum(terms, axis=1, keepdims=True)
            heat = jnp.where(slot + start < count, heat, 0.0).astype(BF16).astype(F32)
            spread[start : start + chunk, level * LANES : (level + 1) * LANES] = (
                heat * interp[start : start + chunk, :].astype(F32)
            ).astype(BF16)
    row = slot_rows(blocks[...], across, lat_pad)
    tiles = max(t for t in range(1, 8) if across % t == 0)
    height = tiles * lat_pad
    copies = []
    for first in range(0, across, tiles):
        match = row == lax.broadcasted_iota(jnp.int32, (height, slots), 0) + first * lat_pad
        left = jnp.where(match, 1.0, 0.0).astype(BF16)
        summed = jnp.dot(left, spread[...], preferred_element_type=F32).astype(BF16)
        for level in range(mine):
            for tile in range(tiles):
                result[level, :, (first + tile) * LANES : (first + tile + 1) * LANES] = summed[
                    tile * lat_pad : tile * lat_pad + lat, level * LANES : (level + 1) * LANES
                ]
        columns = pl.ds(first * LANES, tiles * LANES)
        copies.append(
            pltpu.make_async_copy(
                result.at[:, :, columns], out.at[:, :, columns], sems.at[first // tiles]
            )
        )
        copies[-1].start()
    for copy in copies:
        copy.wait()


def call(kernel, outs, specs, scratch, args, flops, size, name, out_spec=VMEM, limit=LIMIT):
    shapes = [jax.ShapeDtypeStruct(shape, dtype) for shape, dtype in outs]
    single = len(outs) == 1
    return pl.pallas_call(
        kernel,
        out_shape=shapes[0] if single else shapes,
        in_specs=specs,
        out_specs=out_spec if single else [out_spec] * len(outs),
        scratch_shapes=scratch,
        compiler_params=pltpu.CompilerParams(vmem_limit_bytes=limit),
        cost_estimate=pl.CostEstimate(flops=flops, bytes_accessed=size, transcendentals=0),
        name=name,
    )(*args)


def body(grid, legendre, counts, blocks, interp, source_weights, inverses):
    n_sec = lax.axis_size("sec")
    n_band = lax.axis_size("band")
    n_fld = lax.axis_size("fld")
    lev, lat, lon = grid.shape[1:]
    wave_dev, _, degrees = legendre.shape
    slots = blocks.shape[0]
    across = lon // LANES
    lat_pad = -(-lat // 16) * 16
    rest = 2 * wave_dev // THIRDS
    piece = rest * lev
    block_row = blocks.reshape(1, slots)

    table = jnp.asarray(dft_table(lon, wave_dev, n_band, n_fld))
    group = n_fld * n_band * rest
    padded_group = -(-group // LANES) * LANES
    depth = -(-across * lat_pad // LANES) * LANES
    parts = max(t for t in range(1, 8) if across % t == 0)
    state_rows = slots * lev // LANES
    message_rows = n_band * piece + state_rows
    message = call(
        functools.partial(local_kernel, lat_pad, parts),
        [((n_fld, message_rows, LANES), BF16)],
        [HBM] * 4,
        [
            pltpu.VMEM((lev, lat, lon), BF16),
            pltpu.VMEM((1, slots), jnp.int32),
            pltpu.VMEM((slots, LANES), BF16),
            pltpu.VMEM(table.shape, BF16),
            pltpu.VMEM((depth, lev * LANES), BF16),
            pltpu.VMEM((slots, LANES), jnp.int32),
            pltpu.VMEM((slots, depth), BF16),
            pltpu.VMEM((n_fld, message_rows, LANES), BF16),
            pltpu.VMEM((LANES, padded_group), F32),
            pltpu.VMEM((group * lev, LANES), F32),
            pltpu.SemaphoreType.DMA((2 * parts + 2,)),
            pltpu.SemaphoreType.DMA((1,)),
        ],
        (grid.reshape(lev, lat, lon), block_row, interp, table),
        2 * slots * depth * lev * LANES + 2 * lev * lat * lon * THIRDS * group,
        2 * lev * lat * lon + 2 * slots * LANES,
        "local",
        HBM,
        WHOLE,
    )
    arrived = lax.all_to_all(message, "fld", 0, 0, tiled=True)
    spec_bands, flux_rows, _ = inverses.shape
    basis, inverse_rows = call(
        functools.partial(prepare_kernel, lat, n_band),
        [
            ((n_band, 2, THIRDS * degrees, LANES), BF16),
            ((spec_bands * flux_rows, flux_rows), BF16),
        ],
        [VMEM, VMEM],
        [
            pltpu.VMEM((degrees, (n_band * lat // LANES + 2) * LANES), F32),
            pltpu.VMEM((flux_rows * flux_rows, spec_bands), F32),
            pltpu.VMEM((spec_bands * flux_rows, flux_rows), F32),
        ],
        (jnp.swapaxes(legendre, 1, 2), jnp.transpose(inverses, (1, 2, 0))),
        0,
        8 * wave_dev * degrees * n_band * LANES,
        "prepare",
    )
    sent, near = call(
        functools.partial(regroup_kernel, n_band),
        [((n_sec * n_band, n_fld, piece, LANES), BF16), ((n_fld, state_rows, LANES), BF16)],
        [HBM, HBM],
        [pltpu.SemaphoreType.DMA((n_sec * n_band + 1,))],
        (arrived, basis),
        0,
        4 * n_sec * n_band * n_fld * piece * LANES,
        "regroup",
        HBM,
    )
    far = lax.ppermute(near, "sec", [(i, 1 - i) for i in range(n_sec)])
    pieces = lax.all_to_all(sent, ("sec", "band"), 0, 0, tiled=True)
    sources = spec_bands * flux_rows
    states = source_weights.shape[0]
    mine = n_sec * lev // (n_sec * n_fld)
    heating = call(
        functools.partial(column_kernel, n_sec, n_fld, lat_pad, slots),
        [((mine, lat, lon), BF16)],
        [SMEM] + [VMEM] * 6,
        [
            pltpu.VMEM((states, slots), F32),
            pltpu.VMEM((slots, mine * LANES), BF16),
            pltpu.VMEM((mine, lat, lon), BF16),
            pltpu.SemaphoreType.DMA((across,)),
        ],
        (counts, source_weights, inverse_rows, block_row, interp, near, far),
        8 * slots * slots * 1024,
        2 * slots * slots,
        "columns",
        HBM,
    )

    spectral = call(
        functools.partial(legendre_kernel, n_sec, n_band, n_fld, lev),
        [((wave_dev, 2, n_fld, n_sec * lev, degrees), BF16)],
        [VMEM, VMEM],
        [],
        (basis, pieces),
        4 * n_sec * n_fld * piece * n_band * LANES * degrees * THIRDS,
        2 * n_sec * n_band * n_fld * piece * LANES,
        "legendre",
    )
    return (spectral, heating)


def solution(mesh):
    return jax.shard_map(
        body,
        mesh=mesh,
        in_specs=(
            P("fld", "sec", "band", None),
            P(("band", "fld"), None, "sec"),
            P(),
            P("band"),
            P("band", None),
            P(),
            P(),
        ),
        out_specs=(P(("band", "fld"), None, None, None, "sec"), P(("sec", "fld"), "band", None)),
        check_vma=False,
    )
```

```python
import functools
import math

import jax
import jax.numpy as jnp
import numpy as np
from jax import lax
from jax.experimental import pallas as pl
from jax.experimental.pallas import tpu as pltpu
from jax.sharding import PartitionSpec as P

BF16 = jnp.bfloat16
F32 = jnp.float32
LANES = 128
THIRDS = 3
LN_2 = math.log(2.0)
VMEM = pl.BlockSpec(memory_space=pltpu.VMEM)
HBM = pl.BlockSpec(memory_space=pltpu.HBM)
SMEM = pl.BlockSpec(memory_space=pltpu.SMEM)
LIMIT = 40 * 1024 * 1024
ROOM = 1200 * 1024
WHOLE = 64 * 1024 * 1024 - ROOM
NT = (((1,), (1,)), ((), ()))


def dft_table(lon, wave_dev, n_band, n_fld):
    values_dev = 2 * wave_dev
    rest = values_dev // THIRDS
    third, band, fld, low = np.meshgrid(
        np.arange(THIRDS), np.arange(n_band), np.arange(n_fld), np.arange(rest), indexing="ij"
    )
    value = third * rest + low
    wave = ((band * n_fld + fld) * wave_dev + value // 2).reshape(-1)
    part = (value % 2).reshape(-1)
    phase = np.arange(lon, dtype=np.int64)[:, None] * wave[None, :] % lon
    angle = phase * (2.0 * math.pi / lon)
    values = np.where(part[None, :] == 0, np.cos(angle), -np.sin(angle)) / math.sqrt(lon)
    return values.astype(np.float32).astype(BF16)


def pack(lev, lat, coeffs, packed, padded, rows):
    group = coeffs.shape[1] // THIRDS
    padded[...] = jnp.zeros_like(padded)
    for level in range(lev):
        for third in range(THIRDS):
            padded[third * lat : (third + 1) * lat, :group] = coeffs[
                level * lat : (level + 1) * lat, third * group : (third + 1) * group
            ]
        rows[pl.ds(level, group, stride=lev), :] = jnp.transpose(padded[...])[:group]
    packed[...] = rows[...].astype(BF16).reshape(packed.shape)


def prepare_kernel(lat, n_band, legendre, inverses, out, out_inverses, wide, rows, turned):
    flux_rows, _, spec_bands = inverses.shape
    for row in range(flux_rows):
        rows[row * flux_rows : (row + 1) * flux_rows, :] = inverses[row].astype(F32)
    for row in range(flux_rows):
        turned[pl.ds(row, spec_bands, stride=flux_rows), :] = jnp.transpose(
            rows[pl.ds(row, flux_rows, stride=flux_rows), :]
        )
    out_inverses[...] = turned[...].astype(BF16)
    waves, degrees, _ = legendre.shape
    wide[...] = jnp.zeros_like(wide)
    lane = lax.broadcasted_iota(jnp.int32, (degrees, LANES), 1)
    for wave in range(waves):
        third, parity = wave // 2, wave % 2
        wide[:, : n_band * lat] = legendre[wave].astype(F32)
        place = third * lat
        live = (lane >= place) & (lane < place + lat)
        for band in range(n_band):
            base = band * lat // LANES * LANES
            moved = pltpu.roll(
                wide[:, base : base + 2 * LANES], (place - (band * lat - base)) % (2 * LANES), 1
            )
            out[band, parity, third * degrees : (third + 1) * degrees, :] = jnp.where(
                live, moved[:, :LANES], 0.0
            ).astype(BF16)


def legendre_kernel(n_sec, n_band, n_fld, lev, weights, pieces, out):
    degrees = out.shape[4]
    half = pieces.shape[1] // 2
    for parity in range(2):
        rows = slice(parity * half, (parity + 1) * half)
        basis = jnp.concatenate([weights[band, parity] for band in range(n_band)], axis=1)
        left = jnp.concatenate(
            [
                jnp.concatenate(
                    [
                        pieces[(sec * n_band + band) * n_fld + fld, rows, :]
                        for band in range(n_band)
                    ],
                    axis=1,
                )
                for fld in range(n_fld)
                for sec in range(n_sec)
            ],
            axis=0,
        )
        result = lax.dot_general(left, basis, NT, preferred_element_type=F32)
        for third in range(THIRDS):
            part = result[:, third * degrees : (third + 1) * degrees]
            for fld in range(n_fld):
                for real in range(2):
                    levels = [
                        part[(fld * n_sec + sec) * half + real * lev :][:lev]
                        for sec in range(n_sec)
                    ]
                    out[2 * third + parity, real, fld] = jnp.concatenate(levels, axis=0).astype(
                        BF16
                    )


def slot_rows(blocks, across, lat_pad):
    shift = 16
    factor = -(-(1 << shift) // across)
    lat = lax.shift_right_logical(blocks * factor, shift)
    return (blocks - lat * across) * lat_pad + lat


def local_kernel(lat_pad, parts, grid_hbm, blocks_hbm, interp_hbm, table_hbm, out,
                 out_fourier, grid, blocks, interp, table, patch, column, selector, state, packed,
                 padded, rows, sems, sends):
    lev, lat, lon = grid.shape
    across = lon // LANES
    slots = interp.shape[0]
    depth = patch.shape[0]
    step = lon // parts
    small = [
        pltpu.make_async_copy(blocks_hbm, blocks, sems.at[parts]),
        pltpu.make_async_copy(interp_hbm, interp, sems.at[parts + 1]),
        pltpu.make_async_copy(table_hbm, table, sems.at[parts + 2]),
    ]
    loads = [
        pltpu.make_async_copy(
            grid_hbm.at[:, :, pl.ds(part * step, step)],
            grid.at[:, :, pl.ds(part * step, step)],
            sems.at[part],
        )
        for part in range(parts)
    ]
    small[0].start()
    for copy in loads:
        copy.start()
    small[1].start()
    small[2].start()
    small[0].wait()
    row = slot_rows(blocks[...], across, lat_pad)
    column[...] = jnp.transpose(jnp.broadcast_to(row, (LANES, slots)))
    chunk = 256
    lane = lax.broadcasted_iota(jnp.int32, (chunk, LANES), 1)
    for start in range(0, slots, chunk):
        mine = column[start : start + chunk, :]
        for base in range(0, depth, LANES):
            selector[start : start + chunk, base : base + LANES] = jnp.where(
                mine == lane + base, 1.0, 0.0
            ).astype(BF16)
    for part in range(parts):
        loads[part].wait()
        for tile in range(part * across // parts, (part + 1) * across // parts):
            patch[tile * lat_pad + lat : (tile + 1) * lat_pad, :] = jnp.zeros(
                (lat_pad - lat, lev * LANES), BF16
            )
            for level in range(lev):
                patch[
                    tile * lat_pad : tile * lat_pad + lat, level * LANES : (level + 1) * LANES
                ] = grid[level, :, tile * LANES : (tile + 1) * LANES]
    if depth > across * lat_pad:
        patch[across * lat_pad :, :] = jnp.zeros((depth - across * lat_pad, lev * LANES), BF16)
    small[1].wait()
    for start in range(0, slots, chunk):
        picked = jnp.dot(
            selector[start : start + chunk, :], patch[...], preferred_element_type=F32
        )
        weights = interp[start : start + chunk, :].astype(F32)
        total = jnp.zeros((chunk, LANES), F32)
        for level in range(lev):
            product = picked[:, level * LANES : (level + 1) * LANES] * weights
            total = jnp.where(lane == level, jnp.sum(product, axis=1, keepdims=True), total)
        state[:, start : start + chunk] = jnp.transpose(total * (1.0 / LN_2))[:lev].astype(BF16)
    copies = [pltpu.make_async_copy(state, out.at[0], sends.at[0])]
    copies[0].start()
    small[2].wait()
    flat = jnp.concatenate([grid[level] for level in range(lev)], axis=0)
    coeffs = jnp.dot(flat, table[...], preferred_element_type=F32)
    pack(lev, lat, coeffs, packed, padded, rows)
    copies.append(pltpu.make_async_copy(packed, out_fourier, sends.at[1]))
    copies[1].start()
    for copy in copies:
        copy.wait()


def merge_kernel(state, other, packed, out_state, out, sems):
    devices = packed.shape[0]
    copies = [
        pltpu.make_async_copy(state, out_state.at[pl.ds(0, 1)], sems.at[0]),
        pltpu.make_async_copy(other, out_state.at[pl.ds(1, 1)], sems.at[1]),
    ]
    for sec in range(out.shape[0] // devices):
        copies.append(
            pltpu.make_async_copy(packed, out.at[pl.ds(sec * devices, devices)], sems.at[2 + sec])
        )
    for copy in copies:
        copy.start()
    for copy in copies:
        copy.wait()


def softplus(x):
    power = jnp.exp2(jnp.minimum(x, 120.0))
    return jnp.where(x < -13.0, power, jnp.maximum(x * LN_2, jnp.log(1.0 + power)))


def column_kernel(n_sec, n_fld, lat_pad, slots, counts, weights, inverses, blocks, interp,
                  near, far, out, state, spread, result, sems):
    lev = near.shape[1]
    place = lax.axis_index("sec")
    for fld in range(n_fld):
        for shift, pieces in enumerate((near, far)):
            row = ((lax.axis_index("fld") ^ fld) * n_sec + (place ^ shift)) * lev
            state[pl.ds(pl.multiple_of(row, lev), lev), :] = pieces[fld].astype(F32)
    mine, lat, lon = result.shape
    across = lon // LANES
    sources, flux_rows = inverses.shape
    levels = flux_rows // 2
    count = counts[lax.axis_index("band")]
    base = (place * n_fld + lax.axis_index("fld")) * mine
    chunk = 256
    lane = lax.broadcasted_iota(jnp.int32, (1, flux_rows), 1)
    slot = lax.broadcasted_iota(jnp.int32, (chunk, 1), 0)
    for start in range(0, slots, chunk):
        column = jnp.transpose(state[:, start : start + chunk]).astype(BF16)
        flux = jnp.zeros((chunk, flux_rows), F32)
        for source in range(0, sources, chunk):
            gates = jnp.dot(
                column, weights[:, source : source + chunk], preferred_element_type=F32
            )
            flux = flux + jnp.dot(
                softplus(gates).astype(BF16),
                inverses[source : source + chunk, :],
                preferred_element_type=F32,
            )
        for level in range(mine):
            at = base + level
            plus = (lane == at) | ((lane == at + levels + 1) & (at + 1 < levels))
            minus = (lane == at + levels) | ((lane == at + 1) & (at + 1 < levels))
            terms = jnp.where(plus, flux, 0.0) - jnp.where(minus, flux, 0.0)
            heat = jnp.sum(terms, axis=1, keepdims=True)
            heat = jnp.where(slot + start < count, heat, 0.0).astype(BF16).astype(F32)
            spread[start : start + chunk, level * LANES : (level + 1) * LANES] = (
                heat * interp[start : start + chunk, :].astype(F32)
            ).astype(BF16)
    row = slot_rows(blocks[...], across, lat_pad)
    tiles = max(t for t in range(1, 8) if across % t == 0)
    height = tiles * lat_pad
    copies = []
    for first in range(0, across, tiles):
        match = row == lax.broadcasted_iota(jnp.int32, (height, slots), 0) + first * lat_pad
        left = jnp.where(match, 1.0, 0.0).astype(BF16)
        summed = jnp.dot(left, spread[...], preferred_element_type=F32).astype(BF16)
        for level in range(mine):
            for tile in range(tiles):
                result[level, :, (first + tile) * LANES : (first + tile + 1) * LANES] = summed[
                    tile * lat_pad : tile * lat_pad + lat, level * LANES : (level + 1) * LANES
                ]
        columns = pl.ds(first * LANES, tiles * LANES)
        copies.append(
            pltpu.make_async_copy(
                result.at[:, :, columns], out.at[:, :, columns], sems.at[first // tiles]
            )
        )
        copies[-1].start()
    for copy in copies:
        copy.wait()


def call(kernel, outs, specs, scratch, args, flops, size, name, out_spec=VMEM, limit=LIMIT):
    shapes = [jax.ShapeDtypeStruct(shape, dtype) for shape, dtype in outs]
    single = len(outs) == 1
    return pl.pallas_call(
        kernel,
        out_shape=shapes[0] if single else shapes,
        in_specs=specs,
        out_specs=out_spec if single else [out_spec] * len(outs),
        scratch_shapes=scratch,
        compiler_params=pltpu.CompilerParams(vmem_limit_bytes=limit),
        cost_estimate=pl.CostEstimate(flops=flops, bytes_accessed=size, transcendentals=0),
        name=name,
    )(*args)


def exchange(value, axis, shift):
    return lax.ppermute(value, axis, [(i, i ^ shift) for i in range(lax.axis_size(axis))])


def body(grid, legendre, counts, blocks, interp, source_weights, inverses):
    n_sec = lax.axis_size("sec")
    n_band = lax.axis_size("band")
    n_fld = lax.axis_size("fld")
    lev, lat, lon = grid.shape[1:]
    wave_dev, _, degrees = legendre.shape
    slots = blocks.shape[0]
    across = lon // LANES
    lat_pad = -(-lat // 16) * 16
    rest = 2 * wave_dev // THIRDS
    piece = rest * lev
    block_row = blocks.reshape(1, slots)

    table = jnp.asarray(dft_table(lon, wave_dev, n_band, n_fld))
    group = n_fld * n_band * rest
    padded_group = -(-group // LANES) * LANES
    depth = -(-across * lat_pad // LANES) * LANES
    parts = max(t for t in range(1, 8) if across % t == 0)
    state, packed = call(
        functools.partial(local_kernel, lat_pad, parts),
        [((1, lev, slots), BF16), ((n_band * n_fld, piece, LANES), BF16)],
        [HBM] * 4,
        [
            pltpu.VMEM((lev, lat, lon), BF16),
            pltpu.VMEM((1, slots), jnp.int32),
            pltpu.VMEM((slots, LANES), BF16),
            pltpu.VMEM(table.shape, BF16),
            pltpu.VMEM((depth, lev * LANES), BF16),
            pltpu.VMEM((slots, LANES), jnp.int32),
            pltpu.VMEM((slots, depth), BF16),
            pltpu.VMEM((lev, slots), BF16),
            pltpu.VMEM((n_band * n_fld, piece, LANES), BF16),
            pltpu.VMEM((LANES, padded_group), F32),
            pltpu.VMEM((group * lev, LANES), F32),
            pltpu.SemaphoreType.DMA((parts + 3,)),
            pltpu.SemaphoreType.DMA((2,)),
        ],
        (grid.reshape(lev, lat, lon), block_row, interp, table),
        2 * slots * depth * lev * LANES + 2 * lev * lat * lon * THIRDS * group,
        2 * lev * lat * lon + 2 * slots * LANES,
        "local",
        HBM,
        WHOLE,
    )
    other = exchange(state, "fld", 1)
    spec_bands, flux_rows, _ = inverses.shape
    basis, inverse_rows = call(
        functools.partial(prepare_kernel, lat, n_band),
        [
            ((n_band, 2, THIRDS * degrees, LANES), BF16),
            ((spec_bands * flux_rows, flux_rows), BF16),
        ],
        [VMEM, VMEM],
        [
            pltpu.VMEM((degrees, (n_band * lat // LANES + 2) * LANES), F32),
            pltpu.VMEM((flux_rows * flux_rows, spec_bands), F32),
            pltpu.VMEM((spec_bands * flux_rows, flux_rows), F32),
        ],
        (jnp.swapaxes(legendre, 1, 2), jnp.transpose(inverses, (1, 2, 0))),
        0,
        8 * wave_dev * degrees * n_band * LANES,
        "prepare",
    )
    near, sent = call(
        merge_kernel,
        [((2, lev, slots), BF16), ((n_sec * n_band * n_fld, piece, LANES), BF16)],
        [HBM] * 3,
        [pltpu.SemaphoreType.DMA((2 + n_sec,))],
        (state, other, packed),
        0,
        4 * n_sec * n_band * n_fld * piece * LANES,
        "merge",
        HBM,
    )
    bit = 2
    while bit < n_fld:
        near = jnp.concatenate([near, exchange(near, "fld", bit)], axis=0)
        bit *= 2
    pieces = lax.all_to_all(sent, ("sec", "band", "fld"), 0, 0, tiled=True)
    far = exchange(near, "sec", 1)
    sources = spec_bands * flux_rows
    states = source_weights.shape[0]
    mine = n_sec * lev // (n_sec * n_fld)
    heating = call(
        functools.partial(column_kernel, n_sec, n_fld, lat_pad, slots),
        [((mine, lat, lon), BF16)],
        [SMEM] + [VMEM] * 6,
        [
            pltpu.VMEM((states, slots), F32),
            pltpu.VMEM((slots, mine * LANES), BF16),
            pltpu.VMEM((mine, lat, lon), BF16),
            pltpu.SemaphoreType.DMA((across,)),
        ],
        (counts, source_weights, inverse_rows, block_row, interp, near, far),
        8 * slots * slots * 1024,
        2 * slots * slots,
        "columns",
        HBM,
    )

    spectral = call(
        functools.partial(legendre_kernel, n_sec, n_band, n_fld, lev),
        [((wave_dev, 2, n_fld, n_sec * lev, degrees), BF16)],
        [VMEM, VMEM],
        [],
        (basis, pieces),
        4 * n_sec * n_fld * piece * n_band * LANES * degrees * THIRDS,
        2 * n_sec * n_band * n_fld * piece * LANES,
        "legendre",
    )
    return (spectral, heating)


def solution(mesh):
    return jax.shard_map(
        body,
        mesh=mesh,
        in_specs=(
            P("fld", "sec", "band", None),
            P(("band", "fld"), None, "sec"),
            P(),
            P("band"),
            P("band", None),
            P(),
            P(),
        ),
        out_specs=(P(("band", "fld"), None, None, None, "sec"), P(("sec", "fld"), "band", None)),
        check_vma=False,
    )
```

```python
import functools
import math

import jax
import jax.numpy as jnp
import numpy as np
from jax import lax
from jax.experimental import pallas as pl
from jax.experimental.pallas import tpu as pltpu
from jax.sharding import PartitionSpec as P

BF16 = jnp.bfloat16
F32 = jnp.float32
LANES = 128
THIRDS = 3
VMEM = pl.BlockSpec(memory_space=pltpu.VMEM)
HBM = pl.BlockSpec(memory_space=pltpu.HBM)
SMEM = pl.BlockSpec(memory_space=pltpu.SMEM)
LIMIT = 40 * 1024 * 1024
ROOM = 1200 * 1024
WHOLE = 64 * 1024 * 1024 - ROOM
NT = (((1,), (1,)), ((), ()))


def dft_table(lon, wave_dev, n_band, n_fld):
    values_dev = 2 * wave_dev
    rest = values_dev // THIRDS
    third, fld, band, low = np.meshgrid(
        np.arange(THIRDS), np.arange(n_fld), np.arange(n_band), np.arange(rest), indexing="ij"
    )
    value = third * rest + low
    wave = ((band * n_fld + fld) * wave_dev + value // 2).reshape(-1)
    part = (value % 2).reshape(-1)
    phase = np.arange(lon, dtype=np.int64)[:, None] * wave[None, :] % lon
    angle = phase * (2.0 * math.pi / lon)
    values = np.where(part[None, :] == 0, np.cos(angle), -np.sin(angle)) / math.sqrt(lon)
    return values.astype(np.float32).astype(BF16)


def pack(lev, lat, coeffs, message, padded, rows):
    group = coeffs.shape[1] // THIRDS
    padded[...] = jnp.zeros_like(padded)
    for level in range(lev):
        for third in range(THIRDS):
            padded[third * lat : (third + 1) * lat, :group] = coeffs[
                level * lat : (level + 1) * lat, third * group : (third + 1) * group
            ]
        rows[pl.ds(level, group, stride=lev), :] = jnp.transpose(padded[...])[:group]
    targets = message.shape[0]
    size = rows.shape[0] // targets
    message[:, :size, :] = rows[...].astype(BF16).reshape(targets, size, LANES)


def prepare_kernel(lat, n_band, legendre, inverses, out, out_inverses, wide, rows, turned):
    flux_rows, _, spec_bands = inverses.shape
    for row in range(flux_rows):
        rows[row * flux_rows : (row + 1) * flux_rows, :] = inverses[row].astype(F32)
    for row in range(flux_rows):
        turned[pl.ds(row, spec_bands, stride=flux_rows), :] = jnp.transpose(
            rows[pl.ds(row, flux_rows, stride=flux_rows), :]
        )
    out_inverses[...] = turned[...].astype(BF16)
    waves, degrees, _ = legendre.shape
    wide[...] = jnp.zeros_like(wide)
    lane = lax.broadcasted_iota(jnp.int32, (degrees, LANES), 1)
    for wave in range(waves):
        third, parity = wave // 2, wave % 2
        wide[:, : n_band * lat] = legendre[wave].astype(F32)
        place = third * lat
        live = (lane >= place) & (lane < place + lat)
        for band in range(n_band):
            base = band * lat // LANES * LANES
            moved = pltpu.roll(
                wide[:, base : base + 2 * LANES], (place - (band * lat - base)) % (2 * LANES), 1
            )
            out[band, parity, third * degrees : (third + 1) * degrees, :] = jnp.where(
                live, moved[:, :LANES], 0.0
            ).astype(BF16)


def legendre_kernel(n_sec, n_band, n_fld, lev, weights, pieces, out):
    degrees = out.shape[4]
    half = pieces.shape[2] // 2
    for parity in range(2):
        rows = slice(parity * half, (parity + 1) * half)
        basis = jnp.concatenate([weights[band, parity] for band in range(n_band)], axis=1)
        left = jnp.concatenate(
            [
                jnp.concatenate(
                    [
                        pieces[sec * n_band + band, fld, rows, :]
                        for band in range(n_band)
                    ],
                    axis=1,
                )
                for fld in range(n_fld)
                for sec in range(n_sec)
            ],
            axis=0,
        )
        result = lax.dot_general(left, basis, NT, preferred_element_type=F32)
        for third in range(THIRDS):
            part = result[:, third * degrees : (third + 1) * degrees]
            for fld in range(n_fld):
                for real in range(2):
                    levels = [
                        part[(fld * n_sec + sec) * half + real * lev :][:lev]
                        for sec in range(n_sec)
                    ]
                    out[2 * third + parity, real, fld] = jnp.concatenate(levels, axis=0).astype(
                        BF16
                    )


def slot_rows(blocks, across, lat_pad):
    shift = 16
    factor = -(-(1 << shift) // across)
    lat = lax.shift_right_logical(blocks * factor, shift)
    return (blocks - lat * across) * lat_pad + lat


def local_kernel(lat_pad, parts, grid_hbm, blocks_hbm, interp_hbm, table_hbm, out,
                 grid, blocks, interp, table, patch, column, selector, message, padded, rows,
                 sems, send):
    lev, lat, lon = grid.shape
    across = lon // LANES
    slots = interp.shape[0]
    depth = patch.shape[0]
    step = lon // parts
    small = [
        pltpu.make_async_copy(blocks_hbm, blocks, sems.at[parts]),
        pltpu.make_async_copy(interp_hbm, interp, sems.at[parts + 1]),
        pltpu.make_async_copy(table_hbm, table, sems.at[parts + 2]),
    ]
    loads = [
        pltpu.make_async_copy(
            grid_hbm.at[:, :, pl.ds(part * step, step)],
            grid.at[:, :, pl.ds(part * step, step)],
            sems.at[part],
        )
        for part in range(parts)
    ]
    small[0].start()
    for copy in loads:
        copy.start()
    small[1].start()
    small[2].start()
    small[0].wait()
    row = slot_rows(blocks[...], across, lat_pad)
    column[...] = jnp.transpose(jnp.broadcast_to(row, (LANES, slots)))
    chunk = 256
    lane = lax.broadcasted_iota(jnp.int32, (chunk, LANES), 1)
    for start in range(0, slots, chunk):
        mine = column[start : start + chunk, :]
        for base in range(0, depth, LANES):
            selector[start : start + chunk, base : base + LANES] = jnp.where(
                mine == lane + base, 1.0, 0.0
            ).astype(BF16)
    for part in range(parts):
        loads[part].wait()
        for tile in range(part * across // parts, (part + 1) * across // parts):
            patch[tile * lat_pad + lat : (tile + 1) * lat_pad, :] = jnp.zeros(
                (lat_pad - lat, lev * LANES), BF16
            )
            for level in range(lev):
                patch[
                    tile * lat_pad : tile * lat_pad + lat, level * LANES : (level + 1) * LANES
                ] = grid[level, :, tile * LANES : (tile + 1) * LANES]
    if depth > across * lat_pad:
        patch[across * lat_pad :, :] = jnp.zeros((depth - across * lat_pad, lev * LANES), BF16)
    small[1].wait()
    first_state = message.shape[1] - slots // LANES * lev
    copies = [
        pltpu.make_async_copy(message.at[:, rows_of, :], out.at[:, rows_of, :], send.at[i])
        for i, rows_of in enumerate(
            (pl.ds(0, first_state), pl.ds(first_state, message.shape[1] - first_state))
        )
    ]
    for start in range(0, slots, chunk):
        picked = jnp.dot(
            selector[start : start + chunk, :], patch[...], preferred_element_type=F32
        )
        weights = interp[start : start + chunk, :].astype(F32)
        total = jnp.zeros((chunk, LANES), F32)
        for level in range(lev):
            product = picked[:, level * LANES : (level + 1) * LANES] * weights
            total = jnp.where(lane == level, jnp.sum(product, axis=1, keepdims=True), total)
        state = jnp.transpose(total)[:lev].astype(BF16)
        for tile in range(chunk // LANES):
            row = first_state + (start // LANES + tile) * lev
            for target in range(message.shape[0]):
                message[target, row : row + lev, :] = state[:, tile * LANES : (tile + 1) * LANES]
        if start == chunk:
            small[2].wait()
            flat = jnp.concatenate([grid[level] for level in range(lev)], axis=0)
            coeffs = jnp.dot(flat, table[...], preferred_element_type=F32)
            pack(lev, lat, coeffs, message, padded, rows)
            copies[0].start()
    copies[1].start()
    for copy in copies:
        copy.wait()


def regroup_kernel(n_band, arrived, _, out, out_state, sems):
    size = out.shape[2]
    copies = []
    for target in range(out.shape[0]):
        rows = pl.ds(target % n_band * size, size)
        copies.append(
            pltpu.make_async_copy(arrived.at[:, rows, :], out.at[target], sems.at[target])
        )
    rows = pl.ds(n_band * size, out_state.shape[1])
    copies.append(
        pltpu.make_async_copy(arrived.at[:, rows, :], out_state, sems.at[out.shape[0]])
    )
    for copy in copies:
        copy.start()
    for copy in copies:
        copy.wait()


def softplus(x):
    power = jnp.exp(jnp.minimum(x, 80.0))
    return jnp.where(x < -8.0, power, jnp.maximum(x, jnp.log(1.0 + power)))


def column_kernel(n_sec, n_fld, lat_pad, slots, counts, weights, inverses, blocks, interp,
                  near, far, out, state, spread, result, sems):
    lev = near.shape[1] * LANES // slots
    place = lax.axis_index("sec")
    for fld in range(n_fld):
        for shift, pieces in enumerate((near, far)):
            row = (fld * n_sec + (place ^ shift)) * lev
            for tile in range(slots // LANES):
                state[
                    pl.ds(pl.multiple_of(row, lev), lev), tile * LANES : (tile + 1) * LANES
                ] = pieces[fld, tile * lev : (tile + 1) * lev, :].astype(F32)
    mine, lat, lon = result.shape
    across = lon // LANES
    sources, flux_rows = inverses.shape
    levels = flux_rows // 2
    count = counts[lax.axis_index("band")]
    base = (place * n_fld + lax.axis_index("fld")) * mine
    chunk = 256
    lane = lax.broadcasted_iota(jnp.int32, (1, flux_rows), 1)
    slot = lax.broadcasted_iota(jnp.int32, (chunk, 1), 0)
    column = jnp.transpose(state[...]).astype(BF16)

    def gates_of(source):
        return jnp.dot(column, weights[:, source : source + chunk], preferred_element_type=F32)

    flux = jnp.zeros((slots, flux_rows), F32)
    gates = gates_of(0)
    for source in range(0, sources, chunk):
        later = gates_of(source + chunk) if source + chunk < sources else None
        flux = flux + jnp.dot(
            softplus(gates).astype(BF16),
            inverses[source : source + chunk, :],
            preferred_element_type=F32,
        )
        gates = later
    for start in range(0, slots, chunk):
        rows = flux[start : start + chunk]
        for level in range(mine):
            at = base + level
            plus = (lane == at) | ((lane == at + levels + 1) & (at + 1 < levels))
            minus = (lane == at + levels) | ((lane == at + 1) & (at + 1 < levels))
            terms = jnp.where(plus, rows, 0.0) - jnp.where(minus, rows, 0.0)
            heat = jnp.sum(terms, axis=1, keepdims=True)
            heat = jnp.where(slot + start < count, heat, 0.0).astype(BF16).astype(F32)
            spread[start : start + chunk, level * LANES : (level + 1) * LANES] = (
                heat * interp[start : start + chunk, :].astype(F32)
            ).astype(BF16)
    row = slot_rows(blocks[...], across, lat_pad)
    tiles = max(t for t in range(1, 8) if across % t == 0)
    height = tiles * lat_pad
    copies = []
    for first in range(0, across, tiles):
        match = row == lax.broadcasted_iota(jnp.int32, (height, slots), 0) + first * lat_pad
        left = jnp.where(match, 1.0, 0.0).astype(BF16)
        summed = jnp.dot(left, spread[...], preferred_element_type=F32).astype(BF16)
        for level in range(mine):
            for tile in range(tiles):
                result[level, :, (first + tile) * LANES : (first + tile + 1) * LANES] = summed[
                    tile * lat_pad : tile * lat_pad + lat, level * LANES : (level + 1) * LANES
                ]
        columns = pl.ds(first * LANES, tiles * LANES)
        copies.append(
            pltpu.make_async_copy(
                result.at[:, :, columns], out.at[:, :, columns], sems.at[first // tiles]
            )
        )
        copies[-1].start()
    for copy in copies:
        copy.wait()


def call(kernel, outs, specs, scratch, args, flops, size, name, out_spec=VMEM, limit=LIMIT):
    shapes = [jax.ShapeDtypeStruct(shape, dtype) for shape, dtype in outs]
    single = len(outs) == 1
    return pl.pallas_call(
        kernel,
        out_shape=shapes[0] if single else shapes,
        in_specs=specs,
        out_specs=out_spec if single else [out_spec] * len(outs),
        scratch_shapes=scratch,
        compiler_params=pltpu.CompilerParams(vmem_limit_bytes=limit),
        cost_estimate=pl.CostEstimate(flops=flops, bytes_accessed=size, transcendentals=0),
        name=name,
    )(*args)


def body(grid, legendre, counts, blocks, interp, source_weights, inverses):
    n_sec = lax.axis_size("sec")
    n_band = lax.axis_size("band")
    n_fld = lax.axis_size("fld")
    lev, lat, lon = grid.shape[1:]
    wave_dev, _, degrees = legendre.shape
    slots = blocks.shape[0]
    across = lon // LANES
    lat_pad = -(-lat // 16) * 16
    rest = 2 * wave_dev // THIRDS
    piece = rest * lev
    block_row = blocks.reshape(1, slots)

    table = jnp.asarray(dft_table(lon, wave_dev, n_band, n_fld))
    group = n_fld * n_band * rest
    padded_group = -(-group // LANES) * LANES
    depth = -(-across * lat_pad // LANES) * LANES
    parts = max(t for t in range(1, 8) if across % t == 0)
    state_rows = slots * lev // LANES
    message_rows = n_band * piece + state_rows
    message = call(
        functools.partial(local_kernel, lat_pad, parts),
        [((n_fld, message_rows, LANES), BF16)],
        [HBM] * 4,
        [
            pltpu.VMEM((lev, lat, lon), BF16),
            pltpu.VMEM((1, slots), jnp.int32),
            pltpu.VMEM((slots, LANES), BF16),
            pltpu.VMEM(table.shape, BF16),
            pltpu.VMEM((depth, lev * LANES), BF16),
            pltpu.VMEM((slots, LANES), jnp.int32),
            pltpu.VMEM((slots, depth), BF16),
            pltpu.VMEM((n_fld, message_rows, LANES), BF16),
            pltpu.VMEM((LANES, padded_group), F32),
            pltpu.VMEM((group * lev, LANES), F32),
            pltpu.SemaphoreType.DMA((parts + 3,)),
            pltpu.SemaphoreType.DMA((2,)),
        ],
        (grid.reshape(lev, lat, lon), block_row, interp, table),
        2 * slots * depth * lev * LANES + 2 * lev * lat * lon * THIRDS * group,
        2 * lev * lat * lon + 2 * slots * LANES,
        "local",
        HBM,
        WHOLE,
    )
    arrived = lax.all_to_all(message, "fld", 0, 0, tiled=True)
    spec_bands, flux_rows, _ = inverses.shape
    basis, inverse_rows = call(
        functools.partial(prepare_kernel, lat, n_band),
        [
            ((n_band, 2, THIRDS * degrees, LANES), BF16),
            ((spec_bands * flux_rows, flux_rows), BF16),
        ],
        [VMEM, VMEM],
        [
            pltpu.VMEM((degrees, (n_band * lat // LANES + 2) * LANES), F32),
            pltpu.VMEM((flux_rows * flux_rows, spec_bands), F32),
            pltpu.VMEM((spec_bands * flux_rows, flux_rows), F32),
        ],
        (jnp.swapaxes(legendre, 1, 2), jnp.transpose(inverses, (1, 2, 0))),
        0,
        8 * wave_dev * degrees * n_band * LANES,
        "prepare",
    )
    sent, near = call(
        functools.partial(regroup_kernel, n_band),
        [((n_sec * n_band, n_fld, piece, LANES), BF16), ((n_fld, state_rows, LANES), BF16)],
        [HBM, HBM],
        [pltpu.SemaphoreType.DMA((n_sec * n_band + 1,))],
        (arrived, basis),
        0,
        4 * n_sec * n_band * n_fld * piece * LANES,
        "regroup",
        HBM,
    )
    far = lax.ppermute(near, "sec", [(i, 1 - i) for i in range(n_sec)])
    pieces = lax.all_to_all(sent, ("sec", "band"), 0, 0, tiled=True)
    sources = spec_bands * flux_rows
    states = source_weights.shape[0]
    mine = n_sec * lev // (n_sec * n_fld)
    heating = call(
        functools.partial(column_kernel, n_sec, n_fld, lat_pad, slots),
        [((mine, lat, lon), BF16)],
        [SMEM] + [VMEM] * 6,
        [
            pltpu.VMEM((states, slots), F32),
            pltpu.VMEM((slots, mine * LANES), BF16),
            pltpu.VMEM((mine, lat, lon), BF16),
            pltpu.SemaphoreType.DMA((across,)),
        ],
        (counts, source_weights, inverse_rows, block_row, interp, near, far),
        8 * slots * slots * 1024,
        2 * slots * slots,
        "columns",
        HBM,
    )

    spectral = call(
        functools.partial(legendre_kernel, n_sec, n_band, n_fld, lev),
        [((wave_dev, 2, n_fld, n_sec * lev, degrees), BF16)],
        [VMEM, VMEM],
        [],
        (basis, pieces),
        4 * n_sec * n_fld * piece * n_band * LANES * degrees * THIRDS,
        2 * n_sec * n_band * n_fld * piece * LANES,
        "legendre",
    )
    return (spectral, heating)


def solution(mesh):
    return jax.shard_map(
        body,
        mesh=mesh,
        in_specs=(
            P("fld", "sec", "band", None),
            P(("band", "fld"), None, "sec"),
            P(),
            P("band"),
            P("band", None),
            P(),
            P(),
        ),
        out_specs=(P(("band", "fld"), None, None, None, "sec"), P(("sec", "fld"), "band", None)),
        check_vma=False,
    )
```

```python
import functools
import math

import jax
import jax.numpy as jnp
import numpy as np
from jax import lax
from jax.experimental import pallas as pl
from jax.experimental.pallas import tpu as pltpu
from jax.sharding import PartitionSpec as P

BF16 = jnp.bfloat16
F32 = jnp.float32
LANES = 128
THIRDS = 3
VMEM = pl.BlockSpec(memory_space=pltpu.VMEM)
HBM = pl.BlockSpec(memory_space=pltpu.HBM)
SMEM = pl.BlockSpec(memory_space=pltpu.SMEM)
LIMIT = 40 * 1024 * 1024
ROOM = 1200 * 1024
WHOLE = 64 * 1024 * 1024 - ROOM
NT = (((1,), (1,)), ((), ()))


def dft_table(lon, wave_dev, n_band, n_fld):
    values_dev = 2 * wave_dev
    rest = values_dev // THIRDS
    third, fld, band, low = np.meshgrid(
        np.arange(THIRDS), np.arange(n_fld), np.arange(n_band), np.arange(rest), indexing="ij"
    )
    value = third * rest + low
    wave = ((band * n_fld + fld) * wave_dev + value // 2).reshape(-1)
    part = (value % 2).reshape(-1)
    phase = np.arange(lon, dtype=np.int64)[:, None] * wave[None, :] % lon
    angle = phase * (2.0 * math.pi / lon)
    values = np.where(part[None, :] == 0, np.cos(angle), -np.sin(angle)) / math.sqrt(lon)
    return values.astype(np.float32).astype(BF16)


def pack(lev, lat, coeffs, message, padded, rows):
    group = coeffs.shape[1] // THIRDS
    padded[...] = jnp.zeros_like(padded)
    for level in range(lev):
        for third in range(THIRDS):
            padded[third * lat : (third + 1) * lat, :group] = coeffs[
                level * lat : (level + 1) * lat, third * group : (third + 1) * group
            ]
        rows[pl.ds(level, group, stride=lev), :] = jnp.transpose(padded[...])[:group]
    targets = message.shape[0]
    size = rows.shape[0] // targets
    message[:, :size, :] = rows[...].astype(BF16).reshape(targets, size, LANES)


def prepare_kernel(lat, n_band, legendre, inverses, out, out_inverses, wide, rows, turned):
    flux_rows, _, spec_bands = inverses.shape
    for row in range(flux_rows):
        rows[row * flux_rows : (row + 1) * flux_rows, :] = inverses[row].astype(F32)
    for row in range(flux_rows):
        turned[pl.ds(row, spec_bands, stride=flux_rows), :] = jnp.transpose(
            rows[pl.ds(row, flux_rows, stride=flux_rows), :]
        )
    out_inverses[...] = turned[...].astype(BF16)
    waves, degrees, _ = legendre.shape
    wide[...] = jnp.zeros_like(wide)
    lane = lax.broadcasted_iota(jnp.int32, (degrees, LANES), 1)
    for wave in range(waves):
        third, parity = wave // 2, wave % 2
        wide[:, : n_band * lat] = legendre[wave].astype(F32)
        place = third * lat
        live = (lane >= place) & (lane < place + lat)
        for band in range(n_band):
            base = band * lat // LANES * LANES
            moved = pltpu.roll(
                wide[:, base : base + 2 * LANES], (place - (band * lat - base)) % (2 * LANES), 1
            )
            out[band, parity, third * degrees : (third + 1) * degrees, :] = jnp.where(
                live, moved[:, :LANES], 0.0
            ).astype(BF16)


def legendre_kernel(n_sec, n_band, n_fld, lev, weights, pieces, out):
    degrees = out.shape[4]
    half = pieces.shape[2] // 2
    for parity in range(2):
        rows = slice(parity * half, (parity + 1) * half)
        basis = jnp.concatenate([weights[band, parity] for band in range(n_band)], axis=1)
        left = jnp.concatenate(
            [
                jnp.concatenate(
                    [
                        pieces[sec * n_band + band, fld, rows, :]
                        for band in range(n_band)
                    ],
                    axis=1,
                )
                for fld in range(n_fld)
                for sec in range(n_sec)
            ],
            axis=0,
        )
        result = lax.dot_general(left, basis, NT, preferred_element_type=F32)
        for third in range(THIRDS):
            part = result[:, third * degrees : (third + 1) * degrees]
            for fld in range(n_fld):
                for real in range(2):
                    levels = [
                        part[(fld * n_sec + sec) * half + real * lev :][:lev]
                        for sec in range(n_sec)
                    ]
                    out[2 * third + parity, real, fld] = jnp.concatenate(levels, axis=0).astype(
                        BF16
                    )


def slot_rows(blocks, across, lat_pad):
    shift = 16
    factor = -(-(1 << shift) // across)
    lat = lax.shift_right_logical(blocks * factor, shift)
    return (blocks - lat * across) * lat_pad + lat


def local_kernel(lat_pad, parts, grid_hbm, blocks_hbm, interp_hbm, table_hbm, out,
                 grid, blocks, interp, table, patch, column, selector, message, padded, rows,
                 totals, sems, send):
    lev, lat, lon = grid.shape
    across = lon // LANES
    slots = interp.shape[0]
    depth = patch.shape[0]
    step = lon // parts
    small = [
        pltpu.make_async_copy(blocks_hbm, blocks, sems.at[parts]),
        pltpu.make_async_copy(interp_hbm, interp, sems.at[parts + 1]),
        pltpu.make_async_copy(table_hbm, table, sems.at[parts + 2]),
    ]
    loads = [
        pltpu.make_async_copy(
            grid_hbm.at[:, :, pl.ds(part * step, step)],
            grid.at[:, :, pl.ds(part * step, step)],
            sems.at[part],
        )
        for part in range(parts)
    ]
    small[0].start()
    for copy in loads:
        copy.start()
    small[1].start()
    small[2].start()
    small[0].wait()
    row = slot_rows(blocks[...], across, lat_pad)
    column[...] = jnp.transpose(jnp.broadcast_to(row, (LANES, slots)))
    chunk = 256
    lane = lax.broadcasted_iota(jnp.int32, (chunk, LANES), 1)
    for start in range(0, slots, chunk):
        mine = column[start : start + chunk, :]
        for base in range(0, depth, LANES):
            selector[start : start + chunk, base : base + LANES] = jnp.where(
                mine == lane + base, 1.0, 0.0
            ).astype(BF16)
    for part in range(parts):
        loads[part].wait()
        for tile in range(part * across // parts, (part + 1) * across // parts):
            patch[tile * lat_pad + lat : (tile + 1) * lat_pad, :] = jnp.zeros(
                (lat_pad - lat, lev * LANES), BF16
            )
            for level in range(lev):
                patch[
                    tile * lat_pad : tile * lat_pad + lat, level * LANES : (level + 1) * LANES
                ] = grid[level, :, tile * LANES : (tile + 1) * LANES]
    if depth > across * lat_pad:
        patch[across * lat_pad :, :] = jnp.zeros((depth - across * lat_pad, lev * LANES), BF16)
    small[1].wait()
    first_state = message.shape[1] - slots // LANES * lev
    copies = [
        pltpu.make_async_copy(message.at[:, rows_of, :], out.at[:, rows_of, :], send.at[i])
        for i, rows_of in enumerate(
            (pl.ds(0, first_state), pl.ds(first_state, message.shape[1] - first_state))
        )
    ]
    pair = 2 * LANES
    for start in range(0, lev * LANES, pair):
        picked = jnp.dot(
            selector[...], patch[:, start : start + pair], preferred_element_type=F32
        )
        for side in range(2):
            level = start // LANES + side
            for top in range(0, slots, chunk):
                product = picked[top : top + chunk, side * LANES : (side + 1) * LANES] * interp[
                    top : top + chunk, :
                ].astype(F32)
                value = jnp.sum(product, axis=1, keepdims=True)
                if level == 0:
                    totals[top : top + chunk, :] = jnp.where(lane == level, value, 0.0)
                else:
                    totals[top : top + chunk, :] = jnp.where(
                        lane == level, value, totals[top : top + chunk, :]
                    )
        if start == pair:
            small[2].wait()
            flat = jnp.concatenate([grid[level] for level in range(lev)], axis=0)
            coeffs = jnp.dot(flat, table[...], preferred_element_type=F32)
            pack(lev, lat, coeffs, message, padded, rows)
            copies[0].start()
    for top in range(0, slots, LANES):
        state = jnp.transpose(totals[top : top + LANES, :])[:lev].astype(BF16)
        row = first_state + top // LANES * lev
        for target in range(message.shape[0]):
            message[target, row : row + lev, :] = state
    copies[1].start()
    for copy in copies:
        copy.wait()


def regroup_kernel(n_band, arrived, _, out, out_state, sems):
    size = out.shape[2]
    copies = []
    for target in range(out.shape[0]):
        rows = pl.ds(target % n_band * size, size)
        copies.append(
            pltpu.make_async_copy(arrived.at[:, rows, :], out.at[target], sems.at[target])
        )
    rows = pl.ds(n_band * size, out_state.shape[1])
    copies.append(
        pltpu.make_async_copy(arrived.at[:, rows, :], out_state, sems.at[out.shape[0]])
    )
    for copy in copies:
        copy.start()
    for copy in copies:
        copy.wait()


def softplus(x):
    power = jnp.exp(jnp.minimum(x, 80.0))
    return jnp.where(x < -8.0, power, jnp.maximum(x, jnp.log(1.0 + power)))


def column_kernel(n_sec, n_fld, lat_pad, slots, counts, weights, inverses, blocks, interp,
                  near, far, out, state, spread, result, sems):
    lev = near.shape[1] * LANES // slots
    place = lax.axis_index("sec")
    for fld in range(n_fld):
        for shift, pieces in enumerate((near, far)):
            row = (fld * n_sec + (place ^ shift)) * lev
            for tile in range(slots // LANES):
                state[
                    pl.ds(pl.multiple_of(row, lev), lev), tile * LANES : (tile + 1) * LANES
                ] = pieces[fld, tile * lev : (tile + 1) * lev, :].astype(F32)
    mine, lat, lon = result.shape
    across = lon // LANES
    sources, flux_rows = inverses.shape
    levels = flux_rows // 2
    count = counts[lax.axis_index("band")]
    base = (place * n_fld + lax.axis_index("fld")) * mine
    chunk = 256
    lane = lax.broadcasted_iota(jnp.int32, (1, flux_rows), 1)
    slot = lax.broadcasted_iota(jnp.int32, (chunk, 1), 0)
    column = jnp.transpose(state[...]).astype(BF16)

    def gates_of(source):
        return jnp.dot(column, weights[:, source : source + chunk], preferred_element_type=F32)

    flux = jnp.zeros((slots, flux_rows), F32)
    gates = gates_of(0)
    for source in range(0, sources, chunk):
        later = gates_of(source + chunk) if source + chunk < sources else None
        flux = flux + jnp.dot(
            softplus(gates).astype(BF16),
            inverses[source : source + chunk, :],
            preferred_element_type=F32,
        )
        gates = later
    for start in range(0, slots, chunk):
        rows = flux[start : start + chunk]
        for level in range(mine):
            at = base + level
            plus = (lane == at) | ((lane == at + levels + 1) & (at + 1 < levels))
            minus = (lane == at + levels) | ((lane == at + 1) & (at + 1 < levels))
            terms = jnp.where(plus, rows, 0.0) - jnp.where(minus, rows, 0.0)
            heat = jnp.sum(terms, axis=1, keepdims=True)
            heat = jnp.where(slot + start < count, heat, 0.0).astype(BF16).astype(F32)
            spread[start : start + chunk, level * LANES : (level + 1) * LANES] = (
                heat * interp[start : start + chunk, :].astype(F32)
            ).astype(BF16)
    row = slot_rows(blocks[...], across, lat_pad)
    tiles = max(t for t in range(1, 8) if across % t == 0)
    height = across * lat_pad
    match = row == lax.broadcasted_iota(jnp.int32, (height, slots), 0)
    left = jnp.where(match, 1.0, 0.0).astype(BF16)
    summed = jnp.dot(left, spread[...], preferred_element_type=F32).astype(BF16)
    copies = []
    for first in range(0, across, tiles):
        for level in range(mine):
            for tile in range(tiles):
                result[level, :, (first + tile) * LANES : (first + tile + 1) * LANES] = summed[
                    (first + tile) * lat_pad : (first + tile) * lat_pad + lat, level * LANES : (level + 1) * LANES
                ]
        columns = pl.ds(first * LANES, tiles * LANES)
        copies.append(
            pltpu.make_async_copy(
                result.at[:, :, columns], out.at[:, :, columns], sems.at[first // tiles]
            )
        )
        copies[-1].start()
    for copy in copies:
        copy.wait()


def call(kernel, outs, specs, scratch, args, flops, size, name, out_spec=VMEM, limit=LIMIT):
    shapes = [jax.ShapeDtypeStruct(shape, dtype) for shape, dtype in outs]
    single = len(outs) == 1
    return pl.pallas_call(
        kernel,
        out_shape=shapes[0] if single else shapes,
        in_specs=specs,
        out_specs=out_spec if single else [out_spec] * len(outs),
        scratch_shapes=scratch,
        compiler_params=pltpu.CompilerParams(vmem_limit_bytes=limit),
        cost_estimate=pl.CostEstimate(flops=flops, bytes_accessed=size, transcendentals=0),
        name=name,
    )(*args)


def body(grid, legendre, counts, blocks, interp, source_weights, inverses):
    n_sec = lax.axis_size("sec")
    n_band = lax.axis_size("band")
    n_fld = lax.axis_size("fld")
    lev, lat, lon = grid.shape[1:]
    wave_dev, _, degrees = legendre.shape
    slots = blocks.shape[0]
    across = lon // LANES
    lat_pad = -(-lat // 16) * 16
    rest = 2 * wave_dev // THIRDS
    piece = rest * lev
    block_row = blocks.reshape(1, slots)

    table = jnp.asarray(dft_table(lon, wave_dev, n_band, n_fld))
    group = n_fld * n_band * rest
    padded_group = -(-group // LANES) * LANES
    depth = -(-across * lat_pad // LANES) * LANES
    parts = max(t for t in range(1, 8) if across % t == 0)
    state_rows = slots * lev // LANES
    message_rows = n_band * piece + state_rows
    message = call(
        functools.partial(local_kernel, lat_pad, parts),
        [((n_fld, message_rows, LANES), BF16)],
        [HBM] * 4,
        [
            pltpu.VMEM((lev, lat, lon), BF16),
            pltpu.VMEM((1, slots), jnp.int32),
            pltpu.VMEM((slots, LANES), BF16),
            pltpu.VMEM(table.shape, BF16),
            pltpu.VMEM((depth, lev * LANES), BF16),
            pltpu.VMEM((slots, LANES), jnp.int32),
            pltpu.VMEM((slots, depth), BF16),
            pltpu.VMEM((n_fld, message_rows, LANES), BF16),
            pltpu.VMEM((LANES, padded_group), F32),
            pltpu.VMEM((group * lev, LANES), F32),
            pltpu.VMEM((slots, LANES), F32),
            pltpu.SemaphoreType.DMA((parts + 3,)),
            pltpu.SemaphoreType.DMA((2,)),
        ],
        (grid.reshape(lev, lat, lon), block_row, interp, table),
        2 * slots * depth * lev * LANES + 2 * lev * lat * lon * THIRDS * group,
        2 * lev * lat * lon + 2 * slots * LANES,
        "local",
        HBM,
        WHOLE,
    )
    arrived = lax.all_to_all(message, "fld", 0, 0, tiled=True)
    spec_bands, flux_rows, _ = inverses.shape
    basis, inverse_rows = call(
        functools.partial(prepare_kernel, lat, n_band),
        [
            ((n_band, 2, THIRDS * degrees, LANES), BF16),
            ((spec_bands * flux_rows, flux_rows), BF16),
        ],
        [VMEM, VMEM],
        [
            pltpu.VMEM((degrees, (n_band * lat // LANES + 2) * LANES), F32),
            pltpu.VMEM((flux_rows * flux_rows, spec_bands), F32),
            pltpu.VMEM((spec_bands * flux_rows, flux_rows), F32),
        ],
        (jnp.swapaxes(legendre, 1, 2), jnp.transpose(inverses, (1, 2, 0))),
        0,
        8 * wave_dev * degrees * n_band * LANES,
        "prepare",
    )
    sent, near = call(
        functools.partial(regroup_kernel, n_band),
        [((n_sec * n_band, n_fld, piece, LANES), BF16), ((n_fld, state_rows, LANES), BF16)],
        [HBM, HBM],
        [pltpu.SemaphoreType.DMA((n_sec * n_band + 1,))],
        (arrived, basis),
        0,
        4 * n_sec * n_band * n_fld * piece * LANES,
        "regroup",
        HBM,
    )
    far = lax.ppermute(near, "sec", [(i, 1 - i) for i in range(n_sec)])
    pieces = lax.all_to_all(sent, ("sec", "band"), 0, 0, tiled=True)
    sources = spec_bands * flux_rows
    states = source_weights.shape[0]
    mine = n_sec * lev // (n_sec * n_fld)
    heating = call(
        functools.partial(column_kernel, n_sec, n_fld, lat_pad, slots),
        [((mine, lat, lon), BF16)],
        [SMEM] + [VMEM] * 6,
        [
            pltpu.VMEM((states, slots), F32),
            pltpu.VMEM((slots, mine * LANES), BF16),
            pltpu.VMEM((mine, lat, lon), BF16),
            pltpu.SemaphoreType.DMA((across,)),
        ],
        (counts, source_weights, inverse_rows, block_row, interp, near, far),
        8 * slots * slots * 1024,
        2 * slots * slots,
        "columns",
        HBM,
    )

    spectral = call(
        functools.partial(legendre_kernel, n_sec, n_band, n_fld, lev),
        [((wave_dev, 2, n_fld, n_sec * lev, degrees), BF16)],
        [VMEM, VMEM],
        [],
        (basis, pieces),
        4 * n_sec * n_fld * piece * n_band * LANES * degrees * THIRDS,
        2 * n_sec * n_band * n_fld * piece * LANES,
        "legendre",
    )
    return (spectral, heating)


def solution(mesh):
    return jax.shard_map(
        body,
        mesh=mesh,
        in_specs=(
            P("fld", "sec", "band", None),
            P(("band", "fld"), None, "sec"),
            P(),
            P("band"),
            P("band", None),
            P(),
            P(),
        ),
        out_specs=(P(("band", "fld"), None, None, None, "sec"), P(("sec", "fld"), "band", None)),
        check_vma=False,
    )
```

```python
import functools
import math

import jax
import jax.numpy as jnp
import numpy as np
from jax import lax
from jax.experimental import pallas as pl
from jax.experimental.pallas import tpu as pltpu
from jax.sharding import PartitionSpec as P

BF16 = jnp.bfloat16
F32 = jnp.float32
LANES = 128
THIRDS = 3
VMEM = pl.BlockSpec(memory_space=pltpu.VMEM)
HBM = pl.BlockSpec(memory_space=pltpu.HBM)
SMEM = pl.BlockSpec(memory_space=pltpu.SMEM)
LIMIT = 40 * 1024 * 1024
ROOM = 1200 * 1024
WHOLE = 64 * 1024 * 1024 - ROOM
NT = (((1,), (1,)), ((), ()))


def dft_table(lon, wave_dev, n_band, n_fld):
    values_dev = 2 * wave_dev
    rest = values_dev // THIRDS
    third, fld, band, low = np.meshgrid(
        np.arange(THIRDS), np.arange(n_fld), np.arange(n_band), np.arange(rest), indexing="ij"
    )
    value = third * rest + low
    wave = ((band * n_fld + fld) * wave_dev + value // 2).reshape(-1)
    part = (value % 2).reshape(-1)
    phase = np.arange(lon, dtype=np.int64)[:, None] * wave[None, :] % lon
    angle = phase * (2.0 * math.pi / lon)
    values = np.where(part[None, :] == 0, np.cos(angle), -np.sin(angle)) / math.sqrt(lon)
    return values.astype(np.float32).astype(BF16)


def pack(lev, lat, coeffs, message, padded, rows):
    group = coeffs.shape[1] // THIRDS
    padded[...] = jnp.zeros_like(padded)
    for level in range(lev):
        for third in range(THIRDS):
            padded[third * lat : (third + 1) * lat, :group] = coeffs[
                level * lat : (level + 1) * lat, third * group : (third + 1) * group
            ]
        rows[pl.ds(level, group, stride=lev), :] = jnp.transpose(padded[...])[:group]
    targets = message.shape[0]
    size = rows.shape[0] // targets
    message[:, :size, :] = rows[...].astype(BF16).reshape(targets, size, LANES)


def prepare_kernel(lat, n_band, legendre, inverses, out, out_inverses, wide, rows, turned):
    flux_rows, _, spec_bands = inverses.shape
    for row in range(flux_rows):
        rows[row * flux_rows : (row + 1) * flux_rows, :] = inverses[row].astype(F32)
    for row in range(flux_rows):
        turned[pl.ds(row, spec_bands, stride=flux_rows), :] = jnp.transpose(
            rows[pl.ds(row, flux_rows, stride=flux_rows), :]
        )
    out_inverses[...] = turned[...].astype(BF16)
    waves, degrees, _ = legendre.shape
    wide[...] = jnp.zeros_like(wide)
    lane = lax.broadcasted_iota(jnp.int32, (degrees, LANES), 1)
    for wave in range(waves):
        third, parity = wave // 2, wave % 2
        wide[:, : n_band * lat] = legendre[wave].astype(F32)
        place = third * lat
        live = (lane >= place) & (lane < place + lat)
        for band in range(n_band):
            base = band * lat // LANES * LANES
            moved = pltpu.roll(
                wide[:, base : base + 2 * LANES], (place - (band * lat - base)) % (2 * LANES), 1
            )
            out[band, parity, third * degrees : (third + 1) * degrees, :] = jnp.where(
                live, moved[:, :LANES], 0.0
            ).astype(BF16)


def legendre_kernel(n_sec, n_band, n_fld, lev, weights, pieces, out):
    degrees = out.shape[4]
    half = pieces.shape[2] // 2
    for parity in range(2):
        rows = slice(parity * half, (parity + 1) * half)
        basis = jnp.concatenate([weights[band, parity] for band in range(n_band)], axis=1)
        left = jnp.concatenate(
            [
                jnp.concatenate(
                    [
                        pieces[sec * n_band + band, fld, rows, :]
                        for band in range(n_band)
                    ],
                    axis=1,
                )
                for fld in range(n_fld)
                for sec in range(n_sec)
            ],
            axis=0,
        )
        result = lax.dot_general(left, basis, NT, preferred_element_type=F32)
        for third in range(THIRDS):
            part = result[:, third * degrees : (third + 1) * degrees]
            for fld in range(n_fld):
                for real in range(2):
                    levels = [
                        part[(fld * n_sec + sec) * half + real * lev :][:lev]
                        for sec in range(n_sec)
                    ]
                    out[2 * third + parity, real, fld] = jnp.concatenate(levels, axis=0).astype(
                        BF16
                    )


def slot_rows(blocks, across, lat_pad):
    shift = 16
    factor = -(-(1 << shift) // across)
    lat = lax.shift_right_logical(blocks * factor, shift)
    return (blocks - lat * across) * lat_pad + lat


def local_kernel(lat_pad, grid_hbm, blocks_hbm, interp_hbm, table_hbm, out,
                 grid, blocks, interp, table, patch, column, selector, message, padded, rows,
                 totals, sems, send):
    lev, lat, lon = grid.shape
    across = lon // LANES
    slots = interp.shape[0]
    depth = patch.shape[0]
    small = [
        pltpu.make_async_copy(blocks_hbm, blocks, sems.at[lev]),
        pltpu.make_async_copy(interp_hbm, interp, sems.at[lev + 1]),
        pltpu.make_async_copy(table_hbm, table, sems.at[lev + 2]),
    ]
    loads = [
        pltpu.make_async_copy(
            grid_hbm.at[pl.ds(level, 1)], grid.at[pl.ds(level, 1)], sems.at[level]
        )
        for level in range(lev)
    ]
    small[0].start()
    for level in range(lev):
        loads[level].start()
        if level == 1:
            small[1].start()
    small[2].start()
    small[0].wait()
    row = slot_rows(blocks[...], across, lat_pad)
    column[...] = jnp.transpose(jnp.broadcast_to(row, (LANES, slots)))
    chunk = 256
    lane = lax.broadcasted_iota(jnp.int32, (chunk, LANES), 1)
    for start in range(0, slots, chunk):
        mine = column[start : start + chunk, :]
        for base in range(0, depth, LANES):
            selector[start : start + chunk, base : base + LANES] = jnp.where(
                mine == lane + base, 1.0, 0.0
            ).astype(BF16)
    first_state = message.shape[1] - slots // LANES * lev
    copies = [
        pltpu.make_async_copy(message.at[:, rows_of, :], out.at[:, rows_of, :], send.at[i])
        for i, rows_of in enumerate(
            (pl.ds(0, first_state), pl.ds(first_state, message.shape[1] - first_state))
        )
    ]
    for tile in range(across):
        patch[tile * lat_pad + lat : (tile + 1) * lat_pad, :] = jnp.zeros(
            (lat_pad - lat, lev * LANES), BF16
        )
    if depth > across * lat_pad:
        patch[across * lat_pad :, :] = jnp.zeros((depth - across * lat_pad, lev * LANES), BF16)
    pair = 2 * LANES
    for base in range(0, lev, 2):
        for level in (base, base + 1):
            loads[level].wait()
            for tile in range(across):
                patch[
                    tile * lat_pad : tile * lat_pad + lat, level * LANES : (level + 1) * LANES
                ] = grid[level, :, tile * LANES : (tile + 1) * LANES]
        if base == 0:
            small[1].wait()
        for start in range(0, slots, chunk):
            top = slice(start, start + chunk)
            picked = jnp.dot(
                selector[top, :],
                patch[:, base * LANES : base * LANES + pair],
                preferred_element_type=F32,
            )
            weights = interp[top, :].astype(F32)
            values = [
                jnp.sum(picked[:, i * LANES : (i + 1) * LANES] * weights, axis=1, keepdims=True)
                for i in range(2)
            ]
            both = jnp.where(lane == base, values[0], values[1])
            totals[top, :] = both if base == 0 else jnp.where(lane < base, totals[top, :], both)
    small[2].wait()
    flat = jnp.concatenate([grid[level] for level in range(lev)], axis=0)
    coeffs = jnp.dot(flat, table[...], preferred_element_type=F32)
    for top in range(0, slots, LANES):
        state = jnp.transpose(totals[top : top + LANES, :])[:lev].astype(BF16)
        row = first_state + top // LANES * lev
        for target in range(message.shape[0]):
            message[target, row : row + lev, :] = state
    copies[1].start()
    pack(lev, lat, coeffs, message, padded, rows)
    copies[0].start()
    for copy in copies:
        copy.wait()


def regroup_kernel(n_band, arrived, _, out, out_state, sems):
    size = out.shape[2]
    copies = []
    for target in range(out.shape[0]):
        rows = pl.ds(target % n_band * size, size)
        copies.append(
            pltpu.make_async_copy(arrived.at[:, rows, :], out.at[target], sems.at[target])
        )
    rows = pl.ds(n_band * size, out_state.shape[1])
    copies.append(
        pltpu.make_async_copy(arrived.at[:, rows, :], out_state, sems.at[out.shape[0]])
    )
    for copy in copies:
        copy.start()
    for copy in copies:
        copy.wait()


def softplus(x):
    power = jnp.exp(jnp.minimum(x, 80.0))
    return jnp.where(x < -8.0, power, jnp.maximum(x, jnp.log(1.0 + power)))


def column_kernel(n_sec, n_fld, lat_pad, slots, counts, weights, inverses, blocks, interp,
                  near, far, out, state, spread, result, sems):
    lev = near.shape[1] * LANES // slots
    place = lax.axis_index("sec")
    for fld in range(n_fld):
        for shift, pieces in enumerate((near, far)):
            row = (fld * n_sec + (place ^ shift)) * lev
            for tile in range(slots // LANES):
                state[
                    pl.ds(pl.multiple_of(row, lev), lev), tile * LANES : (tile + 1) * LANES
                ] = pieces[fld, tile * lev : (tile + 1) * lev, :].astype(F32)
    mine, lat, lon = result.shape
    across = lon // LANES
    sources, flux_rows = inverses.shape
    levels = flux_rows // 2
    count = counts[lax.axis_index("band")]
    base = (place * n_fld + lax.axis_index("fld")) * mine
    chunk = 256
    lane = lax.broadcasted_iota(jnp.int32, (1, flux_rows), 1)
    slot = lax.broadcasted_iota(jnp.int32, (chunk, 1), 0)
    column = jnp.transpose(state[...]).astype(BF16)
    tiles = [(top, at) for top in range(0, slots, chunk) for at in range(0, sources, chunk)]

    def gates_of(top, at):
        return jnp.dot(
            column[top : top + chunk], weights[:, at : at + chunk], preferred_element_type=F32
        )

    fluxes = {top: jnp.zeros((chunk, flux_rows), F32) for top in range(0, slots, chunk)}

    def add_flux(top, at, source):
        fluxes[top] = fluxes[top] + jnp.dot(
            source, inverses[at : at + chunk, :], preferred_element_type=F32
        )

    gates = gates_of(*tiles[0])
    before = None
    for i, tile in enumerate(tiles):
        later = gates_of(*tiles[i + 1]) if i + 1 < len(tiles) else None
        source = softplus(gates).astype(BF16)
        if before is not None:
            add_flux(*tiles[i - 1], before)
        gates, before = later, source
    add_flux(*tiles[-1], before)
    for start in range(0, slots, chunk):
        rows = fluxes[start]
        for level in range(mine):
            at = base + level
            plus = (lane == at) | ((lane == at + levels + 1) & (at + 1 < levels))
            minus = (lane == at + levels) | ((lane == at + 1) & (at + 1 < levels))
            terms = jnp.where(plus, rows, 0.0) - jnp.where(minus, rows, 0.0)
            heat = jnp.sum(terms, axis=1, keepdims=True)
            heat = jnp.where(slot + start < count, heat, 0.0).astype(BF16).astype(F32)
            spread[start : start + chunk, level * LANES : (level + 1) * LANES] = (
                heat * interp[start : start + chunk, :].astype(F32)
            ).astype(BF16)
    row = slot_rows(blocks[...], across, lat_pad)
    tiles = max(t for t in range(1, 8) if across % t == 0)
    height = tiles * lat_pad
    copies = []
    for first in range(0, across, tiles):
        match = row == lax.broadcasted_iota(jnp.int32, (height, slots), 0) + first * lat_pad
        left = jnp.where(match, 1.0, 0.0).astype(BF16)
        summed = jnp.dot(left, spread[...], preferred_element_type=F32).astype(BF16)
        for level in range(mine):
            for tile in range(tiles):
                result[level, :, (first + tile) * LANES : (first + tile + 1) * LANES] = summed[
                    tile * lat_pad : tile * lat_pad + lat, level * LANES : (level + 1) * LANES
                ]
        columns = pl.ds(first * LANES, tiles * LANES)
        copies.append(
            pltpu.make_async_copy(
                result.at[:, :, columns], out.at[:, :, columns], sems.at[first // tiles]
            )
        )
        copies[-1].start()
    for copy in copies:
        copy.wait()


def call(kernel, outs, specs, scratch, args, flops, size, name, out_spec=VMEM, limit=LIMIT):
    shapes = [jax.ShapeDtypeStruct(shape, dtype) for shape, dtype in outs]
    single = len(outs) == 1
    return pl.pallas_call(
        kernel,
        out_shape=shapes[0] if single else shapes,
        in_specs=specs,
        out_specs=out_spec if single else [out_spec] * len(outs),
        scratch_shapes=scratch,
        compiler_params=pltpu.CompilerParams(vmem_limit_bytes=limit),
        cost_estimate=pl.CostEstimate(flops=flops, bytes_accessed=size, transcendentals=0),
        name=name,
    )(*args)


def body(grid, legendre, counts, blocks, interp, source_weights, inverses):
    n_sec = lax.axis_size("sec")
    n_band = lax.axis_size("band")
    n_fld = lax.axis_size("fld")
    lev, lat, lon = grid.shape[1:]
    wave_dev, _, degrees = legendre.shape
    slots = blocks.shape[0]
    across = lon // LANES
    lat_pad = -(-lat // 16) * 16
    rest = 2 * wave_dev // THIRDS
    piece = rest * lev
    block_row = blocks.reshape(1, slots)

    table = jnp.asarray(dft_table(lon, wave_dev, n_band, n_fld))
    group = n_fld * n_band * rest
    padded_group = -(-group // LANES) * LANES
    depth = -(-across * lat_pad // LANES) * LANES
    state_rows = slots * lev // LANES
    message_rows = n_band * piece + state_rows
    message = call(
        functools.partial(local_kernel, lat_pad),
        [((n_fld, message_rows, LANES), BF16)],
        [HBM] * 4,
        [
            pltpu.VMEM((lev, lat, lon), BF16),
            pltpu.VMEM((1, slots), jnp.int32),
            pltpu.VMEM((slots, LANES), BF16),
            pltpu.VMEM(table.shape, BF16),
            pltpu.VMEM((depth, lev * LANES), BF16),
            pltpu.VMEM((slots, LANES), jnp.int32),
            pltpu.VMEM((slots, depth), BF16),
            pltpu.VMEM((n_fld, message_rows, LANES), BF16),
            pltpu.VMEM((LANES, padded_group), F32),
            pltpu.VMEM((group * lev, LANES), F32),
            pltpu.VMEM((slots, LANES), F32),
            pltpu.SemaphoreType.DMA((lev + 3,)),
            pltpu.SemaphoreType.DMA((2,)),
        ],
        (grid.reshape(lev, lat, lon), block_row, interp, table),
        2 * slots * depth * lev * LANES + 2 * lev * lat * lon * THIRDS * group,
        2 * lev * lat * lon + 2 * slots * LANES,
        "local",
        HBM,
        WHOLE,
    )
    arrived = lax.all_to_all(message, "fld", 0, 0, tiled=True)
    spec_bands, flux_rows, _ = inverses.shape
    basis, inverse_rows = call(
        functools.partial(prepare_kernel, lat, n_band),
        [
            ((n_band, 2, THIRDS * degrees, LANES), BF16),
            ((spec_bands * flux_rows, flux_rows), BF16),
        ],
        [VMEM, VMEM],
        [
            pltpu.VMEM((degrees, (n_band * lat // LANES + 2) * LANES), F32),
            pltpu.VMEM((flux_rows * flux_rows, spec_bands), F32),
            pltpu.VMEM((spec_bands * flux_rows, flux_rows), F32),
        ],
        (jnp.swapaxes(legendre, 1, 2), jnp.transpose(inverses, (1, 2, 0))),
        0,
        8 * wave_dev * degrees * n_band * LANES,
        "prepare",
    )
    sent, near = call(
        functools.partial(regroup_kernel, n_band),
        [((n_sec * n_band, n_fld, piece, LANES), BF16), ((n_fld, state_rows, LANES), BF16)],
        [HBM, HBM],
        [pltpu.SemaphoreType.DMA((n_sec * n_band + 1,))],
        (arrived, basis),
        0,
        4 * n_sec * n_band * n_fld * piece * LANES,
        "regroup",
        HBM,
    )
    far = lax.ppermute(near, "sec", [(i, 1 - i) for i in range(n_sec)])
    pieces = lax.all_to_all(sent, ("sec", "band"), 0, 0, tiled=True)
    sources = spec_bands * flux_rows
    states = source_weights.shape[0]
    mine = n_sec * lev // (n_sec * n_fld)
    heating = call(
        functools.partial(column_kernel, n_sec, n_fld, lat_pad, slots),
        [((mine, lat, lon), BF16)],
        [SMEM] + [VMEM] * 6,
        [
            pltpu.VMEM((states, slots), F32),
            pltpu.VMEM((slots, mine * LANES), BF16),
            pltpu.VMEM((mine, lat, lon), BF16),
            pltpu.SemaphoreType.DMA((across,)),
        ],
        (counts, source_weights, inverse_rows, block_row, interp, near, far),
        8 * slots * slots * 1024,
        2 * slots * slots,
        "columns",
        HBM,
    )

    spectral = call(
        functools.partial(legendre_kernel, n_sec, n_band, n_fld, lev),
        [((wave_dev, 2, n_fld, n_sec * lev, degrees), BF16)],
        [VMEM, VMEM],
        [],
        (basis, pieces),
        4 * n_sec * n_fld * piece * n_band * LANES * degrees * THIRDS,
        2 * n_sec * n_band * n_fld * piece * LANES,
        "legendre",
    )
    return (spectral, heating)


def solution(mesh):
    return jax.shard_map(
        body,
        mesh=mesh,
        in_specs=(
            P("fld", "sec", "band", None),
            P(("band", "fld"), None, "sec"),
            P(),
            P("band"),
            P("band", None),
            P(),
            P(),
        ),
        out_specs=(P(("band", "fld"), None, None, None, "sec"), P(("sec", "fld"), "band", None)),
        check_vma=False,
    )
```

```python
import functools
import math

import jax
import jax.numpy as jnp
import numpy as np
from jax import lax
from jax.experimental import pallas as pl
from jax.experimental.pallas import tpu as pltpu
from jax.sharding import PartitionSpec as P

BF16 = jnp.bfloat16
F32 = jnp.float32
LANES = 128
THIRDS = 3
VMEM = pl.BlockSpec(memory_space=pltpu.VMEM)
HBM = pl.BlockSpec(memory_space=pltpu.HBM)
SMEM = pl.BlockSpec(memory_space=pltpu.SMEM)
LIMIT = 40 * 1024 * 1024
ROOM = 1200 * 1024
WHOLE = 64 * 1024 * 1024 - ROOM
NT = (((1,), (1,)), ((), ()))


def dft_table(lon, wave_dev, n_band, n_fld):
    values_dev = 2 * wave_dev
    rest = values_dev // THIRDS
    third, fld, band, low = np.meshgrid(
        np.arange(THIRDS), np.arange(n_fld), np.arange(n_band), np.arange(rest), indexing="ij"
    )
    value = third * rest + low
    wave = ((band * n_fld + fld) * wave_dev + value // 2).reshape(-1)
    part = (value % 2).reshape(-1)
    phase = np.arange(lon, dtype=np.int64)[:, None] * wave[None, :] % lon
    angle = phase * (2.0 * math.pi / lon)
    values = np.where(part[None, :] == 0, np.cos(angle), -np.sin(angle)) / math.sqrt(lon)
    return values.astype(np.float32).astype(BF16)


def pack(lev, lat, coeffs, message, padded, rows):
    group = coeffs.shape[1] // THIRDS
    padded[...] = jnp.zeros_like(padded)
    for level in range(lev):
        for third in range(THIRDS):
            padded[third * lat : (third + 1) * lat, :group] = coeffs[
                level * lat : (level + 1) * lat, third * group : (third + 1) * group
            ]
        rows[pl.ds(level, group, stride=lev), :] = jnp.transpose(padded[...])[:group]
    targets = message.shape[0]
    size = rows.shape[0] // targets
    message[:, :size, :] = rows[...].astype(BF16).reshape(targets, size, LANES)


def prepare_kernel(lat, n_band, legendre, inverses, out, out_inverses, wide, rows, turned):
    flux_rows, _, spec_bands = inverses.shape
    for row in range(flux_rows):
        rows[row * flux_rows : (row + 1) * flux_rows, :] = inverses[row].astype(F32)
    for row in range(flux_rows):
        turned[pl.ds(row, spec_bands, stride=flux_rows), :] = jnp.transpose(
            rows[pl.ds(row, flux_rows, stride=flux_rows), :]
        )
    out_inverses[...] = turned[...].astype(BF16)
    waves, degrees, _ = legendre.shape
    wide[...] = jnp.zeros_like(wide)
    lane = lax.broadcasted_iota(jnp.int32, (degrees, LANES), 1)
    for wave in range(waves):
        third, parity = wave // 2, wave % 2
        wide[:, : n_band * lat] = legendre[wave].astype(F32)
        place = third * lat
        live = (lane >= place) & (lane < place + lat)
        for band in range(n_band):
            base = band * lat // LANES * LANES
            moved = pltpu.roll(
                wide[:, base : base + 2 * LANES], (place - (band * lat - base)) % (2 * LANES), 1
            )
            out[band, parity, third * degrees : (third + 1) * degrees, :] = jnp.where(
                live, moved[:, :LANES], 0.0
            ).astype(BF16)


def legendre_kernel(n_sec, n_band, n_fld, lev, weights, pieces, out):
    degrees = out.shape[4]
    half = pieces.shape[2] // 2
    for parity in range(2):
        rows = slice(parity * half, (parity + 1) * half)
        basis = jnp.concatenate([weights[band, parity] for band in range(n_band)], axis=1)
        left = jnp.concatenate(
            [
                jnp.concatenate(
                    [
                        pieces[sec * n_band + band, fld, rows, :]
                        for band in range(n_band)
                    ],
                    axis=1,
                )
                for fld in range(n_fld)
                for sec in range(n_sec)
            ],
            axis=0,
        )
        result = lax.dot_general(left, basis, NT, preferred_element_type=F32)
        for third in range(THIRDS):
            part = result[:, third * degrees : (third + 1) * degrees]
            for fld in range(n_fld):
                for real in range(2):
                    levels = [
                        part[(fld * n_sec + sec) * half + real * lev :][:lev]
                        for sec in range(n_sec)
                    ]
                    out[2 * third + parity, real, fld] = jnp.concatenate(levels, axis=0).astype(
                        BF16
                    )


def slot_rows(blocks, across, lat_pad):
    shift = 16
    factor = -(-(1 << shift) // across)
    lat = lax.shift_right_logical(blocks * factor, shift)
    return (blocks - lat * across) * lat_pad + lat


def local_kernel(lat_pad, grid_hbm, blocks_hbm, interp_hbm, table_hbm, out,
                 grid, blocks, interp, table, patch, column, selector, message, padded, rows,
                 sems, send):
    lev, lat, lon = grid.shape
    across = lon // LANES
    slots = interp.shape[0]
    depth = patch.shape[0]
    small = [
        pltpu.make_async_copy(blocks_hbm, blocks, sems.at[lev]),
        pltpu.make_async_copy(interp_hbm, interp, sems.at[lev + 1]),
        pltpu.make_async_copy(table_hbm, table, sems.at[lev + 2]),
    ]
    loads = [
        pltpu.make_async_copy(
            grid_hbm.at[pl.ds(level, 1)], grid.at[pl.ds(level, 1)], sems.at[level]
        )
        for level in range(lev)
    ]
    small[0].start()
    for copy in loads:
        copy.start()
    small[1].start()
    small[2].start()
    small[0].wait()
    row = slot_rows(blocks[...], across, lat_pad)
    column[...] = jnp.transpose(jnp.broadcast_to(row, (LANES, slots)))
    chunk = 256
    lane = lax.broadcasted_iota(jnp.int32, (chunk, LANES), 1)
    for start in range(0, slots, chunk):
        mine = column[start : start + chunk, :]
        for base in range(0, depth, LANES):
            selector[start : start + chunk, base : base + LANES] = jnp.where(
                mine == lane + base, 1.0, 0.0
            ).astype(BF16)
    for tile in range(across):
        patch[tile * lat_pad + lat : (tile + 1) * lat_pad, :] = jnp.zeros(
            (lat_pad - lat, lev * LANES), BF16
        )
    ones = (
        lax.broadcasted_iota(jnp.int32, (lev * LANES, LANES), 0) // LANES
        == lax.broadcasted_iota(jnp.int32, (lev * LANES, LANES), 1)
    ).astype(F32).astype(BF16)
    for level in range(lev):
        loads[level].wait()
        for tile in range(across):
            patch[
                tile * lat_pad : tile * lat_pad + lat, level * LANES : (level + 1) * LANES
            ] = grid[level, :, tile * LANES : (tile + 1) * LANES]
    if depth > across * lat_pad:
        patch[across * lat_pad :, :] = jnp.zeros((depth - across * lat_pad, lev * LANES), BF16)
    small[1].wait()
    first_state = message.shape[1] - slots // LANES * lev
    copies = [
        pltpu.make_async_copy(message.at[:, rows_of, :], out.at[:, rows_of, :], send.at[i])
        for i, rows_of in enumerate(
            (pl.ds(0, first_state), pl.ds(first_state, message.shape[1] - first_state))
        )
    ]
    for start in range(0, slots, chunk):
        picked = jnp.dot(
            selector[start : start + chunk, :], patch[...], preferred_element_type=F32
        )
        weights = interp[start : start + chunk, :].astype(F32)
        products = jnp.concatenate(
            [
                (picked[:, level * LANES : (level + 1) * LANES] * weights).astype(BF16)
                for level in range(lev)
            ],
            axis=1,
        )
        total = jnp.dot(products, ones, preferred_element_type=F32)
        state = jnp.transpose(total)[:lev].astype(BF16)
        for tile in range(chunk // LANES):
            row = first_state + (start // LANES + tile) * lev
            for target in range(message.shape[0]):
                message[target, row : row + lev, :] = state[:, tile * LANES : (tile + 1) * LANES]
        if start == chunk:
            small[2].wait()
            flat = jnp.concatenate([grid[level] for level in range(lev)], axis=0)
            coeffs = jnp.dot(flat, table[...], preferred_element_type=F32)
            pack(lev, lat, coeffs, message, padded, rows)
            copies[0].start()
    copies[1].start()
    for copy in copies:
        copy.wait()


def regroup_kernel(n_band, arrived, _, out, out_state, sems):
    size = out.shape[2]
    copies = []
    for target in range(out.shape[0]):
        rows = pl.ds(target % n_band * size, size)
        copies.append(
            pltpu.make_async_copy(arrived.at[:, rows, :], out.at[target], sems.at[target])
        )
    rows = pl.ds(n_band * size, out_state.shape[1])
    copies.append(
        pltpu.make_async_copy(arrived.at[:, rows, :], out_state, sems.at[out.shape[0]])
    )
    for copy in copies:
        copy.start()
    for copy in copies:
        copy.wait()


def softplus(x):
    power = jnp.exp(jnp.minimum(x, 80.0))
    return jnp.where(x < -8.0, power, jnp.maximum(x, jnp.log(1.0 + power)))


def column_kernel(n_sec, n_fld, lat_pad, slots, counts, weights, inverses, blocks, interp,
                  near, far, out, state, spread, result, sems):
    lev = near.shape[1] * LANES // slots
    place = lax.axis_index("sec")
    for fld in range(n_fld):
        for shift, pieces in enumerate((near, far)):
            row = (fld * n_sec + (place ^ shift)) * lev
            for tile in range(slots // LANES):
                state[
                    pl.ds(pl.multiple_of(row, lev), lev), tile * LANES : (tile + 1) * LANES
                ] = pieces[fld, tile * lev : (tile + 1) * lev, :].astype(F32)
    mine, lat, lon = result.shape
    across = lon // LANES
    sources, flux_rows = inverses.shape
    levels = flux_rows // 2
    count = counts[lax.axis_index("band")]
    base = (place * n_fld + lax.axis_index("fld")) * mine
    chunk = 256
    lane = lax.broadcasted_iota(jnp.int32, (1, flux_rows), 1)
    slot = lax.broadcasted_iota(jnp.int32, (chunk, 1), 0)
    column = jnp.transpose(state[...]).astype(BF16)
    tiles = [(top, at) for top in range(0, slots, chunk) for at in range(0, sources, chunk)]

    def gates_of(top, at):
        return jnp.dot(
            column[top : top + chunk], weights[:, at : at + chunk], preferred_element_type=F32
        )

    fluxes = {top: jnp.zeros((chunk, flux_rows), F32) for top in range(0, slots, chunk)}

    def add_flux(top, at, source):
        fluxes[top] = fluxes[top] + jnp.dot(
            source, inverses[at : at + chunk, :], preferred_element_type=F32
        )

    gates = gates_of(*tiles[0])
    before = None
    for i, tile in enumerate(tiles):
        later = gates_of(*tiles[i + 1]) if i + 1 < len(tiles) else None
        source = softplus(gates).astype(BF16)
        if before is not None:
            add_flux(*tiles[i - 1], before)
        gates, before = later, source
    add_flux(*tiles[-1], before)
    for start in range(0, slots, chunk):
        rows = fluxes[start]
        for level in range(mine):
            at = base + level
            plus = (lane == at) | ((lane == at + levels + 1) & (at + 1 < levels))
            minus = (lane == at + levels) | ((lane == at + 1) & (at + 1 < levels))
            terms = jnp.where(plus, rows, 0.0) - jnp.where(minus, rows, 0.0)
            heat = jnp.sum(terms, axis=1, keepdims=True)
            heat = jnp.where(slot + start < count, heat, 0.0).astype(BF16).astype(F32)
            spread[start : start + chunk, level * LANES : (level + 1) * LANES] = (
                heat * interp[start : start + chunk, :].astype(F32)
            ).astype(BF16)
    row = slot_rows(blocks[...], across, lat_pad)
    tiles = max(t for t in range(1, 8) if across % t == 0)
    height = tiles * lat_pad
    copies = []
    for first in range(0, across, tiles):
        match = row == lax.broadcasted_iota(jnp.int32, (height, slots), 0) + first * lat_pad
        left = jnp.where(match, 1.0, 0.0).astype(BF16)
        summed = jnp.dot(left, spread[...], preferred_element_type=F32).astype(BF16)
        for level in range(mine):
            for tile in range(tiles):
                result[level, :, (first + tile) * LANES : (first + tile + 1) * LANES] = summed[
                    tile * lat_pad : tile * lat_pad + lat, level * LANES : (level + 1) * LANES
                ]
        columns = pl.ds(first * LANES, tiles * LANES)
        copies.append(
            pltpu.make_async_copy(
                result.at[:, :, columns], out.at[:, :, columns], sems.at[first // tiles]
            )
        )
        copies[-1].start()
    for copy in copies:
        copy.wait()


def call(kernel, outs, specs, scratch, args, flops, size, name, out_spec=VMEM, limit=LIMIT):
    shapes = [jax.ShapeDtypeStruct(shape, dtype) for shape, dtype in outs]
    single = len(outs) == 1
    return pl.pallas_call(
        kernel,
        out_shape=shapes[0] if single else shapes,
        in_specs=specs,
        out_specs=out_spec if single else [out_spec] * len(outs),
        scratch_shapes=scratch,
        compiler_params=pltpu.CompilerParams(vmem_limit_bytes=limit),
        cost_estimate=pl.CostEstimate(flops=flops, bytes_accessed=size, transcendentals=0),
        name=name,
    )(*args)


def body(grid, legendre, counts, blocks, interp, source_weights, inverses):
    n_sec = lax.axis_size("sec")
    n_band = lax.axis_size("band")
    n_fld = lax.axis_size("fld")
    lev, lat, lon = grid.shape[1:]
    wave_dev, _, degrees = legendre.shape
    slots = blocks.shape[0]
    across = lon // LANES
    lat_pad = -(-lat // 16) * 16
    rest = 2 * wave_dev // THIRDS
    piece = rest * lev
    block_row = blocks.reshape(1, slots)

    table = jnp.asarray(dft_table(lon, wave_dev, n_band, n_fld))
    group = n_fld * n_band * rest
    padded_group = -(-group // LANES) * LANES
    depth = -(-across * lat_pad // LANES) * LANES
    state_rows = slots * lev // LANES
    message_rows = n_band * piece + state_rows
    message = call(
        functools.partial(local_kernel, lat_pad),
        [((n_fld, message_rows, LANES), BF16)],
        [HBM] * 4,
        [
            pltpu.VMEM((lev, lat, lon), BF16),
            pltpu.VMEM((1, slots), jnp.int32),
            pltpu.VMEM((slots, LANES), BF16),
            pltpu.VMEM(table.shape, BF16),
            pltpu.VMEM((depth, lev * LANES), BF16),
            pltpu.VMEM((slots, LANES), jnp.int32),
            pltpu.VMEM((slots, depth), BF16),
            pltpu.VMEM((n_fld, message_rows, LANES), BF16),
            pltpu.VMEM((LANES, padded_group), F32),
            pltpu.VMEM((group * lev, LANES), F32),
            pltpu.SemaphoreType.DMA((lev + 3,)),
            pltpu.SemaphoreType.DMA((2,)),
        ],
        (grid.reshape(lev, lat, lon), block_row, interp, table),
        2 * slots * depth * lev * LANES + 2 * lev * lat * lon * THIRDS * group,
        2 * lev * lat * lon + 2 * slots * LANES,
        "local",
        HBM,
        WHOLE,
    )
    arrived = lax.all_to_all(message, "fld", 0, 0, tiled=True)
    spec_bands, flux_rows, _ = inverses.shape
    basis, inverse_rows = call(
        functools.partial(prepare_kernel, lat, n_band),
        [
            ((n_band, 2, THIRDS * degrees, LANES), BF16),
            ((spec_bands * flux_rows, flux_rows), BF16),
        ],
        [VMEM, VMEM],
        [
            pltpu.VMEM((degrees, (n_band * lat // LANES + 2) * LANES), F32),
            pltpu.VMEM((flux_rows * flux_rows, spec_bands), F32),
            pltpu.VMEM((spec_bands * flux_rows, flux_rows), F32),
        ],
        (jnp.swapaxes(legendre, 1, 2), jnp.transpose(inverses, (1, 2, 0))),
        0,
        8 * wave_dev * degrees * n_band * LANES,
        "prepare",
    )
    sent, near = call(
        functools.partial(regroup_kernel, n_band),
        [((n_sec * n_band, n_fld, piece, LANES), BF16), ((n_fld, state_rows, LANES), BF16)],
        [HBM, HBM],
        [pltpu.SemaphoreType.DMA((n_sec * n_band + 1,))],
        (arrived, basis),
        0,
        4 * n_sec * n_band * n_fld * piece * LANES,
        "regroup",
        HBM,
    )
    far = lax.ppermute(near, "sec", [(i, 1 - i) for i in range(n_sec)])
    pieces = lax.all_to_all(sent, ("sec", "band"), 0, 0, tiled=True)
    sources = spec_bands * flux_rows
    states = source_weights.shape[0]
    mine = n_sec * lev // (n_sec * n_fld)
    heating = call(
        functools.partial(column_kernel, n_sec, n_fld, lat_pad, slots),
        [((mine, lat, lon), BF16)],
        [SMEM] + [VMEM] * 6,
        [
            pltpu.VMEM((states, slots), F32),
            pltpu.VMEM((slots, mine * LANES), BF16),
            pltpu.VMEM((mine, lat, lon), BF16),
            pltpu.SemaphoreType.DMA((across,)),
        ],
        (counts, source_weights, inverse_rows, block_row, interp, near, far),
        8 * slots * slots * 1024,
        2 * slots * slots,
        "columns",
        HBM,
    )

    spectral = call(
        functools.partial(legendre_kernel, n_sec, n_band, n_fld, lev),
        [((wave_dev, 2, n_fld, n_sec * lev, degrees), BF16)],
        [VMEM, VMEM],
        [],
        (basis, pieces),
        4 * n_sec * n_fld * piece * n_band * LANES * degrees * THIRDS,
        2 * n_sec * n_band * n_fld * piece * LANES,
        "legendre",
    )
    return (spectral, heating)


def solution(mesh):
    return jax.shard_map(
        body,
        mesh=mesh,
        in_specs=(
            P("fld", "sec", "band", None),
            P(("band", "fld"), None, "sec"),
            P(),
            P("band"),
            P("band", None),
            P(),
            P(),
        ),
        out_specs=(P(("band", "fld"), None, None, None, "sec"), P(("sec", "fld"), "band", None)),
        check_vma=False,
    )
```

```python
import functools
import math

import jax
import jax.numpy as jnp
import numpy as np
from jax import lax
from jax.experimental import pallas as pl
from jax.experimental.pallas import tpu as pltpu
from jax.sharding import PartitionSpec as P

BF16 = jnp.bfloat16
F32 = jnp.float32
LANES = 128
THIRDS = 3
VMEM = pl.BlockSpec(memory_space=pltpu.VMEM)
HBM = pl.BlockSpec(memory_space=pltpu.HBM)
SMEM = pl.BlockSpec(memory_space=pltpu.SMEM)
LIMIT = 40 * 1024 * 1024
ROOM = 1200 * 1024
WHOLE = 64 * 1024 * 1024 - ROOM
NT = (((1,), (1,)), ((), ()))


def dft_table(lon, wave_dev, n_band, n_fld):
    values_dev = 2 * wave_dev
    rest = values_dev // THIRDS
    third, fld, band, low = np.meshgrid(
        np.arange(THIRDS), np.arange(n_fld), np.arange(n_band), np.arange(rest), indexing="ij"
    )
    value = third * rest + low
    wave = ((band * n_fld + fld) * wave_dev + value // 2).reshape(-1)
    part = (value % 2).reshape(-1)
    phase = np.arange(lon, dtype=np.int64)[:, None] * wave[None, :] % lon
    angle = phase * (2.0 * math.pi / lon)
    values = np.where(part[None, :] == 0, np.cos(angle), -np.sin(angle)) / math.sqrt(lon)
    return values.astype(np.float32).astype(BF16)


def pack(lev, lat, coeffs, message, padded, rows):
    group = coeffs.shape[1] // THIRDS
    padded[...] = jnp.zeros_like(padded)
    for level in range(lev):
        for third in range(THIRDS):
            padded[third * lat : (third + 1) * lat, :group] = coeffs[
                level * lat : (level + 1) * lat, third * group : (third + 1) * group
            ]
        rows[pl.ds(level, group, stride=lev), :] = jnp.transpose(padded[...])[:group]
    targets = message.shape[0]
    size = rows.shape[0] // targets
    message[:, :size, :] = rows[...].astype(BF16).reshape(targets, size, LANES)


def prepare_kernel(lat, n_band, legendre, inverses, out, out_inverses, wide, rows, turned):
    flux_rows, _, spec_bands = inverses.shape
    for row in range(flux_rows):
        rows[row * flux_rows : (row + 1) * flux_rows, :] = inverses[row].astype(F32)
    for row in range(flux_rows):
        turned[pl.ds(row, spec_bands, stride=flux_rows), :] = jnp.transpose(
            rows[pl.ds(row, flux_rows, stride=flux_rows), :]
        )
    out_inverses[...] = turned[...].astype(BF16)
    waves, degrees, _ = legendre.shape
    wide[...] = jnp.zeros_like(wide)
    lane = lax.broadcasted_iota(jnp.int32, (degrees, LANES), 1)
    for wave in range(waves):
        third, parity = wave // 2, wave % 2
        wide[:, : n_band * lat] = legendre[wave].astype(F32)
        place = third * lat
        live = (lane >= place) & (lane < place + lat)
        for band in range(n_band):
            base = band * lat // LANES * LANES
            moved = pltpu.roll(
                wide[:, base : base + 2 * LANES], (place - (band * lat - base)) % (2 * LANES), 1
            )
            out[band, parity, third * degrees : (third + 1) * degrees, :] = jnp.where(
                live, moved[:, :LANES], 0.0
            ).astype(BF16)


def legendre_kernel(n_sec, n_band, n_fld, lev, weights, pieces, out):
    degrees = out.shape[4]
    half = pieces.shape[2] // 2
    for parity in range(2):
        rows = slice(parity * half, (parity + 1) * half)
        basis = jnp.concatenate([weights[band, parity] for band in range(n_band)], axis=1)
        left = jnp.concatenate(
            [
                jnp.concatenate(
                    [
                        pieces[sec * n_band + band, fld, rows, :]
                        for band in range(n_band)
                    ],
                    axis=1,
                )
                for fld in range(n_fld)
                for sec in range(n_sec)
            ],
            axis=0,
        )
        result = lax.dot_general(left, basis, NT, preferred_element_type=F32)
        for third in range(THIRDS):
            part = result[:, third * degrees : (third + 1) * degrees]
            for fld in range(n_fld):
                for real in range(2):
                    levels = [
                        part[(fld * n_sec + sec) * half + real * lev :][:lev]
                        for sec in range(n_sec)
                    ]
                    out[2 * third + parity, real, fld] = jnp.concatenate(levels, axis=0).astype(
                        BF16
                    )


def slot_rows(blocks, across, lat_pad):
    shift = 16
    factor = -(-(1 << shift) // across)
    lat = lax.shift_right_logical(blocks * factor, shift)
    return (blocks - lat * across) * lat_pad + lat


def local_kernel(lat_pad, parts, grid_hbm, blocks_hbm, interp_hbm, table_hbm, out,
                 grid, blocks, interp, table, patch, column, selector, message, padded, rows,
                 sems, send):
    lev, lat, lon = grid.shape
    across = lon // LANES
    slots = interp.shape[0]
    depth = patch.shape[0]
    step = lon // parts
    small = [
        pltpu.make_async_copy(blocks_hbm, blocks, sems.at[parts]),
        pltpu.make_async_copy(interp_hbm, interp, sems.at[parts + 1]),
        pltpu.make_async_copy(table_hbm, table, sems.at[parts + 2]),
    ]
    loads = [
        pltpu.make_async_copy(
            grid_hbm.at[:, :, pl.ds(part * step, step)],
            grid.at[:, :, pl.ds(part * step, step)],
            sems.at[part],
        )
        for part in range(parts)
    ]
    small[0].start()
    for copy in loads:
        copy.start()
    small[1].start()
    small[2].start()
    small[0].wait()
    row = slot_rows(blocks[...], across, lat_pad)
    column[...] = jnp.transpose(jnp.broadcast_to(row, (LANES, slots)))
    chunk = 256
    lane = lax.broadcasted_iota(jnp.int32, (chunk, LANES), 1)
    for start in range(0, slots, chunk):
        mine = column[start : start + chunk, :]
        for base in range(0, depth, LANES):
            selector[start : start + chunk, base : base + LANES] = jnp.where(
                mine == lane + base, 1.0, 0.0
            ).astype(BF16)
    for part in range(parts):
        loads[part].wait()
        for tile in range(part * across // parts, (part + 1) * across // parts):
            patch[tile * lat_pad + lat : (tile + 1) * lat_pad, :] = jnp.zeros(
                (lat_pad - lat, lev * LANES), BF16
            )
            for level in range(lev):
                patch[
                    tile * lat_pad : tile * lat_pad + lat, level * LANES : (level + 1) * LANES
                ] = grid[level, :, tile * LANES : (tile + 1) * LANES]
    if depth > across * lat_pad:
        patch[across * lat_pad :, :] = jnp.zeros((depth - across * lat_pad, lev * LANES), BF16)
    small[1].wait()
    first_state = message.shape[1] - slots // LANES * lev
    copies = [
        pltpu.make_async_copy(message.at[:, rows_of, :], out.at[:, rows_of, :], send.at[i])
        for i, rows_of in enumerate(
            (pl.ds(0, first_state), pl.ds(first_state, message.shape[1] - first_state))
        )
    ]
    for start in range(0, slots, chunk):
        picked = jnp.dot(
            selector[start : start + chunk, :], patch[...], preferred_element_type=F32
        )
        weights = interp[start : start + chunk, :].astype(F32)
        total = jnp.zeros((chunk, LANES), F32)
        for level in range(lev):
            product = picked[:, level * LANES : (level + 1) * LANES] * weights
            total = jnp.where(lane == level, jnp.sum(product, axis=1, keepdims=True), total)
        state = jnp.transpose(total)[:lev].astype(BF16)
        for tile in range(chunk // LANES):
            row = first_state + (start // LANES + tile) * lev
            for target in range(message.shape[0]):
                message[target, row : row + lev, :] = state[:, tile * LANES : (tile + 1) * LANES]
        if start == chunk:
            small[2].wait()
            flat = jnp.concatenate([grid[level] for level in range(lev)], axis=0)
            coeffs = jnp.dot(flat, table[...], preferred_element_type=F32)
            pack(lev, lat, coeffs, message, padded, rows)
            copies[0].start()
    copies[1].start()
    for copy in copies:
        copy.wait()


def regroup_kernel(n_band, arrived, _, out, out_state, sems):
    size = out.shape[2]
    copies = []
    for target in range(out.shape[0]):
        rows = pl.ds(target % n_band * size, size)
        copies.append(
            pltpu.make_async_copy(arrived.at[:, rows, :], out.at[target], sems.at[target])
        )
    rows = pl.ds(n_band * size, out_state.shape[1])
    copies.append(
        pltpu.make_async_copy(arrived.at[:, rows, :], out_state, sems.at[out.shape[0]])
    )
    for copy in copies:
        copy.start()
    for copy in copies:
        copy.wait()


def softplus(x):
    power = jnp.exp(jnp.minimum(x, 80.0))
    return jnp.where(x < -8.0, power, jnp.maximum(x, jnp.log(1.0 + power)))


def column_kernel(n_sec, n_fld, lat_pad, slots, counts, weights, inverses, blocks, interp,
                  near, far, out, state, total, result, sems):
    lev = near.shape[1] * LANES // slots
    place = lax.axis_index("sec")
    for fld in range(n_fld):
        for shift, pieces in enumerate((near, far)):
            row = (fld * n_sec + (place ^ shift)) * lev
            for tile in range(slots // LANES):
                state[
                    pl.ds(pl.multiple_of(row, lev), lev), tile * LANES : (tile + 1) * LANES
                ] = pieces[fld, tile * lev : (tile + 1) * lev, :].astype(F32)
    mine, lat, lon = result.shape
    across = lon // LANES
    sources, flux_rows = inverses.shape
    levels = flux_rows // 2
    count = counts[lax.axis_index("band")]
    base = (place * n_fld + lax.axis_index("fld")) * mine
    chunk = 256
    lane = lax.broadcasted_iota(jnp.int32, (1, flux_rows), 1)
    slot = lax.broadcasted_iota(jnp.int32, (chunk, 1), 0)
    column = jnp.transpose(state[...]).astype(BF16)
    row = slot_rows(blocks[...], across, lat_pad)
    group = max(t for t in range(1, 4) if across % t == 0)
    height = group * lat_pad
    line = lax.broadcasted_iota(jnp.int32, (height, chunk), 0)
    copies = []

    def gates_of(top, at):
        return jnp.dot(
            column[top : top + chunk], weights[:, at : at + chunk], preferred_element_type=F32
        )

    def spread_of(top, flux):
        parts = []
        for level in range(mine):
            at = base + level
            plus = (lane == at) | ((lane == at + levels + 1) & (at + 1 < levels))
            minus = (lane == at + levels) | ((lane == at + 1) & (at + 1 < levels))
            terms = jnp.where(plus, flux, 0.0) - jnp.where(minus, flux, 0.0)
            heat = jnp.sum(terms, axis=1, keepdims=True)
            heat = jnp.where(slot + top < count, heat, 0.0).astype(BF16).astype(F32)
            parts.append((heat * interp[top : top + chunk, :].astype(F32)).astype(BF16))
        return jnp.concatenate(parts, axis=1)

    def add_spread(top, spread, first):
        match = row[:, top : top + chunk] == line + first * lat_pad
        part = jnp.dot(
            jnp.where(match, 1.0, 0.0).astype(BF16), spread, preferred_element_type=F32
        )
        rows = slice(first * lat_pad, first * lat_pad + height)
        if top > 0:
            part = part + total[rows, :]
        if top + chunk < slots:
            total[rows, :] = part
            return
        part = part.astype(BF16)
        for level in range(mine):
            for tile in range(group):
                result[level, :, (first + tile) * LANES : (first + tile + 1) * LANES] = part[
                    tile * lat_pad : tile * lat_pad + lat, level * LANES : (level + 1) * LANES
                ]
        columns = pl.ds(first * LANES, group * LANES)
        copies.append(
            pltpu.make_async_copy(
                result.at[:, :, columns], out.at[:, :, columns], sems.at[first // group]
            )
        )
        copies[-1].start()

    tiles = [(top, at) for top in range(0, slots, chunk) for at in range(0, sources, chunk)]
    pending = []
    flux = jnp.zeros((chunk, flux_rows), F32)
    gates = gates_of(*tiles[0])
    before = None
    for i, (top, at) in enumerate(tiles):
        later = gates_of(*tiles[i + 1]) if i + 1 < len(tiles) else None
        source = softplus(gates).astype(BF16)
        if before is not None:
            done, place_of = tiles[i - 1]
            flux = flux + jnp.dot(
                before, inverses[place_of : place_of + chunk, :], preferred_element_type=F32
            )
            if top != done:
                spread = spread_of(done, flux)
                pending = [(done, spread, first) for first in range(0, across, group)]
                flux = jnp.zeros((chunk, flux_rows), F32)
        if pending:
            add_spread(*pending.pop(0))
        gates, before = later, source
    for one in pending:
        add_spread(*one)
    top, at = tiles[-1]
    flux = flux + jnp.dot(before, inverses[at : at + chunk, :], preferred_element_type=F32)
    spread = spread_of(top, flux)
    for first in range(0, across, group):
        add_spread(top, spread, first)
    for copy in copies:
        copy.wait()


def call(kernel, outs, specs, scratch, args, flops, size, name, out_spec=VMEM, limit=LIMIT):
    shapes = [jax.ShapeDtypeStruct(shape, dtype) for shape, dtype in outs]
    single = len(outs) == 1
    return pl.pallas_call(
        kernel,
        out_shape=shapes[0] if single else shapes,
        in_specs=specs,
        out_specs=out_spec if single else [out_spec] * len(outs),
        scratch_shapes=scratch,
        compiler_params=pltpu.CompilerParams(vmem_limit_bytes=limit),
        cost_estimate=pl.CostEstimate(flops=flops, bytes_accessed=size, transcendentals=0),
        name=name,
    )(*args)


def body(grid, legendre, counts, blocks, interp, source_weights, inverses):
    n_sec = lax.axis_size("sec")
    n_band = lax.axis_size("band")
    n_fld = lax.axis_size("fld")
    lev, lat, lon = grid.shape[1:]
    wave_dev, _, degrees = legendre.shape
    slots = blocks.shape[0]
    across = lon // LANES
    lat_pad = -(-lat // 16) * 16
    rest = 2 * wave_dev // THIRDS
    piece = rest * lev
    block_row = blocks.reshape(1, slots)

    table = jnp.asarray(dft_table(lon, wave_dev, n_band, n_fld))
    group = n_fld * n_band * rest
    padded_group = -(-group // LANES) * LANES
    depth = -(-across * lat_pad // LANES) * LANES
    parts = max(t for t in range(1, 8) if across % t == 0)
    state_rows = slots * lev // LANES
    message_rows = n_band * piece + state_rows
    message = call(
        functools.partial(local_kernel, lat_pad, parts),
        [((n_fld, message_rows, LANES), BF16)],
        [HBM] * 4,
        [
            pltpu.VMEM((lev, lat, lon), BF16),
            pltpu.VMEM((1, slots), jnp.int32),
            pltpu.VMEM((slots, LANES), BF16),
            pltpu.VMEM(table.shape, BF16),
            pltpu.VMEM((depth, lev * LANES), BF16),
            pltpu.VMEM((slots, LANES), jnp.int32),
            pltpu.VMEM((slots, depth), BF16),
            pltpu.VMEM((n_fld, message_rows, LANES), BF16),
            pltpu.VMEM((LANES, padded_group), F32),
            pltpu.VMEM((group * lev, LANES), F32),
            pltpu.SemaphoreType.DMA((parts + 3,)),
            pltpu.SemaphoreType.DMA((2,)),
        ],
        (grid.reshape(lev, lat, lon), block_row, interp, table),
        2 * slots * depth * lev * LANES + 2 * lev * lat * lon * THIRDS * group,
        2 * lev * lat * lon + 2 * slots * LANES,
        "local",
        HBM,
        WHOLE,
    )
    arrived = lax.all_to_all(message, "fld", 0, 0, tiled=True)
    spec_bands, flux_rows, _ = inverses.shape
    basis, inverse_rows = call(
        functools.partial(prepare_kernel, lat, n_band),
        [
            ((n_band, 2, THIRDS * degrees, LANES), BF16),
            ((spec_bands * flux_rows, flux_rows), BF16),
        ],
        [VMEM, VMEM],
        [
            pltpu.VMEM((degrees, (n_band * lat // LANES + 2) * LANES), F32),
            pltpu.VMEM((flux_rows * flux_rows, spec_bands), F32),
            pltpu.VMEM((spec_bands * flux_rows, flux_rows), F32),
        ],
        (jnp.swapaxes(legendre, 1, 2), jnp.transpose(inverses, (1, 2, 0))),
        0,
        8 * wave_dev * degrees * n_band * LANES,
        "prepare",
    )
    sent, near = call(
        functools.partial(regroup_kernel, n_band),
        [((n_sec * n_band, n_fld, piece, LANES), BF16), ((n_fld, state_rows, LANES), BF16)],
        [HBM, HBM],
        [pltpu.SemaphoreType.DMA((n_sec * n_band + 1,))],
        (arrived, basis),
        0,
        4 * n_sec * n_band * n_fld * piece * LANES,
        "regroup",
        HBM,
    )
    far = lax.ppermute(near, "sec", [(i, 1 - i) for i in range(n_sec)])
    pieces = lax.all_to_all(sent, ("sec", "band"), 0, 0, tiled=True)
    sources = spec_bands * flux_rows
    states = source_weights.shape[0]
    mine = n_sec * lev // (n_sec * n_fld)
    heating = call(
        functools.partial(column_kernel, n_sec, n_fld, lat_pad, slots),
        [((mine, lat, lon), BF16)],
        [SMEM] + [VMEM] * 6,
        [
            pltpu.VMEM((states, slots), F32),
            pltpu.VMEM((across * lat_pad, mine * LANES), F32),
            pltpu.VMEM((mine, lat, lon), BF16),
            pltpu.SemaphoreType.DMA((across,)),
        ],
        (counts, source_weights, inverse_rows, block_row, interp, near, far),
        8 * slots * slots * 1024,
        2 * slots * slots,
        "columns",
        HBM,
    )

    spectral = call(
        functools.partial(legendre_kernel, n_sec, n_band, n_fld, lev),
        [((wave_dev, 2, n_fld, n_sec * lev, degrees), BF16)],
        [VMEM, VMEM],
        [],
        (basis, pieces),
        4 * n_sec * n_fld * piece * n_band * LANES * degrees * THIRDS,
        2 * n_sec * n_band * n_fld * piece * LANES,
        "legendre",
    )
    return (spectral, heating)


def solution(mesh):
    return jax.shard_map(
        body,
        mesh=mesh,
        in_specs=(
            P("fld", "sec", "band", None),
            P(("band", "fld"), None, "sec"),
            P(),
            P("band"),
            P("band", None),
            P(),
            P(),
        ),
        out_specs=(P(("band", "fld"), None, None, None, "sec"), P(("sec", "fld"), "band", None)),
        check_vma=False,
    )
```

```python
import functools
import math

import jax
import jax.numpy as jnp
import numpy as np
from jax import lax
from jax.experimental import pallas as pl
from jax.experimental.pallas import tpu as pltpu
from jax.sharding import PartitionSpec as P

BF16 = jnp.bfloat16
F32 = jnp.float32
LANES = 128
THIRDS = 3
VMEM = pl.BlockSpec(memory_space=pltpu.VMEM)
HBM = pl.BlockSpec(memory_space=pltpu.HBM)
SMEM = pl.BlockSpec(memory_space=pltpu.SMEM)
LIMIT = 40 * 1024 * 1024
ROOM = 1200 * 1024
WHOLE = 64 * 1024 * 1024 - ROOM
NT = (((1,), (1,)), ((), ()))


def dft_table(lon, wave_dev, n_band, n_fld):
    values_dev = 2 * wave_dev
    rest = values_dev // THIRDS
    third, fld, band, low = np.meshgrid(
        np.arange(THIRDS), np.arange(n_fld), np.arange(n_band), np.arange(rest), indexing="ij"
    )
    value = third * rest + low
    wave = ((band * n_fld + fld) * wave_dev + value // 2).reshape(-1)
    part = (value % 2).reshape(-1)
    phase = np.arange(lon, dtype=np.int64)[:, None] * wave[None, :] % lon
    angle = phase * (2.0 * math.pi / lon)
    values = np.where(part[None, :] == 0, np.cos(angle), -np.sin(angle)) / math.sqrt(lon)
    return values.astype(np.float32).astype(BF16)


def pack(lev, lat, coeffs, message, padded, rows):
    group = coeffs.shape[1] // THIRDS
    padded[...] = jnp.zeros_like(padded)
    for level in range(lev):
        for third in range(THIRDS):
            padded[third * lat : (third + 1) * lat, :group] = coeffs[
                level * lat : (level + 1) * lat, third * group : (third + 1) * group
            ]
        rows[pl.ds(level, group, stride=lev), :] = jnp.transpose(padded[...])[:group]
    targets = message.shape[0]
    size = rows.shape[0] // targets
    message[:, :size, :] = rows[...].astype(BF16).reshape(targets, size, LANES)


def prepare_kernel(lat, n_band, legendre, inverses, out, out_inverses, wide, rows, turned):
    flux_rows, _, spec_bands = inverses.shape
    for row in range(flux_rows):
        rows[row * flux_rows : (row + 1) * flux_rows, :] = inverses[row].astype(F32)
    for row in range(flux_rows):
        turned[pl.ds(row, spec_bands, stride=flux_rows), :] = jnp.transpose(
            rows[pl.ds(row, flux_rows, stride=flux_rows), :]
        )
    out_inverses[...] = turned[...].astype(BF16)
    waves, degrees, _ = legendre.shape
    wide[...] = jnp.zeros_like(wide)
    lane = lax.broadcasted_iota(jnp.int32, (degrees, LANES), 1)
    for wave in range(waves):
        third, parity = wave // 2, wave % 2
        wide[:, : n_band * lat] = legendre[wave].astype(F32)
        place = third * lat
        live = (lane >= place) & (lane < place + lat)
        for band in range(n_band):
            base = band * lat // LANES * LANES
            moved = pltpu.roll(
                wide[:, base : base + 2 * LANES], (place - (band * lat - base)) % (2 * LANES), 1
            )
            out[band, parity, third * degrees : (third + 1) * degrees, :] = jnp.where(
                live, moved[:, :LANES], 0.0
            ).astype(BF16)


def legendre_kernel(n_sec, n_band, n_fld, lev, weights, pieces, out):
    degrees = out.shape[4]
    half = pieces.shape[2] // 2
    for parity in range(2):
        rows = slice(parity * half, (parity + 1) * half)
        basis = jnp.concatenate([weights[band, parity] for band in range(n_band)], axis=1)
        left = jnp.concatenate(
            [
                jnp.concatenate(
                    [
                        pieces[sec * n_band + band, fld, rows, :]
                        for band in range(n_band)
                    ],
                    axis=1,
                )
                for fld in range(n_fld)
                for sec in range(n_sec)
            ],
            axis=0,
        )
        result = lax.dot_general(left, basis, NT, preferred_element_type=F32)
        for third in range(THIRDS):
            part = result[:, third * degrees : (third + 1) * degrees]
            for fld in range(n_fld):
                for real in range(2):
                    levels = [
                        part[(fld * n_sec + sec) * half + real * lev :][:lev]
                        for sec in range(n_sec)
                    ]
                    out[2 * third + parity, real, fld] = jnp.concatenate(levels, axis=0).astype(
                        BF16
                    )


def slot_rows(blocks, across, lat_pad):
    shift = 16
    factor = -(-(1 << shift) // across)
    lat = lax.shift_right_logical(blocks * factor, shift)
    return (blocks - lat * across) * lat_pad + lat


def local_kernel(lat_pad, parts, grid_hbm, blocks_hbm, interp_hbm, table_hbm, out,
                 grid, blocks, interp, table, patch, column, selector, message, padded, rows,
                 sems, send):
    lev, lat, lon = grid.shape
    across = lon // LANES
    slots = interp.shape[0]
    depth = patch.shape[0]
    step = lon // parts
    small = [
        pltpu.make_async_copy(blocks_hbm, blocks, sems.at[parts]),
        pltpu.make_async_copy(interp_hbm, interp, sems.at[parts + 1]),
        pltpu.make_async_copy(table_hbm, table, sems.at[parts + 2]),
    ]
    loads = [
        pltpu.make_async_copy(
            grid_hbm.at[:, :, pl.ds(part * step, step)],
            grid.at[:, :, pl.ds(part * step, step)],
            sems.at[part],
        )
        for part in range(parts)
    ]
    small[0].start()
    for copy in loads:
        copy.start()
    small[1].start()
    small[2].start()
    small[0].wait()
    row = slot_rows(blocks[...], across, lat_pad)
    column[...] = jnp.transpose(jnp.broadcast_to(row, (LANES, slots)))
    chunk = 256
    lane = lax.broadcasted_iota(jnp.int32, (chunk, LANES), 1)
    for start in range(0, slots, chunk):
        mine = column[start : start + chunk, :]
        for base in range(0, depth, LANES):
            selector[start : start + chunk, base : base + LANES] = jnp.where(
                mine == lane + base, 1.0, 0.0
            ).astype(BF16)
    for part in range(parts):
        loads[part].wait()
        for tile in range(part * across // parts, (part + 1) * across // parts):
            patch[tile * lat_pad + lat : (tile + 1) * lat_pad, :] = jnp.zeros(
                (lat_pad - lat, lev * LANES), BF16
            )
            for level in range(lev):
                patch[
                    tile * lat_pad : tile * lat_pad + lat, level * LANES : (level + 1) * LANES
                ] = grid[level, :, tile * LANES : (tile + 1) * LANES]
    if depth > across * lat_pad:
        patch[across * lat_pad :, :] = jnp.zeros((depth - across * lat_pad, lev * LANES), BF16)
    small[1].wait()
    first_state = message.shape[1] - slots // LANES * lev
    copies = [
        pltpu.make_async_copy(message.at[:, rows_of, :], out.at[:, rows_of, :], send.at[i])
        for i, rows_of in enumerate(
            (pl.ds(0, first_state), pl.ds(first_state, message.shape[1] - first_state))
        )
    ]
    for start in range(0, slots, chunk):
        picked = jnp.dot(
            selector[start : start + chunk, :], patch[...], preferred_element_type=F32
        )
        weights = interp[start : start + chunk, :].astype(F32)
        total = jnp.zeros((chunk, LANES), F32)
        for level in range(lev):
            product = picked[:, level * LANES : (level + 1) * LANES] * weights
            total = jnp.where(lane == level, jnp.sum(product, axis=1, keepdims=True), total)
        state = jnp.transpose(total)[:lev].astype(BF16)
        for tile in range(chunk // LANES):
            row = first_state + (start // LANES + tile) * lev
            for target in range(message.shape[0]):
                message[target, row : row + lev, :] = state[:, tile * LANES : (tile + 1) * LANES]
        if start == chunk:
            small[2].wait()
            flat = jnp.concatenate([grid[level] for level in range(lev)], axis=0)
            coeffs = jnp.dot(flat, table[...], preferred_element_type=F32)
            pack(lev, lat, coeffs, message, padded, rows)
            copies[0].start()
    copies[1].start()
    for copy in copies:
        copy.wait()


def regroup_kernel(n_band, arrived, _, out, out_state, sems):
    size = out.shape[2]
    copies = []
    for target in range(out.shape[0]):
        rows = pl.ds(target % n_band * size, size)
        copies.append(
            pltpu.make_async_copy(arrived.at[:, rows, :], out.at[target], sems.at[target])
        )
    rows = pl.ds(n_band * size, out_state.shape[1])
    copies.append(
        pltpu.make_async_copy(arrived.at[:, rows, :], out_state, sems.at[out.shape[0]])
    )
    for copy in copies:
        copy.start()
    for copy in copies:
        copy.wait()


TAIL = (0.041015625, -0.1591796875, 0.306640625, -0.49609375, 1.0)


def softplus(x):
    u = jnp.exp(-jnp.abs(x)).astype(BF16)
    tail = u * TAIL[0] + TAIL[1]
    for coefficient in TAIL[2:]:
        tail = tail * u + coefficient
    return jnp.maximum(x.astype(BF16), 0.0) + u * tail


def column_kernel(n_sec, n_fld, lat_pad, slots, counts, weights, inverses, blocks, interp,
                  near, far, out, state, spread, result, sems):
    lev = near.shape[1] * LANES // slots
    place = lax.axis_index("sec")
    for fld in range(n_fld):
        for shift, pieces in enumerate((near, far)):
            row = (fld * n_sec + (place ^ shift)) * lev
            for tile in range(slots // LANES):
                state[
                    pl.ds(pl.multiple_of(row, lev), lev), tile * LANES : (tile + 1) * LANES
                ] = pieces[fld, tile * lev : (tile + 1) * lev, :].astype(F32)
    mine, lat, lon = result.shape
    across = lon // LANES
    sources, flux_rows = inverses.shape
    levels = flux_rows // 2
    count = counts[lax.axis_index("band")]
    base = (place * n_fld + lax.axis_index("fld")) * mine
    chunk = 256
    lane = lax.broadcasted_iota(jnp.int32, (1, flux_rows), 1)
    slot = lax.broadcasted_iota(jnp.int32, (chunk, 1), 0)
    column = jnp.transpose(state[...]).astype(BF16)
    tiles = [(top, at) for top in range(0, slots, chunk) for at in range(0, sources, chunk)]

    def gates_of(top, at):
        return jnp.dot(
            column[top : top + chunk], weights[:, at : at + chunk], preferred_element_type=F32
        )

    fluxes = {top: jnp.zeros((chunk, flux_rows), F32) for top in range(0, slots, chunk)}

    def add_flux(top, at, source):
        fluxes[top] = fluxes[top] + jnp.dot(
            source, inverses[at : at + chunk, :], preferred_element_type=F32
        )

    gates = gates_of(*tiles[0])
    before = None
    for i, tile in enumerate(tiles):
        later = gates_of(*tiles[i + 1]) if i + 1 < len(tiles) else None
        source = softplus(gates)
        if before is not None:
            add_flux(*tiles[i - 1], before)
        gates, before = later, source
    add_flux(*tiles[-1], before)
    for start in range(0, slots, chunk):
        rows = fluxes[start]
        for level in range(mine):
            at = base + level
            plus = (lane == at) | ((lane == at + levels + 1) & (at + 1 < levels))
            minus = (lane == at + levels) | ((lane == at + 1) & (at + 1 < levels))
            terms = jnp.where(plus, rows, 0.0) - jnp.where(minus, rows, 0.0)
            heat = jnp.sum(terms, axis=1, keepdims=True)
            heat = jnp.where(slot + start < count, heat, 0.0).astype(BF16).astype(F32)
            spread[start : start + chunk, level * LANES : (level + 1) * LANES] = (
                heat * interp[start : start + chunk, :].astype(F32)
            ).astype(BF16)
    row = slot_rows(blocks[...], across, lat_pad)
    tiles = max(t for t in range(1, 8) if across % t == 0)
    height = tiles * lat_pad
    copies = []
    for first in range(0, across, tiles):
        match = row == lax.broadcasted_iota(jnp.int32, (height, slots), 0) + first * lat_pad
        left = jnp.where(match, 1.0, 0.0).astype(BF16)
        summed = jnp.dot(left, spread[...], preferred_element_type=F32).astype(BF16)
        for level in range(mine):
            for tile in range(tiles):
                result[level, :, (first + tile) * LANES : (first + tile + 1) * LANES] = summed[
                    tile * lat_pad : tile * lat_pad + lat, level * LANES : (level + 1) * LANES
                ]
        columns = pl.ds(first * LANES, tiles * LANES)
        copies.append(
            pltpu.make_async_copy(
                result.at[:, :, columns], out.at[:, :, columns], sems.at[first // tiles]
            )
        )
        copies[-1].start()
    for copy in copies:
        copy.wait()


def call(kernel, outs, specs, scratch, args, flops, size, name, out_spec=VMEM, limit=LIMIT):
    shapes = [jax.ShapeDtypeStruct(shape, dtype) for shape, dtype in outs]
    single = len(outs) == 1
    return pl.pallas_call(
        kernel,
        out_shape=shapes[0] if single else shapes,
        in_specs=specs,
        out_specs=out_spec if single else [out_spec] * len(outs),
        scratch_shapes=scratch,
        compiler_params=pltpu.CompilerParams(vmem_limit_bytes=limit),
        cost_estimate=pl.CostEstimate(flops=flops, bytes_accessed=size, transcendentals=0),
        name=name,
    )(*args)


def body(grid, legendre, counts, blocks, interp, source_weights, inverses):
    n_sec = lax.axis_size("sec")
    n_band = lax.axis_size("band")
    n_fld = lax.axis_size("fld")
    lev, lat, lon = grid.shape[1:]
    wave_dev, _, degrees = legendre.shape
    slots = blocks.shape[0]
    across = lon // LANES
    lat_pad = -(-lat // 16) * 16
    rest = 2 * wave_dev // THIRDS
    piece = rest * lev
    block_row = blocks.reshape(1, slots)

    table = jnp.asarray(dft_table(lon, wave_dev, n_band, n_fld))
    group = n_fld * n_band * rest
    padded_group = -(-group // LANES) * LANES
    depth = -(-across * lat_pad // LANES) * LANES
    parts = max(t for t in range(1, 8) if across % t == 0)
    state_rows = slots * lev // LANES
    message_rows = n_band * piece + state_rows
    message = call(
        functools.partial(local_kernel, lat_pad, parts),
        [((n_fld, message_rows, LANES), BF16)],
        [HBM] * 4,
        [
            pltpu.VMEM((lev, lat, lon), BF16),
            pltpu.VMEM((1, slots), jnp.int32),
            pltpu.VMEM((slots, LANES), BF16),
            pltpu.VMEM(table.shape, BF16),
            pltpu.VMEM((depth, lev * LANES), BF16),
            pltpu.VMEM((slots, LANES), jnp.int32),
            pltpu.VMEM((slots, depth), BF16),
            pltpu.VMEM((n_fld, message_rows, LANES), BF16),
            pltpu.VMEM((LANES, padded_group), F32),
            pltpu.VMEM((group * lev, LANES), F32),
            pltpu.SemaphoreType.DMA((parts + 3,)),
            pltpu.SemaphoreType.DMA((2,)),
        ],
        (grid.reshape(lev, lat, lon), block_row, interp, table),
        2 * slots * depth * lev * LANES + 2 * lev * lat * lon * THIRDS * group,
        2 * lev * lat * lon + 2 * slots * LANES,
        "local",
        HBM,
        WHOLE,
    )
    arrived = lax.all_to_all(message, "fld", 0, 0, tiled=True)
    spec_bands, flux_rows, _ = inverses.shape
    basis, inverse_rows = call(
        functools.partial(prepare_kernel, lat, n_band),
        [
            ((n_band, 2, THIRDS * degrees, LANES), BF16),
            ((spec_bands * flux_rows, flux_rows), BF16),
        ],
        [VMEM, VMEM],
        [
            pltpu.VMEM((degrees, (n_band * lat // LANES + 2) * LANES), F32),
            pltpu.VMEM((flux_rows * flux_rows, spec_bands), F32),
            pltpu.VMEM((spec_bands * flux_rows, flux_rows), F32),
        ],
        (jnp.swapaxes(legendre, 1, 2), jnp.transpose(inverses, (1, 2, 0))),
        0,
        8 * wave_dev * degrees * n_band * LANES,
        "prepare",
    )
    sent, near = call(
        functools.partial(regroup_kernel, n_band),
        [((n_sec * n_band, n_fld, piece, LANES), BF16), ((n_fld, state_rows, LANES), BF16)],
        [HBM, HBM],
        [pltpu.SemaphoreType.DMA((n_sec * n_band + 1,))],
        (arrived, basis),
        0,
        4 * n_sec * n_band * n_fld * piece * LANES,
        "regroup",
        HBM,
    )
    far = lax.ppermute(near, "sec", [(i, 1 - i) for i in range(n_sec)])
    pieces = lax.all_to_all(sent, ("sec", "band"), 0, 0, tiled=True)
    sources = spec_bands * flux_rows
    states = source_weights.shape[0]
    mine = n_sec * lev // (n_sec * n_fld)
    heating = call(
        functools.partial(column_kernel, n_sec, n_fld, lat_pad, slots),
        [((mine, lat, lon), BF16)],
        [SMEM] + [VMEM] * 6,
        [
            pltpu.VMEM((states, slots), F32),
            pltpu.VMEM((slots, mine * LANES), BF16),
            pltpu.VMEM((mine, lat, lon), BF16),
            pltpu.SemaphoreType.DMA((across,)),
        ],
        (counts, source_weights, inverse_rows, block_row, interp, near, far),
        8 * slots * slots * 1024,
        2 * slots * slots,
        "columns",
        HBM,
    )

    spectral = call(
        functools.partial(legendre_kernel, n_sec, n_band, n_fld, lev),
        [((wave_dev, 2, n_fld, n_sec * lev, degrees), BF16)],
        [VMEM, VMEM],
        [],
        (basis, pieces),
        4 * n_sec * n_fld * piece * n_band * LANES * degrees * THIRDS,
        2 * n_sec * n_band * n_fld * piece * LANES,
        "legendre",
    )
    return (spectral, heating)


def solution(mesh):
    return jax.shard_map(
        body,
        mesh=mesh,
        in_specs=(
            P("fld", "sec", "band", None),
            P(("band", "fld"), None, "sec"),
            P(),
            P("band"),
            P("band", None),
            P(),
            P(),
        ),
        out_specs=(P(("band", "fld"), None, None, None, "sec"), P(("sec", "fld"), "band", None)),
        check_vma=False,
    )
```

```python
import functools
import math

import jax
import jax.numpy as jnp
import numpy as np
from jax import lax
from jax.experimental import pallas as pl
from jax.experimental.pallas import tpu as pltpu
from jax.sharding import PartitionSpec as P

BF16 = jnp.bfloat16
F32 = jnp.float32
LANES = 128
THIRDS = 3
VMEM = pl.BlockSpec(memory_space=pltpu.VMEM)
HBM = pl.BlockSpec(memory_space=pltpu.HBM)
SMEM = pl.BlockSpec(memory_space=pltpu.SMEM)
LIMIT = 40 * 1024 * 1024
ROOM = 1200 * 1024
WHOLE = 64 * 1024 * 1024 - ROOM
NT = (((1,), (1,)), ((), ()))


def dft_table(lon, wave_dev, n_band, n_fld):
    values_dev = 2 * wave_dev
    rest = values_dev // THIRDS
    third, fld, band, low = np.meshgrid(
        np.arange(THIRDS), np.arange(n_fld), np.arange(n_band), np.arange(rest), indexing="ij"
    )
    value = third * rest + low
    wave = ((band * n_fld + fld) * wave_dev + value // 2).reshape(-1)
    part = (value % 2).reshape(-1)
    phase = np.arange(lon, dtype=np.int64)[:, None] * wave[None, :] % lon
    angle = phase * (2.0 * math.pi / lon)
    values = np.where(part[None, :] == 0, np.cos(angle), -np.sin(angle)) / math.sqrt(lon)
    return values.astype(np.float32).astype(BF16)


def pack(lev, lat, coeffs, message, padded, rows):
    group = coeffs.shape[1] // THIRDS
    padded[...] = jnp.zeros_like(padded)
    for level in range(lev):
        for third in range(THIRDS):
            padded[third * lat : (third + 1) * lat, :group] = coeffs[
                level * lat : (level + 1) * lat, third * group : (third + 1) * group
            ]
        rows[pl.ds(level, group, stride=lev), :] = jnp.transpose(padded[...])[:group]
    targets = message.shape[0]
    size = rows.shape[0] // targets
    message[:, :size, :] = rows[...].astype(BF16).reshape(targets, size, LANES)


def prepare_kernel(lat, n_band, legendre, inverses, out, out_inverses, wide, rows, turned):
    flux_rows, _, spec_bands = inverses.shape
    for row in range(flux_rows):
        rows[row * flux_rows : (row + 1) * flux_rows, :] = inverses[row].astype(F32)
    for row in range(flux_rows):
        turned[pl.ds(row, spec_bands, stride=flux_rows), :] = jnp.transpose(
            rows[pl.ds(row, flux_rows, stride=flux_rows), :]
        )
    out_inverses[...] = turned[...].astype(BF16)
    waves, degrees, _ = legendre.shape
    wide[...] = jnp.zeros_like(wide)
    lane = lax.broadcasted_iota(jnp.int32, (degrees, LANES), 1)
    for wave in range(waves):
        third, parity = wave // 2, wave % 2
        wide[:, : n_band * lat] = legendre[wave].astype(F32)
        place = third * lat
        live = (lane >= place) & (lane < place + lat)
        for band in range(n_band):
            base = band * lat // LANES * LANES
            moved = pltpu.roll(
                wide[:, base : base + 2 * LANES], (place - (band * lat - base)) % (2 * LANES), 1
            )
            out[band, parity, third * degrees : (third + 1) * degrees, :] = jnp.where(
                live, moved[:, :LANES], 0.0
            ).astype(BF16)


def legendre_kernel(n_sec, n_band, n_fld, lev, weights, pieces, out):
    degrees = out.shape[4]
    half = pieces.shape[2] // 2
    for parity in range(2):
        rows = slice(parity * half, (parity + 1) * half)
        basis = jnp.concatenate([weights[band, parity] for band in range(n_band)], axis=1)
        left = jnp.concatenate(
            [
                jnp.concatenate(
                    [
                        pieces[sec * n_band + band, fld, rows, :]
                        for band in range(n_band)
                    ],
                    axis=1,
                )
                for fld in range(n_fld)
                for sec in range(n_sec)
            ],
            axis=0,
        )
        result = lax.dot_general(left, basis, NT, preferred_element_type=F32)
        for third in range(THIRDS):
            part = result[:, third * degrees : (third + 1) * degrees]
            for fld in range(n_fld):
                for real in range(2):
                    levels = [
                        part[(fld * n_sec + sec) * half + real * lev :][:lev]
                        for sec in range(n_sec)
                    ]
                    out[2 * third + parity, real, fld] = jnp.concatenate(levels, axis=0).astype(
                        BF16
                    )


def slot_rows(blocks, across, lat_pad):
    shift = 16
    factor = -(-(1 << shift) // across)
    lat = lax.shift_right_logical(blocks * factor, shift)
    return (blocks - lat * across) * lat_pad + lat


def local_kernel(lat_pad, parts, grid_hbm, blocks_hbm, interp_hbm, table_hbm, out,
                 grid, blocks, interp, table, patch, column, selector, message, padded, rows,
                 sems, send):
    lev, lat, lon = grid.shape
    across = lon // LANES
    slots = interp.shape[0]
    depth = patch.shape[0]
    step = lon // parts
    small = [
        pltpu.make_async_copy(blocks_hbm, blocks, sems.at[parts]),
        pltpu.make_async_copy(interp_hbm, interp, sems.at[parts + 1]),
        pltpu.make_async_copy(table_hbm, table, sems.at[parts + 2]),
    ]
    loads = [
        pltpu.make_async_copy(
            grid_hbm.at[:, :, pl.ds(part * step, step)],
            grid.at[:, :, pl.ds(part * step, step)],
            sems.at[part],
        )
        for part in range(parts)
    ]
    small[0].start()
    for copy in loads:
        copy.start()
    small[1].start()
    small[2].start()
    small[0].wait()
    row = slot_rows(blocks[...], across, lat_pad)
    column[...] = jnp.transpose(jnp.broadcast_to(row, (LANES, slots)))
    chunk = 256
    lane = lax.broadcasted_iota(jnp.int32, (chunk, LANES), 1)
    for start in range(0, slots, chunk):
        mine = column[start : start + chunk, :]
        for base in range(0, depth, LANES):
            selector[start : start + chunk, base : base + LANES] = jnp.where(
                mine == lane + base, 1.0, 0.0
            ).astype(BF16)
    for part in range(parts):
        loads[part].wait()
        for tile in range(part * across // parts, (part + 1) * across // parts):
            patch[tile * lat_pad + lat : (tile + 1) * lat_pad, :] = jnp.zeros(
                (lat_pad - lat, lev * LANES), BF16
            )
            for level in range(lev):
                patch[
                    tile * lat_pad : tile * lat_pad + lat, level * LANES : (level + 1) * LANES
                ] = grid[level, :, tile * LANES : (tile + 1) * LANES]
    if depth > across * lat_pad:
        patch[across * lat_pad :, :] = jnp.zeros((depth - across * lat_pad, lev * LANES), BF16)
    small[1].wait()
    first_state = message.shape[1] - slots // LANES * lev
    copies = [
        pltpu.make_async_copy(message.at[:, rows_of, :], out.at[:, rows_of, :], send.at[i])
        for i, rows_of in enumerate(
            (pl.ds(0, first_state), pl.ds(first_state, message.shape[1] - first_state))
        )
    ]
    height = 512
    lane = lax.broadcasted_iota(jnp.int32, (height, LANES), 1)
    for start in range(0, slots, height):
        picked = jnp.dot(
            selector[start : start + height, :], patch[...], preferred_element_type=F32
        )
        weights = interp[start : start + height, :].astype(F32)
        total = jnp.zeros((height, LANES), F32)
        for level in range(lev):
            product = picked[:, level * LANES : (level + 1) * LANES] * weights
            total = jnp.where(lane == level, jnp.sum(product, axis=1, keepdims=True), total)
        state = jnp.transpose(total)[:lev].astype(BF16)
        for tile in range(height // LANES):
            row = first_state + (start // LANES + tile) * lev
            for target in range(message.shape[0]):
                message[target, row : row + lev, :] = state[:, tile * LANES : (tile + 1) * LANES]
        if start == 0:
            small[2].wait()
            flat = jnp.concatenate([grid[level] for level in range(lev)], axis=0)
            coeffs = jnp.dot(flat, table[...], preferred_element_type=F32)
            pack(lev, lat, coeffs, message, padded, rows)
            copies[0].start()
    copies[1].start()
    for copy in copies:
        copy.wait()


def regroup_kernel(n_band, arrived, _, out, out_state, sems):
    size = out.shape[2]
    copies = []
    for target in range(out.shape[0]):
        rows = pl.ds(target % n_band * size, size)
        copies.append(
            pltpu.make_async_copy(arrived.at[:, rows, :], out.at[target], sems.at[target])
        )
    rows = pl.ds(n_band * size, out_state.shape[1])
    copies.append(
        pltpu.make_async_copy(arrived.at[:, rows, :], out_state, sems.at[out.shape[0]])
    )
    for copy in copies:
        copy.start()
    for copy in copies:
        copy.wait()


def softplus(x):
    power = jnp.exp(jnp.minimum(x, 80.0))
    return jnp.where(x < -8.0, power, jnp.maximum(x, jnp.log(1.0 + power)))


def column_kernel(n_sec, n_fld, lat_pad, slots, counts, weights, inverses, blocks, interp,
                  near, far, out, state, spread, result, sems):
    lev = near.shape[1] * LANES // slots
    place = lax.axis_index("sec")
    for fld in range(n_fld):
        for shift, pieces in enumerate((near, far)):
            row = (fld * n_sec + (place ^ shift)) * lev
            for tile in range(slots // LANES):
                state[
                    pl.ds(pl.multiple_of(row, lev), lev), tile * LANES : (tile + 1) * LANES
                ] = pieces[fld, tile * lev : (tile + 1) * lev, :].astype(F32)
    mine, lat, lon = result.shape
    across = lon // LANES
    sources, flux_rows = inverses.shape
    levels = flux_rows // 2
    count = counts[lax.axis_index("band")]
    base = (place * n_fld + lax.axis_index("fld")) * mine
    chunk, height = 256, 512
    lane = lax.broadcasted_iota(jnp.int32, (1, flux_rows), 1)
    slot = lax.broadcasted_iota(jnp.int32, (height, 1), 0)
    column = jnp.transpose(state[...]).astype(BF16)
    tiles = [(top, at) for top in range(0, slots, height) for at in range(0, sources, chunk)]

    def gates_of(top, at):
        return jnp.dot(
            column[top : top + height], weights[:, at : at + chunk], preferred_element_type=F32
        )

    fluxes = {top: jnp.zeros((height, flux_rows), F32) for top in range(0, slots, height)}

    def add_flux(top, at, source):
        fluxes[top] = fluxes[top] + jnp.dot(
            source, inverses[at : at + chunk, :], preferred_element_type=F32
        )

    gates = gates_of(*tiles[0])
    before = None
    for i, tile in enumerate(tiles):
        later = gates_of(*tiles[i + 1]) if i + 1 < len(tiles) else None
        source = softplus(gates).astype(BF16)
        if before is not None:
            add_flux(*tiles[i - 1], before)
        gates, before = later, source
    add_flux(*tiles[-1], before)
    for start in range(0, slots, height):
        rows = fluxes[start]
        for level in range(mine):
            at = base + level
            plus = (lane == at) | ((lane == at + levels + 1) & (at + 1 < levels))
            minus = (lane == at + levels) | ((lane == at + 1) & (at + 1 < levels))
            terms = jnp.where(plus, rows, 0.0) - jnp.where(minus, rows, 0.0)
            heat = jnp.sum(terms, axis=1, keepdims=True)
            heat = jnp.where(slot + start < count, heat, 0.0).astype(BF16).astype(F32)
            spread[start : start + height, level * LANES : (level + 1) * LANES] = (
                heat * interp[start : start + height, :].astype(F32)
            ).astype(BF16)
    row = slot_rows(blocks[...], across, lat_pad)
    tiles = max(t for t in range(1, 8) if across % t == 0)
    height = tiles * lat_pad
    copies = []
    for first in range(0, across, tiles):
        match = row == lax.broadcasted_iota(jnp.int32, (height, slots), 0) + first * lat_pad
        left = jnp.where(match, 1.0, 0.0).astype(BF16)
        summed = jnp.dot(left, spread[...], preferred_element_type=F32).astype(BF16)
        for level in range(mine):
            for tile in range(tiles):
                result[level, :, (first + tile) * LANES : (first + tile + 1) * LANES] = summed[
                    tile * lat_pad : tile * lat_pad + lat, level * LANES : (level + 1) * LANES
                ]
        columns = pl.ds(first * LANES, tiles * LANES)
        copies.append(
            pltpu.make_async_copy(
                result.at[:, :, columns], out.at[:, :, columns], sems.at[first // tiles]
            )
        )
        copies[-1].start()
    for copy in copies:
        copy.wait()


def call(kernel, outs, specs, scratch, args, flops, size, name, out_spec=VMEM, limit=LIMIT):
    shapes = [jax.ShapeDtypeStruct(shape, dtype) for shape, dtype in outs]
    single = len(outs) == 1
    return pl.pallas_call(
        kernel,
        out_shape=shapes[0] if single else shapes,
        in_specs=specs,
        out_specs=out_spec if single else [out_spec] * len(outs),
        scratch_shapes=scratch,
        compiler_params=pltpu.CompilerParams(vmem_limit_bytes=limit),
        cost_estimate=pl.CostEstimate(flops=flops, bytes_accessed=size, transcendentals=0),
        name=name,
    )(*args)


def body(grid, legendre, counts, blocks, interp, source_weights, inverses):
    n_sec = lax.axis_size("sec")
    n_band = lax.axis_size("band")
    n_fld = lax.axis_size("fld")
    lev, lat, lon = grid.shape[1:]
    wave_dev, _, degrees = legendre.shape
    slots = blocks.shape[0]
    across = lon // LANES
    lat_pad = -(-lat // 16) * 16
    rest = 2 * wave_dev // THIRDS
    piece = rest * lev
    block_row = blocks.reshape(1, slots)

    table = jnp.asarray(dft_table(lon, wave_dev, n_band, n_fld))
    group = n_fld * n_band * rest
    padded_group = -(-group // LANES) * LANES
    depth = -(-across * lat_pad // LANES) * LANES
    parts = max(t for t in range(1, 8) if across % t == 0)
    state_rows = slots * lev // LANES
    message_rows = n_band * piece + state_rows
    message = call(
        functools.partial(local_kernel, lat_pad, parts),
        [((n_fld, message_rows, LANES), BF16)],
        [HBM] * 4,
        [
            pltpu.VMEM((lev, lat, lon), BF16),
            pltpu.VMEM((1, slots), jnp.int32),
            pltpu.VMEM((slots, LANES), BF16),
            pltpu.VMEM(table.shape, BF16),
            pltpu.VMEM((depth, lev * LANES), BF16),
            pltpu.VMEM((slots, LANES), jnp.int32),
            pltpu.VMEM((slots, depth), BF16),
            pltpu.VMEM((n_fld, message_rows, LANES), BF16),
            pltpu.VMEM((LANES, padded_group), F32),
            pltpu.VMEM((group * lev, LANES), F32),
            pltpu.SemaphoreType.DMA((parts + 3,)),
            pltpu.SemaphoreType.DMA((2,)),
        ],
        (grid.reshape(lev, lat, lon), block_row, interp, table),
        2 * slots * depth * lev * LANES + 2 * lev * lat * lon * THIRDS * group,
        2 * lev * lat * lon + 2 * slots * LANES,
        "local",
        HBM,
        WHOLE,
    )
    arrived = lax.all_to_all(message, "fld", 0, 0, tiled=True)
    spec_bands, flux_rows, _ = inverses.shape
    basis, inverse_rows = call(
        functools.partial(prepare_kernel, lat, n_band),
        [
            ((n_band, 2, THIRDS * degrees, LANES), BF16),
            ((spec_bands * flux_rows, flux_rows), BF16),
        ],
        [VMEM, VMEM],
        [
            pltpu.VMEM((degrees, (n_band * lat // LANES + 2) * LANES), F32),
            pltpu.VMEM((flux_rows * flux_rows, spec_bands), F32),
            pltpu.VMEM((spec_bands * flux_rows, flux_rows), F32),
        ],
        (jnp.swapaxes(legendre, 1, 2), jnp.transpose(inverses, (1, 2, 0))),
        0,
        8 * wave_dev * degrees * n_band * LANES,
        "prepare",
    )
    sent, near = call(
        functools.partial(regroup_kernel, n_band),
        [((n_sec * n_band, n_fld, piece, LANES), BF16), ((n_fld, state_rows, LANES), BF16)],
        [HBM, HBM],
        [pltpu.SemaphoreType.DMA((n_sec * n_band + 1,))],
        (arrived, basis),
        0,
        4 * n_sec * n_band * n_fld * piece * LANES,
        "regroup",
        HBM,
    )
    far = lax.ppermute(near, "sec", [(i, 1 - i) for i in range(n_sec)])
    pieces = lax.all_to_all(sent, ("sec", "band"), 0, 0, tiled=True)
    sources = spec_bands * flux_rows
    states = source_weights.shape[0]
    mine = n_sec * lev // (n_sec * n_fld)
    heating = call(
        functools.partial(column_kernel, n_sec, n_fld, lat_pad, slots),
        [((mine, lat, lon), BF16)],
        [SMEM] + [VMEM] * 6,
        [
            pltpu.VMEM((states, slots), F32),
            pltpu.VMEM((slots, mine * LANES), BF16),
            pltpu.VMEM((mine, lat, lon), BF16),
            pltpu.SemaphoreType.DMA((across,)),
        ],
        (counts, source_weights, inverse_rows, block_row, interp, near, far),
        8 * slots * slots * 1024,
        2 * slots * slots,
        "columns",
        HBM,
    )

    spectral = call(
        functools.partial(legendre_kernel, n_sec, n_band, n_fld, lev),
        [((wave_dev, 2, n_fld, n_sec * lev, degrees), BF16)],
        [VMEM, VMEM],
        [],
        (basis, pieces),
        4 * n_sec * n_fld * piece * n_band * LANES * degrees * THIRDS,
        2 * n_sec * n_band * n_fld * piece * LANES,
        "legendre",
    )
    return (spectral, heating)


def solution(mesh):
    return jax.shard_map(
        body,
        mesh=mesh,
        in_specs=(
            P("fld", "sec", "band", None),
            P(("band", "fld"), None, "sec"),
            P(),
            P("band"),
            P("band", None),
            P(),
            P(),
        ),
        out_specs=(P(("band", "fld"), None, None, None, "sec"), P(("sec", "fld"), "band", None)),
        check_vma=False,
    )
```

```python
import functools
import math

import jax
import jax.numpy as jnp
import numpy as np
from jax import lax
from jax.experimental import pallas as pl
from jax.experimental.pallas import tpu as pltpu
from jax.sharding import PartitionSpec as P

BF16 = jnp.bfloat16
F32 = jnp.float32
LANES = 128
THIRDS = 3
VMEM = pl.BlockSpec(memory_space=pltpu.VMEM)
HBM = pl.BlockSpec(memory_space=pltpu.HBM)
SMEM = pl.BlockSpec(memory_space=pltpu.SMEM)
LIMIT = 40 * 1024 * 1024
ROOM = 1200 * 1024
WHOLE = 64 * 1024 * 1024 - ROOM
NT = (((1,), (1,)), ((), ()))


def dft_table(lon, wave_dev, n_band, n_fld):
    values_dev = 2 * wave_dev
    rest = values_dev // THIRDS
    third, fld, band, low = np.meshgrid(
        np.arange(THIRDS), np.arange(n_fld), np.arange(n_band), np.arange(rest), indexing="ij"
    )
    value = third * rest + low
    wave = ((band * n_fld + fld) * wave_dev + value // 2).reshape(-1)
    part = (value % 2).reshape(-1)
    phase = np.arange(lon, dtype=np.int64)[:, None] * wave[None, :] % lon
    angle = phase * (2.0 * math.pi / lon)
    values = np.where(part[None, :] == 0, np.cos(angle), -np.sin(angle)) / math.sqrt(lon)
    return values.astype(np.float32).astype(BF16)


def pack(lev, lat, coeffs, message, padded, rows):
    group = coeffs.shape[1] // THIRDS
    padded[...] = jnp.zeros_like(padded)
    for level in range(lev):
        for third in range(THIRDS):
            padded[third * lat : (third + 1) * lat, :group] = coeffs[
                level * lat : (level + 1) * lat, third * group : (third + 1) * group
            ]
        rows[pl.ds(level, group, stride=lev), :] = jnp.transpose(padded[...])[:group]
    targets = message.shape[0]
    size = rows.shape[0] // targets
    message[:, :size, :] = rows[...].astype(BF16).reshape(targets, size, LANES)


def prepare_kernel(lat, n_band, across, legendre, inverses, blocks, out, out_inverses, onehot,
                   wide, rows, turned):
    lat_pad = onehot.shape[0] // across
    row = slot_rows(blocks[...], across, lat_pad)
    for tile in range(across):
        line = lax.broadcasted_iota(jnp.int32, (lat_pad, blocks.shape[1]), 0) + tile * lat_pad
        onehot[tile * lat_pad : (tile + 1) * lat_pad, :] = jnp.where(row == line, 1.0, 0.0).astype(
            BF16
        )
    flux_rows, _, spec_bands = inverses.shape
    for row in range(flux_rows):
        rows[row * flux_rows : (row + 1) * flux_rows, :] = inverses[row].astype(F32)
    for row in range(flux_rows):
        turned[pl.ds(row, spec_bands, stride=flux_rows), :] = jnp.transpose(
            rows[pl.ds(row, flux_rows, stride=flux_rows), :]
        )
    out_inverses[...] = turned[...].astype(BF16)
    waves, degrees, _ = legendre.shape
    wide[...] = jnp.zeros_like(wide)
    lane = lax.broadcasted_iota(jnp.int32, (degrees, LANES), 1)
    for wave in range(waves):
        third, parity = wave // 2, wave % 2
        wide[:, : n_band * lat] = legendre[wave].astype(F32)
        place = third * lat
        live = (lane >= place) & (lane < place + lat)
        for band in range(n_band):
            base = band * lat // LANES * LANES
            moved = pltpu.roll(
                wide[:, base : base + 2 * LANES], (place - (band * lat - base)) % (2 * LANES), 1
            )
            out[band, parity, third * degrees : (third + 1) * degrees, :] = jnp.where(
                live, moved[:, :LANES], 0.0
            ).astype(BF16)


def legendre_kernel(n_sec, n_band, n_fld, lev, weights, pieces, out_hbm, out, sems):
    degrees = out.shape[4]
    copies = []
    half = pieces.shape[2] // 2
    for parity in range(2):
        rows = slice(parity * half, (parity + 1) * half)
        basis = jnp.concatenate([weights[band, parity] for band in range(n_band)], axis=1)
        left = jnp.concatenate(
            [
                jnp.concatenate(
                    [
                        pieces[sec * n_band + band, fld, rows, :]
                        for band in range(n_band)
                    ],
                    axis=1,
                )
                for fld in range(n_fld)
                for sec in range(n_sec)
            ],
            axis=0,
        )
        result = lax.dot_general(left, basis, NT, preferred_element_type=F32)
        for third in range(THIRDS):
            part = result[:, third * degrees : (third + 1) * degrees]
            for fld in range(n_fld):
                for real in range(2):
                    levels = [
                        part[(fld * n_sec + sec) * half + real * lev :][:lev]
                        for sec in range(n_sec)
                    ]
                    out[2 * third + parity, real, fld] = jnp.concatenate(levels, axis=0).astype(
                        BF16
                    )
            wave = 2 * third + parity
            copies.append(
                pltpu.make_async_copy(out.at[wave], out_hbm.at[wave], sems.at[wave])
            )
            copies[-1].start()
    for copy in copies:
        copy.wait()


def slot_rows(blocks, across, lat_pad):
    shift = 16
    factor = -(-(1 << shift) // across)
    lat = lax.shift_right_logical(blocks * factor, shift)
    return (blocks - lat * across) * lat_pad + lat


def local_kernel(lat_pad, grid_hbm, blocks_hbm, interp_hbm, table_hbm, out,
                 grid, blocks, interp, table, patch, column, selector, message, padded, rows,
                 totals, sems, send):
    lev, lat, lon = grid.shape
    across = lon // LANES
    slots = interp.shape[0]
    depth = patch.shape[0]
    small = [
        pltpu.make_async_copy(blocks_hbm, blocks, sems.at[lev]),
        pltpu.make_async_copy(interp_hbm, interp, sems.at[lev + 1]),
        pltpu.make_async_copy(table_hbm, table, sems.at[lev + 2]),
    ]
    loads = [
        pltpu.make_async_copy(
            grid_hbm.at[pl.ds(level, 1)], grid.at[pl.ds(level, 1)], sems.at[level]
        )
        for level in range(lev)
    ]
    half = lev // 2
    small[0].start()
    for copy in loads[:half]:
        copy.start()
    small[1].start()
    for copy in loads[half:]:
        copy.start()
    small[2].start()
    small[0].wait()
    row = slot_rows(blocks[...], across, lat_pad)
    column[...] = jnp.transpose(jnp.broadcast_to(row, (LANES, slots)))
    chunk = 256
    lane = lax.broadcasted_iota(jnp.int32, (chunk, LANES), 1)
    for start in range(0, slots, chunk):
        mine = column[start : start + chunk, :]
        for base in range(0, depth, LANES):
            selector[start : start + chunk, base : base + LANES] = jnp.where(
                mine == lane + base, 1.0, 0.0
            ).astype(BF16)
    first_state = message.shape[1] - slots // LANES * lev
    copies = [
        pltpu.make_async_copy(message.at[:, rows_of, :], out.at[:, rows_of, :], send.at[i])
        for i, rows_of in enumerate(
            (pl.ds(0, first_state), pl.ds(first_state, message.shape[1] - first_state))
        )
    ]
    for tile in range(across):
        patch[tile * lat_pad + lat : (tile + 1) * lat_pad, :] = jnp.zeros(
            (lat_pad - lat, lev * LANES), BF16
        )
    if depth > across * lat_pad:
        patch[across * lat_pad :, :] = jnp.zeros((depth - across * lat_pad, lev * LANES), BF16)
    for base in (0, half):
        for level in range(base, base + half):
            loads[level].wait()
            for tile in range(across):
                patch[
                    tile * lat_pad : tile * lat_pad + lat, level * LANES : (level + 1) * LANES
                ] = grid[level, :, tile * LANES : (tile + 1) * LANES]
        if base == 0:
            small[1].wait()
        else:
            small[2].wait()
            flat = jnp.concatenate([grid[level] for level in range(lev)], axis=0)
            coeffs = jnp.dot(flat, table[...], preferred_element_type=F32)
            pack(lev, lat, coeffs, message, padded, rows)
            copies[0].start()
        for start in range(0, slots, chunk):
            top = slice(start, start + chunk)
            picked = jnp.dot(
                selector[top, :],
                patch[:, base * LANES : (base + half) * LANES],
                preferred_element_type=F32,
            )
            weights = interp[top, :].astype(F32)
            total = jnp.zeros((chunk, LANES), F32) if base == 0 else totals[top, :]
            for i in range(half):
                product = picked[:, i * LANES : (i + 1) * LANES] * weights
                total = jnp.where(
                    lane == base + i, jnp.sum(product, axis=1, keepdims=True), total
                )
            if base == 0:
                totals[top, :] = total
                continue
            state = jnp.transpose(total)[:lev].astype(BF16)
            for tile in range(chunk // LANES):
                row = first_state + (start // LANES + tile) * lev
                for target in range(message.shape[0]):
                    message[target, row : row + lev, :] = state[
                        :, tile * LANES : (tile + 1) * LANES
                    ]
    copies[1].start()
    for copy in copies:
        copy.wait()


def regroup_kernel(n_band, arrived, _, out, out_state, sems):
    size = out.shape[2]
    copies = []
    for target in range(out.shape[0]):
        rows = pl.ds(target % n_band * size, size)
        copies.append(
            pltpu.make_async_copy(arrived.at[:, rows, :], out.at[target], sems.at[target])
        )
    rows = pl.ds(n_band * size, out_state.shape[1])
    copies.append(
        pltpu.make_async_copy(arrived.at[:, rows, :], out_state, sems.at[out.shape[0]])
    )
    for copy in copies:
        copy.start()
    for copy in copies:
        copy.wait()


def softplus(x):
    power = jnp.exp(jnp.minimum(x, 80.0))
    return jnp.where(x < -8.0, power, jnp.maximum(x, jnp.log(1.0 + power)))


def column_kernel(n_sec, n_fld, lat_pad, slots, counts, weights, inverses, onehot, interp,
                  near, far, out, state, spread, result, sems):
    lev = near.shape[1] * LANES // slots
    place = lax.axis_index("sec")
    for fld in range(n_fld):
        for shift, pieces in enumerate((near, far)):
            row = (fld * n_sec + (place ^ shift)) * lev
            for tile in range(slots // LANES):
                state[
                    pl.ds(pl.multiple_of(row, lev), lev), tile * LANES : (tile + 1) * LANES
                ] = pieces[fld, tile * lev : (tile + 1) * lev, :].astype(F32)
    mine, lat, lon = result.shape
    across = lon // LANES
    sources, flux_rows = inverses.shape
    levels = flux_rows // 2
    count = counts[lax.axis_index("band")]
    base = (place * n_fld + lax.axis_index("fld")) * mine
    chunk = 256
    lane = lax.broadcasted_iota(jnp.int32, (1, flux_rows), 1)
    slot = lax.broadcasted_iota(jnp.int32, (chunk, 1), 0)
    column = jnp.transpose(state[...]).astype(BF16)
    tiles = [(top, at) for top in range(0, slots, chunk) for at in range(0, sources, chunk)]

    def gates_of(top, at):
        return jnp.dot(
            column[top : top + chunk], weights[:, at : at + chunk], preferred_element_type=F32
        )

    fluxes = {top: jnp.zeros((chunk, flux_rows), F32) for top in range(0, slots, chunk)}

    def add_flux(top, at, source):
        fluxes[top] = fluxes[top] + jnp.dot(
            source, inverses[at : at + chunk, :], preferred_element_type=F32
        )

    gates = gates_of(*tiles[0])
    before = None
    for i, tile in enumerate(tiles):
        later = gates_of(*tiles[i + 1]) if i + 1 < len(tiles) else None
        source = softplus(gates).astype(BF16)
        if before is not None:
            add_flux(*tiles[i - 1], before)
        gates, before = later, source
    add_flux(*tiles[-1], before)
    for start in range(0, slots, chunk):
        rows = fluxes[start]
        for level in range(mine):
            at = base + level
            plus = (lane == at) | ((lane == at + levels + 1) & (at + 1 < levels))
            minus = (lane == at + levels) | ((lane == at + 1) & (at + 1 < levels))
            terms = jnp.where(plus, rows, 0.0) - jnp.where(minus, rows, 0.0)
            heat = jnp.sum(terms, axis=1, keepdims=True)
            heat = jnp.where(slot + start < count, heat, 0.0).astype(BF16).astype(F32)
            spread[start : start + chunk, level * LANES : (level + 1) * LANES] = (
                heat * interp[start : start + chunk, :].astype(F32)
            ).astype(BF16)
    tiles = max(t for t in range(1, 8) if across % t == 0)
    height = tiles * lat_pad
    copies = []
    for first in range(0, across, tiles):
        left = onehot[first * lat_pad : first * lat_pad + height, :]
        summed = jnp.dot(left, spread[...], preferred_element_type=F32).astype(BF16)
        for level in range(mine):
            for tile in range(tiles):
                result[level, :, (first + tile) * LANES : (first + tile + 1) * LANES] = summed[
                    tile * lat_pad : tile * lat_pad + lat, level * LANES : (level + 1) * LANES
                ]
        columns = pl.ds(first * LANES, tiles * LANES)
        copies.append(
            pltpu.make_async_copy(
                result.at[:, :, columns], out.at[:, :, columns], sems.at[first // tiles]
            )
        )
        copies[-1].start()
    for copy in copies:
        copy.wait()


def call(kernel, outs, specs, scratch, args, flops, size, name, out_spec=VMEM, limit=LIMIT):
    shapes = [jax.ShapeDtypeStruct(shape, dtype) for shape, dtype in outs]
    single = len(outs) == 1
    return pl.pallas_call(
        kernel,
        out_shape=shapes[0] if single else shapes,
        in_specs=specs,
        out_specs=out_spec if single else [out_spec] * len(outs),
        scratch_shapes=scratch,
        compiler_params=pltpu.CompilerParams(vmem_limit_bytes=limit),
        cost_estimate=pl.CostEstimate(flops=flops, bytes_accessed=size, transcendentals=0),
        name=name,
    )(*args)


def body(grid, legendre, counts, blocks, interp, source_weights, inverses):
    n_sec = lax.axis_size("sec")
    n_band = lax.axis_size("band")
    n_fld = lax.axis_size("fld")
    lev, lat, lon = grid.shape[1:]
    wave_dev, _, degrees = legendre.shape
    slots = blocks.shape[0]
    across = lon // LANES
    lat_pad = -(-lat // 16) * 16
    rest = 2 * wave_dev // THIRDS
    piece = rest * lev
    block_row = blocks.reshape(1, slots)

    table = jnp.asarray(dft_table(lon, wave_dev, n_band, n_fld))
    group = n_fld * n_band * rest
    padded_group = -(-group // LANES) * LANES
    depth = -(-across * lat_pad // LANES) * LANES
    state_rows = slots * lev // LANES
    message_rows = n_band * piece + state_rows
    message = call(
        functools.partial(local_kernel, lat_pad),
        [((n_fld, message_rows, LANES), BF16)],
        [HBM] * 4,
        [
            pltpu.VMEM((lev, lat, lon), BF16),
            pltpu.VMEM((1, slots), jnp.int32),
            pltpu.VMEM((slots, LANES), BF16),
            pltpu.VMEM(table.shape, BF16),
            pltpu.VMEM((depth, lev * LANES), BF16),
            pltpu.VMEM((slots, LANES), jnp.int32),
            pltpu.VMEM((slots, depth), BF16),
            pltpu.VMEM((n_fld, message_rows, LANES), BF16),
            pltpu.VMEM((LANES, padded_group), F32),
            pltpu.VMEM((group * lev, LANES), F32),
            pltpu.VMEM((slots, LANES), F32),
            pltpu.SemaphoreType.DMA((lev + 3,)),
            pltpu.SemaphoreType.DMA((2,)),
        ],
        (grid.reshape(lev, lat, lon), block_row, interp, table),
        2 * slots * depth * lev * LANES + 2 * lev * lat * lon * THIRDS * group,
        2 * lev * lat * lon + 2 * slots * LANES,
        "local",
        HBM,
        WHOLE,
    )
    arrived = lax.all_to_all(message, "fld", 0, 0, tiled=True)
    spec_bands, flux_rows, _ = inverses.shape
    basis, inverse_rows, onehot = call(
        functools.partial(prepare_kernel, lat, n_band, across),
        [
            ((n_band, 2, THIRDS * degrees, LANES), BF16),
            ((spec_bands * flux_rows, flux_rows), BF16),
            ((across * lat_pad, slots), BF16),
        ],
        [VMEM, VMEM, VMEM],
        [
            pltpu.VMEM((degrees, (n_band * lat // LANES + 2) * LANES), F32),
            pltpu.VMEM((flux_rows * flux_rows, spec_bands), F32),
            pltpu.VMEM((spec_bands * flux_rows, flux_rows), F32),
        ],
        (jnp.swapaxes(legendre, 1, 2), jnp.transpose(inverses, (1, 2, 0)), block_row),
        0,
        8 * wave_dev * degrees * n_band * LANES,
        "prepare",
    )
    sent, near = call(
        functools.partial(regroup_kernel, n_band),
        [((n_sec * n_band, n_fld, piece, LANES), BF16), ((n_fld, state_rows, LANES), BF16)],
        [HBM, HBM],
        [pltpu.SemaphoreType.DMA((n_sec * n_band + 1,))],
        (arrived, basis),
        0,
        4 * n_sec * n_band * n_fld * piece * LANES,
        "regroup",
        HBM,
    )
    far = lax.ppermute(near, "sec", [(i, 1 - i) for i in range(n_sec)])
    pieces = lax.all_to_all(sent, ("sec", "band"), 0, 0, tiled=True)
    sources = spec_bands * flux_rows
    states = source_weights.shape[0]
    mine = n_sec * lev // (n_sec * n_fld)
    heating = call(
        functools.partial(column_kernel, n_sec, n_fld, lat_pad, slots),
        [((mine, lat, lon), BF16)],
        [SMEM] + [VMEM] * 6,
        [
            pltpu.VMEM((states, slots), F32),
            pltpu.VMEM((slots, mine * LANES), BF16),
            pltpu.VMEM((mine, lat, lon), BF16),
            pltpu.SemaphoreType.DMA((across,)),
        ],
        (counts, source_weights, inverse_rows, onehot, interp, near, far),
        8 * slots * slots * 1024,
        2 * slots * slots,
        "columns",
        HBM,
    )

    spectral = call(
        functools.partial(legendre_kernel, n_sec, n_band, n_fld, lev),
        [((wave_dev, 2, n_fld, n_sec * lev, degrees), BF16)],
        [VMEM, VMEM],
        [
            pltpu.VMEM((wave_dev, 2, n_fld, n_sec * lev, degrees), BF16),
            pltpu.SemaphoreType.DMA((wave_dev,)),
        ],
        (basis, pieces),
        4 * n_sec * n_fld * piece * n_band * LANES * degrees * THIRDS,
        2 * n_sec * n_band * n_fld * piece * LANES,
        "legendre",
        HBM,
    )
    return (spectral, heating)


def solution(mesh):
    return jax.shard_map(
        body,
        mesh=mesh,
        in_specs=(
            P("fld", "sec", "band", None),
            P(("band", "fld"), None, "sec"),
            P(),
            P("band"),
            P("band", None),
            P(),
            P(),
        ),
        out_specs=(P(("band", "fld"), None, None, None, "sec"), P(("sec", "fld"), "band", None)),
        check_vma=False,
    )
```

```python
import functools
import math

import jax
import jax.numpy as jnp
import numpy as np
from jax import lax
from jax.experimental import pallas as pl
from jax.experimental.pallas import tpu as pltpu
from jax.sharding import PartitionSpec as P

BF16 = jnp.bfloat16
F32 = jnp.float32
LANES = 128
THIRDS = 3
VMEM = pl.BlockSpec(memory_space=pltpu.VMEM)
HBM = pl.BlockSpec(memory_space=pltpu.HBM)
SMEM = pl.BlockSpec(memory_space=pltpu.SMEM)
LIMIT = 40 * 1024 * 1024
SMALL = 4 * 1024 * 1024
ROOM = 1200 * 1024
WHOLE = 64 * 1024 * 1024 - ROOM
NT = (((1,), (1,)), ((), ()))


def dft_table(lon, wave_dev, n_band, n_fld):
    values_dev = 2 * wave_dev
    rest = values_dev // THIRDS
    third, fld, band, low = np.meshgrid(
        np.arange(THIRDS), np.arange(n_fld), np.arange(n_band), np.arange(rest), indexing="ij"
    )
    value = third * rest + low
    wave = ((band * n_fld + fld) * wave_dev + value // 2).reshape(-1)
    part = (value % 2).reshape(-1)
    phase = np.arange(lon, dtype=np.int64)[:, None] * wave[None, :] % lon
    angle = phase * (2.0 * math.pi / lon)
    values = np.where(part[None, :] == 0, np.cos(angle), -np.sin(angle)) / math.sqrt(lon)
    return values.astype(np.float32).astype(BF16)


def pack(lev, lat, coeffs, message, padded, rows):
    group = coeffs.shape[1] // THIRDS
    padded[...] = jnp.zeros_like(padded)
    for level in range(lev):
        for third in range(THIRDS):
            padded[third * lat : (third + 1) * lat, :group] = coeffs[
                level * lat : (level + 1) * lat, third * group : (third + 1) * group
            ]
        rows[pl.ds(level, group, stride=lev), :] = jnp.transpose(padded[...])[:group]
    targets, size = message.shape[0], message.shape[2]
    bands = rows.shape[0] // targets // size
    message[:, :bands] = rows[...].astype(BF16).reshape(targets, bands, size, LANES)


def prepare_kernel(lat, n_band, legendre, inverses, out, out_inverses, wide, rows, turned):
    flux_rows, _, spec_bands = inverses.shape
    for row in range(flux_rows):
        rows[row * flux_rows : (row + 1) * flux_rows, :] = inverses[row].astype(F32)
    for row in range(flux_rows):
        turned[pl.ds(row, spec_bands, stride=flux_rows), :] = jnp.transpose(
            rows[pl.ds(row, flux_rows, stride=flux_rows), :]
        )
    out_inverses[...] = turned[...].astype(BF16)
    waves, degrees, _ = legendre.shape
    wide[...] = jnp.zeros_like(wide)
    lane = lax.broadcasted_iota(jnp.int32, (degrees, LANES), 1)
    for wave in range(waves):
        third, parity = wave // 2, wave % 2
        wide[:, : n_band * lat] = legendre[wave].astype(F32)
        place = third * lat
        live = (lane >= place) & (lane < place + lat)
        for band in range(n_band):
            base = band * lat // LANES * LANES
            moved = pltpu.roll(
                wide[:, base : base + 2 * LANES], (place - (band * lat - base)) % (2 * LANES), 1
            )
            out[band, parity, third * degrees : (third + 1) * degrees, :] = jnp.where(
                live, moved[:, :LANES], 0.0
            ).astype(BF16)


def legendre_kernel(n_sec, n_band, n_fld, lev, weights, pieces, out_hbm, out, sems):
    degrees = out.shape[4]
    copies = []
    half = pieces.shape[2] // 2
    for parity in range(2):
        rows = slice(parity * half, (parity + 1) * half)
        basis = jnp.concatenate([weights[band, parity] for band in range(n_band)], axis=1)
        left = jnp.concatenate(
            [
                jnp.concatenate(
                    [
                        pieces[sec * n_band + band, fld, rows, :]
                        for band in range(n_band)
                    ],
                    axis=1,
                )
                for fld in range(n_fld)
                for sec in range(n_sec)
            ],
            axis=0,
        )
        result = lax.dot_general(left, basis, NT, preferred_element_type=F32)
        for third in range(THIRDS):
            part = result[:, third * degrees : (third + 1) * degrees]
            for fld in range(n_fld):
                for real in range(2):
                    levels = [
                        part[(fld * n_sec + sec) * half + real * lev :][:lev]
                        for sec in range(n_sec)
                    ]
                    out[2 * third + parity, real, fld] = jnp.concatenate(levels, axis=0).astype(
                        BF16
                    )
            wave = 2 * third + parity
            copies.append(
                pltpu.make_async_copy(out.at[wave], out_hbm.at[wave], sems.at[wave])
            )
            copies[-1].start()
    for copy in copies:
        copy.wait()


def slot_rows(blocks, across, lat_pad):
    shift = 16
    factor = -(-(1 << shift) // across)
    lat = lax.shift_right_logical(blocks * factor, shift)
    return (blocks - lat * across) * lat_pad + lat


def local_kernel(lat_pad, grid_hbm, blocks_hbm, interp_hbm, table_hbm, *refs):
    targets = len(refs) - 14
    outs = refs[:targets]
    (grid, blocks, interp, table, patch, column, selector, message, padded, rows, totals, sems,
     send_fourier, send_state) = refs[targets:]
    lev, lat, lon = grid.shape
    across = lon // LANES
    slots = interp.shape[0]
    depth = patch.shape[0]
    small = [
        pltpu.make_async_copy(blocks_hbm, blocks, sems.at[lev]),
        pltpu.make_async_copy(interp_hbm, interp, sems.at[lev + 1]),
        pltpu.make_async_copy(table_hbm, table, sems.at[lev + 2]),
    ]
    loads = [
        pltpu.make_async_copy(
            grid_hbm.at[pl.ds(level, 1)], grid.at[pl.ds(level, 1)], sems.at[level]
        )
        for level in range(lev)
    ]
    half = lev // 2
    small[0].start()
    for copy in loads[:half]:
        copy.start()
    small[1].start()
    for copy in loads[half:]:
        copy.start()
    small[2].start()
    small[0].wait()
    row = slot_rows(blocks[...], across, lat_pad)
    column[...] = jnp.transpose(jnp.broadcast_to(row, (LANES, slots)))
    chunk = 256
    lane = lax.broadcasted_iota(jnp.int32, (chunk, LANES), 1)
    for start in range(0, slots, chunk):
        mine = column[start : start + chunk, :]
        for base in range(0, depth, LANES):
            selector[start : start + chunk, base : base + LANES] = jnp.where(
                mine == lane + base, 1.0, 0.0
            ).astype(BF16)
    state_blocks = slots * lev // LANES // message.shape[2]
    bands = message.shape[1] - state_blocks
    place = lax.axis_index("fld")
    fourier_copies, state_copies = [], []
    for shift in reversed(range(targets)):
        mine = message.at[place ^ shift]
        fourier_copies.append(
            pltpu.make_async_copy(
                mine.at[pl.ds(0, bands)], outs[shift].at[pl.ds(0, bands)], send_fourier.at[shift]
            )
        )
        state_copies.append(
            pltpu.make_async_copy(
                mine.at[pl.ds(bands, state_blocks)],
                outs[shift].at[pl.ds(bands, state_blocks)],
                send_state.at[shift],
            )
        )
    for tile in range(across):
        patch[tile * lat_pad + lat : (tile + 1) * lat_pad, :] = jnp.zeros(
            (lat_pad - lat, lev * LANES), BF16
        )
    if depth > across * lat_pad:
        patch[across * lat_pad :, :] = jnp.zeros((depth - across * lat_pad, lev * LANES), BF16)
    for base in (0, half):
        for level in range(base, base + half):
            loads[level].wait()
            for tile in range(across):
                patch[
                    tile * lat_pad : tile * lat_pad + lat, level * LANES : (level + 1) * LANES
                ] = grid[level, :, tile * LANES : (tile + 1) * LANES]
        if base == 0:
            small[1].wait()
        else:
            small[2].wait()
            flat = jnp.concatenate([grid[level] for level in range(lev)], axis=0)
            coeffs = jnp.dot(flat, table[...], preferred_element_type=F32)
            pack(lev, lat, coeffs, message, padded, rows)
            for copy in fourier_copies:
                copy.start()
        for start in range(0, slots, chunk):
            top = slice(start, start + chunk)
            picked = jnp.dot(
                selector[top, :],
                patch[:, base * LANES : (base + half) * LANES],
                preferred_element_type=F32,
            )
            weights = interp[top, :].astype(F32)
            total = jnp.zeros((chunk, LANES), F32) if base == 0 else totals[top, :]
            for i in range(half):
                product = picked[:, i * LANES : (i + 1) * LANES] * weights
                total = jnp.where(
                    lane == base + i, jnp.sum(product, axis=1, keepdims=True), total
                )
            if base == 0:
                totals[top, :] = total
                continue
            state = jnp.transpose(total)[:lev].astype(BF16)
            for tile in range(chunk // LANES):
                block, row = divmod((start // LANES + tile) * lev, message.shape[2])
                for target in range(targets):
                    message[target, bands + block, row : row + lev, :] = state[
                        :, tile * LANES : (tile + 1) * LANES
                    ]
    for copy in state_copies:
        copy.start()
    for copy in fourier_copies + state_copies:
        copy.wait()


def regroup_kernel(n_sec, n_band, *refs):
    pieces, (_, out, out_state, sems) = refs[:-4], refs[-4:]
    blocks = out_state.shape[1]
    place = lax.axis_index("fld")
    copies = []
    for shift, piece in enumerate(pieces):
        fld = place ^ shift
        copies.append((piece.at[pl.ds(n_band, blocks)], out_state.at[fld]))
        for sec in range(n_sec):
            copies.append(
                (piece.at[pl.ds(0, n_band)], out.at[pl.ds(sec * n_band, n_band), fld])
            )
    copies = [pltpu.make_async_copy(*pair, sems.at[i]) for i, pair in enumerate(copies)]
    for copy in copies:
        copy.start()
    for copy in copies:
        copy.wait()


def softplus(x):
    power = jnp.exp(jnp.minimum(x, 80.0))
    return jnp.where(x < -8.0, power, jnp.maximum(x, jnp.log(1.0 + power)))


def column_kernel(n_sec, n_fld, lat_pad, slots, counts, weights, inverses, blocks, interp,
                  near, far, out, state, spread, result, sems):
    lev = near.shape[1] * near.shape[2] * LANES // slots
    place = lax.axis_index("sec")
    for fld in range(n_fld):
        for shift, pieces in enumerate((near, far)):
            row = (fld * n_sec + (place ^ shift)) * lev
            for tile in range(slots // LANES):
                state[
                    pl.ds(pl.multiple_of(row, lev), lev), tile * LANES : (tile + 1) * LANES
                ] = pieces[fld, tile * lev // near.shape[2]][
                    tile * lev % near.shape[2] : tile * lev % near.shape[2] + lev
                ].astype(F32)
    mine, lat, lon = result.shape
    across = lon // LANES
    sources, flux_rows = inverses.shape
    levels = flux_rows // 2
    count = counts[lax.axis_index("band")]
    base = (place * n_fld + lax.axis_index("fld")) * mine
    chunk = 256
    lane = lax.broadcasted_iota(jnp.int32, (1, flux_rows), 1)
    slot = lax.broadcasted_iota(jnp.int32, (chunk, 1), 0)
    column = jnp.transpose(state[...]).astype(BF16)
    tiles = [(top, at) for top in range(0, slots, chunk) for at in range(0, sources, chunk)]

    def gates_of(top, at):
        return jnp.dot(
            column[top : top + chunk], weights[:, at : at + chunk], preferred_element_type=F32
        )

    fluxes = {top: jnp.zeros((chunk, flux_rows), F32) for top in range(0, slots, chunk)}

    def add_flux(top, at, source):
        fluxes[top] = fluxes[top] + jnp.dot(
            source, inverses[at : at + chunk, :], preferred_element_type=F32
        )

    gates = gates_of(*tiles[0])
    before = None
    for i, tile in enumerate(tiles):
        later = gates_of(*tiles[i + 1]) if i + 1 < len(tiles) else None
        source = softplus(gates).astype(BF16)
        if before is not None:
            add_flux(*tiles[i - 1], before)
        gates, before = later, source
    add_flux(*tiles[-1], before)
    for start in range(0, slots, chunk):
        rows = fluxes[start]
        for level in range(mine):
            at = base + level
            plus = (lane == at) | ((lane == at + levels + 1) & (at + 1 < levels))
            minus = (lane == at + levels) | ((lane == at + 1) & (at + 1 < levels))
            terms = jnp.where(plus, rows, 0.0) - jnp.where(minus, rows, 0.0)
            heat = jnp.sum(terms, axis=1, keepdims=True)
            heat = jnp.where(slot + start < count, heat, 0.0).astype(BF16).astype(F32)
            spread[start : start + chunk, level * LANES : (level + 1) * LANES] = (
                heat * interp[start : start + chunk, :].astype(F32)
            ).astype(BF16)
    row = slot_rows(blocks[...], across, lat_pad)
    tiles = max(t for t in range(1, 8) if across % t == 0)
    height = tiles * lat_pad
    copies = []
    for first in range(0, across, tiles):
        match = row == lax.broadcasted_iota(jnp.int32, (height, slots), 0) + first * lat_pad
        left = jnp.where(match, 1.0, 0.0).astype(BF16)
        summed = jnp.dot(left, spread[...], preferred_element_type=F32).astype(BF16)
        for level in range(mine):
            for tile in range(tiles):
                result[level, :, (first + tile) * LANES : (first + tile + 1) * LANES] = summed[
                    tile * lat_pad : tile * lat_pad + lat, level * LANES : (level + 1) * LANES
                ]
        columns = pl.ds(first * LANES, tiles * LANES)
        copies.append(
            pltpu.make_async_copy(
                result.at[:, :, columns], out.at[:, :, columns], sems.at[first // tiles]
            )
        )
        copies[-1].start()
    for copy in copies:
        copy.wait()


def call(kernel, outs, specs, scratch, args, flops, size, name, out_spec=VMEM, limit=LIMIT):
    shapes = [jax.ShapeDtypeStruct(shape, dtype) for shape, dtype in outs]
    single = len(outs) == 1
    return pl.pallas_call(
        kernel,
        out_shape=shapes[0] if single else shapes,
        in_specs=specs,
        out_specs=out_spec if single else [out_spec] * len(outs),
        scratch_shapes=scratch,
        compiler_params=pltpu.CompilerParams(vmem_limit_bytes=limit),
        cost_estimate=pl.CostEstimate(flops=flops, bytes_accessed=size, transcendentals=0),
        name=name,
    )(*args)


def exchange(value, axis, shift):
    return lax.ppermute(value, axis, [(i, i ^ shift) for i in range(lax.axis_size(axis))])


def body(grid, legendre, counts, blocks, interp, source_weights, inverses):
    n_sec = lax.axis_size("sec")
    n_band = lax.axis_size("band")
    n_fld = lax.axis_size("fld")
    lev, lat, lon = grid.shape[1:]
    wave_dev, _, degrees = legendre.shape
    slots = blocks.shape[0]
    across = lon // LANES
    lat_pad = -(-lat // 16) * 16
    rest = 2 * wave_dev // THIRDS
    piece = rest * lev
    block_row = blocks.reshape(1, slots)

    table = jnp.asarray(dft_table(lon, wave_dev, n_band, n_fld))
    group = n_fld * n_band * rest
    padded_group = -(-group // LANES) * LANES
    depth = -(-across * lat_pad // LANES) * LANES
    state_blocks = slots * lev // LANES // piece
    message_blocks = n_band + state_blocks
    messages = call(
        functools.partial(local_kernel, lat_pad),
        [((message_blocks, piece, LANES), BF16)] * n_fld,
        [HBM] * 4,
        [
            pltpu.VMEM((lev, lat, lon), BF16),
            pltpu.VMEM((1, slots), jnp.int32),
            pltpu.VMEM((slots, LANES), BF16),
            pltpu.VMEM(table.shape, BF16),
            pltpu.VMEM((depth, lev * LANES), BF16),
            pltpu.VMEM((slots, LANES), jnp.int32),
            pltpu.VMEM((slots, depth), BF16),
            pltpu.VMEM((n_fld, message_blocks, piece, LANES), BF16),
            pltpu.VMEM((LANES, padded_group), F32),
            pltpu.VMEM((group * lev, LANES), F32),
            pltpu.VMEM((slots, LANES), F32),
            pltpu.SemaphoreType.DMA((lev + 3,)),
            pltpu.SemaphoreType.DMA((n_fld,)),
            pltpu.SemaphoreType.DMA((n_fld,)),
        ],
        (grid.reshape(lev, lat, lon), block_row, interp, table),
        2 * slots * depth * lev * LANES + 2 * lev * lat * lon * THIRDS * group,
        2 * lev * lat * lon + 2 * slots * LANES,
        "local",
        HBM,
        WHOLE,
    )
    arrived = [messages[0]] + [None] * (n_fld - 1)
    for shift in reversed(range(1, n_fld)):
        arrived[shift] = exchange(messages[shift], "fld", shift)
    spec_bands, flux_rows, _ = inverses.shape
    basis, inverse_rows = call(
        functools.partial(prepare_kernel, lat, n_band),
        [
            ((n_band, 2, THIRDS * degrees, LANES), BF16),
            ((spec_bands * flux_rows, flux_rows), BF16),
        ],
        [VMEM, VMEM],
        [
            pltpu.VMEM((degrees, (n_band * lat // LANES + 2) * LANES), F32),
            pltpu.VMEM((flux_rows * flux_rows, spec_bands), F32),
            pltpu.VMEM((spec_bands * flux_rows, flux_rows), F32),
        ],
        (jnp.swapaxes(legendre, 1, 2), jnp.transpose(inverses, (1, 2, 0))),
        0,
        8 * wave_dev * degrees * n_band * LANES,
        "prepare",
    )
    sent, near = call(
        functools.partial(regroup_kernel, n_sec, n_band),
        [
            ((n_sec * n_band, n_fld, piece, LANES), BF16),
            ((n_fld, state_blocks, piece, LANES), BF16),
        ],
        [HBM] * (n_fld + 1),
        [pltpu.SemaphoreType.DMA((n_fld * (1 + n_sec),))],
        (*arrived, basis),
        0,
        4 * n_sec * n_band * n_fld * piece * LANES,
        "regroup",
        HBM,
        SMALL,
    )
    far = exchange(near, "sec", 1)
    pieces = lax.all_to_all(sent, ("sec", "band"), 0, 0, tiled=True)
    sources = spec_bands * flux_rows
    states = source_weights.shape[0]
    mine = n_sec * lev // (n_sec * n_fld)
    heating = call(
        functools.partial(column_kernel, n_sec, n_fld, lat_pad, slots),
        [((mine, lat, lon), BF16)],
        [SMEM] + [VMEM] * 6,
        [
            pltpu.VMEM((states, slots), F32),
            pltpu.VMEM((slots, mine * LANES), BF16),
            pltpu.VMEM((mine, lat, lon), BF16),
            pltpu.SemaphoreType.DMA((across,)),
        ],
        (counts, source_weights, inverse_rows, block_row, interp, near, far),
        8 * slots * slots * 1024,
        2 * slots * slots,
        "columns",
        HBM,
    )

    spectral = call(
        functools.partial(legendre_kernel, n_sec, n_band, n_fld, lev),
        [((wave_dev, 2, n_fld, n_sec * lev, degrees), BF16)],
        [VMEM, VMEM],
        [
            pltpu.VMEM((wave_dev, 2, n_fld, n_sec * lev, degrees), BF16),
            pltpu.SemaphoreType.DMA((wave_dev,)),
        ],
        (basis, pieces),
        4 * n_sec * n_fld * piece * n_band * LANES * degrees * THIRDS,
        2 * n_sec * n_band * n_fld * piece * LANES,
        "legendre",
        HBM,
    )
    return (spectral, heating)


def solution(mesh):
    return jax.shard_map(
        body,
        mesh=mesh,
        in_specs=(
            P("fld", "sec", "band", None),
            P(("band", "fld"), None, "sec"),
            P(),
            P("band"),
            P("band", None),
            P(),
            P(),
        ),
        out_specs=(P(("band", "fld"), None, None, None, "sec"), P(("sec", "fld"), "band", None)),
        check_vma=False,
    )
```

```python
import functools
import math

import jax
import jax.numpy as jnp
import numpy as np
from jax import lax
from jax.experimental import pallas as pl
from jax.experimental.pallas import tpu as pltpu
from jax.sharding import PartitionSpec as P

BF16 = jnp.bfloat16
F32 = jnp.float32
LANES = 128
THIRDS = 3
VMEM = pl.BlockSpec(memory_space=pltpu.VMEM)
HBM = pl.BlockSpec(memory_space=pltpu.HBM)
SMEM = pl.BlockSpec(memory_space=pltpu.SMEM)
LIMIT = 40 * 1024 * 1024
SMALL = 4 * 1024 * 1024
ROOM = 1200 * 1024
WHOLE = 64 * 1024 * 1024 - ROOM
NT = (((1,), (1,)), ((), ()))


def dft_table(lon, wave_dev, n_band, n_fld):
    values_dev = 2 * wave_dev
    rest = values_dev // THIRDS
    third, fld, band, low = np.meshgrid(
        np.arange(THIRDS), np.arange(n_fld), np.arange(n_band), np.arange(rest), indexing="ij"
    )
    value = third * rest + low
    wave = ((band * n_fld + fld) * wave_dev + value // 2).reshape(-1)
    part = (value % 2).reshape(-1)
    phase = np.arange(lon, dtype=np.int64)[:, None] * wave[None, :] % lon
    angle = phase * (2.0 * math.pi / lon)
    values = np.where(part[None, :] == 0, np.cos(angle), -np.sin(angle)) / math.sqrt(lon)
    return values.astype(np.float32).astype(BF16)


def pack(lev, lat, coeffs, message, padded, rows):
    group = coeffs.shape[1] // THIRDS
    padded[...] = jnp.zeros_like(padded)
    for level in range(lev):
        for third in range(THIRDS):
            padded[third * lat : (third + 1) * lat, :group] = coeffs[
                level * lat : (level + 1) * lat, third * group : (third + 1) * group
            ]
        rows[pl.ds(level, group, stride=lev), :] = jnp.transpose(padded[...])[:group]
    targets, size = message.shape[0], message.shape[2]
    bands = rows.shape[0] // targets // size
    message[:, :bands] = rows[...].astype(BF16).reshape(targets, bands, size, LANES)


def prepare_kernel(lat, n_band, legendre, inverses, out, out_inverses, wide, rows, turned):
    flux_rows, _, spec_bands = inverses.shape
    for row in range(flux_rows):
        rows[row * flux_rows : (row + 1) * flux_rows, :] = inverses[row].astype(F32)
    for row in range(flux_rows):
        turned[pl.ds(row, spec_bands, stride=flux_rows), :] = jnp.transpose(
            rows[pl.ds(row, flux_rows, stride=flux_rows), :]
        )
    out_inverses[...] = turned[...].astype(BF16)
    waves, degrees, _ = legendre.shape
    wide[...] = jnp.zeros_like(wide)
    lane = lax.broadcasted_iota(jnp.int32, (degrees, LANES), 1)
    for wave in range(waves):
        third, parity = wave // 2, wave % 2
        wide[:, : n_band * lat] = legendre[wave].astype(F32)
        place = third * lat
        live = (lane >= place) & (lane < place + lat)
        for band in range(n_band):
            base = band * lat // LANES * LANES
            moved = pltpu.roll(
                wide[:, base : base + 2 * LANES], (place - (band * lat - base)) % (2 * LANES), 1
            )
            out[band, parity, third * degrees : (third + 1) * degrees, :] = jnp.where(
                live, moved[:, :LANES], 0.0
            ).astype(BF16)


def legendre_kernel(n_sec, n_band, n_fld, lev, weights, pieces, out_hbm, out, sems):
    degrees = out.shape[4]
    copies = []
    half = pieces.shape[2] // 2
    for parity in range(2):
        rows = slice(parity * half, (parity + 1) * half)
        basis = jnp.concatenate([weights[band, parity] for band in range(n_band)], axis=1)
        left = jnp.concatenate(
            [
                jnp.concatenate(
                    [
                        pieces[sec * n_band + band, fld, rows, :]
                        for band in range(n_band)
                    ],
                    axis=1,
                )
                for fld in range(n_fld)
                for sec in range(n_sec)
            ],
            axis=0,
        )
        result = lax.dot_general(left, basis, NT, preferred_element_type=F32)
        for third in range(THIRDS):
            part = result[:, third * degrees : (third + 1) * degrees]
            for fld in range(n_fld):
                for real in range(2):
                    levels = [
                        part[(fld * n_sec + sec) * half + real * lev :][:lev]
                        for sec in range(n_sec)
                    ]
                    out[2 * third + parity, real, fld] = jnp.concatenate(levels, axis=0).astype(
                        BF16
                    )
            wave = 2 * third + parity
            copies.append(
                pltpu.make_async_copy(out.at[wave], out_hbm.at[wave], sems.at[wave])
            )
            copies[-1].start()
    for copy in copies:
        copy.wait()


def slot_rows(blocks, across, lat_pad):
    shift = 16
    factor = -(-(1 << shift) // across)
    lat = lax.shift_right_logical(blocks * factor, shift)
    return (blocks - lat * across) * lat_pad + lat


def local_kernel(lat_pad, grid_hbm, blocks_hbm, interp_hbm, table_hbm, *refs):
    (grid, blocks, interp, table, patch, column, selector, message, padded, rows, totals, sems,
     send_fourier, send_state) = refs[-14:]
    *outs, out, out_state = refs[:-14]
    targets = message.shape[0]
    lev, lat, lon = grid.shape
    across = lon // LANES
    slots = interp.shape[0]
    depth = patch.shape[0]
    small = [
        pltpu.make_async_copy(blocks_hbm, blocks, sems.at[lev]),
        pltpu.make_async_copy(interp_hbm, interp, sems.at[lev + 1]),
        pltpu.make_async_copy(table_hbm, table, sems.at[lev + 2]),
    ]
    loads = [
        pltpu.make_async_copy(
            grid_hbm.at[pl.ds(level, 1)], grid.at[pl.ds(level, 1)], sems.at[level]
        )
        for level in range(lev)
    ]
    half = lev // 2
    small[0].start()
    for copy in loads[:half]:
        copy.start()
    small[1].start()
    for copy in loads[half:]:
        copy.start()
    small[2].start()
    small[0].wait()
    row = slot_rows(blocks[...], across, lat_pad)
    column[...] = jnp.transpose(jnp.broadcast_to(row, (LANES, slots)))
    chunk = 256
    lane = lax.broadcasted_iota(jnp.int32, (chunk, LANES), 1)
    for start in range(0, slots, chunk):
        mine = column[start : start + chunk, :]
        for base in range(0, depth, LANES):
            selector[start : start + chunk, base : base + LANES] = jnp.where(
                mine == lane + base, 1.0, 0.0
            ).astype(BF16)
    state_blocks = slots * lev // LANES // message.shape[2]
    bands = message.shape[1] - state_blocks
    place = lax.axis_index("fld")
    mine = message.at[place]
    pairs = [
        (message.at[place ^ (i + 1)].at[pl.ds(0, bands)], other.at[pl.ds(0, bands)])
        for i, other in enumerate(outs)
    ]
    for first in range(0, out.shape[0], bands):
        pairs.append((mine.at[pl.ds(0, bands)], out.at[pl.ds(first, bands), place]))
    fourier_copies = [
        pltpu.make_async_copy(*pair, send_fourier.at[i]) for i, pair in enumerate(pairs)
    ]
    behind = pl.ds(bands, state_blocks)
    pairs = [
        (message.at[place ^ (i + 1)].at[behind], other.at[behind]) for i, other in enumerate(outs)
    ]
    pairs.append((mine.at[behind], out_state.at[place]))
    state_copies = [pltpu.make_async_copy(*pair, send_state.at[i]) for i, pair in enumerate(pairs)]
    for tile in range(across):
        patch[tile * lat_pad + lat : (tile + 1) * lat_pad, :] = jnp.zeros(
            (lat_pad - lat, lev * LANES), BF16
        )
    if depth > across * lat_pad:
        patch[across * lat_pad :, :] = jnp.zeros((depth - across * lat_pad, lev * LANES), BF16)
    for base in (0, half):
        for level in range(base, base + half):
            loads[level].wait()
            for tile in range(across):
                patch[
                    tile * lat_pad : tile * lat_pad + lat, level * LANES : (level + 1) * LANES
                ] = grid[level, :, tile * LANES : (tile + 1) * LANES]
        if base == 0:
            small[1].wait()
        else:
            small[2].wait()
            flat = jnp.concatenate([grid[level] for level in range(lev)], axis=0)
            coeffs = jnp.dot(flat, table[...], preferred_element_type=F32)
            pack(lev, lat, coeffs, message, padded, rows)
            for copy in fourier_copies:
                copy.start()
        for start in range(0, slots, chunk):
            top = slice(start, start + chunk)
            picked = jnp.dot(
                selector[top, :],
                patch[:, base * LANES : (base + half) * LANES],
                preferred_element_type=F32,
            )
            weights = interp[top, :].astype(F32)
            total = jnp.zeros((chunk, LANES), F32) if base == 0 else totals[top, :]
            for i in range(half):
                product = picked[:, i * LANES : (i + 1) * LANES] * weights
                total = jnp.where(
                    lane == base + i, jnp.sum(product, axis=1, keepdims=True), total
                )
            if base == 0:
                totals[top, :] = total
                continue
            state = jnp.transpose(total)[:lev].astype(BF16)
            for tile in range(chunk // LANES):
                block, row = divmod((start // LANES + tile) * lev, message.shape[2])
                for target in range(targets):
                    message[target, bands + block, row : row + lev, :] = state[
                        :, tile * LANES : (tile + 1) * LANES
                    ]
    for copy in state_copies:
        copy.start()
    for copy in fourier_copies + state_copies:
        copy.wait()


def regroup_kernel(n_sec, n_band, *refs):
    pieces, (_, _, _, out, out_state, sems) = refs[:-6], refs[-6:]
    blocks = out_state.shape[1]
    place = lax.axis_index("fld")
    copies = []
    for i, piece in enumerate(pieces):
        fld = place ^ (len(pieces) - i)
        copies.append((piece.at[pl.ds(n_band, blocks)], out_state.at[fld]))
        for sec in range(n_sec):
            copies.append(
                (piece.at[pl.ds(0, n_band)], out.at[pl.ds(sec * n_band, n_band), fld])
            )
    copies = [pltpu.make_async_copy(*pair, sems.at[i]) for i, pair in enumerate(copies)]
    for copy in copies:
        copy.start()
    for copy in copies:
        copy.wait()


def softplus(x):
    power = jnp.exp(jnp.minimum(x, 80.0))
    return jnp.where(x < -8.0, power, jnp.maximum(x, jnp.log(1.0 + power)))


def column_kernel(n_sec, n_fld, lat_pad, slots, counts, weights, inverses, blocks, interp,
                  near, far, out, state, spread, result, sems):
    lev = near.shape[1] * near.shape[2] * LANES // slots
    place = lax.axis_index("sec")
    for fld in range(n_fld):
        for shift, pieces in enumerate((near, far)):
            row = (fld * n_sec + (place ^ shift)) * lev
            for tile in range(slots // LANES):
                state[
                    pl.ds(pl.multiple_of(row, lev), lev), tile * LANES : (tile + 1) * LANES
                ] = pieces[fld, tile * lev // near.shape[2]][
                    tile * lev % near.shape[2] : tile * lev % near.shape[2] + lev
                ].astype(F32)
    mine, lat, lon = result.shape
    across = lon // LANES
    sources, flux_rows = inverses.shape
    levels = flux_rows // 2
    count = counts[lax.axis_index("band")]
    base = (place * n_fld + lax.axis_index("fld")) * mine
    chunk = 256
    lane = lax.broadcasted_iota(jnp.int32, (1, flux_rows), 1)
    slot = lax.broadcasted_iota(jnp.int32, (chunk, 1), 0)
    column = jnp.transpose(state[...]).astype(BF16)
    tiles = [(top, at) for top in range(0, slots, chunk) for at in range(0, sources, chunk)]

    def gates_of(top, at):
        return jnp.dot(
            column[top : top + chunk], weights[:, at : at + chunk], preferred_element_type=F32
        )

    fluxes = {top: jnp.zeros((chunk, flux_rows), F32) for top in range(0, slots, chunk)}

    def add_flux(top, at, source):
        fluxes[top] = fluxes[top] + jnp.dot(
            source, inverses[at : at + chunk, :], preferred_element_type=F32
        )

    gates = gates_of(*tiles[0])
    before = None
    for i, tile in enumerate(tiles):
        later = gates_of(*tiles[i + 1]) if i + 1 < len(tiles) else None
        source = softplus(gates).astype(BF16)
        if before is not None:
            add_flux(*tiles[i - 1], before)
        gates, before = later, source
    add_flux(*tiles[-1], before)
    for start in range(0, slots, chunk):
        rows = fluxes[start]
        for level in range(mine):
            at = base + level
            plus = (lane == at) | ((lane == at + levels + 1) & (at + 1 < levels))
            minus = (lane == at + levels) | ((lane == at + 1) & (at + 1 < levels))
            terms = jnp.where(plus, rows, 0.0) - jnp.where(minus, rows, 0.0)
            heat = jnp.sum(terms, axis=1, keepdims=True)
            heat = jnp.where(slot + start < count, heat, 0.0).astype(BF16).astype(F32)
            spread[start : start + chunk, level * LANES : (level + 1) * LANES] = (
                heat * interp[start : start + chunk, :].astype(F32)
            ).astype(BF16)
    row = slot_rows(blocks[...], across, lat_pad)
    tiles = max(t for t in range(1, 8) if across % t == 0)
    height = tiles * lat_pad
    copies = []
    for first in range(0, across, tiles):
        match = row == lax.broadcasted_iota(jnp.int32, (height, slots), 0) + first * lat_pad
        left = jnp.where(match, 1.0, 0.0).astype(BF16)
        summed = jnp.dot(left, spread[...], preferred_element_type=F32).astype(BF16)
        for level in range(mine):
            for tile in range(tiles):
                result[level, :, (first + tile) * LANES : (first + tile + 1) * LANES] = summed[
                    tile * lat_pad : tile * lat_pad + lat, level * LANES : (level + 1) * LANES
                ]
        columns = pl.ds(first * LANES, tiles * LANES)
        copies.append(
            pltpu.make_async_copy(
                result.at[:, :, columns], out.at[:, :, columns], sems.at[first // tiles]
            )
        )
        copies[-1].start()
    for copy in copies:
        copy.wait()


def call(kernel, outs, specs, scratch, args, flops, size, name, out_spec=VMEM, limit=LIMIT,
         aliases={}):
    shapes = [jax.ShapeDtypeStruct(shape, dtype) for shape, dtype in outs]
    single = len(outs) == 1
    return pl.pallas_call(
        kernel,
        out_shape=shapes[0] if single else shapes,
        in_specs=specs,
        out_specs=out_spec if single else [out_spec] * len(outs),
        scratch_shapes=scratch,
        compiler_params=pltpu.CompilerParams(vmem_limit_bytes=limit),
        cost_estimate=pl.CostEstimate(flops=flops, bytes_accessed=size, transcendentals=0),
        name=name,
        input_output_aliases=aliases,
    )(*args)


def exchange(value, axis, shift):
    return lax.ppermute(value, axis, [(i, i ^ shift) for i in range(lax.axis_size(axis))])


def body(grid, legendre, counts, blocks, interp, source_weights, inverses):
    n_sec = lax.axis_size("sec")
    n_band = lax.axis_size("band")
    n_fld = lax.axis_size("fld")
    lev, lat, lon = grid.shape[1:]
    wave_dev, _, degrees = legendre.shape
    slots = blocks.shape[0]
    across = lon // LANES
    lat_pad = -(-lat // 16) * 16
    rest = 2 * wave_dev // THIRDS
    piece = rest * lev
    block_row = blocks.reshape(1, slots)

    table = jnp.asarray(dft_table(lon, wave_dev, n_band, n_fld))
    group = n_fld * n_band * rest
    padded_group = -(-group // LANES) * LANES
    depth = -(-across * lat_pad // LANES) * LANES
    state_blocks = slots * lev // LANES // piece
    message_blocks = n_band + state_blocks
    *messages, sent, near = call(
        functools.partial(local_kernel, lat_pad),
        [((message_blocks, piece, LANES), BF16)] * (n_fld - 1)
        + [
            ((n_sec * n_band, n_fld, piece, LANES), BF16),
            ((n_fld, state_blocks, piece, LANES), BF16),
        ],
        [HBM] * 4,
        [
            pltpu.VMEM((lev, lat, lon), BF16),
            pltpu.VMEM((1, slots), jnp.int32),
            pltpu.VMEM((slots, LANES), BF16),
            pltpu.VMEM(table.shape, BF16),
            pltpu.VMEM((depth, lev * LANES), BF16),
            pltpu.VMEM((slots, LANES), jnp.int32),
            pltpu.VMEM((slots, depth), BF16),
            pltpu.VMEM((n_fld, message_blocks, piece, LANES), BF16),
            pltpu.VMEM((LANES, padded_group), F32),
            pltpu.VMEM((group * lev, LANES), F32),
            pltpu.VMEM((slots, LANES), F32),
            pltpu.SemaphoreType.DMA((lev + 3,)),
            pltpu.SemaphoreType.DMA((n_fld - 1 + n_sec,)),
            pltpu.SemaphoreType.DMA((n_fld,)),
        ],
        (grid.reshape(lev, lat, lon), block_row, interp, table),
        2 * slots * depth * lev * LANES + 2 * lev * lat * lon * THIRDS * group,
        2 * lev * lat * lon + 2 * slots * LANES,
        "local",
        HBM,
        WHOLE,
    )
    arrived = [exchange(messages[shift - 1], "fld", shift) for shift in reversed(range(1, n_fld))]
    spec_bands, flux_rows, _ = inverses.shape
    basis, inverse_rows = call(
        functools.partial(prepare_kernel, lat, n_band),
        [
            ((n_band, 2, THIRDS * degrees, LANES), BF16),
            ((spec_bands * flux_rows, flux_rows), BF16),
        ],
        [VMEM, VMEM],
        [
            pltpu.VMEM((degrees, (n_band * lat // LANES + 2) * LANES), F32),
            pltpu.VMEM((flux_rows * flux_rows, spec_bands), F32),
            pltpu.VMEM((spec_bands * flux_rows, flux_rows), F32),
        ],
        (jnp.swapaxes(legendre, 1, 2), jnp.transpose(inverses, (1, 2, 0))),
        0,
        8 * wave_dev * degrees * n_band * LANES,
        "prepare",
    )
    sent, near = call(
        functools.partial(regroup_kernel, n_sec, n_band),
        [
            ((n_sec * n_band, n_fld, piece, LANES), BF16),
            ((n_fld, state_blocks, piece, LANES), BF16),
        ],
        [HBM] * (n_fld + 2),
        [pltpu.SemaphoreType.DMA(((n_fld - 1) * (1 + n_sec),))],
        (*arrived, basis, sent, near),
        0,
        4 * n_sec * n_band * n_fld * piece * LANES,
        "regroup",
        HBM,
        SMALL,
        {n_fld: 0, n_fld + 1: 1},
    )
    far = exchange(near, "sec", 1)
    pieces = lax.all_to_all(sent, ("sec", "band"), 0, 0, tiled=True)
    sources = spec_bands * flux_rows
    states = source_weights.shape[0]
    mine = n_sec * lev // (n_sec * n_fld)
    heating = call(
        functools.partial(column_kernel, n_sec, n_fld, lat_pad, slots),
        [((mine, lat, lon), BF16)],
        [SMEM] + [VMEM] * 6,
        [
            pltpu.VMEM((states, slots), F32),
            pltpu.VMEM((slots, mine * LANES), BF16),
            pltpu.VMEM((mine, lat, lon), BF16),
            pltpu.SemaphoreType.DMA((across,)),
        ],
        (counts, source_weights, inverse_rows, block_row, interp, near, far),
        8 * slots * slots * 1024,
        2 * slots * slots,
        "columns",
        HBM,
    )

    spectral = call(
        functools.partial(legendre_kernel, n_sec, n_band, n_fld, lev),
        [((wave_dev, 2, n_fld, n_sec * lev, degrees), BF16)],
        [VMEM, VMEM],
        [
            pltpu.VMEM((wave_dev, 2, n_fld, n_sec * lev, degrees), BF16),
            pltpu.SemaphoreType.DMA((wave_dev,)),
        ],
        (basis, pieces),
        4 * n_sec * n_fld * piece * n_band * LANES * degrees * THIRDS,
        2 * n_sec * n_band * n_fld * piece * LANES,
        "legendre",
        HBM,
    )
    return (spectral, heating)


def solution(mesh):
    return jax.shard_map(
        body,
        mesh=mesh,
        in_specs=(
            P("fld", "sec", "band", None),
            P(("band", "fld"), None, "sec"),
            P(),
            P("band"),
            P("band", None),
            P(),
            P(),
        ),
        out_specs=(P(("band", "fld"), None, None, None, "sec"), P(("sec", "fld"), "band", None)),
        check_vma=False,
    )
```

```python
import functools
import math

import jax
import jax.numpy as jnp
import numpy as np
from jax import lax
from jax.experimental import pallas as pl
from jax.experimental.pallas import tpu as pltpu
from jax.sharding import PartitionSpec as P

BF16 = jnp.bfloat16
F32 = jnp.float32
LANES = 128
THIRDS = 3
VMEM = pl.BlockSpec(memory_space=pltpu.VMEM)
HBM = pl.BlockSpec(memory_space=pltpu.HBM)
SMEM = pl.BlockSpec(memory_space=pltpu.SMEM)
LIMIT = 40 * 1024 * 1024
SMALL = 4 * 1024 * 1024
ROOM = 1200 * 1024
WHOLE = 64 * 1024 * 1024 - ROOM
NT = (((1,), (1,)), ((), ()))


def dft_table(lon, wave_dev, n_band, n_fld):
    values_dev = 2 * wave_dev
    rest = values_dev // THIRDS
    third, fld, band, low = np.meshgrid(
        np.arange(THIRDS), np.arange(n_fld), np.arange(n_band), np.arange(rest), indexing="ij"
    )
    value = third * rest + low
    wave = ((band * n_fld + fld) * wave_dev + value // 2).reshape(-1)
    part = (value % 2).reshape(-1)
    phase = np.arange(lon, dtype=np.int64)[:, None] * wave[None, :] % lon
    angle = phase * (2.0 * math.pi / lon)
    values = np.where(part[None, :] == 0, np.cos(angle), -np.sin(angle)) / math.sqrt(lon)
    return values.astype(np.float32).astype(BF16)


def pack(lev, lat, coeffs, message, padded, rows):
    group = coeffs.shape[1] // THIRDS
    padded[...] = jnp.zeros_like(padded)
    for level in range(lev):
        for third in range(THIRDS):
            padded[third * lat : (third + 1) * lat, :group] = coeffs[
                level * lat : (level + 1) * lat, third * group : (third + 1) * group
            ]
        rows[pl.ds(level, group, stride=lev), :] = jnp.transpose(padded[...])[:group]
    targets, size = message.shape[0], message.shape[2]
    bands = rows.shape[0] // targets // size
    message[:, :bands] = rows[...].astype(BF16).reshape(targets, bands, size, LANES)


def prepare_kernel(lat, n_band, legendre, inverses, _, out, out_inverses, wide, rows, turned):
    flux_rows, _, spec_bands = inverses.shape
    for row in range(flux_rows):
        rows[row * flux_rows : (row + 1) * flux_rows, :] = inverses[row].astype(F32)
    for row in range(flux_rows):
        turned[pl.ds(row, spec_bands, stride=flux_rows), :] = jnp.transpose(
            rows[pl.ds(row, flux_rows, stride=flux_rows), :]
        )
    out_inverses[...] = turned[...].astype(BF16)
    waves, degrees, _ = legendre.shape
    wide[...] = jnp.zeros_like(wide)
    lane = lax.broadcasted_iota(jnp.int32, (degrees, LANES), 1)
    for wave in range(waves):
        third, parity = wave // 2, wave % 2
        wide[:, : n_band * lat] = legendre[wave].astype(F32)
        place = third * lat
        live = (lane >= place) & (lane < place + lat)
        for band in range(n_band):
            base = band * lat // LANES * LANES
            moved = pltpu.roll(
                wide[:, base : base + 2 * LANES], (place - (band * lat - base)) % (2 * LANES), 1
            )
            out[band, parity, third * degrees : (third + 1) * degrees, :] = jnp.where(
                live, moved[:, :LANES], 0.0
            ).astype(BF16)


def legendre_kernel(n_sec, n_band, n_fld, lev, weights, pieces, out_hbm, out, sems):
    degrees = out.shape[4]
    copies = []
    half = pieces.shape[2] // 2
    for parity in range(2):
        rows = slice(parity * half, (parity + 1) * half)
        basis = jnp.concatenate([weights[band, parity] for band in range(n_band)], axis=1)
        left = jnp.concatenate(
            [
                jnp.concatenate(
                    [
                        pieces[sec * n_band + band, fld, rows, :]
                        for band in range(n_band)
                    ],
                    axis=1,
                )
                for fld in range(n_fld)
                for sec in range(n_sec)
            ],
            axis=0,
        )
        result = lax.dot_general(left, basis, NT, preferred_element_type=F32)
        for third in range(THIRDS):
            part = result[:, third * degrees : (third + 1) * degrees]
            for fld in range(n_fld):
                for real in range(2):
                    levels = [
                        part[(fld * n_sec + sec) * half + real * lev :][:lev]
                        for sec in range(n_sec)
                    ]
                    out[2 * third + parity, real, fld] = jnp.concatenate(levels, axis=0).astype(
                        BF16
                    )
            wave = 2 * third + parity
            copies.append(
                pltpu.make_async_copy(out.at[wave], out_hbm.at[wave], sems.at[wave])
            )
            copies[-1].start()
    for copy in copies:
        copy.wait()


def slot_rows(blocks, across, lat_pad):
    shift = 16
    factor = -(-(1 << shift) // across)
    lat = lax.shift_right_logical(blocks * factor, shift)
    return (blocks - lat * across) * lat_pad + lat


def local_kernel(lat_pad, grid_hbm, blocks_hbm, interp_hbm, table_hbm, *refs):
    targets = len(refs) - 14
    outs = refs[:targets]
    (grid, blocks, interp, table, patch, column, selector, message, padded, rows, totals, sems,
     send_fourier, send_state) = refs[targets:]
    lev, lat, lon = grid.shape
    across = lon // LANES
    slots = interp.shape[0]
    depth = patch.shape[0]
    small = [
        pltpu.make_async_copy(blocks_hbm, blocks, sems.at[lev]),
        pltpu.make_async_copy(interp_hbm, interp, sems.at[lev + 1]),
        pltpu.make_async_copy(table_hbm, table, sems.at[lev + 2]),
    ]
    loads = [
        pltpu.make_async_copy(
            grid_hbm.at[pl.ds(level, 1)], grid.at[pl.ds(level, 1)], sems.at[level]
        )
        for level in range(lev)
    ]
    half = lev // 2
    small[0].start()
    for copy in loads[:half]:
        copy.start()
    small[1].start()
    for copy in loads[half:]:
        copy.start()
    small[2].start()
    small[0].wait()
    row = slot_rows(blocks[...], across, lat_pad)
    column[...] = jnp.transpose(jnp.broadcast_to(row, (LANES, slots)))
    chunk = 256
    lane = lax.broadcasted_iota(jnp.int32, (chunk, LANES), 1)
    for start in range(0, slots, chunk):
        mine = column[start : start + chunk, :]
        for base in range(0, depth, LANES):
            selector[start : start + chunk, base : base + LANES] = jnp.where(
                mine == lane + base, 1.0, 0.0
            ).astype(BF16)
    state_blocks = slots * lev // LANES // message.shape[2]
    bands = message.shape[1] - state_blocks
    place = lax.axis_index("fld")
    fourier_copies, state_copies = [], []
    for shift in reversed(range(targets)):
        mine = message.at[place ^ shift]
        fourier_copies.append(
            pltpu.make_async_copy(
                mine.at[pl.ds(0, bands)], outs[shift].at[pl.ds(0, bands)], send_fourier.at[shift]
            )
        )
        state_copies.append(
            pltpu.make_async_copy(
                mine.at[pl.ds(bands, state_blocks)],
                outs[shift].at[pl.ds(bands, state_blocks)],
                send_state.at[shift],
            )
        )
    for tile in range(across):
        patch[tile * lat_pad + lat : (tile + 1) * lat_pad, :] = jnp.zeros(
            (lat_pad - lat, lev * LANES), BF16
        )
    if depth > across * lat_pad:
        patch[across * lat_pad :, :] = jnp.zeros((depth - across * lat_pad, lev * LANES), BF16)
    for base in (0, half):
        for level in range(base, base + half):
            loads[level].wait()
            for tile in range(across):
                patch[
                    tile * lat_pad : tile * lat_pad + lat, level * LANES : (level + 1) * LANES
                ] = grid[level, :, tile * LANES : (tile + 1) * LANES]
        if base == 0:
            small[1].wait()
        else:
            small[2].wait()
            flat = jnp.concatenate([grid[level] for level in range(lev)], axis=0)
            coeffs = jnp.dot(flat, table[...], preferred_element_type=F32)
            pack(lev, lat, coeffs, message, padded, rows)
            for copy in fourier_copies:
                copy.start()
        for start in range(0, slots, chunk):
            top = slice(start, start + chunk)
            picked = jnp.dot(
                selector[top, :],
                patch[:, base * LANES : (base + half) * LANES],
                preferred_element_type=F32,
            )
            weights = interp[top, :].astype(F32)
            total = jnp.zeros((chunk, LANES), F32) if base == 0 else totals[top, :]
            for i in range(half):
                product = picked[:, i * LANES : (i + 1) * LANES] * weights
                total = jnp.where(
                    lane == base + i, jnp.sum(product, axis=1, keepdims=True), total
                )
            if base == 0:
                totals[top, :] = total
                continue
            state = jnp.transpose(total)[:lev].astype(BF16)
            for tile in range(chunk // LANES):
                block, row = divmod((start // LANES + tile) * lev, message.shape[2])
                for target in range(targets):
                    message[target, bands + block, row : row + lev, :] = state[
                        :, tile * LANES : (tile + 1) * LANES
                    ]
    for copy in state_copies:
        copy.start()
    for copy in fourier_copies + state_copies:
        copy.wait()


def regroup_kernel(n_sec, n_band, *refs):
    pieces, (_, out, out_state, sems) = refs[:-4], refs[-4:]
    blocks = out_state.shape[1]
    place = lax.axis_index("fld")
    copies = []
    for i, piece in enumerate(pieces):
        fld = place ^ (len(pieces) - 1 - i)
        copies.append((piece.at[pl.ds(n_band, blocks)], out_state.at[fld]))
        for sec in range(n_sec):
            copies.append(
                (piece.at[pl.ds(0, n_band)], out.at[pl.ds(sec * n_band, n_band), fld])
            )
    copies = [pltpu.make_async_copy(*pair, sems.at[i]) for i, pair in enumerate(copies)]
    for copy in copies:
        copy.start()
    for copy in copies:
        copy.wait()


def softplus(x):
    power = jnp.exp(jnp.minimum(x, 80.0))
    return jnp.where(x < -8.0, power, jnp.maximum(x, jnp.log(1.0 + power)))


def column_kernel(n_sec, n_fld, lat_pad, slots, counts, weights, inverses, blocks, interp,
                  near, far, out, state, spread, result, sems):
    lev = near.shape[1] * near.shape[2] * LANES // slots
    place = lax.axis_index("sec")
    for fld in range(n_fld):
        for shift, pieces in enumerate((near, far)):
            row = (fld * n_sec + (place ^ shift)) * lev
            for tile in range(slots // LANES):
                state[
                    pl.ds(pl.multiple_of(row, lev), lev), tile * LANES : (tile + 1) * LANES
                ] = pieces[fld, tile * lev // near.shape[2]][
                    tile * lev % near.shape[2] : tile * lev % near.shape[2] + lev
                ].astype(F32)
    mine, lat, lon = result.shape
    across = lon // LANES
    sources, flux_rows = inverses.shape
    levels = flux_rows // 2
    count = counts[lax.axis_index("band")]
    base = (place * n_fld + lax.axis_index("fld")) * mine
    chunk = 256
    lane = lax.broadcasted_iota(jnp.int32, (1, flux_rows), 1)
    slot = lax.broadcasted_iota(jnp.int32, (chunk, 1), 0)
    column = jnp.transpose(state[...]).astype(BF16)
    tiles = [(top, at) for top in range(0, slots, chunk) for at in range(0, sources, chunk)]

    def gates_of(top, at):
        return jnp.dot(
            column[top : top + chunk], weights[:, at : at + chunk], preferred_element_type=F32
        )

    fluxes = {top: jnp.zeros((chunk, flux_rows), F32) for top in range(0, slots, chunk)}

    def add_flux(top, at, source):
        fluxes[top] = fluxes[top] + jnp.dot(
            source, inverses[at : at + chunk, :], preferred_element_type=F32
        )

    gates = gates_of(*tiles[0])
    before = None
    for i, tile in enumerate(tiles):
        later = gates_of(*tiles[i + 1]) if i + 1 < len(tiles) else None
        source = softplus(gates).astype(BF16)
        if before is not None:
            add_flux(*tiles[i - 1], before)
        gates, before = later, source
    add_flux(*tiles[-1], before)
    for start in range(0, slots, chunk):
        rows = fluxes[start]
        for level in range(mine):
            at = base + level
            plus = (lane == at) | ((lane == at + levels + 1) & (at + 1 < levels))
            minus = (lane == at + levels) | ((lane == at + 1) & (at + 1 < levels))
            terms = jnp.where(plus, rows, 0.0) - jnp.where(minus, rows, 0.0)
            heat = jnp.sum(terms, axis=1, keepdims=True)
            heat = jnp.where(slot + start < count, heat, 0.0).astype(BF16).astype(F32)
            spread[start : start + chunk, level * LANES : (level + 1) * LANES] = (
                heat * interp[start : start + chunk, :].astype(F32)
            ).astype(BF16)
    row = slot_rows(blocks[...], across, lat_pad)
    tiles = max(t for t in range(1, 8) if across % t == 0)
    height = tiles * lat_pad
    copies = []
    for first in range(0, across, tiles):
        match = row == lax.broadcasted_iota(jnp.int32, (height, slots), 0) + first * lat_pad
        left = jnp.where(match, 1.0, 0.0).astype(BF16)
        summed = jnp.dot(left, spread[...], preferred_element_type=F32).astype(BF16)
        for level in range(mine):
            for tile in range(tiles):
                result[level, :, (first + tile) * LANES : (first + tile + 1) * LANES] = summed[
                    tile * lat_pad : tile * lat_pad + lat, level * LANES : (level + 1) * LANES
                ]
        columns = pl.ds(first * LANES, tiles * LANES)
        copies.append(
            pltpu.make_async_copy(
                result.at[:, :, columns], out.at[:, :, columns], sems.at[first // tiles]
            )
        )
        copies[-1].start()
    for copy in copies:
        copy.wait()


def call(kernel, outs, specs, scratch, args, flops, size, name, out_spec=VMEM, limit=LIMIT):
    shapes = [jax.ShapeDtypeStruct(shape, dtype) for shape, dtype in outs]
    single = len(outs) == 1
    return pl.pallas_call(
        kernel,
        out_shape=shapes[0] if single else shapes,
        in_specs=specs,
        out_specs=out_spec if single else [out_spec] * len(outs),
        scratch_shapes=scratch,
        compiler_params=pltpu.CompilerParams(vmem_limit_bytes=limit),
        cost_estimate=pl.CostEstimate(flops=flops, bytes_accessed=size, transcendentals=0),
        name=name,
    )(*args)


def exchange(value, axis, shift):
    return lax.ppermute(value, axis, [(i, i ^ shift) for i in range(lax.axis_size(axis))])


def body(grid, legendre, counts, blocks, interp, source_weights, inverses):
    n_sec = lax.axis_size("sec")
    n_band = lax.axis_size("band")
    n_fld = lax.axis_size("fld")
    lev, lat, lon = grid.shape[1:]
    wave_dev, _, degrees = legendre.shape
    slots = blocks.shape[0]
    across = lon // LANES
    lat_pad = -(-lat // 16) * 16
    rest = 2 * wave_dev // THIRDS
    piece = rest * lev
    block_row = blocks.reshape(1, slots)

    table = jnp.asarray(dft_table(lon, wave_dev, n_band, n_fld))
    group = n_fld * n_band * rest
    padded_group = -(-group // LANES) * LANES
    depth = -(-across * lat_pad // LANES) * LANES
    state_blocks = slots * lev // LANES // piece
    message_blocks = n_band + state_blocks
    messages = call(
        functools.partial(local_kernel, lat_pad),
        [((message_blocks, piece, LANES), BF16)] * n_fld,
        [HBM] * 4,
        [
            pltpu.VMEM((lev, lat, lon), BF16),
            pltpu.VMEM((1, slots), jnp.int32),
            pltpu.VMEM((slots, LANES), BF16),
            pltpu.VMEM(table.shape, BF16),
            pltpu.VMEM((depth, lev * LANES), BF16),
            pltpu.VMEM((slots, LANES), jnp.int32),
            pltpu.VMEM((slots, depth), BF16),
            pltpu.VMEM((n_fld, message_blocks, piece, LANES), BF16),
            pltpu.VMEM((LANES, padded_group), F32),
            pltpu.VMEM((group * lev, LANES), F32),
            pltpu.VMEM((slots, LANES), F32),
            pltpu.SemaphoreType.DMA((lev + 3,)),
            pltpu.SemaphoreType.DMA((n_fld,)),
            pltpu.SemaphoreType.DMA((n_fld,)),
        ],
        (grid.reshape(lev, lat, lon), block_row, interp, table),
        2 * slots * depth * lev * LANES + 2 * lev * lat * lon * THIRDS * group,
        2 * lev * lat * lon + 2 * slots * LANES,
        "local",
        HBM,
        WHOLE,
    )
    arrived = [exchange(messages[shift], "fld", shift) for shift in reversed(range(1, n_fld))]
    arrived.append(messages[0])
    spec_bands, flux_rows, _ = inverses.shape
    basis, inverse_rows = call(
        functools.partial(prepare_kernel, lat, n_band),
        [
            ((n_band, 2, THIRDS * degrees, LANES), BF16),
            ((spec_bands * flux_rows, flux_rows), BF16),
        ],
        [VMEM, VMEM, VMEM],
        [
            pltpu.VMEM((degrees, (n_band * lat // LANES + 2) * LANES), F32),
            pltpu.VMEM((flux_rows * flux_rows, spec_bands), F32),
            pltpu.VMEM((spec_bands * flux_rows, flux_rows), F32),
        ],
        (jnp.swapaxes(legendre, 1, 2), jnp.transpose(inverses, (1, 2, 0)), messages[0]),
        0,
        8 * wave_dev * degrees * n_band * LANES,
        "prepare",
    )
    sent, near = call(
        functools.partial(regroup_kernel, n_sec, n_band),
        [
            ((n_sec * n_band, n_fld, piece, LANES), BF16),
            ((n_fld, state_blocks, piece, LANES), BF16),
        ],
        [HBM] * (n_fld + 1),
        [pltpu.SemaphoreType.DMA((n_fld * (1 + n_sec),))],
        (*arrived, basis),
        0,
        4 * n_sec * n_band * n_fld * piece * LANES,
        "regroup",
        HBM,
        SMALL,
    )
    far = exchange(near, "sec", 1)
    pieces = lax.all_to_all(sent, ("sec", "band"), 0, 0, tiled=True)
    sources = spec_bands * flux_rows
    states = source_weights.shape[0]
    mine = n_sec * lev // (n_sec * n_fld)
    heating = call(
        functools.partial(column_kernel, n_sec, n_fld, lat_pad, slots),
        [((mine, lat, lon), BF16)],
        [SMEM] + [VMEM] * 6,
        [
            pltpu.VMEM((states, slots), F32),
            pltpu.VMEM((slots, mine * LANES), BF16),
            pltpu.VMEM((mine, lat, lon), BF16),
            pltpu.SemaphoreType.DMA((across,)),
        ],
        (counts, source_weights, inverse_rows, block_row, interp, near, far),
        8 * slots * slots * 1024,
        2 * slots * slots,
        "columns",
        HBM,
    )

    spectral = call(
        functools.partial(legendre_kernel, n_sec, n_band, n_fld, lev),
        [((wave_dev, 2, n_fld, n_sec * lev, degrees), BF16)],
        [VMEM, VMEM],
        [
            pltpu.VMEM((wave_dev, 2, n_fld, n_sec * lev, degrees), BF16),
            pltpu.SemaphoreType.DMA((wave_dev,)),
        ],
        (basis, pieces),
        4 * n_sec * n_fld * piece * n_band * LANES * degrees * THIRDS,
        2 * n_sec * n_band * n_fld * piece * LANES,
        "legendre",
        HBM,
    )
    return (spectral, heating)


def solution(mesh):
    return jax.shard_map(
        body,
        mesh=mesh,
        in_specs=(
            P("fld", "sec", "band", None),
            P(("band", "fld"), None, "sec"),
            P(),
            P("band"),
            P("band", None),
            P(),
            P(),
        ),
        out_specs=(P(("band", "fld"), None, None, None, "sec"), P(("sec", "fld"), "band", None)),
        check_vma=False,
    )
```

```python
import functools
import math

import jax
import jax.numpy as jnp
import numpy as np
from jax import lax
from jax.experimental import pallas as pl
from jax.experimental.pallas import tpu as pltpu
from jax.sharding import PartitionSpec as P

BF16 = jnp.bfloat16
F32 = jnp.float32
LANES = 128
THIRDS = 3
VMEM = pl.BlockSpec(memory_space=pltpu.VMEM)
HBM = pl.BlockSpec(memory_space=pltpu.HBM)
SMEM = pl.BlockSpec(memory_space=pltpu.SMEM)
LIMIT = 40 * 1024 * 1024
SMALL = 4 * 1024 * 1024
ROOM = 12000 * 1024
WHOLE = 64 * 1024 * 1024 - ROOM
NT = (((1,), (1,)), ((), ()))


def dft_table(lon, wave_dev, n_band, n_fld):
    values_dev = 2 * wave_dev
    rest = values_dev // THIRDS
    third, fld, band, low = np.meshgrid(
        np.arange(THIRDS), np.arange(n_fld), np.arange(n_band), np.arange(rest), indexing="ij"
    )
    value = third * rest + low
    wave = ((band * n_fld + fld) * wave_dev + value // 2).reshape(-1)
    part = (value % 2).reshape(-1)
    phase = np.arange(lon, dtype=np.int64)[:, None] * wave[None, :] % lon
    angle = phase * (2.0 * math.pi / lon)
    values = np.where(part[None, :] == 0, np.cos(angle), -np.sin(angle)) / math.sqrt(lon)
    return values.astype(np.float32).astype(BF16)


def pack(lev, lat, coeffs, padded, rows):
    group = coeffs.shape[1] // THIRDS
    padded[...] = jnp.zeros_like(padded)
    for level in range(lev):
        for third in range(THIRDS):
            padded[third * lat : (third + 1) * lat, :group] = coeffs[
                level * lat : (level + 1) * lat, third * group : (third + 1) * group
            ]
        rows[pl.ds(level, group, stride=lev), :] = jnp.transpose(padded[...])[:group]


def prepare_kernel(lat, n_band, legendre, inverses, out, out_inverses, wide, rows, turned):
    flux_rows, _, spec_bands = inverses.shape
    for row in range(flux_rows):
        rows[row * flux_rows : (row + 1) * flux_rows, :] = inverses[row].astype(F32)
    for row in range(flux_rows):
        turned[pl.ds(row, spec_bands, stride=flux_rows), :] = jnp.transpose(
            rows[pl.ds(row, flux_rows, stride=flux_rows), :]
        )
    out_inverses[...] = turned[...].astype(BF16)
    waves, degrees, _ = legendre.shape
    wide[...] = jnp.zeros_like(wide)
    lane = lax.broadcasted_iota(jnp.int32, (degrees, LANES), 1)
    for wave in range(waves):
        third, parity = wave // 2, wave % 2
        wide[:, : n_band * lat] = legendre[wave].astype(F32)
        place = third * lat
        live = (lane >= place) & (lane < place + lat)
        for band in range(n_band):
            base = band * lat // LANES * LANES
            moved = pltpu.roll(
                wide[:, base : base + 2 * LANES], (place - (band * lat - base)) % (2 * LANES), 1
            )
            out[band, parity, third * degrees : (third + 1) * degrees, :] = jnp.where(
                live, moved[:, :LANES], 0.0
            ).astype(BF16)


def legendre_kernel(n_sec, n_band, n_fld, lev, weights, pieces, out_hbm, out, sems):
    degrees = out.shape[4]
    copies = []
    half = pieces.shape[2] // 2
    for parity in range(2):
        rows = slice(parity * half, (parity + 1) * half)
        basis = jnp.concatenate([weights[band, parity] for band in range(n_band)], axis=1)
        left = jnp.concatenate(
            [
                jnp.concatenate(
                    [
                        pieces[sec * n_band + band, fld, rows, :]
                        for band in range(n_band)
                    ],
                    axis=1,
                )
                for fld in range(n_fld)
                for sec in range(n_sec)
            ],
            axis=0,
        )
        result = lax.dot_general(left, basis, NT, preferred_element_type=F32)
        for third in range(THIRDS):
            part = result[:, third * degrees : (third + 1) * degrees]
            for fld in range(n_fld):
                for real in range(2):
                    levels = [
                        part[(fld * n_sec + sec) * half + real * lev :][:lev]
                        for sec in range(n_sec)
                    ]
                    out[2 * third + parity, real, fld] = jnp.concatenate(levels, axis=0).astype(
                        BF16
                    )
            wave = 2 * third + parity
            copies.append(
                pltpu.make_async_copy(out.at[wave], out_hbm.at[wave], sems.at[wave])
            )
            copies[-1].start()
    for copy in copies:
        copy.wait()


def slot_rows(blocks, across, lat_pad):
    shift = 16
    factor = -(-(1 << shift) // across)
    lat = lax.shift_right_logical(blocks * factor, shift)
    return (blocks - lat * across) * lat_pad + lat


def local_kernel(lat_pad, grid_hbm, blocks_hbm, interp_hbm, table_hbm, *refs):
    outs = refs[:-11]
    grid, blocks, interp, table, patch, column, selector, padded, rows, totals, sems = refs[-11:]
    lev, lat, lon = grid.shape
    across = lon // LANES
    slots = interp.shape[0]
    depth = patch.shape[0]
    small = [
        pltpu.make_async_copy(blocks_hbm, blocks, sems.at[lev]),
        pltpu.make_async_copy(interp_hbm, interp, sems.at[lev + 1]),
        pltpu.make_async_copy(table_hbm, table, sems.at[lev + 2]),
    ]
    loads = [
        pltpu.make_async_copy(
            grid_hbm.at[pl.ds(level, 1)], grid.at[pl.ds(level, 1)], sems.at[level]
        )
        for level in range(lev)
    ]
    half = lev // 2
    small[0].start()
    for copy in loads[:half]:
        copy.start()
    small[1].start()
    for copy in loads[half:]:
        copy.start()
    small[2].start()
    small[0].wait()
    row = slot_rows(blocks[...], across, lat_pad)
    column[...] = jnp.transpose(jnp.broadcast_to(row, (LANES, slots)))
    chunk = 256
    lane = lax.broadcasted_iota(jnp.int32, (chunk, LANES), 1)
    for start in range(0, slots, chunk):
        mine = column[start : start + chunk, :]
        for base in range(0, depth, LANES):
            selector[start : start + chunk, base : base + LANES] = jnp.where(
                mine == lane + base, 1.0, 0.0
            ).astype(BF16)
    size = outs[0].shape[1]
    bands = outs[0].shape[0] - slots * lev // LANES // size
    place = lax.axis_index("fld")
    for tile in range(across):
        patch[tile * lat_pad + lat : (tile + 1) * lat_pad, :] = jnp.zeros(
            (lat_pad - lat, lev * LANES), BF16
        )
    if depth > across * lat_pad:
        patch[across * lat_pad :, :] = jnp.zeros((depth - across * lat_pad, lev * LANES), BF16)
    for base in (0, half):
        for level in range(base, base + half):
            loads[level].wait()
            for tile in range(across):
                patch[
                    tile * lat_pad : tile * lat_pad + lat, level * LANES : (level + 1) * LANES
                ] = grid[level, :, tile * LANES : (tile + 1) * LANES]
        if base == 0:
            small[1].wait()
        else:
            small[2].wait()
            flat = jnp.concatenate([grid[level] for level in range(lev)], axis=0)
            coeffs = jnp.dot(flat, table[...], preferred_element_type=F32)
            pack(lev, lat, coeffs, padded, rows)
            height = bands * size
            for shift, out in enumerate(outs):
                first = pl.multiple_of((place ^ shift) * height, height)
                part = rows[pl.ds(first, height), :].astype(BF16)
                out[:bands] = part.reshape(bands, size, LANES)
        for start in range(0, slots, chunk):
            top = slice(start, start + chunk)
            picked = jnp.dot(
                selector[top, :],
                patch[:, base * LANES : (base + half) * LANES],
                preferred_element_type=F32,
            )
            weights = interp[top, :].astype(F32)
            total = jnp.zeros((chunk, LANES), F32) if base == 0 else totals[top, :]
            for i in range(half):
                product = picked[:, i * LANES : (i + 1) * LANES] * weights
                total = jnp.where(
                    lane == base + i, jnp.sum(product, axis=1, keepdims=True), total
                )
            if base == 0:
                totals[top, :] = total
                continue
            state = jnp.transpose(total)[:lev].astype(BF16)
            for tile in range(chunk // LANES):
                block, row = divmod((start // LANES + tile) * lev, size)
                for out in outs:
                    out[bands + block, row : row + lev, :] = state[
                        :, tile * LANES : (tile + 1) * LANES
                    ]


def regroup_kernel(n_sec, n_band, *refs):
    pieces, (_, out, out_state, sems) = refs[:-4], refs[-4:]
    blocks = out_state.shape[1]
    place = lax.axis_index("fld")
    copies = []
    for i, piece in enumerate(pieces):
        fld = place ^ (len(pieces) - 1 - i)
        copies.append((piece.at[pl.ds(n_band, blocks)], out_state.at[fld]))
        for sec in range(n_sec):
            copies.append(
                (piece.at[pl.ds(0, n_band)], out.at[pl.ds(sec * n_band, n_band), fld])
            )
    copies = [pltpu.make_async_copy(*pair, sems.at[i]) for i, pair in enumerate(copies)]
    for copy in copies:
        copy.start()
    for copy in copies:
        copy.wait()


def softplus(x):
    power = jnp.exp(jnp.minimum(x, 80.0))
    return jnp.where(x < -8.0, power, jnp.maximum(x, jnp.log(1.0 + power)))


def column_kernel(n_sec, n_fld, lat_pad, slots, counts, weights, inverses, blocks, interp,
                  near, far, out, state, spread, result, sems):
    lev = near.shape[1] * near.shape[2] * LANES // slots
    place = lax.axis_index("sec")
    for fld in range(n_fld):
        for shift, pieces in enumerate((near, far)):
            row = (fld * n_sec + (place ^ shift)) * lev
            for tile in range(slots // LANES):
                state[
                    pl.ds(pl.multiple_of(row, lev), lev), tile * LANES : (tile + 1) * LANES
                ] = pieces[fld, tile * lev // near.shape[2]][
                    tile * lev % near.shape[2] : tile * lev % near.shape[2] + lev
                ].astype(F32)
    mine, lat, lon = result.shape
    across = lon // LANES
    sources, flux_rows = inverses.shape
    levels = flux_rows // 2
    count = counts[lax.axis_index("band")]
    base = (place * n_fld + lax.axis_index("fld")) * mine
    chunk = 256
    lane = lax.broadcasted_iota(jnp.int32, (1, flux_rows), 1)
    slot = lax.broadcasted_iota(jnp.int32, (chunk, 1), 0)
    column = jnp.transpose(state[...]).astype(BF16)
    tiles = [(top, at) for top in range(0, slots, chunk) for at in range(0, sources, chunk)]

    def gates_of(top, at):
        return jnp.dot(
            column[top : top + chunk], weights[:, at : at + chunk], preferred_element_type=F32
        )

    fluxes = {top: jnp.zeros((chunk, flux_rows), F32) for top in range(0, slots, chunk)}

    def add_flux(top, at, source):
        fluxes[top] = fluxes[top] + jnp.dot(
            source, inverses[at : at + chunk, :], preferred_element_type=F32
        )

    gates = gates_of(*tiles[0])
    before = None
    for i, tile in enumerate(tiles):
        later = gates_of(*tiles[i + 1]) if i + 1 < len(tiles) else None
        source = softplus(gates).astype(BF16)
        if before is not None:
            add_flux(*tiles[i - 1], before)
        gates, before = later, source
    add_flux(*tiles[-1], before)
    for start in range(0, slots, chunk):
        rows = fluxes[start]
        for level in range(mine):
            at = base + level
            plus = (lane == at) | ((lane == at + levels + 1) & (at + 1 < levels))
            minus = (lane == at + levels) | ((lane == at + 1) & (at + 1 < levels))
            terms = jnp.where(plus, rows, 0.0) - jnp.where(minus, rows, 0.0)
            heat = jnp.sum(terms, axis=1, keepdims=True)
            heat = jnp.where(slot + start < count, heat, 0.0).astype(BF16).astype(F32)
            spread[start : start + chunk, level * LANES : (level + 1) * LANES] = (
                heat * interp[start : start + chunk, :].astype(F32)
            ).astype(BF16)
    row = slot_rows(blocks[...], across, lat_pad)
    tiles = max(t for t in range(1, 8) if across % t == 0)
    height = tiles * lat_pad
    copies = []
    for first in range(0, across, tiles):
        match = row == lax.broadcasted_iota(jnp.int32, (height, slots), 0) + first * lat_pad
        left = jnp.where(match, 1.0, 0.0).astype(BF16)
        summed = jnp.dot(left, spread[...], preferred_element_type=F32).astype(BF16)
        for level in range(mine):
            for tile in range(tiles):
                result[level, :, (first + tile) * LANES : (first + tile + 1) * LANES] = summed[
                    tile * lat_pad : tile * lat_pad + lat, level * LANES : (level + 1) * LANES
                ]
        columns = pl.ds(first * LANES, tiles * LANES)
        copies.append(
            pltpu.make_async_copy(
                result.at[:, :, columns], out.at[:, :, columns], sems.at[first // tiles]
            )
        )
        copies[-1].start()
    for copy in copies:
        copy.wait()


def call(kernel, outs, specs, scratch, args, flops, size, name, out_spec=VMEM, limit=LIMIT):
    shapes = [jax.ShapeDtypeStruct(shape, dtype) for shape, dtype in outs]
    single = len(outs) == 1
    return pl.pallas_call(
        kernel,
        out_shape=shapes[0] if single else shapes,
        in_specs=specs,
        out_specs=out_spec if single else [out_spec] * len(outs),
        scratch_shapes=scratch,
        compiler_params=pltpu.CompilerParams(vmem_limit_bytes=limit),
        cost_estimate=pl.CostEstimate(flops=flops, bytes_accessed=size, transcendentals=0),
        name=name,
    )(*args)


def exchange(value, axis, shift):
    return lax.ppermute(value, axis, [(i, i ^ shift) for i in range(lax.axis_size(axis))])


def body(grid, legendre, counts, blocks, interp, source_weights, inverses):
    n_sec = lax.axis_size("sec")
    n_band = lax.axis_size("band")
    n_fld = lax.axis_size("fld")
    lev, lat, lon = grid.shape[1:]
    wave_dev, _, degrees = legendre.shape
    slots = blocks.shape[0]
    across = lon // LANES
    lat_pad = -(-lat // 16) * 16
    rest = 2 * wave_dev // THIRDS
    piece = rest * lev
    block_row = blocks.reshape(1, slots)

    table = jnp.asarray(dft_table(lon, wave_dev, n_band, n_fld))
    group = n_fld * n_band * rest
    padded_group = -(-group // LANES) * LANES
    depth = -(-across * lat_pad // LANES) * LANES
    state_blocks = slots * lev // LANES // piece
    message_blocks = n_band + state_blocks
    messages = call(
        functools.partial(local_kernel, lat_pad),
        [((message_blocks, piece, LANES), BF16)] * n_fld,
        [HBM] * 4,
        [
            pltpu.VMEM((lev, lat, lon), BF16),
            pltpu.VMEM((1, slots), jnp.int32),
            pltpu.VMEM((slots, LANES), BF16),
            pltpu.VMEM(table.shape, BF16),
            pltpu.VMEM((depth, lev * LANES), BF16),
            pltpu.VMEM((slots, LANES), jnp.int32),
            pltpu.VMEM((slots, depth), BF16),
            pltpu.VMEM((LANES, padded_group), F32),
            pltpu.VMEM((group * lev, LANES), F32),
            pltpu.VMEM((slots, LANES), F32),
            pltpu.SemaphoreType.DMA((lev + 3,)),
        ],
        (grid.reshape(lev, lat, lon), block_row, interp, table),
        2 * slots * depth * lev * LANES + 2 * lev * lat * lon * THIRDS * group,
        2 * lev * lat * lon + 2 * slots * LANES,
        "local",
        VMEM,
        WHOLE,
    )
    arrived = [exchange(messages[shift], "fld", shift) for shift in reversed(range(1, n_fld))]
    arrived.append(messages[0])
    spec_bands, flux_rows, _ = inverses.shape
    basis, inverse_rows = call(
        functools.partial(prepare_kernel, lat, n_band),
        [
            ((n_band, 2, THIRDS * degrees, LANES), BF16),
            ((spec_bands * flux_rows, flux_rows), BF16),
        ],
        [VMEM, VMEM],
        [
            pltpu.VMEM((degrees, (n_band * lat // LANES + 2) * LANES), F32),
            pltpu.VMEM((flux_rows * flux_rows, spec_bands), F32),
            pltpu.VMEM((spec_bands * flux_rows, flux_rows), F32),
        ],
        (jnp.swapaxes(legendre, 1, 2), jnp.transpose(inverses, (1, 2, 0))),
        0,
        8 * wave_dev * degrees * n_band * LANES,
        "prepare",
    )
    sent, near = call(
        functools.partial(regroup_kernel, n_sec, n_band),
        [
            ((n_sec * n_band, n_fld, piece, LANES), BF16),
            ((n_fld, state_blocks, piece, LANES), BF16),
        ],
        [HBM] * (n_fld + 1),
        [pltpu.SemaphoreType.DMA((n_fld * (1 + n_sec),))],
        (*arrived, basis),
        0,
        4 * n_sec * n_band * n_fld * piece * LANES,
        "regroup",
        HBM,
        SMALL,
    )
    far = exchange(near, "sec", 1)
    pieces = lax.all_to_all(sent, ("sec", "band"), 0, 0, tiled=True)
    sources = spec_bands * flux_rows
    states = source_weights.shape[0]
    mine = n_sec * lev // (n_sec * n_fld)
    heating = call(
        functools.partial(column_kernel, n_sec, n_fld, lat_pad, slots),
        [((mine, lat, lon), BF16)],
        [SMEM] + [VMEM] * 6,
        [
            pltpu.VMEM((states, slots), F32),
            pltpu.VMEM((slots, mine * LANES), BF16),
            pltpu.VMEM((mine, lat, lon), BF16),
            pltpu.SemaphoreType.DMA((across,)),
        ],
        (counts, source_weights, inverse_rows, block_row, interp, near, far),
        8 * slots * slots * 1024,
        2 * slots * slots,
        "columns",
        HBM,
    )

    spectral = call(
        functools.partial(legendre_kernel, n_sec, n_band, n_fld, lev),
        [((wave_dev, 2, n_fld, n_sec * lev, degrees), BF16)],
        [VMEM, VMEM],
        [
            pltpu.VMEM((wave_dev, 2, n_fld, n_sec * lev, degrees), BF16),
            pltpu.SemaphoreType.DMA((wave_dev,)),
        ],
        (basis, pieces),
        4 * n_sec * n_fld * piece * n_band * LANES * degrees * THIRDS,
        2 * n_sec * n_band * n_fld * piece * LANES,
        "legendre",
        HBM,
    )
    return (spectral, heating)


def solution(mesh):
    return jax.shard_map(
        body,
        mesh=mesh,
        in_specs=(
            P("fld", "sec", "band", None),
            P(("band", "fld"), None, "sec"),
            P(),
            P("band"),
            P("band", None),
            P(),
            P(),
        ),
        out_specs=(P(("band", "fld"), None, None, None, "sec"), P(("sec", "fld"), "band", None)),
        check_vma=False,
    )
```

```python
import functools
import math

import jax
import jax.numpy as jnp
import numpy as np
from jax import lax
from jax.experimental import pallas as pl
from jax.experimental.pallas import tpu as pltpu
from jax.sharding import PartitionSpec as P

BF16 = jnp.bfloat16
F32 = jnp.float32
LANES = 128
THIRDS = 3
VMEM = pl.BlockSpec(memory_space=pltpu.VMEM)
HBM = pl.BlockSpec(memory_space=pltpu.HBM)
SMEM = pl.BlockSpec(memory_space=pltpu.SMEM)
LIMIT = 40 * 1024 * 1024
SMALL = 4 * 1024 * 1024
ROOM = 12000 * 1024
WHOLE = 64 * 1024 * 1024 - ROOM
NT = (((1,), (1,)), ((), ()))


def dft_table(lon, wave_dev, n_band, n_fld):
    values_dev = 2 * wave_dev
    rest = values_dev // THIRDS
    third, fld, band, low = np.meshgrid(
        np.arange(THIRDS), np.arange(n_fld), np.arange(n_band), np.arange(rest), indexing="ij"
    )
    value = third * rest + low
    wave = ((band * n_fld + fld) * wave_dev + value // 2).reshape(-1)
    part = (value % 2).reshape(-1)
    phase = np.arange(lon, dtype=np.int64)[:, None] * wave[None, :] % lon
    angle = phase * (2.0 * math.pi / lon)
    values = np.where(part[None, :] == 0, np.cos(angle), -np.sin(angle)) / math.sqrt(lon)
    return values.astype(np.float32).astype(BF16)


def pack(lev, lat, coeffs, padded, rows):
    group = coeffs.shape[1] // THIRDS
    padded[...] = jnp.zeros_like(padded)
    for level in range(lev):
        for third in range(THIRDS):
            padded[third * lat : (third + 1) * lat, :group] = coeffs[
                level * lat : (level + 1) * lat, third * group : (third + 1) * group
            ]
        rows[pl.ds(level, group, stride=lev), :] = jnp.transpose(padded[...])[:group]


def prepare_kernel(lat, n_band, legendre, inverses, out, out_inverses, wide, rows, turned):
    flux_rows, _, spec_bands = inverses.shape
    for row in range(flux_rows):
        rows[row * flux_rows : (row + 1) * flux_rows, :] = inverses[row].astype(F32)
    for row in range(flux_rows):
        turned[pl.ds(row, spec_bands, stride=flux_rows), :] = jnp.transpose(
            rows[pl.ds(row, flux_rows, stride=flux_rows), :]
        )
    out_inverses[...] = turned[...].astype(BF16)
    waves, degrees, _ = legendre.shape
    wide[...] = jnp.zeros_like(wide)
    lane = lax.broadcasted_iota(jnp.int32, (degrees, LANES), 1)
    for wave in range(waves):
        third, parity = wave // 2, wave % 2
        wide[:, : n_band * lat] = legendre[wave].astype(F32)
        place = third * lat
        live = (lane >= place) & (lane < place + lat)
        for band in range(n_band):
            base = band * lat // LANES * LANES
            moved = pltpu.roll(
                wide[:, base : base + 2 * LANES], (place - (band * lat - base)) % (2 * LANES), 1
            )
            out[band, parity, third * degrees : (third + 1) * degrees, :] = jnp.where(
                live, moved[:, :LANES], 0.0
            ).astype(BF16)


def legendre_kernel(n_sec, n_band, n_fld, lev, weights, pieces, out_hbm, out, sems):
    degrees = out.shape[4]
    copies = []
    half = pieces.shape[2] // 2
    for parity in range(2):
        rows = slice(parity * half, (parity + 1) * half)
        basis = jnp.concatenate([weights[band, parity] for band in range(n_band)], axis=1)
        left = jnp.concatenate(
            [
                jnp.concatenate(
                    [
                        pieces[sec * n_band + band, fld, rows, :]
                        for band in range(n_band)
                    ],
                    axis=1,
                )
                for fld in range(n_fld)
                for sec in range(n_sec)
            ],
            axis=0,
        )
        result = lax.dot_general(left, basis, NT, preferred_element_type=F32)
        for third in range(THIRDS):
            part = result[:, third * degrees : (third + 1) * degrees]
            for fld in range(n_fld):
                for real in range(2):
                    levels = [
                        part[(fld * n_sec + sec) * half + real * lev :][:lev]
                        for sec in range(n_sec)
                    ]
                    out[2 * third + parity, real, fld] = jnp.concatenate(levels, axis=0).astype(
                        BF16
                    )
            wave = 2 * third + parity
            copies.append(
                pltpu.make_async_copy(out.at[wave], out_hbm.at[wave], sems.at[wave])
            )
            copies[-1].start()
    for copy in copies:
        copy.wait()


def slot_rows(blocks, across, lat_pad):
    shift = 16
    factor = -(-(1 << shift) // across)
    lat = lax.shift_right_logical(blocks * factor, shift)
    return (blocks - lat * across) * lat_pad + lat


def local_kernel(lat_pad, grid_hbm, blocks_hbm, interp_hbm, table_hbm, *refs):
    outs = refs[:-11]
    grid, blocks, interp, table, patch, column, selector, padded, rows, totals, sems = refs[-11:]
    lev, lat, lon = grid.shape
    across = lon // LANES
    slots = interp.shape[0]
    depth = patch.shape[0]
    small = [
        pltpu.make_async_copy(blocks_hbm, blocks, sems.at[lev]),
        pltpu.make_async_copy(interp_hbm, interp, sems.at[lev + 1]),
        pltpu.make_async_copy(table_hbm, table, sems.at[lev + 2]),
    ]
    loads = [
        pltpu.make_async_copy(
            grid_hbm.at[pl.ds(level, 1)], grid.at[pl.ds(level, 1)], sems.at[level]
        )
        for level in range(lev)
    ]
    half = lev // 2
    small[0].start()
    for copy in loads[:half]:
        copy.start()
    small[1].start()
    for copy in loads[half:]:
        copy.start()
    small[2].start()
    small[0].wait()
    row = slot_rows(blocks[...], across, lat_pad)
    column[...] = jnp.transpose(jnp.broadcast_to(row, (LANES, slots)))
    chunk = 256
    lane = lax.broadcasted_iota(jnp.int32, (chunk, LANES), 1)
    for start in range(0, slots, chunk):
        mine = column[start : start + chunk, :]
        for base in range(0, depth, LANES):
            selector[start : start + chunk, base : base + LANES] = jnp.where(
                mine == lane + base, 1.0, 0.0
            ).astype(BF16)
    size = outs[0].shape[1]
    bands = outs[0].shape[0] - slots * lev // LANES // size
    place = lax.axis_index("fld")
    for tile in range(across):
        patch[tile * lat_pad + lat : (tile + 1) * lat_pad, :] = jnp.zeros(
            (lat_pad - lat, lev * LANES), BF16
        )
    if depth > across * lat_pad:
        patch[across * lat_pad :, :] = jnp.zeros((depth - across * lat_pad, lev * LANES), BF16)
    for base in (0, half):
        for level in range(base, base + half):
            loads[level].wait()
            for tile in range(across):
                patch[
                    tile * lat_pad : tile * lat_pad + lat, level * LANES : (level + 1) * LANES
                ] = grid[level, :, tile * LANES : (tile + 1) * LANES]
        if base == 0:
            small[1].wait()
        else:
            small[2].wait()
            flat = jnp.concatenate([grid[level] for level in range(lev)], axis=0)
            coeffs = jnp.dot(flat, table[...], preferred_element_type=F32)
            pack(lev, lat, coeffs, padded, rows)
            height = bands * size
            for shift, out in enumerate(outs):
                first = pl.multiple_of((place ^ shift) * height, height)
                part = rows[pl.ds(first, height), :].astype(BF16)
                out[:bands] = part.reshape(bands, size, LANES)
        for start in range(0, slots, chunk):
            top = slice(start, start + chunk)
            picked = jnp.dot(
                selector[top, :],
                patch[:, base * LANES : (base + half) * LANES],
                preferred_element_type=F32,
            )
            weights = interp[top, :].astype(F32)
            total = jnp.zeros((chunk, LANES), F32) if base == 0 else totals[top, :]
            for i in range(half):
                product = picked[:, i * LANES : (i + 1) * LANES] * weights
                total = jnp.where(
                    lane == base + i, jnp.sum(product, axis=1, keepdims=True), total
                )
            if base == 0:
                totals[top, :] = total
                continue
            state = jnp.transpose(total)[:lev].astype(BF16)
            for tile in range(chunk // LANES):
                block, row = divmod((start // LANES + tile) * lev, size)
                for out in outs:
                    out[bands + block, row : row + lev, :] = state[
                        :, tile * LANES : (tile + 1) * LANES
                    ]


def regroup_kernel(n_sec, n_band, *refs):
    pieces, (_, out, out_state, sems) = refs[:-4], refs[-4:]
    blocks = out_state.shape[1]
    place = lax.axis_index("fld")
    copies = []
    for i, piece in enumerate(pieces):
        fld = place ^ (len(pieces) - 1 - i)
        copies.append((piece.at[pl.ds(n_band, blocks)], out_state.at[fld]))
        for sec in range(n_sec):
            copies.append(
                (piece.at[pl.ds(0, n_band)], out.at[pl.ds(sec * n_band, n_band), fld])
            )
    copies = [pltpu.make_async_copy(*pair, sems.at[i]) for i, pair in enumerate(copies)]
    for copy in copies:
        copy.start()
    for copy in copies:
        copy.wait()


def softplus(x):
    power = jnp.exp(jnp.minimum(x, 80.0))
    return jnp.where(x < -8.0, power, jnp.maximum(x, jnp.log(1.0 + power)))


def column_kernel(n_sec, n_fld, lat_pad, slots, counts, weights, inverses, blocks, interp,
                  near, far, out, state, spread, result, sems):
    lev = near.shape[1] * near.shape[2] * LANES // slots
    place = lax.axis_index("sec")
    for fld in range(n_fld):
        for shift, pieces in enumerate((near, far)):
            row = (fld * n_sec + (place ^ shift)) * lev
            for tile in range(slots // LANES):
                state[
                    pl.ds(pl.multiple_of(row, lev), lev), tile * LANES : (tile + 1) * LANES
                ] = pieces[fld, tile * lev // near.shape[2]][
                    tile * lev % near.shape[2] : tile * lev % near.shape[2] + lev
                ].astype(F32)
    mine, lat, lon = result.shape
    across = lon // LANES
    sources, flux_rows = inverses.shape
    levels = flux_rows // 2
    count = counts[lax.axis_index("band")]
    base = (place * n_fld + lax.axis_index("fld")) * mine
    chunk = 256
    lane = lax.broadcasted_iota(jnp.int32, (1, flux_rows), 1)
    slot = lax.broadcasted_iota(jnp.int32, (chunk, 1), 0)
    column = jnp.transpose(state[...]).astype(BF16)
    tiles = [(top, at) for top in range(0, slots, chunk) for at in range(0, sources, chunk)]

    def gates_of(top, at):
        return jnp.dot(
            column[top : top + chunk], weights[:, at : at + chunk], preferred_element_type=F32
        )

    fluxes = {top: jnp.zeros((chunk, flux_rows), F32) for top in range(0, slots, chunk)}

    def add_flux(top, at, source):
        fluxes[top] = fluxes[top] + jnp.dot(
            source, inverses[at : at + chunk, :], preferred_element_type=F32
        )

    gates = gates_of(*tiles[0])
    before = None
    for i, tile in enumerate(tiles):
        later = gates_of(*tiles[i + 1]) if i + 1 < len(tiles) else None
        source = softplus(gates).astype(BF16)
        if before is not None:
            add_flux(*tiles[i - 1], before)
        gates, before = later, source
    add_flux(*tiles[-1], before)
    for start in range(0, slots, chunk):
        rows = fluxes[start]
        for level in range(mine):
            at = base + level
            plus = (lane == at) | ((lane == at + levels + 1) & (at + 1 < levels))
            minus = (lane == at + levels) | ((lane == at + 1) & (at + 1 < levels))
            terms = jnp.where(plus, rows, 0.0) - jnp.where(minus, rows, 0.0)
            heat = jnp.sum(terms, axis=1, keepdims=True)
            heat = jnp.where(slot + start < count, heat, 0.0).astype(BF16).astype(F32)
            spread[start : start + chunk, level * LANES : (level + 1) * LANES] = (
                heat * interp[start : start + chunk, :].astype(F32)
            ).astype(BF16)
    row = slot_rows(blocks[...], across, lat_pad)
    tiles = max(t for t in range(1, 8) if across % t == 0)
    height = tiles * lat_pad
    copies = []
    for first in range(0, across, tiles):
        match = row == lax.broadcasted_iota(jnp.int32, (height, slots), 0) + first * lat_pad
        left = jnp.where(match, 1.0, 0.0).astype(BF16)
        summed = jnp.dot(left, spread[...], preferred_element_type=F32).astype(BF16)
        for level in range(mine):
            for tile in range(tiles):
                result[level, :, (first + tile) * LANES : (first + tile + 1) * LANES] = summed[
                    tile * lat_pad : tile * lat_pad + lat, level * LANES : (level + 1) * LANES
                ]
        columns = pl.ds(first * LANES, tiles * LANES)
        copies.append(
            pltpu.make_async_copy(
                result.at[:, :, columns], out.at[:, :, columns], sems.at[first // tiles]
            )
        )
        copies[-1].start()
    for copy in copies:
        copy.wait()


def call(kernel, outs, specs, scratch, args, flops, size, name, out_spec=VMEM, limit=LIMIT):
    shapes = [jax.ShapeDtypeStruct(shape, dtype) for shape, dtype in outs]
    single = len(outs) == 1
    return pl.pallas_call(
        kernel,
        out_shape=shapes[0] if single else shapes,
        in_specs=specs,
        out_specs=out_spec if single else [out_spec] * len(outs),
        scratch_shapes=scratch,
        compiler_params=pltpu.CompilerParams(vmem_limit_bytes=limit),
        cost_estimate=pl.CostEstimate(flops=flops, bytes_accessed=size, transcendentals=0),
        name=name,
    )(*args)


def exchange(value, axis, shift):
    return lax.ppermute(value, axis, [(i, i ^ shift) for i in range(lax.axis_size(axis))])


def body(grid, legendre, counts, blocks, interp, source_weights, inverses):
    n_sec = lax.axis_size("sec")
    n_band = lax.axis_size("band")
    n_fld = lax.axis_size("fld")
    lev, lat, lon = grid.shape[1:]
    wave_dev, _, degrees = legendre.shape
    slots = blocks.shape[0]
    across = lon // LANES
    lat_pad = -(-lat // 16) * 16
    rest = 2 * wave_dev // THIRDS
    piece = rest * lev
    block_row = blocks.reshape(1, slots)

    table = jnp.asarray(dft_table(lon, wave_dev, n_band, n_fld))
    group = n_fld * n_band * rest
    padded_group = -(-group // LANES) * LANES
    depth = -(-across * lat_pad // LANES) * LANES
    state_blocks = slots * lev // LANES // piece
    message_blocks = n_band + state_blocks
    messages = call(
        functools.partial(local_kernel, lat_pad),
        [((message_blocks, piece, LANES), BF16)] * n_fld,
        [HBM] * 4,
        [
            pltpu.VMEM((lev, lat, lon), BF16),
            pltpu.VMEM((1, slots), jnp.int32),
            pltpu.VMEM((slots, LANES), BF16),
            pltpu.VMEM(table.shape, BF16),
            pltpu.VMEM((depth, lev * LANES), BF16),
            pltpu.VMEM((slots, LANES), jnp.int32),
            pltpu.VMEM((slots, depth), BF16),
            pltpu.VMEM((LANES, padded_group), F32),
            pltpu.VMEM((group * lev, LANES), F32),
            pltpu.VMEM((slots, LANES), F32),
            pltpu.SemaphoreType.DMA((lev + 3,)),
        ],
        (
            pltpu.with_memory_space_constraint(grid.reshape(lev, lat, lon), pltpu.HBM),
            pltpu.with_memory_space_constraint(block_row, pltpu.HBM),
            pltpu.with_memory_space_constraint(interp, pltpu.HBM),
            table,
        ),
        2 * slots * depth * lev * LANES + 2 * lev * lat * lon * THIRDS * group,
        2 * lev * lat * lon + 2 * slots * LANES,
        "local",
        VMEM,
        WHOLE,
    )
    arrived = [exchange(messages[shift], "fld", shift) for shift in reversed(range(1, n_fld))]
    arrived.append(messages[0])
    spec_bands, flux_rows, _ = inverses.shape
    basis, inverse_rows = call(
        functools.partial(prepare_kernel, lat, n_band),
        [
            ((n_band, 2, THIRDS * degrees, LANES), BF16),
            ((spec_bands * flux_rows, flux_rows), BF16),
        ],
        [VMEM, VMEM],
        [
            pltpu.VMEM((degrees, (n_band * lat // LANES + 2) * LANES), F32),
            pltpu.VMEM((flux_rows * flux_rows, spec_bands), F32),
            pltpu.VMEM((spec_bands * flux_rows, flux_rows), F32),
        ],
        (jnp.swapaxes(legendre, 1, 2), jnp.transpose(inverses, (1, 2, 0))),
        0,
        8 * wave_dev * degrees * n_band * LANES,
        "prepare",
    )
    sent, near = call(
        functools.partial(regroup_kernel, n_sec, n_band),
        [
            ((n_sec * n_band, n_fld, piece, LANES), BF16),
            ((n_fld, state_blocks, piece, LANES), BF16),
        ],
        [HBM] * (n_fld + 1),
        [pltpu.SemaphoreType.DMA((n_fld * (1 + n_sec),))],
        (*arrived, basis),
        0,
        4 * n_sec * n_band * n_fld * piece * LANES,
        "regroup",
        HBM,
        SMALL,
    )
    far = exchange(near, "sec", 1)
    pieces = lax.all_to_all(sent, ("sec", "band"), 0, 0, tiled=True)
    sources = spec_bands * flux_rows
    states = source_weights.shape[0]
    mine = n_sec * lev // (n_sec * n_fld)
    heating = call(
        functools.partial(column_kernel, n_sec, n_fld, lat_pad, slots),
        [((mine, lat, lon), BF16)],
        [SMEM] + [VMEM] * 6,
        [
            pltpu.VMEM((states, slots), F32),
            pltpu.VMEM((slots, mine * LANES), BF16),
            pltpu.VMEM((mine, lat, lon), BF16),
            pltpu.SemaphoreType.DMA((across,)),
        ],
        (counts, source_weights, inverse_rows, block_row, interp, near, far),
        8 * slots * slots * 1024,
        2 * slots * slots,
        "columns",
        HBM,
    )

    spectral = call(
        functools.partial(legendre_kernel, n_sec, n_band, n_fld, lev),
        [((wave_dev, 2, n_fld, n_sec * lev, degrees), BF16)],
        [VMEM, VMEM],
        [
            pltpu.VMEM((wave_dev, 2, n_fld, n_sec * lev, degrees), BF16),
            pltpu.SemaphoreType.DMA((wave_dev,)),
        ],
        (basis, pieces),
        4 * n_sec * n_fld * piece * n_band * LANES * degrees * THIRDS,
        2 * n_sec * n_band * n_fld * piece * LANES,
        "legendre",
        HBM,
    )
    return (spectral, heating)


def solution(mesh):
    return jax.shard_map(
        body,
        mesh=mesh,
        in_specs=(
            P("fld", "sec", "band", None),
            P(("band", "fld"), None, "sec"),
            P(),
            P("band"),
            P("band", None),
            P(),
            P(),
        ),
        out_specs=(P(("band", "fld"), None, None, None, "sec"), P(("sec", "fld"), "band", None)),
        check_vma=False,
    )
```

```python
import functools
import math

import jax
import jax.numpy as jnp
import numpy as np
from jax import lax
from jax.experimental import pallas as pl
from jax.experimental.pallas import tpu as pltpu
from jax.sharding import PartitionSpec as P

BF16 = jnp.bfloat16
F32 = jnp.float32
LANES = 128
THIRDS = 3
VMEM = pl.BlockSpec(memory_space=pltpu.VMEM)
HBM = pl.BlockSpec(memory_space=pltpu.HBM)
SMEM = pl.BlockSpec(memory_space=pltpu.SMEM)
LIMIT = 40 * 1024 * 1024
SMALL = 4 * 1024 * 1024
ROOM = 12000 * 1024
WHOLE = 64 * 1024 * 1024 - ROOM
NT = (((1,), (1,)), ((), ()))


def dft_table(lon, wave_dev, n_band, n_fld):
    values_dev = 2 * wave_dev
    rest = values_dev // THIRDS
    third, fld, band, low = np.meshgrid(
        np.arange(THIRDS), np.arange(n_fld), np.arange(n_band), np.arange(rest), indexing="ij"
    )
    value = third * rest + low
    wave = ((band * n_fld + fld) * wave_dev + value // 2).reshape(-1)
    part = (value % 2).reshape(-1)
    phase = np.arange(lon, dtype=np.int64)[:, None] * wave[None, :] % lon
    angle = phase * (2.0 * math.pi / lon)
    values = np.where(part[None, :] == 0, np.cos(angle), -np.sin(angle)) / math.sqrt(lon)
    return values.astype(np.float32).astype(BF16)


def pack(lev, lat, coeffs, padded, rows):
    group = coeffs.shape[1] // THIRDS
    padded[...] = jnp.zeros_like(padded)
    for level in range(lev):
        for third in range(THIRDS):
            padded[third * lat : (third + 1) * lat, :group] = coeffs[
                level * lat : (level + 1) * lat, third * group : (third + 1) * group
            ]
        rows[pl.ds(level, group, stride=lev), :] = jnp.transpose(padded[...])[:group]


def prepare_kernel(lat, n_band, legendre, inverses, out, out_inverses, wide, rows, turned):
    flux_rows, _, spec_bands = inverses.shape
    for row in range(flux_rows):
        rows[row * flux_rows : (row + 1) * flux_rows, :] = inverses[row].astype(F32)
    for row in range(flux_rows):
        turned[pl.ds(row, spec_bands, stride=flux_rows), :] = jnp.transpose(
            rows[pl.ds(row, flux_rows, stride=flux_rows), :]
        )
    out_inverses[...] = turned[...].astype(BF16)
    waves, degrees, _ = legendre.shape
    wide[...] = jnp.zeros_like(wide)
    lane = lax.broadcasted_iota(jnp.int32, (degrees, LANES), 1)
    for wave in range(waves):
        third, parity = wave // 2, wave % 2
        wide[:, : n_band * lat] = legendre[wave].astype(F32)
        place = third * lat
        live = (lane >= place) & (lane < place + lat)
        for band in range(n_band):
            base = band * lat // LANES * LANES
            moved = pltpu.roll(
                wide[:, base : base + 2 * LANES], (place - (band * lat - base)) % (2 * LANES), 1
            )
            out[band, parity, third * degrees : (third + 1) * degrees, :] = jnp.where(
                live, moved[:, :LANES], 0.0
            ).astype(BF16)


def legendre_kernel(n_sec, n_band, n_fld, lev, weights, pieces, out_hbm, out, sems):
    degrees = out.shape[4]
    copies = []
    half = pieces.shape[2] // 2
    for parity in range(2):
        rows = slice(parity * half, (parity + 1) * half)
        basis = jnp.concatenate([weights[band, parity] for band in range(n_band)], axis=1)
        left = jnp.concatenate(
            [
                jnp.concatenate(
                    [
                        pieces[sec * n_band + band, fld, rows, :]
                        for band in range(n_band)
                    ],
                    axis=1,
                )
                for fld in range(n_fld)
                for sec in range(n_sec)
            ],
            axis=0,
        )
        result = lax.dot_general(left, basis, NT, preferred_element_type=F32)
        for third in range(THIRDS):
            part = result[:, third * degrees : (third + 1) * degrees]
            for fld in range(n_fld):
                for real in range(2):
                    levels = [
                        part[(fld * n_sec + sec) * half + real * lev :][:lev]
                        for sec in range(n_sec)
                    ]
                    out[2 * third + parity, real, fld] = jnp.concatenate(levels, axis=0).astype(
                        BF16
                    )
            wave = 2 * third + parity
            copies.append(
                pltpu.make_async_copy(out.at[wave], out_hbm.at[wave], sems.at[wave])
            )
            copies[-1].start()
    for copy in copies:
        copy.wait()


def slot_rows(blocks, across, lat_pad):
    shift = 16
    factor = -(-(1 << shift) // across)
    lat = lax.shift_right_logical(blocks * factor, shift)
    return (blocks - lat * across) * lat_pad + lat


def local_kernel(lat_pad, grid_hbm, blocks_hbm, interp_hbm, table_hbm, *refs):
    outs = refs[:-11]
    grid, blocks, interp, table, patch, column, selector, padded, rows, totals, sems = refs[-11:]
    lev, lat, lon = grid.shape
    across = lon // LANES
    slots = interp.shape[0]
    depth = patch.shape[0]
    small = [
        pltpu.make_async_copy(blocks_hbm, blocks, sems.at[lev]),
        pltpu.make_async_copy(interp_hbm, interp, sems.at[lev + 1]),
        pltpu.make_async_copy(table_hbm, table, sems.at[lev + 2]),
    ]
    loads = [
        pltpu.make_async_copy(
            grid_hbm.at[pl.ds(level, 1)], grid.at[pl.ds(level, 1)], sems.at[level]
        )
        for level in range(lev)
    ]
    half = lev // 2
    small[0].start()
    for copy in loads[:half]:
        copy.start()
    small[1].start()
    for copy in loads[half:]:
        copy.start()
    small[2].start()
    small[0].wait()
    row = slot_rows(blocks[...], across, lat_pad)
    column[...] = jnp.transpose(jnp.broadcast_to(row, (LANES, slots)))
    chunk = 256
    lane = lax.broadcasted_iota(jnp.int32, (chunk, LANES), 1)
    for start in range(0, slots, chunk):
        mine = column[start : start + chunk, :]
        for base in range(0, depth, LANES):
            selector[start : start + chunk, base : base + LANES] = jnp.where(
                mine == lane + base, 1.0, 0.0
            ).astype(BF16)
    size = outs[0].shape[1]
    bands = outs[0].shape[0] - slots * lev // LANES // size
    place = lax.axis_index("fld")
    for tile in range(across):
        patch[tile * lat_pad + lat : (tile + 1) * lat_pad, :] = jnp.zeros(
            (lat_pad - lat, lev * LANES), BF16
        )
    if depth > across * lat_pad:
        patch[across * lat_pad :, :] = jnp.zeros((depth - across * lat_pad, lev * LANES), BF16)
    for base in (0, half):
        for level in range(base, base + half):
            loads[level].wait()
            for tile in range(across):
                patch[
                    tile * lat_pad : tile * lat_pad + lat, level * LANES : (level + 1) * LANES
                ] = grid[level, :, tile * LANES : (tile + 1) * LANES]
        if base == 0:
            small[1].wait()
        else:
            small[2].wait()
            flat = jnp.concatenate([grid[level] for level in range(lev)], axis=0)
            coeffs = jnp.dot(flat, table[...], preferred_element_type=F32)
            pack(lev, lat, coeffs, padded, rows)
            height = bands * size
            for shift, out in enumerate(outs):
                first = pl.multiple_of((place ^ shift) * height, height)
                part = rows[pl.ds(first, height), :].astype(BF16)
                out[:bands] = part.reshape(bands, size, LANES)
        for start in range(0, slots, chunk):
            top = slice(start, start + chunk)
            picked = jnp.dot(
                selector[top, :],
                patch[:, base * LANES : (base + half) * LANES],
                preferred_element_type=F32,
            )
            weights = interp[top, :].astype(F32)
            total = jnp.zeros((chunk, LANES), F32) if base == 0 else totals[top, :]
            for i in range(half):
                product = picked[:, i * LANES : (i + 1) * LANES] * weights
                total = jnp.where(
                    lane == base + i, jnp.sum(product, axis=1, keepdims=True), total
                )
            if base == 0:
                totals[top, :] = total
                continue
            state = jnp.transpose(total)[:lev].astype(BF16)
            for tile in range(chunk // LANES):
                block, row = divmod((start // LANES + tile) * lev, size)
                for out in outs:
                    out[bands + block, row : row + lev, :] = state[
                        :, tile * LANES : (tile + 1) * LANES
                    ]


def regroup_kernel(n_sec, n_band, *refs):
    pieces, (_, out, out_state, sems) = refs[:-4], refs[-4:]
    blocks = out_state.shape[1]
    place = lax.axis_index("fld")
    copies = []
    for i, piece in enumerate(pieces):
        fld = place ^ (len(pieces) - 1 - i)
        copies.append((piece.at[pl.ds(n_band, blocks)], out_state.at[fld]))
        for sec in range(n_sec):
            copies.append(
                (piece.at[pl.ds(0, n_band)], out.at[pl.ds(sec * n_band, n_band), fld])
            )
    copies = [pltpu.make_async_copy(*pair, sems.at[i]) for i, pair in enumerate(copies)]
    for copy in copies:
        copy.start()
    for copy in copies:
        copy.wait()


def softplus(x):
    power = jnp.exp(jnp.minimum(x, 80.0))
    return jnp.where(x < -8.0, power, jnp.maximum(x, jnp.log(1.0 + power)))


def column_kernel(n_sec, n_fld, lat_pad, slots, counts, weights, inverses, blocks, interp,
                  near, far, out, state, spread, result, sems):
    lev = near.shape[1] * near.shape[2] * LANES // slots
    place = lax.axis_index("sec")
    for fld in range(n_fld):
        for shift, pieces in enumerate((near, far)):
            row = (fld * n_sec + (place ^ shift)) * lev
            for tile in range(slots // LANES):
                state[
                    pl.ds(pl.multiple_of(row, lev), lev), tile * LANES : (tile + 1) * LANES
                ] = pieces[fld, tile * lev // near.shape[2]][
                    tile * lev % near.shape[2] : tile * lev % near.shape[2] + lev
                ].astype(F32)
    mine, lat, lon = result.shape
    across = lon // LANES
    sources, flux_rows = inverses.shape
    levels = flux_rows // 2
    count = counts[lax.axis_index("band")]
    base = (place * n_fld + lax.axis_index("fld")) * mine
    chunk = 256
    lane = lax.broadcasted_iota(jnp.int32, (1, flux_rows), 1)
    slot = lax.broadcasted_iota(jnp.int32, (chunk, 1), 0)
    column = jnp.transpose(state[...]).astype(BF16)
    tiles = [(top, at) for top in range(0, slots, chunk) for at in range(0, sources, chunk)]

    def gates_of(top, at):
        return jnp.dot(
            column[top : top + chunk], weights[:, at : at + chunk], preferred_element_type=F32
        )

    fluxes = {top: jnp.zeros((chunk, flux_rows), F32) for top in range(0, slots, chunk)}

    def add_flux(top, at, source):
        fluxes[top] = fluxes[top] + jnp.dot(
            source, inverses[at : at + chunk, :], preferred_element_type=F32
        )

    gates = gates_of(*tiles[0])
    before = None
    for i, tile in enumerate(tiles):
        later = gates_of(*tiles[i + 1]) if i + 1 < len(tiles) else None
        source = softplus(gates).astype(BF16)
        if before is not None:
            add_flux(*tiles[i - 1], before)
        gates, before = later, source
    add_flux(*tiles[-1], before)
    for start in range(0, slots, chunk):
        rows = fluxes[start]
        for level in range(mine):
            at = base + level
            plus = (lane == at) | ((lane == at + levels + 1) & (at + 1 < levels))
            minus = (lane == at + levels) | ((lane == at + 1) & (at + 1 < levels))
            terms = jnp.where(plus, rows, 0.0) - jnp.where(minus, rows, 0.0)
            heat = jnp.sum(terms, axis=1, keepdims=True)
            heat = jnp.where(slot + start < count, heat, 0.0).astype(BF16).astype(F32)
            spread[start : start + chunk, level * LANES : (level + 1) * LANES] = (
                heat * interp[start : start + chunk, :].astype(F32)
            ).astype(BF16)
    row = slot_rows(blocks[...], across, lat_pad)
    tiles = max(t for t in range(1, 8) if across % t == 0)
    height = tiles * lat_pad
    copies = []
    for first in range(0, across, tiles):
        match = row == lax.broadcasted_iota(jnp.int32, (height, slots), 0) + first * lat_pad
        left = jnp.where(match, 1.0, 0.0).astype(BF16)
        summed = jnp.dot(left, spread[...], preferred_element_type=F32).astype(BF16)
        for level in range(mine):
            for tile in range(tiles):
                result[level, :, (first + tile) * LANES : (first + tile + 1) * LANES] = summed[
                    tile * lat_pad : tile * lat_pad + lat, level * LANES : (level + 1) * LANES
                ]
        columns = pl.ds(first * LANES, tiles * LANES)
        copies.append(
            pltpu.make_async_copy(
                result.at[:, :, columns], out.at[:, :, columns], sems.at[first // tiles]
            )
        )
        copies[-1].start()
    for copy in copies:
        copy.wait()


def call(kernel, outs, specs, scratch, args, flops, size, name, out_spec=VMEM, limit=LIMIT):
    shapes = [jax.ShapeDtypeStruct(shape, dtype) for shape, dtype in outs]
    single = len(outs) == 1
    return pl.pallas_call(
        kernel,
        out_shape=shapes[0] if single else shapes,
        in_specs=specs,
        out_specs=out_spec if single else [out_spec] * len(outs),
        scratch_shapes=scratch,
        compiler_params=pltpu.CompilerParams(vmem_limit_bytes=limit),
        cost_estimate=pl.CostEstimate(flops=flops, bytes_accessed=size, transcendentals=0),
        name=name,
    )(*args)


def exchange(value, axis, shift):
    return lax.ppermute(value, axis, [(i, i ^ shift) for i in range(lax.axis_size(axis))])


def body(grid, legendre, counts, blocks, interp, source_weights, inverses):
    n_sec = lax.axis_size("sec")
    n_band = lax.axis_size("band")
    n_fld = lax.axis_size("fld")
    lev, lat, lon = grid.shape[1:]
    wave_dev, _, degrees = legendre.shape
    slots = blocks.shape[0]
    across = lon // LANES
    lat_pad = -(-lat // 16) * 16
    rest = 2 * wave_dev // THIRDS
    piece = rest * lev
    block_row = blocks.reshape(1, slots)

    table = jnp.asarray(dft_table(lon, wave_dev, n_band, n_fld))
    group = n_fld * n_band * rest
    padded_group = -(-group // LANES) * LANES
    depth = -(-across * lat_pad // LANES) * LANES
    state_blocks = slots * lev // LANES // piece
    message_blocks = n_band + state_blocks
    messages = call(
        functools.partial(local_kernel, lat_pad),
        [((message_blocks, piece, LANES), BF16)] * n_fld,
        [HBM] * 4,
        [
            pltpu.VMEM((lev, lat, lon), BF16),
            pltpu.VMEM((1, slots), jnp.int32),
            pltpu.VMEM((slots, LANES), BF16),
            pltpu.VMEM(table.shape, BF16),
            pltpu.VMEM((depth, lev * LANES), BF16),
            pltpu.VMEM((slots, LANES), jnp.int32),
            pltpu.VMEM((slots, depth), BF16),
            pltpu.VMEM((LANES, padded_group), F32),
            pltpu.VMEM((group * lev, LANES), F32),
            pltpu.VMEM((slots, LANES), F32),
            pltpu.SemaphoreType.DMA((lev + 3,)),
        ],
        [
            pltpu.with_memory_space_constraint(value, pltpu.HBM)
            for value in (grid.reshape(lev, lat, lon), block_row, interp, table)
        ],
        2 * slots * depth * lev * LANES + 2 * lev * lat * lon * THIRDS * group,
        2 * lev * lat * lon + 2 * slots * LANES,
        "local",
        VMEM,
        WHOLE,
    )
    arrived = [exchange(messages[shift], "fld", shift) for shift in reversed(range(1, n_fld))]
    arrived.append(messages[0])
    spec_bands, flux_rows, _ = inverses.shape
    basis, inverse_rows = call(
        functools.partial(prepare_kernel, lat, n_band),
        [
            ((n_band, 2, THIRDS * degrees, LANES), BF16),
            ((spec_bands * flux_rows, flux_rows), BF16),
        ],
        [VMEM, VMEM],
        [
            pltpu.VMEM((degrees, (n_band * lat // LANES + 2) * LANES), F32),
            pltpu.VMEM((flux_rows * flux_rows, spec_bands), F32),
            pltpu.VMEM((spec_bands * flux_rows, flux_rows), F32),
        ],
        (jnp.swapaxes(legendre, 1, 2), jnp.transpose(inverses, (1, 2, 0))),
        0,
        8 * wave_dev * degrees * n_band * LANES,
        "prepare",
    )
    sent, near = call(
        functools.partial(regroup_kernel, n_sec, n_band),
        [
            ((n_sec * n_band, n_fld, piece, LANES), BF16),
            ((n_fld, state_blocks, piece, LANES), BF16),
        ],
        [HBM] * (n_fld + 1),
        [pltpu.SemaphoreType.DMA((n_fld * (1 + n_sec),))],
        (*arrived, basis),
        0,
        4 * n_sec * n_band * n_fld * piece * LANES,
        "regroup",
        HBM,
        SMALL,
    )
    far = exchange(near, "sec", 1)
    pieces = lax.all_to_all(sent, ("sec", "band"), 0, 0, tiled=True)
    sources = spec_bands * flux_rows
    states = source_weights.shape[0]
    mine = n_sec * lev // (n_sec * n_fld)
    heating = call(
        functools.partial(column_kernel, n_sec, n_fld, lat_pad, slots),
        [((mine, lat, lon), BF16)],
        [SMEM] + [VMEM] * 6,
        [
            pltpu.VMEM((states, slots), F32),
            pltpu.VMEM((slots, mine * LANES), BF16),
            pltpu.VMEM((mine, lat, lon), BF16),
            pltpu.SemaphoreType.DMA((across,)),
        ],
        (counts, source_weights, inverse_rows, block_row, interp, near, far),
        8 * slots * slots * 1024,
        2 * slots * slots,
        "columns",
        HBM,
    )

    spectral = call(
        functools.partial(legendre_kernel, n_sec, n_band, n_fld, lev),
        [((wave_dev, 2, n_fld, n_sec * lev, degrees), BF16)],
        [VMEM, VMEM],
        [
            pltpu.VMEM((wave_dev, 2, n_fld, n_sec * lev, degrees), BF16),
            pltpu.SemaphoreType.DMA((wave_dev,)),
        ],
        (basis, pieces),
        4 * n_sec * n_fld * piece * n_band * LANES * degrees * THIRDS,
        2 * n_sec * n_band * n_fld * piece * LANES,
        "legendre",
        HBM,
    )
    return (spectral, heating)


def solution(mesh):
    return jax.shard_map(
        body,
        mesh=mesh,
        in_specs=(
            P("fld", "sec", "band", None),
            P(("band", "fld"), None, "sec"),
            P(),
            P("band"),
            P("band", None),
            P(),
            P(),
        ),
        out_specs=(P(("band", "fld"), None, None, None, "sec"), P(("sec", "fld"), "band", None)),
        check_vma=False,
    )
```

```python
import functools
import math

import jax
import jax.numpy as jnp
import numpy as np
from jax import lax
from jax.experimental import pallas as pl
from jax.experimental.pallas import tpu as pltpu
from jax.sharding import PartitionSpec as P

BF16 = jnp.bfloat16
F32 = jnp.float32
LANES = 128
THIRDS = 3
VMEM = pl.BlockSpec(memory_space=pltpu.VMEM)
HBM = pl.BlockSpec(memory_space=pltpu.HBM)
SMEM = pl.BlockSpec(memory_space=pltpu.SMEM)
LIMIT = 40 * 1024 * 1024
SMALL = 4 * 1024 * 1024
ROOM = 12000 * 1024
WHOLE = 64 * 1024 * 1024 - ROOM
NT = (((1,), (1,)), ((), ()))


def dft_table(lon, wave_dev, n_band, n_fld):
    values_dev = 2 * wave_dev
    rest = values_dev // THIRDS
    third, fld, band, low = np.meshgrid(
        np.arange(THIRDS), np.arange(n_fld), np.arange(n_band), np.arange(rest), indexing="ij"
    )
    value = third * rest + low
    wave = ((band * n_fld + fld) * wave_dev + value // 2).reshape(-1)
    part = (value % 2).reshape(-1)
    phase = np.arange(lon, dtype=np.int64)[:, None] * wave[None, :] % lon
    angle = phase * (2.0 * math.pi / lon)
    values = np.where(part[None, :] == 0, np.cos(angle), -np.sin(angle)) / math.sqrt(lon)
    return values.astype(np.float32).astype(BF16)


def pack(lev, lat, coeffs, padded, rows):
    group = coeffs.shape[1] // THIRDS
    padded[...] = jnp.zeros_like(padded)
    for level in range(lev):
        for third in range(THIRDS):
            padded[third * lat : (third + 1) * lat, :group] = coeffs[
                level * lat : (level + 1) * lat, third * group : (third + 1) * group
            ]
        rows[pl.ds(level, group, stride=lev), :] = jnp.transpose(padded[...])[:group]


def prepare_kernel(lat, n_band, legendre, inverses, out, out_inverses, wide, rows, turned):
    flux_rows, _, spec_bands = inverses.shape
    for row in range(flux_rows):
        rows[row * flux_rows : (row + 1) * flux_rows, :] = inverses[row].astype(F32)
    for row in range(flux_rows):
        turned[pl.ds(row, spec_bands, stride=flux_rows), :] = jnp.transpose(
            rows[pl.ds(row, flux_rows, stride=flux_rows), :]
        )
    out_inverses[...] = turned[...].astype(BF16)
    waves, degrees, _ = legendre.shape
    wide[...] = jnp.zeros_like(wide)
    lane = lax.broadcasted_iota(jnp.int32, (degrees, LANES), 1)
    for wave in range(waves):
        third, parity = wave // 2, wave % 2
        wide[:, : n_band * lat] = legendre[wave].astype(F32)
        place = third * lat
        live = (lane >= place) & (lane < place + lat)
        for band in range(n_band):
            base = band * lat // LANES * LANES
            moved = pltpu.roll(
                wide[:, base : base + 2 * LANES], (place - (band * lat - base)) % (2 * LANES), 1
            )
            out[band, parity, third * degrees : (third + 1) * degrees, :] = jnp.where(
                live, moved[:, :LANES], 0.0
            ).astype(BF16)


def legendre_kernel(n_sec, n_band, n_fld, lev, weights, pieces, out_hbm, out, sems):
    degrees = out.shape[4]
    copies = []
    half = pieces.shape[2] // 2
    for parity in range(2):
        rows = slice(parity * half, (parity + 1) * half)
        basis = jnp.concatenate([weights[band, parity] for band in range(n_band)], axis=1)
        left = jnp.concatenate(
            [
                jnp.concatenate(
                    [
                        pieces[sec * n_band + band, fld, rows, :]
                        for band in range(n_band)
                    ],
                    axis=1,
                )
                for fld in range(n_fld)
                for sec in range(n_sec)
            ],
            axis=0,
        )
        result = lax.dot_general(left, basis, NT, preferred_element_type=F32)
        for third in range(THIRDS):
            part = result[:, third * degrees : (third + 1) * degrees]
            for fld in range(n_fld):
                for real in range(2):
                    levels = [
                        part[(fld * n_sec + sec) * half + real * lev :][:lev]
                        for sec in range(n_sec)
                    ]
                    out[2 * third + parity, real, fld] = jnp.concatenate(levels, axis=0).astype(
                        BF16
                    )
            wave = 2 * third + parity
            copies.append(
                pltpu.make_async_copy(out.at[wave], out_hbm.at[wave], sems.at[wave])
            )
            copies[-1].start()
    for copy in copies:
        copy.wait()


def slot_rows(blocks, across, lat_pad):
    shift = 16
    factor = -(-(1 << shift) // across)
    lat = lax.shift_right_logical(blocks * factor, shift)
    return (blocks - lat * across) * lat_pad + lat


def local_kernel(lat_pad, grid_hbm, blocks_hbm, interp_hbm, table_hbm, *refs):
    outs = refs[:-11]
    grid, blocks, interp, table, patch, column, selector, padded, rows, totals, sems = refs[-11:]
    lev, lat, lon = grid.shape
    across = lon // LANES
    slots = interp.shape[0]
    depth = patch.shape[0]
    small = [
        pltpu.make_async_copy(blocks_hbm, blocks, sems.at[lev]),
        pltpu.make_async_copy(interp_hbm, interp, sems.at[lev + 1]),
        pltpu.make_async_copy(table_hbm, table, sems.at[lev + 2]),
    ]
    loads = [
        pltpu.make_async_copy(
            grid_hbm.at[pl.ds(level, 1)], grid.at[pl.ds(level, 1)], sems.at[level]
        )
        for level in range(lev)
    ]
    half = lev // 2
    small[0].start()
    for copy in loads[:half]:
        copy.start()
    small[1].start()
    for copy in loads[half:]:
        copy.start()
    small[2].start()
    small[0].wait()
    row = slot_rows(blocks[...], across, lat_pad)
    column[...] = jnp.transpose(jnp.broadcast_to(row, (LANES, slots)))
    chunk = 256
    lane = lax.broadcasted_iota(jnp.int32, (chunk, LANES), 1)
    for start in range(0, slots, chunk):
        mine = column[start : start + chunk, :]
        for base in range(0, depth, LANES):
            selector[start : start + chunk, base : base + LANES] = jnp.where(
                mine == lane + base, 1.0, 0.0
            ).astype(BF16)
    size = outs[0].shape[1]
    bands = outs[0].shape[0] - slots * lev // LANES // size
    place = lax.axis_index("fld")
    for tile in range(across):
        patch[tile * lat_pad + lat : (tile + 1) * lat_pad, :] = jnp.zeros(
            (lat_pad - lat, lev * LANES), BF16
        )
    if depth > across * lat_pad:
        patch[across * lat_pad :, :] = jnp.zeros((depth - across * lat_pad, lev * LANES), BF16)
    for base in (0, half):
        for level in range(base, base + half):
            loads[level].wait()
            for tile in range(across):
                patch[
                    tile * lat_pad : tile * lat_pad + lat, level * LANES : (level + 1) * LANES
                ] = grid[level, :, tile * LANES : (tile + 1) * LANES]
        if base == 0:
            small[1].wait()
        else:
            small[2].wait()
            flat = jnp.concatenate([grid[level] for level in range(lev)], axis=0)
            coeffs = jnp.dot(flat, table[...], preferred_element_type=F32)
            pack(lev, lat, coeffs, padded, rows)
            height = bands * size
            for shift, out in enumerate(outs):
                first = pl.multiple_of((place ^ shift) * height, height)
                part = rows[pl.ds(first, height), :].astype(BF16)
                out[:bands] = part.reshape(bands, size, LANES)
        for start in range(0, slots, chunk):
            top = slice(start, start + chunk)
            picked = jnp.dot(
                selector[top, :],
                patch[:, base * LANES : (base + half) * LANES],
                preferred_element_type=F32,
            )
            weights = interp[top, :].astype(F32)
            total = jnp.zeros((chunk, LANES), F32) if base == 0 else totals[top, :]
            for i in range(half):
                product = picked[:, i * LANES : (i + 1) * LANES] * weights
                total = jnp.where(
                    lane == base + i, jnp.sum(product, axis=1, keepdims=True), total
                )
            if base == 0:
                totals[top, :] = total
                continue
            state = jnp.transpose(total)[:lev].astype(BF16)
            for tile in range(chunk // LANES):
                block, row = divmod((start // LANES + tile) * lev, size)
                for out in outs:
                    out[bands + block, row : row + lev, :] = state[
                        :, tile * LANES : (tile + 1) * LANES
                    ]


def regroup_kernel(n_sec, n_band, shifts, *refs):
    pieces, (_, out, out_state, sems) = refs[:-4], refs[-4:]
    blocks = out_state.shape[1]
    place = lax.axis_index("fld")
    copies = []
    for shift, piece in zip(shifts, pieces):
        fld = place ^ shift
        copies.append((piece.at[pl.ds(n_band, blocks)], out_state.at[fld]))
        for sec in range(n_sec):
            copies.append(
                (piece.at[pl.ds(0, n_band)], out.at[pl.ds(sec * n_band, n_band), fld])
            )
    copies = [pltpu.make_async_copy(*pair, sems.at[i]) for i, pair in enumerate(copies)]
    for copy in copies:
        copy.start()
    for copy in copies:
        copy.wait()


def softplus(x):
    power = jnp.exp(jnp.minimum(x, 80.0))
    return jnp.where(x < -8.0, power, jnp.maximum(x, jnp.log(1.0 + power)))


def column_kernel(n_sec, n_fld, lat_pad, slots, counts, weights, inverses, blocks, interp,
                  near, far, out, state, spread, result, sems):
    lev = near.shape[1] * near.shape[2] * LANES // slots
    place = lax.axis_index("sec")
    for fld in range(n_fld):
        for shift, pieces in enumerate((near, far)):
            row = (fld * n_sec + (place ^ shift)) * lev
            for tile in range(slots // LANES):
                state[
                    pl.ds(pl.multiple_of(row, lev), lev), tile * LANES : (tile + 1) * LANES
                ] = pieces[fld, tile * lev // near.shape[2]][
                    tile * lev % near.shape[2] : tile * lev % near.shape[2] + lev
                ].astype(F32)
    mine, lat, lon = result.shape
    across = lon // LANES
    sources, flux_rows = inverses.shape
    levels = flux_rows // 2
    count = counts[lax.axis_index("band")]
    base = (place * n_fld + lax.axis_index("fld")) * mine
    chunk = 256
    lane = lax.broadcasted_iota(jnp.int32, (1, flux_rows), 1)
    slot = lax.broadcasted_iota(jnp.int32, (chunk, 1), 0)
    column = jnp.transpose(state[...]).astype(BF16)
    tiles = [(top, at) for top in range(0, slots, chunk) for at in range(0, sources, chunk)]

    def gates_of(top, at):
        return jnp.dot(
            column[top : top + chunk], weights[:, at : at + chunk], preferred_element_type=F32
        )

    fluxes = {top: jnp.zeros((chunk, flux_rows), F32) for top in range(0, slots, chunk)}

    def add_flux(top, at, source):
        fluxes[top] = fluxes[top] + jnp.dot(
            source, inverses[at : at + chunk, :], preferred_element_type=F32
        )

    gates = gates_of(*tiles[0])
    before = None
    for i, tile in enumerate(tiles):
        later = gates_of(*tiles[i + 1]) if i + 1 < len(tiles) else None
        source = softplus(gates).astype(BF16)
        if before is not None:
            add_flux(*tiles[i - 1], before)
        gates, before = later, source
    add_flux(*tiles[-1], before)
    for start in range(0, slots, chunk):
        rows = fluxes[start]
        for level in range(mine):
            at = base + level
            plus = (lane == at) | ((lane == at + levels + 1) & (at + 1 < levels))
            minus = (lane == at + levels) | ((lane == at + 1) & (at + 1 < levels))
            terms = jnp.where(plus, rows, 0.0) - jnp.where(minus, rows, 0.0)
            heat = jnp.sum(terms, axis=1, keepdims=True)
            heat = jnp.where(slot + start < count, heat, 0.0).astype(BF16).astype(F32)
            spread[start : start + chunk, level * LANES : (level + 1) * LANES] = (
                heat * interp[start : start + chunk, :].astype(F32)
            ).astype(BF16)
    row = slot_rows(blocks[...], across, lat_pad)
    tiles = max(t for t in range(1, 8) if across % t == 0)
    height = tiles * lat_pad
    copies = []
    for first in range(0, across, tiles):
        match = row == lax.broadcasted_iota(jnp.int32, (height, slots), 0) + first * lat_pad
        left = jnp.where(match, 1.0, 0.0).astype(BF16)
        summed = jnp.dot(left, spread[...], preferred_element_type=F32).astype(BF16)
        for level in range(mine):
            for tile in range(tiles):
                result[level, :, (first + tile) * LANES : (first + tile + 1) * LANES] = summed[
                    tile * lat_pad : tile * lat_pad + lat, level * LANES : (level + 1) * LANES
                ]
        columns = pl.ds(first * LANES, tiles * LANES)
        copies.append(
            pltpu.make_async_copy(
                result.at[:, :, columns], out.at[:, :, columns], sems.at[first // tiles]
            )
        )
        copies[-1].start()
    for copy in copies:
        copy.wait()


def call(kernel, outs, specs, scratch, args, flops, size, name, out_spec=VMEM, limit=LIMIT):
    shapes = [jax.ShapeDtypeStruct(shape, dtype) for shape, dtype in outs]
    single = len(outs) == 1
    return pl.pallas_call(
        kernel,
        out_shape=shapes[0] if single else shapes,
        in_specs=specs,
        out_specs=out_spec if single else [out_spec] * len(outs),
        scratch_shapes=scratch,
        compiler_params=pltpu.CompilerParams(vmem_limit_bytes=limit),
        cost_estimate=pl.CostEstimate(flops=flops, bytes_accessed=size, transcendentals=0),
        name=name,
    )(*args)


def exchange(value, axis, shift):
    return lax.ppermute(value, axis, [(i, i ^ shift) for i in range(lax.axis_size(axis))])


def body(grid, legendre, counts, blocks, interp, source_weights, inverses):
    n_sec = lax.axis_size("sec")
    n_band = lax.axis_size("band")
    n_fld = lax.axis_size("fld")
    lev, lat, lon = grid.shape[1:]
    wave_dev, _, degrees = legendre.shape
    slots = blocks.shape[0]
    across = lon // LANES
    lat_pad = -(-lat // 16) * 16
    rest = 2 * wave_dev // THIRDS
    piece = rest * lev
    block_row = blocks.reshape(1, slots)

    table = jnp.asarray(dft_table(lon, wave_dev, n_band, n_fld))
    group = n_fld * n_band * rest
    padded_group = -(-group // LANES) * LANES
    depth = -(-across * lat_pad // LANES) * LANES
    state_blocks = slots * lev // LANES // piece
    message_blocks = n_band + state_blocks
    messages = call(
        functools.partial(local_kernel, lat_pad),
        [((message_blocks, piece, LANES), BF16)] * n_fld,
        [HBM] * 4,
        [
            pltpu.VMEM((lev, lat, lon), BF16),
            pltpu.VMEM((1, slots), jnp.int32),
            pltpu.VMEM((slots, LANES), BF16),
            pltpu.VMEM(table.shape, BF16),
            pltpu.VMEM((depth, lev * LANES), BF16),
            pltpu.VMEM((slots, LANES), jnp.int32),
            pltpu.VMEM((slots, depth), BF16),
            pltpu.VMEM((LANES, padded_group), F32),
            pltpu.VMEM((group * lev, LANES), F32),
            pltpu.VMEM((slots, LANES), F32),
            pltpu.SemaphoreType.DMA((lev + 3,)),
        ],
        [
            pltpu.with_memory_space_constraint(value, pltpu.HBM)
            for value in (grid.reshape(lev, lat, lon), block_row, interp, table)
        ],
        2 * slots * depth * lev * LANES + 2 * lev * lat * lon * THIRDS * group,
        2 * lev * lat * lon + 2 * slots * LANES,
        "local",
        VMEM,
        WHOLE,
    )
    half = n_fld // 2
    shifts = [half] + list(range(n_fld - 1, half, -1)) + list(range(half - 1, 0, -1))
    arrived = [exchange(messages[shift], "fld", shift) for shift in shifts]
    arrived.append(messages[0])
    spec_bands, flux_rows, _ = inverses.shape
    basis, inverse_rows = call(
        functools.partial(prepare_kernel, lat, n_band),
        [
            ((n_band, 2, THIRDS * degrees, LANES), BF16),
            ((spec_bands * flux_rows, flux_rows), BF16),
        ],
        [VMEM, VMEM],
        [
            pltpu.VMEM((degrees, (n_band * lat // LANES + 2) * LANES), F32),
            pltpu.VMEM((flux_rows * flux_rows, spec_bands), F32),
            pltpu.VMEM((spec_bands * flux_rows, flux_rows), F32),
        ],
        (jnp.swapaxes(legendre, 1, 2), jnp.transpose(inverses, (1, 2, 0))),
        0,
        8 * wave_dev * degrees * n_band * LANES,
        "prepare",
    )
    sent, near = call(
        functools.partial(regroup_kernel, n_sec, n_band, (*shifts, 0)),
        [
            ((n_sec * n_band, n_fld, piece, LANES), BF16),
            ((n_fld, state_blocks, piece, LANES), BF16),
        ],
        [HBM] * (n_fld + 1),
        [pltpu.SemaphoreType.DMA((n_fld * (1 + n_sec),))],
        (*arrived, basis),
        0,
        4 * n_sec * n_band * n_fld * piece * LANES,
        "regroup",
        HBM,
        SMALL,
    )
    far = exchange(near, "sec", 1)
    pieces = lax.all_to_all(sent, ("sec", "band"), 0, 0, tiled=True)
    sources = spec_bands * flux_rows
    states = source_weights.shape[0]
    mine = n_sec * lev // (n_sec * n_fld)
    heating = call(
        functools.partial(column_kernel, n_sec, n_fld, lat_pad, slots),
        [((mine, lat, lon), BF16)],
        [SMEM] + [VMEM] * 6,
        [
            pltpu.VMEM((states, slots), F32),
            pltpu.VMEM((slots, mine * LANES), BF16),
            pltpu.VMEM((mine, lat, lon), BF16),
            pltpu.SemaphoreType.DMA((across,)),
        ],
        (counts, source_weights, inverse_rows, block_row, interp, near, far),
        8 * slots * slots * 1024,
        2 * slots * slots,
        "columns",
        HBM,
    )

    spectral = call(
        functools.partial(legendre_kernel, n_sec, n_band, n_fld, lev),
        [((wave_dev, 2, n_fld, n_sec * lev, degrees), BF16)],
        [VMEM, VMEM],
        [
            pltpu.VMEM((wave_dev, 2, n_fld, n_sec * lev, degrees), BF16),
            pltpu.SemaphoreType.DMA((wave_dev,)),
        ],
        (basis, pieces),
        4 * n_sec * n_fld * piece * n_band * LANES * degrees * THIRDS,
        2 * n_sec * n_band * n_fld * piece * LANES,
        "legendre",
        HBM,
    )
    return (spectral, heating)


def solution(mesh):
    return jax.shard_map(
        body,
        mesh=mesh,
        in_specs=(
            P("fld", "sec", "band", None),
            P(("band", "fld"), None, "sec"),
            P(),
            P("band"),
            P("band", None),
            P(),
            P(),
        ),
        out_specs=(P(("band", "fld"), None, None, None, "sec"), P(("sec", "fld"), "band", None)),
        check_vma=False,
    )
```

```python
import functools
import math

import jax
import jax.numpy as jnp
import numpy as np
from jax import lax
from jax.experimental import pallas as pl
from jax.experimental.pallas import tpu as pltpu
from jax.sharding import PartitionSpec as P

BF16 = jnp.bfloat16
F32 = jnp.float32
LANES = 128
THIRDS = 3
VMEM = pl.BlockSpec(memory_space=pltpu.VMEM)
HBM = pl.BlockSpec(memory_space=pltpu.HBM)
SMEM = pl.BlockSpec(memory_space=pltpu.SMEM)
LIMIT = 40 * 1024 * 1024
SMALL = 4 * 1024 * 1024
ROOM = 12000 * 1024
WHOLE = 64 * 1024 * 1024 - ROOM
NT = (((1,), (1,)), ((), ()))


def dft_table(lon, wave_dev, n_band, n_fld):
    values_dev = 2 * wave_dev
    rest = values_dev // THIRDS
    third, fld, band, low = np.meshgrid(
        np.arange(THIRDS), np.arange(n_fld), np.arange(n_band), np.arange(rest), indexing="ij"
    )
    value = third * rest + low
    wave = ((band * n_fld + fld) * wave_dev + value // 2).reshape(-1)
    part = (value % 2).reshape(-1)
    phase = np.arange(lon, dtype=np.int64)[:, None] * wave[None, :] % lon
    angle = phase * (2.0 * math.pi / lon)
    values = np.where(part[None, :] == 0, np.cos(angle), -np.sin(angle)) / math.sqrt(lon)
    return values.astype(np.float32).astype(BF16)


def pack(lev, lat, coeffs, padded, rows):
    group = coeffs.shape[1] // THIRDS
    padded[...] = jnp.zeros_like(padded)
    for level in range(lev):
        for third in range(THIRDS):
            padded[third * lat : (third + 1) * lat, :group] = coeffs[
                level * lat : (level + 1) * lat, third * group : (third + 1) * group
            ]
        rows[pl.ds(level, group, stride=lev), :] = jnp.transpose(padded[...])[:group]


def prepare_kernel(lat, n_band, legendre, inverses, message, out, out_inverses, out_state, wide,
                   rows, turned):
    out_state[...] = message[n_band:]
    flux_rows, _, spec_bands = inverses.shape
    for row in range(flux_rows):
        rows[row * flux_rows : (row + 1) * flux_rows, :] = inverses[row].astype(F32)
    for row in range(flux_rows):
        turned[pl.ds(row, spec_bands, stride=flux_rows), :] = jnp.transpose(
            rows[pl.ds(row, flux_rows, stride=flux_rows), :]
        )
    out_inverses[...] = turned[...].astype(BF16)
    waves, degrees, _ = legendre.shape
    wide[...] = jnp.zeros_like(wide)
    lane = lax.broadcasted_iota(jnp.int32, (degrees, LANES), 1)
    for wave in range(waves):
        third, parity = wave // 2, wave % 2
        wide[:, : n_band * lat] = legendre[wave].astype(F32)
        place = third * lat
        live = (lane >= place) & (lane < place + lat)
        for band in range(n_band):
            base = band * lat // LANES * LANES
            moved = pltpu.roll(
                wide[:, base : base + 2 * LANES], (place - (band * lat - base)) % (2 * LANES), 1
            )
            out[band, parity, third * degrees : (third + 1) * degrees, :] = jnp.where(
                live, moved[:, :LANES], 0.0
            ).astype(BF16)


def legendre_kernel(n_sec, n_band, n_fld, lev, weights, pieces, out_hbm, out, sems):
    degrees = out.shape[4]
    copies = []
    half = pieces.shape[2] // 2
    for parity in range(2):
        rows = slice(parity * half, (parity + 1) * half)
        basis = jnp.concatenate([weights[band, parity] for band in range(n_band)], axis=1)
        left = jnp.concatenate(
            [
                jnp.concatenate(
                    [
                        pieces[sec * n_band + band, fld, rows, :]
                        for band in range(n_band)
                    ],
                    axis=1,
                )
                for fld in range(n_fld)
                for sec in range(n_sec)
            ],
            axis=0,
        )
        result = lax.dot_general(left, basis, NT, preferred_element_type=F32)
        for third in range(THIRDS):
            part = result[:, third * degrees : (third + 1) * degrees]
            for fld in range(n_fld):
                for real in range(2):
                    levels = [
                        part[(fld * n_sec + sec) * half + real * lev :][:lev]
                        for sec in range(n_sec)
                    ]
                    out[2 * third + parity, real, fld] = jnp.concatenate(levels, axis=0).astype(
                        BF16
                    )
            wave = 2 * third + parity
            copies.append(
                pltpu.make_async_copy(out.at[wave], out_hbm.at[wave], sems.at[wave])
            )
            copies[-1].start()
    for copy in copies:
        copy.wait()


def slot_rows(blocks, across, lat_pad):
    shift = 16
    factor = -(-(1 << shift) // across)
    lat = lax.shift_right_logical(blocks * factor, shift)
    return (blocks - lat * across) * lat_pad + lat


def local_kernel(lat_pad, grid_hbm, blocks_hbm, interp_hbm, table_hbm, *refs):
    outs = refs[:-11]
    grid, blocks, interp, table, patch, column, selector, padded, rows, totals, sems = refs[-11:]
    lev, lat, lon = grid.shape
    across = lon // LANES
    slots = interp.shape[0]
    depth = patch.shape[0]
    small = [
        pltpu.make_async_copy(blocks_hbm, blocks, sems.at[lev]),
        pltpu.make_async_copy(interp_hbm, interp, sems.at[lev + 1]),
        pltpu.make_async_copy(table_hbm, table, sems.at[lev + 2]),
    ]
    loads = [
        pltpu.make_async_copy(
            grid_hbm.at[pl.ds(level, 1)], grid.at[pl.ds(level, 1)], sems.at[level]
        )
        for level in range(lev)
    ]
    half = lev // 2
    small[0].start()
    for copy in loads[:half]:
        copy.start()
    small[1].start()
    for copy in loads[half:]:
        copy.start()
    small[2].start()
    small[0].wait()
    row = slot_rows(blocks[...], across, lat_pad)
    column[...] = jnp.transpose(jnp.broadcast_to(row, (LANES, slots)))
    chunk = 256
    lane = lax.broadcasted_iota(jnp.int32, (chunk, LANES), 1)
    for start in range(0, slots, chunk):
        mine = column[start : start + chunk, :]
        for base in range(0, depth, LANES):
            selector[start : start + chunk, base : base + LANES] = jnp.where(
                mine == lane + base, 1.0, 0.0
            ).astype(BF16)
    size = outs[0].shape[1]
    bands = outs[0].shape[0] - slots * lev // LANES // size
    place = lax.axis_index("fld")
    for tile in range(across):
        patch[tile * lat_pad + lat : (tile + 1) * lat_pad, :] = jnp.zeros(
            (lat_pad - lat, lev * LANES), BF16
        )
    if depth > across * lat_pad:
        patch[across * lat_pad :, :] = jnp.zeros((depth - across * lat_pad, lev * LANES), BF16)
    for base in (0, half):
        for level in range(base, base + half):
            loads[level].wait()
            for tile in range(across):
                patch[
                    tile * lat_pad : tile * lat_pad + lat, level * LANES : (level + 1) * LANES
                ] = grid[level, :, tile * LANES : (tile + 1) * LANES]
        if base == 0:
            small[1].wait()
        else:
            small[2].wait()
            flat = jnp.concatenate([grid[level] for level in range(lev)], axis=0)
            coeffs = jnp.dot(flat, table[...], preferred_element_type=F32)
            pack(lev, lat, coeffs, padded, rows)
            height = bands * size
            for shift, out in enumerate(outs):
                first = pl.multiple_of((place ^ shift) * height, height)
                part = rows[pl.ds(first, height), :].astype(BF16)
                out[:bands] = part.reshape(bands, size, LANES)
        for start in range(0, slots, chunk):
            top = slice(start, start + chunk)
            picked = jnp.dot(
                selector[top, :],
                patch[:, base * LANES : (base + half) * LANES],
                preferred_element_type=F32,
            )
            weights = interp[top, :].astype(F32)
            total = jnp.zeros((chunk, LANES), F32) if base == 0 else totals[top, :]
            for i in range(half):
                product = picked[:, i * LANES : (i + 1) * LANES] * weights
                total = jnp.where(
                    lane == base + i, jnp.sum(product, axis=1, keepdims=True), total
                )
            if base == 0:
                totals[top, :] = total
                continue
            state = jnp.transpose(total)[:lev].astype(BF16)
            for tile in range(chunk // LANES):
                block, row = divmod((start // LANES + tile) * lev, size)
                for out in outs:
                    out[bands + block, row : row + lev, :] = state[
                        :, tile * LANES : (tile + 1) * LANES
                    ]


def regroup_kernel(n_sec, n_band, shifts, *refs):
    pieces, (_, out, out_state, sems) = refs[:-4], refs[-4:]
    blocks = out_state.shape[1]
    place = lax.axis_index("fld")
    copies = []
    for shift, piece in zip(shifts, pieces):
        fld = place ^ shift
        copies.append((piece.at[pl.ds(n_band, blocks)], out_state.at[fld]))
        for sec in range(n_sec):
            copies.append(
                (piece.at[pl.ds(0, n_band)], out.at[pl.ds(sec * n_band, n_band), fld])
            )
    copies = [pltpu.make_async_copy(*pair, sems.at[i]) for i, pair in enumerate(copies)]
    for copy in copies:
        copy.start()
    for copy in copies:
        copy.wait()


def softplus(x):
    power = jnp.exp(jnp.minimum(x, 80.0))
    return jnp.where(x < -8.0, power, jnp.maximum(x, jnp.log(1.0 + power)))


def column_kernel(n_sec, n_fld, lat_pad, slots, counts, weights, inverses, blocks, interp,
                  near, *refs):
    far, (out, state, spread, result, sems) = refs[:n_fld], refs[n_fld:]
    lev = near.shape[1] * near.shape[2] * LANES // slots
    size = near.shape[2]
    place = lax.axis_index("sec")
    for fld in range(n_fld):
        sources = (
            (fld * n_sec + place, near.at[fld]),
            ((lax.axis_index("fld") ^ fld) * n_sec + (place ^ 1), far[fld]),
        )
        for at, pieces in sources:
            row = pl.multiple_of(at * lev, lev)
            for tile in range(slots // LANES):
                block, line = divmod(tile * lev, size)
                state[pl.ds(row, lev), tile * LANES : (tile + 1) * LANES] = pieces[
                    block, line : line + lev
                ].astype(F32)
    mine, lat, lon = result.shape
    across = lon // LANES
    sources, flux_rows = inverses.shape
    levels = flux_rows // 2
    count = counts[lax.axis_index("band")]
    base = (place * n_fld + lax.axis_index("fld")) * mine
    chunk = 256
    lane = lax.broadcasted_iota(jnp.int32, (1, flux_rows), 1)
    slot = lax.broadcasted_iota(jnp.int32, (chunk, 1), 0)
    column = jnp.transpose(state[...]).astype(BF16)
    tiles = [(top, at) for top in range(0, slots, chunk) for at in range(0, sources, chunk)]

    def gates_of(top, at):
        return jnp.dot(
            column[top : top + chunk], weights[:, at : at + chunk], preferred_element_type=F32
        )

    fluxes = {top: jnp.zeros((chunk, flux_rows), F32) for top in range(0, slots, chunk)}

    def add_flux(top, at, source):
        fluxes[top] = fluxes[top] + jnp.dot(
            source, inverses[at : at + chunk, :], preferred_element_type=F32
        )

    gates = gates_of(*tiles[0])
    before = None
    for i, tile in enumerate(tiles):
        later = gates_of(*tiles[i + 1]) if i + 1 < len(tiles) else None
        source = softplus(gates).astype(BF16)
        if before is not None:
            add_flux(*tiles[i - 1], before)
        gates, before = later, source
    add_flux(*tiles[-1], before)
    for start in range(0, slots, chunk):
        rows = fluxes[start]
        for level in range(mine):
            at = base + level
            plus = (lane == at) | ((lane == at + levels + 1) & (at + 1 < levels))
            minus = (lane == at + levels) | ((lane == at + 1) & (at + 1 < levels))
            terms = jnp.where(plus, rows, 0.0) - jnp.where(minus, rows, 0.0)
            heat = jnp.sum(terms, axis=1, keepdims=True)
            heat = jnp.where(slot + start < count, heat, 0.0).astype(BF16).astype(F32)
            spread[start : start + chunk, level * LANES : (level + 1) * LANES] = (
                heat * interp[start : start + chunk, :].astype(F32)
            ).astype(BF16)
    row = slot_rows(blocks[...], across, lat_pad)
    tiles = max(t for t in range(1, 8) if across % t == 0)
    height = tiles * lat_pad
    copies = []
    for first in range(0, across, tiles):
        match = row == lax.broadcasted_iota(jnp.int32, (height, slots), 0) + first * lat_pad
        left = jnp.where(match, 1.0, 0.0).astype(BF16)
        summed = jnp.dot(left, spread[...], preferred_element_type=F32).astype(BF16)
        for level in range(mine):
            for tile in range(tiles):
                result[level, :, (first + tile) * LANES : (first + tile + 1) * LANES] = summed[
                    tile * lat_pad : tile * lat_pad + lat, level * LANES : (level + 1) * LANES
                ]
        columns = pl.ds(first * LANES, tiles * LANES)
        copies.append(
            pltpu.make_async_copy(
                result.at[:, :, columns], out.at[:, :, columns], sems.at[first // tiles]
            )
        )
        copies[-1].start()
    for copy in copies:
        copy.wait()


def call(kernel, outs, specs, scratch, args, flops, size, name, out_spec=VMEM, limit=LIMIT):
    shapes = [jax.ShapeDtypeStruct(shape, dtype) for shape, dtype in outs]
    single = len(outs) == 1
    return pl.pallas_call(
        kernel,
        out_shape=shapes[0] if single else shapes,
        in_specs=specs,
        out_specs=out_spec if single else [out_spec] * len(outs),
        scratch_shapes=scratch,
        compiler_params=pltpu.CompilerParams(vmem_limit_bytes=limit),
        cost_estimate=pl.CostEstimate(flops=flops, bytes_accessed=size, transcendentals=0),
        name=name,
    )(*args)


def exchange(value, axes, shifts):
    sizes = [lax.axis_size(axis) for axis in axes]
    pairs = []
    for i in range(math.prod(sizes)):
        at = np.unravel_index(i, sizes)
        to = [int(a) ^ shift for a, shift in zip(at, shifts)]
        pairs.append((i, int(np.ravel_multi_index(to, sizes))))
    return lax.ppermute(value, axes, pairs)


def body(grid, legendre, counts, blocks, interp, source_weights, inverses):
    n_sec = lax.axis_size("sec")
    n_band = lax.axis_size("band")
    n_fld = lax.axis_size("fld")
    lev, lat, lon = grid.shape[1:]
    wave_dev, _, degrees = legendre.shape
    slots = blocks.shape[0]
    across = lon // LANES
    lat_pad = -(-lat // 16) * 16
    rest = 2 * wave_dev // THIRDS
    piece = rest * lev
    block_row = blocks.reshape(1, slots)

    table = jnp.asarray(dft_table(lon, wave_dev, n_band, n_fld))
    group = n_fld * n_band * rest
    padded_group = -(-group // LANES) * LANES
    depth = -(-across * lat_pad // LANES) * LANES
    state_blocks = slots * lev // LANES // piece
    message_blocks = n_band + state_blocks
    messages = call(
        functools.partial(local_kernel, lat_pad),
        [((message_blocks, piece, LANES), BF16)] * n_fld,
        [HBM] * 4,
        [
            pltpu.VMEM((lev, lat, lon), BF16),
            pltpu.VMEM((1, slots), jnp.int32),
            pltpu.VMEM((slots, LANES), BF16),
            pltpu.VMEM(table.shape, BF16),
            pltpu.VMEM((depth, lev * LANES), BF16),
            pltpu.VMEM((slots, LANES), jnp.int32),
            pltpu.VMEM((slots, depth), BF16),
            pltpu.VMEM((LANES, padded_group), F32),
            pltpu.VMEM((group * lev, LANES), F32),
            pltpu.VMEM((slots, LANES), F32),
            pltpu.SemaphoreType.DMA((lev + 3,)),
        ],
        [
            pltpu.with_memory_space_constraint(value, pltpu.HBM)
            for value in (grid.reshape(lev, lat, lon), block_row, interp, table)
        ],
        2 * slots * depth * lev * LANES + 2 * lev * lat * lon * THIRDS * group,
        2 * lev * lat * lon + 2 * slots * LANES,
        "local",
        VMEM,
        WHOLE,
    )
    half = n_fld // 2
    shifts = [half] + list(range(n_fld - 1, half, -1)) + list(range(half - 1, 0, -1))
    arrived = [exchange(messages[shift], ("fld",), (shift,)) for shift in shifts]
    arrived.append(messages[0])
    spec_bands, flux_rows, _ = inverses.shape
    basis, inverse_rows, state = call(
        functools.partial(prepare_kernel, lat, n_band),
        [
            ((n_band, 2, THIRDS * degrees, LANES), BF16),
            ((spec_bands * flux_rows, flux_rows), BF16),
            ((state_blocks, piece, LANES), BF16),
        ],
        [VMEM, VMEM, VMEM],
        [
            pltpu.VMEM((degrees, (n_band * lat // LANES + 2) * LANES), F32),
            pltpu.VMEM((flux_rows * flux_rows, spec_bands), F32),
            pltpu.VMEM((spec_bands * flux_rows, flux_rows), F32),
        ],
        (jnp.swapaxes(legendre, 1, 2), jnp.transpose(inverses, (1, 2, 0)), messages[0]),
        0,
        8 * wave_dev * degrees * n_band * LANES,
        "prepare",
    )
    sent, near = call(
        functools.partial(regroup_kernel, n_sec, n_band, (*shifts, 0)),
        [
            ((n_sec * n_band, n_fld, piece, LANES), BF16),
            ((n_fld, state_blocks, piece, LANES), BF16),
        ],
        [HBM] * (n_fld + 1),
        [pltpu.SemaphoreType.DMA((n_fld * (1 + n_sec),))],
        (*arrived, basis),
        0,
        4 * n_sec * n_band * n_fld * piece * LANES,
        "regroup",
        HBM,
        SMALL,
    )
    far = [exchange(state, ("sec", "fld"), (1, shift)) for shift in range(n_fld)]
    pieces = lax.all_to_all(sent, ("sec", "band"), 0, 0, tiled=True)
    sources = spec_bands * flux_rows
    states = source_weights.shape[0]
    mine = n_sec * lev // (n_sec * n_fld)
    heating = call(
        functools.partial(column_kernel, n_sec, n_fld, lat_pad, slots),
        [((mine, lat, lon), BF16)],
        [SMEM] + [VMEM] * (5 + n_fld),
        [
            pltpu.VMEM((states, slots), F32),
            pltpu.VMEM((slots, mine * LANES), BF16),
            pltpu.VMEM((mine, lat, lon), BF16),
            pltpu.SemaphoreType.DMA((across,)),
        ],
        (counts, source_weights, inverse_rows, block_row, interp, near, *far),
        8 * slots * slots * 1024,
        2 * slots * slots,
        "columns",
        HBM,
    )

    spectral = call(
        functools.partial(legendre_kernel, n_sec, n_band, n_fld, lev),
        [((wave_dev, 2, n_fld, n_sec * lev, degrees), BF16)],
        [VMEM, VMEM],
        [
            pltpu.VMEM((wave_dev, 2, n_fld, n_sec * lev, degrees), BF16),
            pltpu.SemaphoreType.DMA((wave_dev,)),
        ],
        (basis, pieces),
        4 * n_sec * n_fld * piece * n_band * LANES * degrees * THIRDS,
        2 * n_sec * n_band * n_fld * piece * LANES,
        "legendre",
        HBM,
    )
    return (spectral, heating)


def solution(mesh):
    return jax.shard_map(
        body,
        mesh=mesh,
        in_specs=(
            P("fld", "sec", "band", None),
            P(("band", "fld"), None, "sec"),
            P(),
            P("band"),
            P("band", None),
            P(),
            P(),
        ),
        out_specs=(P(("band", "fld"), None, None, None, "sec"), P(("sec", "fld"), "band", None)),
        check_vma=False,
    )
```

```python
import functools
import math

import jax
import jax.numpy as jnp
import numpy as np
from jax import lax
from jax.experimental import pallas as pl
from jax.experimental.pallas import tpu as pltpu
from jax.sharding import PartitionSpec as P

BF16 = jnp.bfloat16
F32 = jnp.float32
LANES = 128
THIRDS = 3
VMEM = pl.BlockSpec(memory_space=pltpu.VMEM)
HBM = pl.BlockSpec(memory_space=pltpu.HBM)
SMEM = pl.BlockSpec(memory_space=pltpu.SMEM)
LIMIT = 40 * 1024 * 1024
SMALL = 4 * 1024 * 1024
ROOM = 12000 * 1024
WHOLE = 64 * 1024 * 1024 - ROOM
NT = (((1,), (1,)), ((), ()))


def dft_table(lon, wave_dev, n_band, n_fld):
    values_dev = 2 * wave_dev
    rest = values_dev // THIRDS
    third, fld, band, low = np.meshgrid(
        np.arange(THIRDS), np.arange(n_fld), np.arange(n_band), np.arange(rest), indexing="ij"
    )
    value = third * rest + low
    wave = ((band * n_fld + fld) * wave_dev + value // 2).reshape(-1)
    part = (value % 2).reshape(-1)
    phase = np.arange(lon, dtype=np.int64)[:, None] * wave[None, :] % lon
    angle = phase * (2.0 * math.pi / lon)
    values = np.where(part[None, :] == 0, np.cos(angle), -np.sin(angle)) / math.sqrt(lon)
    return values.astype(np.float32).astype(BF16)


def pack(lev, lat, coeffs, padded, rows):
    group = coeffs.shape[1] // THIRDS
    padded[...] = jnp.zeros_like(padded)
    for level in range(lev):
        for third in range(THIRDS):
            padded[third * lat : (third + 1) * lat, :group] = coeffs[
                level * lat : (level + 1) * lat, third * group : (third + 1) * group
            ]
        rows[pl.ds(level, group, stride=lev), :] = jnp.transpose(padded[...])[:group]


def prepare_kernel(lat, n_band, legendre_hbm, inverses_hbm, weights_hbm, interp_hbm, out,
                   out_inverses, out_weights, out_interp, legendre, inverses, wide, rows, turned,
                   sems):
    copies = [
        pltpu.make_async_copy(*pair, sems.at[i])
        for i, pair in enumerate(
            (
                (inverses_hbm, inverses),
                (legendre_hbm, legendre),
                (weights_hbm, out_weights),
                (interp_hbm, out_interp),
            )
        )
    ]
    for copy in copies:
        copy.start()
    copies[0].wait()
    flux_rows, _, spec_bands = inverses.shape
    for row in range(flux_rows):
        rows[row * flux_rows : (row + 1) * flux_rows, :] = inverses[row].astype(F32)
    for row in range(flux_rows):
        turned[pl.ds(row, spec_bands, stride=flux_rows), :] = jnp.transpose(
            rows[pl.ds(row, flux_rows, stride=flux_rows), :]
        )
    out_inverses[...] = turned[...].astype(BF16)
    waves, degrees, _ = legendre.shape
    wide[...] = jnp.zeros_like(wide)
    copies[1].wait()
    lane = lax.broadcasted_iota(jnp.int32, (degrees, LANES), 1)
    for wave in range(waves):
        third, parity = wave // 2, wave % 2
        wide[:, : n_band * lat] = legendre[wave].astype(F32)
        place = third * lat
        live = (lane >= place) & (lane < place + lat)
        for band in range(n_band):
            base = band * lat // LANES * LANES
            moved = pltpu.roll(
                wide[:, base : base + 2 * LANES], (place - (band * lat - base)) % (2 * LANES), 1
            )
            out[band, parity, third * degrees : (third + 1) * degrees, :] = jnp.where(
                live, moved[:, :LANES], 0.0
            ).astype(BF16)
    for copy in copies[2:]:
        copy.wait()


def legendre_kernel(n_sec, n_band, n_fld, lev, weights, pieces, out_hbm, out, sems):
    degrees = out.shape[4]
    copies = []
    half = pieces.shape[2] // 2
    for parity in range(2):
        rows = slice(parity * half, (parity + 1) * half)
        basis = jnp.concatenate([weights[band, parity] for band in range(n_band)], axis=1)
        left = jnp.concatenate(
            [
                jnp.concatenate(
                    [
                        pieces[sec * n_band + band, fld, rows, :]
                        for band in range(n_band)
                    ],
                    axis=1,
                )
                for fld in range(n_fld)
                for sec in range(n_sec)
            ],
            axis=0,
        )
        result = lax.dot_general(left, basis, NT, preferred_element_type=F32)
        for third in range(THIRDS):
            part = result[:, third * degrees : (third + 1) * degrees]
            for fld in range(n_fld):
                for real in range(2):
                    levels = [
                        part[(fld * n_sec + sec) * half + real * lev :][:lev]
                        for sec in range(n_sec)
                    ]
                    out[2 * third + parity, real, fld] = jnp.concatenate(levels, axis=0).astype(
                        BF16
                    )
            wave = 2 * third + parity
            copies.append(
                pltpu.make_async_copy(out.at[wave], out_hbm.at[wave], sems.at[wave])
            )
            copies[-1].start()
    for copy in copies:
        copy.wait()


def slot_rows(blocks, across, lat_pad):
    shift = 16
    factor = -(-(1 << shift) // across)
    lat = lax.shift_right_logical(blocks * factor, shift)
    return (blocks - lat * across) * lat_pad + lat


def local_kernel(lat_pad, grid_hbm, blocks_hbm, interp_hbm, table_hbm, *refs):
    outs = refs[:-11]
    grid, blocks, interp, table, patch, column, selector, padded, rows, totals, sems = refs[-11:]
    lev, lat, lon = grid.shape
    across = lon // LANES
    slots = interp.shape[0]
    depth = patch.shape[0]
    small = [
        pltpu.make_async_copy(blocks_hbm, blocks, sems.at[lev]),
        pltpu.make_async_copy(interp_hbm, interp, sems.at[lev + 1]),
        pltpu.make_async_copy(table_hbm, table, sems.at[lev + 2]),
    ]
    loads = [
        pltpu.make_async_copy(
            grid_hbm.at[pl.ds(level, 1)], grid.at[pl.ds(level, 1)], sems.at[level]
        )
        for level in range(lev)
    ]
    half = lev // 2
    small[0].start()
    for copy in loads[:half]:
        copy.start()
    small[1].start()
    for copy in loads[half:]:
        copy.start()
    small[2].start()
    small[0].wait()
    row = slot_rows(blocks[...], across, lat_pad)
    column[...] = jnp.transpose(jnp.broadcast_to(row, (LANES, slots)))
    chunk = 256
    lane = lax.broadcasted_iota(jnp.int32, (chunk, LANES), 1)
    for start in range(0, slots, chunk):
        mine = column[start : start + chunk, :]
        for base in range(0, depth, LANES):
            selector[start : start + chunk, base : base + LANES] = jnp.where(
                mine == lane + base, 1.0, 0.0
            ).astype(BF16)
    size = outs[0].shape[1]
    bands = outs[0].shape[0] - slots * lev // LANES // size
    place = lax.axis_index("fld")
    for tile in range(across):
        patch[tile * lat_pad + lat : (tile + 1) * lat_pad, :] = jnp.zeros(
            (lat_pad - lat, lev * LANES), BF16
        )
    if depth > across * lat_pad:
        patch[across * lat_pad :, :] = jnp.zeros((depth - across * lat_pad, lev * LANES), BF16)
    for base in (0, half):
        for level in range(base, base + half):
            loads[level].wait()
            for tile in range(across):
                patch[
                    tile * lat_pad : tile * lat_pad + lat, level * LANES : (level + 1) * LANES
                ] = grid[level, :, tile * LANES : (tile + 1) * LANES]
        if base == 0:
            small[1].wait()
        else:
            small[2].wait()
            flat = jnp.concatenate([grid[level] for level in range(lev)], axis=0)
            coeffs = jnp.dot(flat, table[...], preferred_element_type=F32)
            pack(lev, lat, coeffs, padded, rows)
            height = bands * size
            for shift, out in enumerate(outs):
                first = pl.multiple_of((place ^ shift) * height, height)
                part = rows[pl.ds(first, height), :].astype(BF16)
                out[:bands] = part.reshape(bands, size, LANES)
        for start in range(0, slots, chunk):
            top = slice(start, start + chunk)
            picked = jnp.dot(
                selector[top, :],
                patch[:, base * LANES : (base + half) * LANES],
                preferred_element_type=F32,
            )
            weights = interp[top, :].astype(F32)
            total = jnp.zeros((chunk, LANES), F32) if base == 0 else totals[top, :]
            for i in range(half):
                product = picked[:, i * LANES : (i + 1) * LANES] * weights
                total = jnp.where(
                    lane == base + i, jnp.sum(product, axis=1, keepdims=True), total
                )
            if base == 0:
                totals[top, :] = total
                continue
            state = jnp.transpose(total)[:lev].astype(BF16)
            for tile in range(chunk // LANES):
                block, row = divmod((start // LANES + tile) * lev, size)
                for out in outs:
                    out[bands + block, row : row + lev, :] = state[
                        :, tile * LANES : (tile + 1) * LANES
                    ]


def regroup_kernel(n_sec, n_band, shifts, *refs):
    pieces, (_, out, out_state, sems) = refs[:-4], refs[-4:]
    blocks = out_state.shape[1]
    place = lax.axis_index("fld")
    copies = []
    for shift, piece in zip(shifts, pieces):
        fld = place ^ shift
        copies.append((piece.at[pl.ds(n_band, blocks)], out_state.at[fld]))
        for sec in range(n_sec):
            copies.append(
                (piece.at[pl.ds(0, n_band)], out.at[pl.ds(sec * n_band, n_band), fld])
            )
    copies = [pltpu.make_async_copy(*pair, sems.at[i]) for i, pair in enumerate(copies)]
    for copy in copies:
        copy.start()
    for copy in copies:
        copy.wait()


def softplus(x):
    power = jnp.exp(jnp.minimum(x, 80.0))
    return jnp.where(x < -8.0, power, jnp.maximum(x, jnp.log(1.0 + power)))


def column_kernel(n_sec, n_fld, lat_pad, slots, counts, weights, inverses, blocks, interp,
                  near, far, out, state, spread, result, sems):
    lev = near.shape[1] * near.shape[2] * LANES // slots
    place = lax.axis_index("sec")
    for fld in range(n_fld):
        for shift, pieces in enumerate((near, far)):
            row = (fld * n_sec + (place ^ shift)) * lev
            for tile in range(slots // LANES):
                state[
                    pl.ds(pl.multiple_of(row, lev), lev), tile * LANES : (tile + 1) * LANES
                ] = pieces[fld, tile * lev // near.shape[2]][
                    tile * lev % near.shape[2] : tile * lev % near.shape[2] + lev
                ].astype(F32)
    mine, lat, lon = result.shape
    across = lon // LANES
    sources, flux_rows = inverses.shape
    levels = flux_rows // 2
    count = counts[lax.axis_index("band")]
    base = (place * n_fld + lax.axis_index("fld")) * mine
    chunk = 256
    lane = lax.broadcasted_iota(jnp.int32, (1, flux_rows), 1)
    slot = lax.broadcasted_iota(jnp.int32, (chunk, 1), 0)
    column = jnp.transpose(state[...]).astype(BF16)
    tiles = [(top, at) for top in range(0, slots, chunk) for at in range(0, sources, chunk)]

    def gates_of(top, at):
        return jnp.dot(
            column[top : top + chunk], weights[:, at : at + chunk], preferred_element_type=F32
        )

    fluxes = {top: jnp.zeros((chunk, flux_rows), F32) for top in range(0, slots, chunk)}

    def add_flux(top, at, source):
        fluxes[top] = fluxes[top] + jnp.dot(
            source, inverses[at : at + chunk, :], preferred_element_type=F32
        )

    gates = gates_of(*tiles[0])
    before = None
    for i, tile in enumerate(tiles):
        later = gates_of(*tiles[i + 1]) if i + 1 < len(tiles) else None
        source = softplus(gates).astype(BF16)
        if before is not None:
            add_flux(*tiles[i - 1], before)
        gates, before = later, source
    add_flux(*tiles[-1], before)
    for start in range(0, slots, chunk):
        rows = fluxes[start]
        for level in range(mine):
            at = base + level
            plus = (lane == at) | ((lane == at + levels + 1) & (at + 1 < levels))
            minus = (lane == at + levels) | ((lane == at + 1) & (at + 1 < levels))
            terms = jnp.where(plus, rows, 0.0) - jnp.where(minus, rows, 0.0)
            heat = jnp.sum(terms, axis=1, keepdims=True)
            heat = jnp.where(slot + start < count, heat, 0.0).astype(BF16).astype(F32)
            spread[start : start + chunk, level * LANES : (level + 1) * LANES] = (
                heat * interp[start : start + chunk, :].astype(F32)
            ).astype(BF16)
    row = slot_rows(blocks[...], across, lat_pad)
    tiles = max(t for t in range(1, 8) if across % t == 0)
    height = tiles * lat_pad
    copies = []
    for first in range(0, across, tiles):
        match = row == lax.broadcasted_iota(jnp.int32, (height, slots), 0) + first * lat_pad
        left = jnp.where(match, 1.0, 0.0).astype(BF16)
        summed = jnp.dot(left, spread[...], preferred_element_type=F32).astype(BF16)
        for level in range(mine):
            for tile in range(tiles):
                result[level, :, (first + tile) * LANES : (first + tile + 1) * LANES] = summed[
                    tile * lat_pad : tile * lat_pad + lat, level * LANES : (level + 1) * LANES
                ]
        columns = pl.ds(first * LANES, tiles * LANES)
        copies.append(
            pltpu.make_async_copy(
                result.at[:, :, columns], out.at[:, :, columns], sems.at[first // tiles]
            )
        )
        copies[-1].start()
    for copy in copies:
        copy.wait()


def call(kernel, outs, specs, scratch, args, flops, size, name, out_spec=VMEM, limit=LIMIT):
    shapes = [jax.ShapeDtypeStruct(shape, dtype) for shape, dtype in outs]
    single = len(outs) == 1
    return pl.pallas_call(
        kernel,
        out_shape=shapes[0] if single else shapes,
        in_specs=specs,
        out_specs=out_spec if single else [out_spec] * len(outs),
        scratch_shapes=scratch,
        compiler_params=pltpu.CompilerParams(vmem_limit_bytes=limit),
        cost_estimate=pl.CostEstimate(flops=flops, bytes_accessed=size, transcendentals=0),
        name=name,
    )(*args)


def exchange(value, axis, shift):
    return lax.ppermute(value, axis, [(i, i ^ shift) for i in range(lax.axis_size(axis))])


def body(grid, legendre, counts, blocks, interp, source_weights, inverses):
    n_sec = lax.axis_size("sec")
    n_band = lax.axis_size("band")
    n_fld = lax.axis_size("fld")
    lev, lat, lon = grid.shape[1:]
    wave_dev, _, degrees = legendre.shape
    slots = blocks.shape[0]
    across = lon // LANES
    lat_pad = -(-lat // 16) * 16
    rest = 2 * wave_dev // THIRDS
    piece = rest * lev
    block_row = blocks.reshape(1, slots)

    table = jnp.asarray(dft_table(lon, wave_dev, n_band, n_fld))
    group = n_fld * n_band * rest
    padded_group = -(-group // LANES) * LANES
    depth = -(-across * lat_pad // LANES) * LANES
    state_blocks = slots * lev // LANES // piece
    message_blocks = n_band + state_blocks
    messages = call(
        functools.partial(local_kernel, lat_pad),
        [((message_blocks, piece, LANES), BF16)] * n_fld,
        [HBM] * 4,
        [
            pltpu.VMEM((lev, lat, lon), BF16),
            pltpu.VMEM((1, slots), jnp.int32),
            pltpu.VMEM((slots, LANES), BF16),
            pltpu.VMEM(table.shape, BF16),
            pltpu.VMEM((depth, lev * LANES), BF16),
            pltpu.VMEM((slots, LANES), jnp.int32),
            pltpu.VMEM((slots, depth), BF16),
            pltpu.VMEM((LANES, padded_group), F32),
            pltpu.VMEM((group * lev, LANES), F32),
            pltpu.VMEM((slots, LANES), F32),
            pltpu.SemaphoreType.DMA((lev + 3,)),
        ],
        [
            pltpu.with_memory_space_constraint(value, pltpu.HBM)
            for value in (grid.reshape(lev, lat, lon), block_row, interp, table)
        ],
        2 * slots * depth * lev * LANES + 2 * lev * lat * lon * THIRDS * group,
        2 * lev * lat * lon + 2 * slots * LANES,
        "local",
        VMEM,
        WHOLE,
    )
    half = n_fld // 2
    shifts = [half] + list(range(n_fld - 1, half, -1)) + list(range(half - 1, 0, -1))
    arrived = [exchange(messages[shift], "fld", shift) for shift in shifts]
    arrived.append(messages[0])
    spec_bands, flux_rows, _ = inverses.shape
    basis, inverse_rows, gate_weights, slot_weights = call(
        functools.partial(prepare_kernel, lat, n_band),
        [
            ((n_band, 2, THIRDS * degrees, LANES), BF16),
            ((spec_bands * flux_rows, flux_rows), BF16),
            (source_weights.shape, BF16),
            (interp.shape, BF16),
        ],
        [HBM] * 4,
        [
            pltpu.VMEM((wave_dev, degrees, n_band * lat), BF16),
            pltpu.VMEM((flux_rows, flux_rows, spec_bands), BF16),
            pltpu.VMEM((degrees, (n_band * lat // LANES + 2) * LANES), F32),
            pltpu.VMEM((flux_rows * flux_rows, spec_bands), F32),
            pltpu.VMEM((spec_bands * flux_rows, flux_rows), F32),
            pltpu.SemaphoreType.DMA((4,)),
        ],
        [
            pltpu.with_memory_space_constraint(value, pltpu.HBM)
            for value in (
                jnp.swapaxes(legendre, 1, 2),
                jnp.transpose(inverses, (1, 2, 0)),
                source_weights,
                interp,
            )
        ],
        0,
        8 * wave_dev * degrees * n_band * LANES,
        "prepare",
    )
    sent, near = call(
        functools.partial(regroup_kernel, n_sec, n_band, (*shifts, 0)),
        [
            ((n_sec * n_band, n_fld, piece, LANES), BF16),
            ((n_fld, state_blocks, piece, LANES), BF16),
        ],
        [HBM] * (n_fld + 1),
        [pltpu.SemaphoreType.DMA((n_fld * (1 + n_sec),))],
        (*arrived, basis),
        0,
        4 * n_sec * n_band * n_fld * piece * LANES,
        "regroup",
        HBM,
        SMALL,
    )
    far = exchange(near, "sec", 1)
    pieces = lax.all_to_all(sent, ("sec", "band"), 0, 0, tiled=True)
    sources = spec_bands * flux_rows
    states = source_weights.shape[0]
    mine = n_sec * lev // (n_sec * n_fld)
    heating = call(
        functools.partial(column_kernel, n_sec, n_fld, lat_pad, slots),
        [((mine, lat, lon), BF16)],
        [SMEM] + [VMEM] * 6,
        [
            pltpu.VMEM((states, slots), F32),
            pltpu.VMEM((slots, mine * LANES), BF16),
            pltpu.VMEM((mine, lat, lon), BF16),
            pltpu.SemaphoreType.DMA((across,)),
        ],
        (counts, gate_weights, inverse_rows, block_row, slot_weights, near, far),
        8 * slots * slots * 1024,
        2 * slots * slots,
        "columns",
        HBM,
    )

    spectral = call(
        functools.partial(legendre_kernel, n_sec, n_band, n_fld, lev),
        [((wave_dev, 2, n_fld, n_sec * lev, degrees), BF16)],
        [VMEM, VMEM],
        [
            pltpu.VMEM((wave_dev, 2, n_fld, n_sec * lev, degrees), BF16),
            pltpu.SemaphoreType.DMA((wave_dev,)),
        ],
        (basis, pieces),
        4 * n_sec * n_fld * piece * n_band * LANES * degrees * THIRDS,
        2 * n_sec * n_band * n_fld * piece * LANES,
        "legendre",
        HBM,
    )
    return (spectral, heating)


def solution(mesh):
    return jax.shard_map(
        body,
        mesh=mesh,
        in_specs=(
            P("fld", "sec", "band", None),
            P(("band", "fld"), None, "sec"),
            P(),
            P("band"),
            P("band", None),
            P(),
            P(),
        ),
        out_specs=(P(("band", "fld"), None, None, None, "sec"), P(("sec", "fld"), "band", None)),
        check_vma=False,
    )
```

```python
import functools
import math

import jax
import jax.numpy as jnp
import numpy as np
from jax import lax
from jax.experimental import pallas as pl
from jax.experimental.pallas import tpu as pltpu
from jax.sharding import PartitionSpec as P

BF16 = jnp.bfloat16
F32 = jnp.float32
LANES = 128
THIRDS = 3
VMEM = pl.BlockSpec(memory_space=pltpu.VMEM)
HBM = pl.BlockSpec(memory_space=pltpu.HBM)
SMEM = pl.BlockSpec(memory_space=pltpu.SMEM)
LIMIT = 40 * 1024 * 1024
SMALL = 4 * 1024 * 1024
ROOM = 12000 * 1024
WHOLE = 64 * 1024 * 1024 - ROOM
NT = (((1,), (1,)), ((), ()))


def dft_table(lon, wave_dev, n_band, n_fld):
    values_dev = 2 * wave_dev
    rest = values_dev // THIRDS
    third, fld, band, low = np.meshgrid(
        np.arange(THIRDS), np.arange(n_fld), np.arange(n_band), np.arange(rest), indexing="ij"
    )
    value = third * rest + low
    wave = ((band * n_fld + fld) * wave_dev + value // 2).reshape(-1)
    part = (value % 2).reshape(-1)
    phase = np.arange(lon, dtype=np.int64)[:, None] * wave[None, :] % lon
    angle = phase * (2.0 * math.pi / lon)
    values = np.where(part[None, :] == 0, np.cos(angle), -np.sin(angle)) / math.sqrt(lon)
    return values.astype(np.float32).astype(BF16)


def pack(level, lev, lat, coeffs, padded, rows):
    group = coeffs.shape[1] // THIRDS
    for third in range(THIRDS):
        padded[level, third * lat : (third + 1) * lat, :group] = coeffs[
            level * lat : (level + 1) * lat, third * group : (third + 1) * group
        ]
    rows[pl.ds(level, group, stride=lev), :] = jnp.transpose(padded[level])[:group]


def prepare_kernel(lat, n_band, legendre, inverses, out, out_inverses, wide, rows, turned):
    flux_rows, _, spec_bands = inverses.shape
    for row in range(flux_rows):
        rows[row * flux_rows : (row + 1) * flux_rows, :] = inverses[row].astype(F32)
    for row in range(flux_rows):
        turned[pl.ds(row, spec_bands, stride=flux_rows), :] = jnp.transpose(
            rows[pl.ds(row, flux_rows, stride=flux_rows), :]
        )
    out_inverses[...] = turned[...].astype(BF16)
    waves, degrees, _ = legendre.shape
    wide[...] = jnp.zeros_like(wide)
    lane = lax.broadcasted_iota(jnp.int32, (degrees, LANES), 1)
    for wave in range(waves):
        third, parity = wave // 2, wave % 2
        wide[:, : n_band * lat] = legendre[wave].astype(F32)
        place = third * lat
        live = (lane >= place) & (lane < place + lat)
        for band in range(n_band):
            base = band * lat // LANES * LANES
            moved = pltpu.roll(
                wide[:, base : base + 2 * LANES], (place - (band * lat - base)) % (2 * LANES), 1
            )
            out[band, parity, third * degrees : (third + 1) * degrees, :] = jnp.where(
                live, moved[:, :LANES], 0.0
            ).astype(BF16)


def legendre_kernel(n_sec, n_band, n_fld, lev, weights, pieces, out_hbm, out, sems):
    degrees = out.shape[4]
    copies = []
    half = pieces.shape[2] // 2
    for parity in range(2):
        rows = slice(parity * half, (parity + 1) * half)
        basis = jnp.concatenate([weights[band, parity] for band in range(n_band)], axis=1)
        left = jnp.concatenate(
            [
                jnp.concatenate(
                    [
                        pieces[sec * n_band + band, fld, rows, :]
                        for band in range(n_band)
                    ],
                    axis=1,
                )
                for fld in range(n_fld)
                for sec in range(n_sec)
            ],
            axis=0,
        )
        result = lax.dot_general(left, basis, NT, preferred_element_type=F32)
        for third in range(THIRDS):
            part = result[:, third * degrees : (third + 1) * degrees]
            for fld in range(n_fld):
                for real in range(2):
                    levels = [
                        part[(fld * n_sec + sec) * half + real * lev :][:lev]
                        for sec in range(n_sec)
                    ]
                    out[2 * third + parity, real, fld] = jnp.concatenate(levels, axis=0).astype(
                        BF16
                    )
            wave = 2 * third + parity
            copies.append(
                pltpu.make_async_copy(out.at[wave], out_hbm.at[wave], sems.at[wave])
            )
            copies[-1].start()
    for copy in copies:
        copy.wait()


def slot_rows(blocks, across, lat_pad):
    shift = 16
    factor = -(-(1 << shift) // across)
    lat = lax.shift_right_logical(blocks * factor, shift)
    return (blocks - lat * across) * lat_pad + lat


def local_kernel(lat_pad, grid_hbm, blocks_hbm, interp_hbm, table_hbm, *refs):
    outs = refs[:-11]
    grid, blocks, interp, table, patch, column, selector, padded, rows, totals, sems = refs[-11:]
    lev, lat, lon = grid.shape
    across = lon // LANES
    slots = interp.shape[0]
    depth = patch.shape[0]
    small = [
        pltpu.make_async_copy(blocks_hbm, blocks, sems.at[lev]),
        pltpu.make_async_copy(interp_hbm, interp, sems.at[lev + 1]),
        pltpu.make_async_copy(table_hbm, table, sems.at[lev + 2]),
    ]
    loads = [
        pltpu.make_async_copy(
            grid_hbm.at[pl.ds(level, 1)], grid.at[pl.ds(level, 1)], sems.at[level]
        )
        for level in range(lev)
    ]
    half = lev // 2
    small[0].start()
    for copy in loads[:half]:
        copy.start()
    small[1].start()
    for copy in loads[half:]:
        copy.start()
    small[2].start()
    small[0].wait()
    row = slot_rows(blocks[...], across, lat_pad)
    column[...] = jnp.transpose(jnp.broadcast_to(row, (LANES, slots)))
    chunk = 256
    lane = lax.broadcasted_iota(jnp.int32, (chunk, LANES), 1)
    for start in range(0, slots, chunk):
        mine = column[start : start + chunk, :]
        for base in range(0, depth, LANES):
            selector[start : start + chunk, base : base + LANES] = jnp.where(
                mine == lane + base, 1.0, 0.0
            ).astype(BF16)
    size = outs[0].shape[1]
    bands = outs[0].shape[0] - slots * lev // LANES // size
    place = lax.axis_index("fld")
    for tile in range(across):
        patch[tile * lat_pad + lat : (tile + 1) * lat_pad, :] = jnp.zeros(
            (lat_pad - lat, lev * LANES), BF16
        )
    if depth > across * lat_pad:
        patch[across * lat_pad :, :] = jnp.zeros((depth - across * lat_pad, lev * LANES), BF16)
    padded[...] = jnp.zeros_like(padded)
    for base in (0, half):
        for level in range(base, base + half):
            loads[level].wait()
            for tile in range(across):
                patch[
                    tile * lat_pad : tile * lat_pad + lat, level * LANES : (level + 1) * LANES
                ] = grid[level, :, tile * LANES : (tile + 1) * LANES]
        if base == 0:
            small[1].wait()
        else:
            small[2].wait()
            flat = jnp.concatenate([grid[level] for level in range(lev)], axis=0)
            coeffs = jnp.dot(flat, table[...], preferred_element_type=F32)
        for start in range(0, slots, chunk):
            top = slice(start, start + chunk)
            picked = jnp.dot(
                selector[top, :],
                patch[:, base * LANES : (base + half) * LANES],
                preferred_element_type=F32,
            )
            if base > 0:
                share = -(-lev * chunk // slots)
                first = start // chunk * share
                for level in range(first, min(first + share, lev)):
                    pack(level, lev, lat, coeffs, padded, rows)
            weights = interp[top, :].astype(F32)
            total = jnp.zeros((chunk, LANES), F32) if base == 0 else totals[top, :]
            for i in range(half):
                product = picked[:, i * LANES : (i + 1) * LANES] * weights
                total = jnp.where(
                    lane == base + i, jnp.sum(product, axis=1, keepdims=True), total
                )
            if base == 0:
                totals[top, :] = total
                continue
            state = jnp.transpose(total)[:lev].astype(BF16)
            for tile in range(chunk // LANES):
                block, row = divmod((start // LANES + tile) * lev, size)
                for out in outs:
                    out[bands + block, row : row + lev, :] = state[
                        :, tile * LANES : (tile + 1) * LANES
                    ]
    height = bands * size
    for shift, out in enumerate(outs):
        first = pl.multiple_of((place ^ shift) * height, height)
        part = rows[pl.ds(first, height), :].astype(BF16)
        out[:bands] = part.reshape(bands, size, LANES)


def regroup_kernel(n_sec, n_band, shifts, *refs):
    pieces, (_, out, out_state, sems) = refs[:-4], refs[-4:]
    blocks = out_state.shape[1]
    place = lax.axis_index("fld")
    copies = []
    for shift, piece in zip(shifts, pieces):
        fld = place ^ shift
        copies.append((piece.at[pl.ds(n_band, blocks)], out_state.at[fld]))
        for sec in range(n_sec):
            copies.append(
                (piece.at[pl.ds(0, n_band)], out.at[pl.ds(sec * n_band, n_band), fld])
            )
    copies = [pltpu.make_async_copy(*pair, sems.at[i]) for i, pair in enumerate(copies)]
    for copy in copies:
        copy.start()
    for copy in copies:
        copy.wait()


def softplus(x):
    power = jnp.exp(jnp.minimum(x, 80.0))
    return jnp.where(x < -8.0, power, jnp.maximum(x, jnp.log(1.0 + power)))


def column_kernel(n_sec, n_fld, lat_pad, slots, counts, weights, inverses, blocks, interp,
                  near, far, out, state, spread, result, sems):
    lev = near.shape[1] * near.shape[2] * LANES // slots
    place = lax.axis_index("sec")
    for fld in range(n_fld):
        for shift, pieces in enumerate((near, far)):
            row = (fld * n_sec + (place ^ shift)) * lev
            for tile in range(slots // LANES):
                state[
                    pl.ds(pl.multiple_of(row, lev), lev), tile * LANES : (tile + 1) * LANES
                ] = pieces[fld, tile * lev // near.shape[2]][
                    tile * lev % near.shape[2] : tile * lev % near.shape[2] + lev
                ].astype(F32)
    mine, lat, lon = result.shape
    across = lon // LANES
    sources, flux_rows = inverses.shape
    levels = flux_rows // 2
    count = counts[lax.axis_index("band")]
    base = (place * n_fld + lax.axis_index("fld")) * mine
    chunk = 256
    lane = lax.broadcasted_iota(jnp.int32, (1, flux_rows), 1)
    slot = lax.broadcasted_iota(jnp.int32, (chunk, 1), 0)
    column = jnp.transpose(state[...]).astype(BF16)
    tiles = [(top, at) for top in range(0, slots, chunk) for at in range(0, sources, chunk)]

    def gates_of(top, at):
        return jnp.dot(
            column[top : top + chunk], weights[:, at : at + chunk], preferred_element_type=F32
        )

    fluxes = {top: jnp.zeros((chunk, flux_rows), F32) for top in range(0, slots, chunk)}

    def add_flux(top, at, source):
        fluxes[top] = fluxes[top] + jnp.dot(
            source, inverses[at : at + chunk, :], preferred_element_type=F32
        )

    gates = gates_of(*tiles[0])
    before = None
    for i, tile in enumerate(tiles):
        later = gates_of(*tiles[i + 1]) if i + 1 < len(tiles) else None
        source = softplus(gates).astype(BF16)
        if before is not None:
            add_flux(*tiles[i - 1], before)
        gates, before = later, source
    add_flux(*tiles[-1], before)
    for start in range(0, slots, chunk):
        rows = fluxes[start]
        for level in range(mine):
            at = base + level
            plus = (lane == at) | ((lane == at + levels + 1) & (at + 1 < levels))
            minus = (lane == at + levels) | ((lane == at + 1) & (at + 1 < levels))
            terms = jnp.where(plus, rows, 0.0) - jnp.where(minus, rows, 0.0)
            heat = jnp.sum(terms, axis=1, keepdims=True)
            heat = jnp.where(slot + start < count, heat, 0.0).astype(BF16).astype(F32)
            spread[start : start + chunk, level * LANES : (level + 1) * LANES] = (
                heat * interp[start : start + chunk, :].astype(F32)
            ).astype(BF16)
    row = slot_rows(blocks[...], across, lat_pad)
    tiles = max(t for t in range(1, 8) if across % t == 0)
    height = tiles * lat_pad
    copies = []
    for first in range(0, across, tiles):
        match = row == lax.broadcasted_iota(jnp.int32, (height, slots), 0) + first * lat_pad
        left = jnp.where(match, 1.0, 0.0).astype(BF16)
        summed = jnp.dot(left, spread[...], preferred_element_type=F32).astype(BF16)
        for level in range(mine):
            for tile in range(tiles):
                result[level, :, (first + tile) * LANES : (first + tile + 1) * LANES] = summed[
                    tile * lat_pad : tile * lat_pad + lat, level * LANES : (level + 1) * LANES
                ]
        columns = pl.ds(first * LANES, tiles * LANES)
        copies.append(
            pltpu.make_async_copy(
                result.at[:, :, columns], out.at[:, :, columns], sems.at[first // tiles]
            )
        )
        copies[-1].start()
    for copy in copies:
        copy.wait()


def call(kernel, outs, specs, scratch, args, flops, size, name, out_spec=VMEM, limit=LIMIT):
    shapes = [jax.ShapeDtypeStruct(shape, dtype) for shape, dtype in outs]
    single = len(outs) == 1
    return pl.pallas_call(
        kernel,
        out_shape=shapes[0] if single else shapes,
        in_specs=specs,
        out_specs=out_spec if single else [out_spec] * len(outs),
        scratch_shapes=scratch,
        compiler_params=pltpu.CompilerParams(vmem_limit_bytes=limit),
        cost_estimate=pl.CostEstimate(flops=flops, bytes_accessed=size, transcendentals=0),
        name=name,
    )(*args)


def exchange(value, axis, shift):
    return lax.ppermute(value, axis, [(i, i ^ shift) for i in range(lax.axis_size(axis))])


def body(grid, legendre, counts, blocks, interp, source_weights, inverses):
    n_sec = lax.axis_size("sec")
    n_band = lax.axis_size("band")
    n_fld = lax.axis_size("fld")
    lev, lat, lon = grid.shape[1:]
    wave_dev, _, degrees = legendre.shape
    slots = blocks.shape[0]
    across = lon // LANES
    lat_pad = -(-lat // 16) * 16
    rest = 2 * wave_dev // THIRDS
    piece = rest * lev
    block_row = blocks.reshape(1, slots)

    table = jnp.asarray(dft_table(lon, wave_dev, n_band, n_fld))
    group = n_fld * n_band * rest
    padded_group = -(-group // LANES) * LANES
    depth = -(-across * lat_pad // LANES) * LANES
    state_blocks = slots * lev // LANES // piece
    message_blocks = n_band + state_blocks
    messages = call(
        functools.partial(local_kernel, lat_pad),
        [((message_blocks, piece, LANES), BF16)] * n_fld,
        [HBM] * 4,
        [
            pltpu.VMEM((lev, lat, lon), BF16),
            pltpu.VMEM((1, slots), jnp.int32),
            pltpu.VMEM((slots, LANES), BF16),
            pltpu.VMEM(table.shape, BF16),
            pltpu.VMEM((depth, lev * LANES), BF16),
            pltpu.VMEM((slots, LANES), jnp.int32),
            pltpu.VMEM((slots, depth), BF16),
            pltpu.VMEM((lev, LANES, padded_group), F32),
            pltpu.VMEM((group * lev, LANES), F32),
            pltpu.VMEM((slots, LANES), F32),
            pltpu.SemaphoreType.DMA((lev + 3,)),
        ],
        [
            pltpu.with_memory_space_constraint(value, pltpu.HBM)
            for value in (grid.reshape(lev, lat, lon), block_row, interp, table)
        ],
        2 * slots * depth * lev * LANES + 2 * lev * lat * lon * THIRDS * group,
        2 * lev * lat * lon + 2 * slots * LANES,
        "local",
        VMEM,
        WHOLE,
    )
    half = n_fld // 2
    shifts = [half] + list(range(n_fld - 1, half, -1)) + list(range(half - 1, 0, -1))
    arrived = [exchange(messages[shift], "fld", shift) for shift in shifts]
    arrived.append(messages[0])
    spec_bands, flux_rows, _ = inverses.shape
    basis, inverse_rows = call(
        functools.partial(prepare_kernel, lat, n_band),
        [
            ((n_band, 2, THIRDS * degrees, LANES), BF16),
            ((spec_bands * flux_rows, flux_rows), BF16),
        ],
        [VMEM, VMEM],
        [
            pltpu.VMEM((degrees, (n_band * lat // LANES + 2) * LANES), F32),
            pltpu.VMEM((flux_rows * flux_rows, spec_bands), F32),
            pltpu.VMEM((spec_bands * flux_rows, flux_rows), F32),
        ],
        (jnp.swapaxes(legendre, 1, 2), jnp.transpose(inverses, (1, 2, 0))),
        0,
        8 * wave_dev * degrees * n_band * LANES,
        "prepare",
    )
    sent, near = call(
        functools.partial(regroup_kernel, n_sec, n_band, (*shifts, 0)),
        [
            ((n_sec * n_band, n_fld, piece, LANES), BF16),
            ((n_fld, state_blocks, piece, LANES), BF16),
        ],
        [HBM] * (n_fld + 1),
        [pltpu.SemaphoreType.DMA((n_fld * (1 + n_sec),))],
        (*arrived, basis),
        0,
        4 * n_sec * n_band * n_fld * piece * LANES,
        "regroup",
        HBM,
        SMALL,
    )
    far = exchange(near, "sec", 1)
    pieces = lax.all_to_all(sent, ("sec", "band"), 0, 0, tiled=True)
    sources = spec_bands * flux_rows
    states = source_weights.shape[0]
    mine = n_sec * lev // (n_sec * n_fld)
    heating = call(
        functools.partial(column_kernel, n_sec, n_fld, lat_pad, slots),
        [((mine, lat, lon), BF16)],
        [SMEM] + [VMEM] * 6,
        [
            pltpu.VMEM((states, slots), F32),
            pltpu.VMEM((slots, mine * LANES), BF16),
            pltpu.VMEM((mine, lat, lon), BF16),
            pltpu.SemaphoreType.DMA((across,)),
        ],
        (counts, source_weights, inverse_rows, block_row, interp, near, far),
        8 * slots * slots * 1024,
        2 * slots * slots,
        "columns",
        HBM,
    )

    spectral = call(
        functools.partial(legendre_kernel, n_sec, n_band, n_fld, lev),
        [((wave_dev, 2, n_fld, n_sec * lev, degrees), BF16)],
        [VMEM, VMEM],
        [
            pltpu.VMEM((wave_dev, 2, n_fld, n_sec * lev, degrees), BF16),
            pltpu.SemaphoreType.DMA((wave_dev,)),
        ],
        (basis, pieces),
        4 * n_sec * n_fld * piece * n_band * LANES * degrees * THIRDS,
        2 * n_sec * n_band * n_fld * piece * LANES,
        "legendre",
        HBM,
    )
    return (spectral, heating)


def solution(mesh):
    return jax.shard_map(
        body,
        mesh=mesh,
        in_specs=(
            P("fld", "sec", "band", None),
            P(("band", "fld"), None, "sec"),
            P(),
            P("band"),
            P("band", None),
            P(),
            P(),
        ),
        out_specs=(P(("band", "fld"), None, None, None, "sec"), P(("sec", "fld"), "band", None)),
        check_vma=False,
    )
```

```python
import functools
import math

import jax
import jax.numpy as jnp
import numpy as np
from jax import lax
from jax.experimental import pallas as pl
from jax.experimental.pallas import tpu as pltpu
from jax.sharding import PartitionSpec as P

BF16 = jnp.bfloat16
F32 = jnp.float32
LANES = 128
THIRDS = 3
VMEM = pl.BlockSpec(memory_space=pltpu.VMEM)
HBM = pl.BlockSpec(memory_space=pltpu.HBM)
SMEM = pl.BlockSpec(memory_space=pltpu.SMEM)
LIMIT = 40 * 1024 * 1024
SMALL = 4 * 1024 * 1024
ROOM = 12000 * 1024
WHOLE = 64 * 1024 * 1024 - ROOM
NT = (((1,), (1,)), ((), ()))


def dft_table(lon, wave_dev, n_band, n_fld):
    values_dev = 2 * wave_dev
    rest = values_dev // THIRDS
    third, fld, band, low = np.meshgrid(
        np.arange(THIRDS), np.arange(n_fld), np.arange(n_band), np.arange(rest), indexing="ij"
    )
    value = third * rest + low
    wave = ((band * n_fld + fld) * wave_dev + value // 2).reshape(-1)
    part = (value % 2).reshape(-1)
    phase = np.arange(lon, dtype=np.int64)[:, None] * wave[None, :] % lon
    angle = phase * (2.0 * math.pi / lon)
    values = np.where(part[None, :] == 0, np.cos(angle), -np.sin(angle)) / math.sqrt(lon)
    return values.astype(np.float32).astype(BF16)


def pack(lev, lat, coeffs, padded, rows):
    group = coeffs.shape[1] // THIRDS
    padded[...] = jnp.zeros_like(padded)
    for level in range(lev):
        for third in range(THIRDS):
            padded[third * lat : (third + 1) * lat, :group] = coeffs[
                level * lat : (level + 1) * lat, third * group : (third + 1) * group
            ]
        rows[pl.ds(level, group, stride=lev), :] = jnp.transpose(padded[...])[:group]


def prepare_kernel(lat, n_band, legendre, inverses, out, out_inverses, wide, rows, turned):
    flux_rows, _, spec_bands = inverses.shape
    for row in range(flux_rows):
        rows[row * flux_rows : (row + 1) * flux_rows, :] = inverses[row].astype(F32)
    for row in range(flux_rows):
        turned[pl.ds(row, spec_bands, stride=flux_rows), :] = jnp.transpose(
            rows[pl.ds(row, flux_rows, stride=flux_rows), :]
        )
    out_inverses[...] = turned[...].astype(BF16)
    waves, degrees, _ = legendre.shape
    wide[...] = jnp.zeros_like(wide)
    lane = lax.broadcasted_iota(jnp.int32, (degrees, LANES), 1)
    for wave in range(waves):
        third, parity = wave // 2, wave % 2
        wide[:, : n_band * lat] = legendre[wave].astype(F32)
        place = third * lat
        live = (lane >= place) & (lane < place + lat)
        for band in range(n_band):
            base = band * lat // LANES * LANES
            moved = pltpu.roll(
                wide[:, base : base + 2 * LANES], (place - (band * lat - base)) % (2 * LANES), 1
            )
            out[band, parity, third * degrees : (third + 1) * degrees, :] = jnp.where(
                live, moved[:, :LANES], 0.0
            ).astype(BF16)


def legendre_kernel(n_sec, n_band, n_fld, lev, weights, pieces, out_hbm, out, sems):
    degrees = out.shape[4]
    copies = []
    half = pieces.shape[2] // 2
    for parity in range(2):
        rows = slice(parity * half, (parity + 1) * half)
        basis = jnp.concatenate([weights[band, parity] for band in range(n_band)], axis=1)
        left = jnp.concatenate(
            [
                jnp.concatenate(
                    [
                        pieces[sec * n_band + band, fld, rows, :]
                        for band in range(n_band)
                    ],
                    axis=1,
                )
                for fld in range(n_fld)
                for sec in range(n_sec)
            ],
            axis=0,
        )
        result = lax.dot_general(left, basis, NT, preferred_element_type=F32)
        for third in range(THIRDS):
            part = result[:, third * degrees : (third + 1) * degrees]
            for fld in range(n_fld):
                for real in range(2):
                    levels = [
                        part[(fld * n_sec + sec) * half + real * lev :][:lev]
                        for sec in range(n_sec)
                    ]
                    out[2 * third + parity, real, fld] = jnp.concatenate(levels, axis=0).astype(
                        BF16
                    )
            wave = 2 * third + parity
            copies.append(
                pltpu.make_async_copy(out.at[wave], out_hbm.at[wave], sems.at[wave])
            )
            copies[-1].start()
    for copy in copies:
        copy.wait()


def slot_rows(blocks, across, lat_pad):
    shift = 16
    factor = -(-(1 << shift) // across)
    lat = lax.shift_right_logical(blocks * factor, shift)
    return (blocks - lat * across) * lat_pad + lat


def local_kernel(lat_pad, grid_hbm, blocks_hbm, interp_hbm, table_hbm, *refs):
    outs = refs[:-11]
    grid, blocks, interp, table, patch, column, selector, padded, rows, totals, sems = refs[-11:]
    lev, lat, lon = grid.shape
    across = lon // LANES
    slots = interp.shape[0]
    depth = patch.shape[0]
    small = [
        pltpu.make_async_copy(blocks_hbm, blocks, sems.at[lev]),
        pltpu.make_async_copy(interp_hbm, interp, sems.at[lev + 1]),
        pltpu.make_async_copy(table_hbm, table, sems.at[lev + 2]),
    ]
    loads = [
        pltpu.make_async_copy(
            grid_hbm.at[pl.ds(level, 1)], grid.at[pl.ds(level, 1)], sems.at[level]
        )
        for level in range(lev)
    ]
    half = lev // 2
    small[0].start()
    for copy in loads[:half]:
        copy.start()
    small[1].start()
    for copy in loads[half:]:
        copy.start()
    small[2].start()
    small[0].wait()
    row = slot_rows(blocks[...], across, lat_pad)
    column[...] = jnp.transpose(jnp.broadcast_to(row, (LANES, slots)))
    chunk = 256
    lane = lax.broadcasted_iota(jnp.int32, (chunk, LANES), 1)
    for start in range(0, slots, chunk):
        mine = column[start : start + chunk, :]
        for base in range(0, depth, LANES):
            selector[start : start + chunk, base : base + LANES] = jnp.where(
                mine == lane + base, 1.0, 0.0
            ).astype(BF16)
    size = outs[0].shape[1]
    bands = outs[0].shape[0] - slots * lev // LANES // size
    place = lax.axis_index("fld")
    for tile in range(across):
        patch[tile * lat_pad + lat : (tile + 1) * lat_pad, :] = jnp.zeros(
            (lat_pad - lat, lev * LANES), BF16
        )
    if depth > across * lat_pad:
        patch[across * lat_pad :, :] = jnp.zeros((depth - across * lat_pad, lev * LANES), BF16)
    for base in (0,):
        for level in range(lev):
            loads[level].wait()
            for tile in range(across):
                patch[
                    tile * lat_pad : tile * lat_pad + lat, level * LANES : (level + 1) * LANES
                ] = grid[level, :, tile * LANES : (tile + 1) * LANES]
        small[1].wait()
        for start in range(0, slots, chunk):
            top = slice(start, start + chunk)
            picked = jnp.dot(
                selector[top, :],
                patch[...],
                preferred_element_type=F32,
            )
            weights = interp[top, :].astype(F32)
            total = jnp.zeros((chunk, LANES), F32)
            for i in range(lev):
                product = picked[:, i * LANES : (i + 1) * LANES] * weights
                total = jnp.where(
                    lane == i, jnp.sum(product, axis=1, keepdims=True), total
                )
            state = jnp.transpose(total)[:lev].astype(BF16)
            for tile in range(chunk // LANES):
                block, row = divmod((start // LANES + tile) * lev, size)
                for out in outs:
                    out[bands + block, row : row + lev, :] = state[
                        :, tile * LANES : (tile + 1) * LANES
                    ]
            if start == chunk:
                small[2].wait()
                flat = jnp.concatenate([grid[level] for level in range(lev)], axis=0)
                coeffs = jnp.dot(flat, table[...], preferred_element_type=F32)
                pack(lev, lat, coeffs, padded, rows)
                height = bands * size
                for shift, out in enumerate(outs):
                    first = pl.multiple_of((place ^ shift) * height, height)
                    part = rows[pl.ds(first, height), :].astype(BF16)
                    out[:bands] = part.reshape(bands, size, LANES)


def regroup_kernel(n_sec, n_band, shifts, *refs):
    pieces, (_, out, out_state, sems) = refs[:-4], refs[-4:]
    blocks = out_state.shape[1]
    place = lax.axis_index("fld")
    copies = []
    for shift, piece in zip(shifts, pieces):
        fld = place ^ shift
        copies.append((piece.at[pl.ds(n_band, blocks)], out_state.at[fld]))
        for sec in range(n_sec):
            copies.append(
                (piece.at[pl.ds(0, n_band)], out.at[pl.ds(sec * n_band, n_band), fld])
            )
    copies = [pltpu.make_async_copy(*pair, sems.at[i]) for i, pair in enumerate(copies)]
    for copy in copies:
        copy.start()
    for copy in copies:
        copy.wait()


def softplus(x):
    power = jnp.exp(jnp.minimum(x, 80.0))
    return jnp.where(x < -8.0, power, jnp.maximum(x, jnp.log(1.0 + power)))


def column_kernel(n_sec, n_fld, lat_pad, slots, counts, weights, inverses, blocks, interp,
                  near, far, out, state, spread, result, sems):
    lev = near.shape[1] * near.shape[2] * LANES // slots
    place = lax.axis_index("sec")
    for fld in range(n_fld):
        for shift, pieces in enumerate((near, far)):
            row = (fld * n_sec + (place ^ shift)) * lev
            for tile in range(slots // LANES):
                state[
                    pl.ds(pl.multiple_of(row, lev), lev), tile * LANES : (tile + 1) * LANES
                ] = pieces[fld, tile * lev // near.shape[2]][
                    tile * lev % near.shape[2] : tile * lev % near.shape[2] + lev
                ].astype(F32)
    mine, lat, lon = result.shape
    across = lon // LANES
    sources, flux_rows = inverses.shape
    levels = flux_rows // 2
    count = counts[lax.axis_index("band")]
    base = (place * n_fld + lax.axis_index("fld")) * mine
    chunk = 256
    lane = lax.broadcasted_iota(jnp.int32, (1, flux_rows), 1)
    slot = lax.broadcasted_iota(jnp.int32, (chunk, 1), 0)
    column = jnp.transpose(state[...]).astype(BF16)
    tiles = [(top, at) for top in range(0, slots, chunk) for at in range(0, sources, chunk)]

    def gates_of(top, at):
        return jnp.dot(
            column[top : top + chunk], weights[:, at : at + chunk], preferred_element_type=F32
        )

    fluxes = {top: jnp.zeros((chunk, flux_rows), F32) for top in range(0, slots, chunk)}

    def add_flux(top, at, source):
        fluxes[top] = fluxes[top] + jnp.dot(
            source, inverses[at : at + chunk, :], preferred_element_type=F32
        )

    gates = gates_of(*tiles[0])
    before = None
    for i, tile in enumerate(tiles):
        later = gates_of(*tiles[i + 1]) if i + 1 < len(tiles) else None
        source = softplus(gates).astype(BF16)
        if before is not None:
            add_flux(*tiles[i - 1], before)
        gates, before = later, source
    add_flux(*tiles[-1], before)
    for start in range(0, slots, chunk):
        rows = fluxes[start]
        for level in range(mine):
            at = base + level
            plus = (lane == at) | ((lane == at + levels + 1) & (at + 1 < levels))
            minus = (lane == at + levels) | ((lane == at + 1) & (at + 1 < levels))
            terms = jnp.where(plus, rows, 0.0) - jnp.where(minus, rows, 0.0)
            heat = jnp.sum(terms, axis=1, keepdims=True)
            heat = jnp.where(slot + start < count, heat, 0.0).astype(BF16).astype(F32)
            spread[start : start + chunk, level * LANES : (level + 1) * LANES] = (
                heat * interp[start : start + chunk, :].astype(F32)
            ).astype(BF16)
    row = slot_rows(blocks[...], across, lat_pad)
    tiles = max(t for t in range(1, 8) if across % t == 0)
    height = tiles * lat_pad
    copies = []
    for first in range(0, across, tiles):
        match = row == lax.broadcasted_iota(jnp.int32, (height, slots), 0) + first * lat_pad
        left = jnp.where(match, 1.0, 0.0).astype(BF16)
        summed = jnp.dot(left, spread[...], preferred_element_type=F32).astype(BF16)
        for level in range(mine):
            for tile in range(tiles):
                result[level, :, (first + tile) * LANES : (first + tile + 1) * LANES] = summed[
                    tile * lat_pad : tile * lat_pad + lat, level * LANES : (level + 1) * LANES
                ]
        columns = pl.ds(first * LANES, tiles * LANES)
        copies.append(
            pltpu.make_async_copy(
                result.at[:, :, columns], out.at[:, :, columns], sems.at[first // tiles]
            )
        )
        copies[-1].start()
    for copy in copies:
        copy.wait()


def call(kernel, outs, specs, scratch, args, flops, size, name, out_spec=VMEM, limit=LIMIT):
    shapes = [jax.ShapeDtypeStruct(shape, dtype) for shape, dtype in outs]
    single = len(outs) == 1
    return pl.pallas_call(
        kernel,
        out_shape=shapes[0] if single else shapes,
        in_specs=specs,
        out_specs=out_spec if single else [out_spec] * len(outs),
        scratch_shapes=scratch,
        compiler_params=pltpu.CompilerParams(vmem_limit_bytes=limit),
        cost_estimate=pl.CostEstimate(flops=flops, bytes_accessed=size, transcendentals=0),
        name=name,
    )(*args)


def exchange(value, axis, shift):
    return lax.ppermute(value, axis, [(i, i ^ shift) for i in range(lax.axis_size(axis))])


def body(grid, legendre, counts, blocks, interp, source_weights, inverses):
    n_sec = lax.axis_size("sec")
    n_band = lax.axis_size("band")
    n_fld = lax.axis_size("fld")
    lev, lat, lon = grid.shape[1:]
    wave_dev, _, degrees = legendre.shape
    slots = blocks.shape[0]
    across = lon // LANES
    lat_pad = -(-lat // 16) * 16
    rest = 2 * wave_dev // THIRDS
    piece = rest * lev
    block_row = blocks.reshape(1, slots)

    table = jnp.asarray(dft_table(lon, wave_dev, n_band, n_fld))
    group = n_fld * n_band * rest
    padded_group = -(-group // LANES) * LANES
    depth = -(-across * lat_pad // LANES) * LANES
    state_blocks = slots * lev // LANES // piece
    message_blocks = n_band + state_blocks
    messages = call(
        functools.partial(local_kernel, lat_pad),
        [((message_blocks, piece, LANES), BF16)] * n_fld,
        [HBM] * 4,
        [
            pltpu.VMEM((lev, lat, lon), BF16),
            pltpu.VMEM((1, slots), jnp.int32),
            pltpu.VMEM((slots, LANES), BF16),
            pltpu.VMEM(table.shape, BF16),
            pltpu.VMEM((depth, lev * LANES), BF16),
            pltpu.VMEM((slots, LANES), jnp.int32),
            pltpu.VMEM((slots, depth), BF16),
            pltpu.VMEM((LANES, padded_group), F32),
            pltpu.VMEM((group * lev, LANES), F32),
            pltpu.VMEM((slots, LANES), F32),
            pltpu.SemaphoreType.DMA((lev + 3,)),
        ],
        [
            pltpu.with_memory_space_constraint(value, pltpu.HBM)
            for value in (grid.reshape(lev, lat, lon), block_row, interp, table)
        ],
        2 * slots * depth * lev * LANES + 2 * lev * lat * lon * THIRDS * group,
        2 * lev * lat * lon + 2 * slots * LANES,
        "local",
        VMEM,
        WHOLE,
    )
    half = n_fld // 2
    shifts = [half] + list(range(n_fld - 1, half, -1)) + list(range(half - 1, 0, -1))
    arrived = [exchange(messages[shift], "fld", shift) for shift in shifts]
    arrived.append(messages[0])
    spec_bands, flux_rows, _ = inverses.shape
    basis, inverse_rows = call(
        functools.partial(prepare_kernel, lat, n_band),
        [
            ((n_band, 2, THIRDS * degrees, LANES), BF16),
            ((spec_bands * flux_rows, flux_rows), BF16),
        ],
        [VMEM, VMEM],
        [
            pltpu.VMEM((degrees, (n_band * lat // LANES + 2) * LANES), F32),
            pltpu.VMEM((flux_rows * flux_rows, spec_bands), F32),
            pltpu.VMEM((spec_bands * flux_rows, flux_rows), F32),
        ],
        (jnp.swapaxes(legendre, 1, 2), jnp.transpose(inverses, (1, 2, 0))),
        0,
        8 * wave_dev * degrees * n_band * LANES,
        "prepare",
    )
    sent, near = call(
        functools.partial(regroup_kernel, n_sec, n_band, (*shifts, 0)),
        [
            ((n_sec * n_band, n_fld, piece, LANES), BF16),
            ((n_fld, state_blocks, piece, LANES), BF16),
        ],
        [HBM] * (n_fld + 1),
        [pltpu.SemaphoreType.DMA((n_fld * (1 + n_sec),))],
        (*arrived, basis),
        0,
        4 * n_sec * n_band * n_fld * piece * LANES,
        "regroup",
        HBM,
        SMALL,
    )
    far = exchange(near, "sec", 1)
    pieces = lax.all_to_all(sent, ("sec", "band"), 0, 0, tiled=True)
    sources = spec_bands * flux_rows
    states = source_weights.shape[0]
    mine = n_sec * lev // (n_sec * n_fld)
    heating = call(
        functools.partial(column_kernel, n_sec, n_fld, lat_pad, slots),
        [((mine, lat, lon), BF16)],
        [SMEM] + [VMEM] * 6,
        [
            pltpu.VMEM((states, slots), F32),
            pltpu.VMEM((slots, mine * LANES), BF16),
            pltpu.VMEM((mine, lat, lon), BF16),
            pltpu.SemaphoreType.DMA((across,)),
        ],
        (counts, source_weights, inverse_rows, block_row, interp, near, far),
        8 * slots * slots * 1024,
        2 * slots * slots,
        "columns",
        HBM,
    )

    spectral = call(
        functools.partial(legendre_kernel, n_sec, n_band, n_fld, lev),
        [((wave_dev, 2, n_fld, n_sec * lev, degrees), BF16)],
        [VMEM, VMEM],
        [
            pltpu.VMEM((wave_dev, 2, n_fld, n_sec * lev, degrees), BF16),
            pltpu.SemaphoreType.DMA((wave_dev,)),
        ],
        (basis, pieces),
        4 * n_sec * n_fld * piece * n_band * LANES * degrees * THIRDS,
        2 * n_sec * n_band * n_fld * piece * LANES,
        "legendre",
        HBM,
    )
    return (spectral, heating)


def solution(mesh):
    return jax.shard_map(
        body,
        mesh=mesh,
        in_specs=(
            P("fld", "sec", "band", None),
            P(("band", "fld"), None, "sec"),
            P(),
            P("band"),
            P("band", None),
            P(),
            P(),
        ),
        out_specs=(P(("band", "fld"), None, None, None, "sec"), P(("sec", "fld"), "band", None)),
        check_vma=False,
    )
```
